32 devices in a mesh: tm: 4 (over y, core), sx: 4 (over z), sy: 2 (over x).
Axes of the slice: x: 2, y: 2, z: 4, core: 2. Of those that a mesh axis runs over, the one named last changes fastest.
Arguments:
- snapshots: bfloat16 [1536, 4, 4096], P('tm', None, ('sx', 'sy')), may hold values from -12 to 12, as said below
- weights: float32 [4096], P(('sx', 'sy')), may hold values from 0.2 to 18, as said below
- block_order: int32 [4], replicated, may hold values from 0 to 3, each once
- owner: int32 [8, 4], P(('sx', 'sy')), may hold values from 0 to 3, as said below
- offsets: int32 [11], replicated, may hold values from 0 to 1280, as said below
Outputs:
- modes: bfloat16 [2, 128, 11, 4, 4096], P(None, None, None, 'tm', ('sx', 'sy'))
- gram: float32 [2, 128, 11, 11], P(None, ('sx', 'sy'))
The draws below stay inside these ranges and needn't reach their ends.
Inputs may be any that keep to these rules, and one draw needn't show every extreme that they name: snapshots: noisy records with a few time signals in common across points. Positive weights. `block_order`: a permutation of the time blocks. `owner`: each row a permutation of the slots. Strictly increasing; offsets[0] = 0 and offsets[10] = 1280.
All inputs are finite; a program needn't handle non-finite values.
Results may differ from the reference program's by a relative error of at most 0.012.
Values may be sent and summed in bfloat16 or wider, within the bound.
No kernel may reach another device: no remote copies, remote signals or barrier semaphores. Data moves between devices by JAX's collectives and lax.ppermute only.
A program may use at most 64 MiB of HBM per device.

```python
import math
import jax
import jax.numpy as jnp
from jax import lax

SAMPLES = 1536
NFFT = 256
NBLK = 11
ROOT_STEPS = 5
NFREQ = 128
LANES = 4
SPACE_GROUPS = 8
POINTS = 4096


def owner_table(key):
    row_keys = jax.random.split(jax.random.fold_in(key, 11), SPACE_GROUPS)

    def one_row(row_key):
        return jax.random.permutation(row_key, LANES)
    return jax.vmap(one_row)(row_keys).astype(jnp.int32)


def draw_owner(key, part):
    table = owner_table(key)
    return table


def draw_snapshots(key, part):
    table = owner_table(key)
    key = jax.random.fold_in(key, 3)
    noise_key = jax.random.fold_in(key, 0)
    signal_key = jax.random.fold_in(key, 1)
    load_key = jax.random.fold_in(key, 2)
    slot_key = jax.random.fold_in(key, 4)
    group_key = jax.random.fold_in(key, 5)
    full_shape = (SAMPLES, LANES, POINTS)
    signals = jax.random.normal(signal_key, (3, SAMPLES), jnp.float32)
    loads = jax.random.normal(load_key, (3, LANES, POINTS), jnp.float32)
    slot_level = jax.random.uniform(slot_key, (3, LANES), jnp.float32, -1.5, 1.5)
    group_level = jax.random.uniform(group_key, (3, SPACE_GROUPS), jnp.float32, -2.5, 2.5)
    lane_level = jnp.transpose(slot_level[:, table], (0, 2, 1))
    level = lane_level + group_level[:, None, :]
    level = jnp.repeat(level, POINTS // SPACE_GROUPS, axis=2)
    gains = jnp.exp(level)
    scale_down = 1.0 / jnp.sqrt(1.0 + jnp.sum(gains * gains, axis=0))
    shaped = gains * loads
    noise = jax.random.normal(noise_key, full_shape, jnp.float32)
    amplitude = 1.3
    common = signals[0][:, None, None] * shaped[0][None] + signals[1][:, None, None] * shaped[1][None] + signals[2][:, None, None] * shaped[2][None]
    return jnp.clip((noise + common) * (amplitude * scale_down)[None], -12.0, 12.0).astype(jnp.bfloat16)


def draw_weights(key, part):
    key = jax.random.fold_in(key, 5)
    spread = jnp.exp(jax.random.uniform(key, (POINTS,), jnp.float32, math.log(0.2), math.log(2.0)))
    rising = 1.0 + 2.0 * jnp.arange(POINTS, dtype=jnp.float32) / POINTS
    return spread * rising


def draw_offsets(key, part):
    key = jax.random.fold_in(key, 7)
    hop_size = (SAMPLES - NFFT) // (NBLK - 1)
    reach = hop_size // 4
    jitter = jax.random.randint(key, (NBLK,), -reach, reach + 1)
    block_ids = jnp.arange(NBLK, dtype=jnp.int32)
    base_start = block_ids * (SAMPLES - NFFT) // (NBLK - 1)
    inner = (block_ids > 0) & (block_ids < NBLK - 1)
    return jnp.where(inner, base_start + jitter, base_start).astype(jnp.int32)


def setup_inputs(seed: int = 0) -> dict:
    key_of = jax.random.split(jax.random.key(seed), 6)
    snapshots = draw_snapshots(jax.random.fold_in(key_of[5], 71), 0)
    weights = draw_weights(jax.random.fold_in(key_of[5], 71), 0)
    block_order = jax.random.permutation(key_of[2], LANES).astype(jnp.int32)
    owner = draw_owner(jax.random.fold_in(key_of[5], 71), 0)
    offsets = draw_offsets(jax.random.fold_in(key_of[5], 71), 0)
    return dict(snapshots=snapshots, weights=weights, block_order=block_order, owner=owner, offsets=offsets)


def fourier_table(window_len, freq_count):
    sample_ids = jnp.arange(window_len, dtype=jnp.int32)
    freq_ids = jnp.arange(freq_count, dtype=jnp.int32)
    angles = (freq_ids[:, None] * sample_ids[None, :] % window_len).astype(jnp.float32) * (2.0 * math.pi / window_len)
    window = 0.5 - 0.5 * jnp.cos(sample_ids.astype(jnp.float32) * (2.0 * math.pi / window_len))
    scaled = window / jnp.sqrt(jnp.float32(0.375 * window_len))
    return jnp.concatenate([jnp.cos(angles) * scaled[None, :], -jnp.sin(angles) * scaled[None, :]], axis=0)

def spectra(record, offsets, fourier):
    window_len = fourier.shape[1]
    freq_count = fourier.shape[0] // 2
    points = record.shape[1]
    block_count = offsets.shape[0]

    def cut_block(offset_at):
        return lax.dynamic_slice_in_dim(record, offset_at, window_len, 0)
    blocks = jax.vmap(cut_block)(offsets)
    coeffs = jnp.einsum('rn,bnp->brp', fourier, blocks.astype(jnp.float32), precision=lax.Precision.HIGHEST)
    coeffs = coeffs.reshape(block_count, 2, freq_count, points).transpose(2, 1, 0, 3)
    return coeffs.reshape(freq_count, 2 * block_count, points)

def weighted_gram(spectrum, weights):
    full_gram = jnp.einsum('kap,kbp->kab', spectrum * weights[None, None, :], spectrum, precision=lax.Precision.HIGHEST)
    half_size = full_gram.shape[1] // 2
    real_part = full_gram[:, :half_size, :half_size] + full_gram[:, half_size:, half_size:]
    imag_part = full_gram[:, :half_size, half_size:] - full_gram[:, half_size:, :half_size]
    return jnp.stack([real_part, imag_part], axis=0)

def inverse_root(gram_sum):
    real_part = gram_sum[0]
    imag_part = gram_sum[1]
    upper_rows = jnp.concatenate([real_part, -imag_part], axis=2)
    bottom = jnp.concatenate([imag_part, real_part], axis=2)
    embedded = jnp.concatenate([upper_rows, bottom], axis=1)
    stacked = jnp.transpose(embedded, (1, 2, 0))
    order_size = stacked.shape[0]
    unit_matrix = jnp.eye(order_size, dtype=jnp.float32)[:, :, None]
    trace_sum = lax.optimization_barrier(jnp.sum(jnp.diagonal(stacked, axis1=0, axis2=1), axis=-1))
    current = stacked / trace_sum[None, None, :]
    other = jnp.broadcast_to(unit_matrix, stacked.shape)
    for iteration in range(ROOT_STEPS):
        factor = 1.5 * unit_matrix - 0.5 * jnp.einsum('abk,bck->ack', other, current, precision=lax.Precision.HIGHEST)
        current = jnp.einsum('abk,bck->ack', current, factor, precision=lax.Precision.HIGHEST)
        other = jnp.einsum('abk,bck->ack', factor, other, precision=lax.Precision.HIGHEST)
    root_full = other / jnp.sqrt(trace_sum)[None, None, :]
    half_size = order_size // 2
    real_root = root_full[:half_size, :half_size]
    imag_root = root_full[half_size:, :half_size]
    upper = jnp.concatenate([real_root, imag_root], axis=1)
    lower = jnp.concatenate([-imag_root, real_root], axis=1)
    return jnp.transpose(jnp.concatenate([upper, lower], axis=0), (2, 0, 1))

def mode_fields(spectrum, root_maps):
    fields = jnp.einsum('kap,kam->kmp', spectrum, root_maps, precision=lax.Precision.HIGHEST)
    freq_count = fields.shape[0]
    block_count = fields.shape[1] // 2
    fields = fields.reshape(freq_count, 2, block_count, fields.shape[2]).transpose(1, 0, 2, 3)
    return fields.astype(jnp.bfloat16)

def reference(snapshots, weights, block_order, owner, offsets):
    fourier = fourier_table(NFFT, NFREQ)
    slot_ids = jnp.arange(LANES, dtype=jnp.int32)
    groups = owner.shape[0]
    sender = lax.optimization_barrier(jnp.sum(jnp.where(owner[:, None, :] == slot_ids[None, :, None], slot_ids[None, None, :], 0), axis=2)).astype(jnp.int32)
    lane_of = jnp.repeat(sender, POINTS // groups, axis=0).T
    arrival = lax.optimization_barrier(jnp.sum(jnp.where(block_order[None, :] == slot_ids[:, None], slot_ids[None, :], 0), axis=1)).astype(jnp.int32)

    def record_for(slot_id):
        lane_index = jnp.broadcast_to(lane_of[slot_id][None, None, :], (SAMPLES, 1, POINTS))
        chosen = jnp.take_along_axis(snapshots, lane_index, axis=1)[:, 0, :]
        pieces = chosen.reshape(LANES, SAMPLES // LANES, POINTS)
        return jnp.take(pieces, arrival, axis=0).reshape(SAMPLES, POINTS)

    def accumulate(running, slot_id):
        spectrum = spectra(record_for(slot_id), offsets, fourier)
        return (running + weighted_gram(spectrum, weights), None)
    start_sum = jnp.zeros((2, NFREQ, NBLK, NBLK), jnp.float32)
    gram_sum, unused = lax.scan(accumulate, start_sum, slot_ids)
    gram_sum = gram_sum / (LANES * POINTS)
    root_maps = inverse_root(gram_sum)

    def shape_modes(slot_id):
        return mode_fields(spectra(record_for(slot_id), offsets, fourier), root_maps)
    stacked = lax.map(shape_modes, slot_ids)
    return (jnp.transpose(stacked, (1, 2, 3, 0, 4)), gram_sum)
```

```python
import functools
import math

import jax
import jax.numpy as jnp
import numpy as np
from jax import lax
from jax.experimental import pallas as pl
from jax.experimental.pallas import tpu as pltpu
from jax.sharding import PartitionSpec as P

NFFT = 256
ROOT_STEPS = 5
NFREQ = 128
NBLK = 11
LANE = 128
SUB = 8
HALF_ROWS = NBLK * SUB
GROUPS = NFREQ // SUB
PAIRS = (NBLK + 1) // 2
PAIR_ROWS = 24
PACKED = PAIRS * PAIR_ROWS
STACK = 4
BF16 = jnp.bfloat16
F32 = jnp.float32


def fourier_tables():
    n = np.arange(NFFT)
    k = np.arange(NFREQ)
    angles = 2.0 * np.pi * ((k[:, None] * n[None, :]) % NFFT) / NFFT
    scaled = (0.5 - 0.5 * np.cos(2.0 * np.pi * n / NFFT)) / math.sqrt(0.375 * NFFT)
    table = np.concatenate([np.cos(angles) * scaled, -np.sin(angles) * scaled], axis=0)
    high = table.astype(jnp.bfloat16)
    low = (table - high.astype(np.float64)).astype(jnp.bfloat16)
    return np.stack([high, low])


def packed_rows():
    rows = {}
    for pair in range(PAIRS):
        row = pair * PAIR_ROWS
        for a in sorted({pair, NBLK - 1 - pair}):
            for e in range(a, NBLK):
                rows[0, a, e] = row
                row += 1
            for e in range(a + 1, NBLK):
                rows[1, a, e] = row
                row += 1
    return rows


def pick_table():
    pick = np.zeros((NBLK, PAIR_ROWS, 2 * LANE), np.float32)
    for (part, a, e), row in packed_rows().items():
        start = part * LANE + e * SUB
        pick[a, row % PAIR_ROWS, start : start + SUB] = 1.0
    return pick.astype(jnp.bfloat16)


def spread_table():
    spread = np.zeros((STACK, 2, LANE, 2 * HALF_ROWS), np.float32)
    for m in range(STACK):
        for b in range(NBLK):
            real = m * 32 + b
            imag = m * 32 + 16 + b
            first = slice(b * SUB, b * SUB + SUB)
            second = slice(HALF_ROWS + b * SUB, HALF_ROWS + b * SUB + SUB)
            spread[m, 0, real, first] = 1.0
            spread[m, 0, imag, second] = 1.0
            spread[m, 1, imag, first] = -1.0
            spread[m, 1, real, second] = 1.0
    return spread.reshape(STACK * 2, LANE, 2 * HALF_ROWS).astype(jnp.bfloat16)


def split(x):
    high = x.astype(BF16)
    return high, (x - high.astype(F32)).astype(BF16)


def dot(a, b):
    return jnp.dot(a, b, preferred_element_type=F32)


def dot_nt(a, b):
    return lax.dot_general(a, b, (((1,), (1,)), ((), ())), preferred_element_type=F32)


def spec(shape):
    return pl.BlockSpec(shape, lambda *_: (0,) * len(shape))


SMEM = pl.BlockSpec(memory_space=pltpu.SMEM)


def pack_kernel(owner_ref, x_ref, *out_refs):
    steps, lanes, width = x_ref.shape
    me = lax.axis_index("tm")
    rows = 2 * LANE // lanes
    out_row = lax.broadcasted_iota(jnp.int32, (2 * LANE, 2 * LANE), 0)
    in_row = lax.broadcasted_iota(jnp.int32, (2 * LANE, 2 * LANE), 1)
    want = jnp.zeros_like(out_row)
    for d in range(lanes):
        slot = me ^ d
        source = jnp.int32(0)
        for lane in range(lanes):
            source = source + jnp.where(owner_ref[0, lane] == slot, lane, 0)
        want = jnp.where(out_row // rows == d, source, want)
    pick = jnp.where(in_row == (out_row % rows) * lanes + want, 1.0, 0.0).astype(BF16)
    x = x_ref[...].reshape(steps * lanes, width)
    for i in range(steps // rows):
        y = dot(pick, x[i * 2 * LANE : (i + 1) * 2 * LANE]).astype(BF16)
        for d in range(lanes):
            out_refs[d][i * rows : (i + 1) * rows, :] = y[d * rows : (d + 1) * rows]


def pack(owner, snapshots, chunk):
    steps, lanes, _ = snapshots.shape
    return pl.pallas_call(
        pack_kernel,
        grid=(1,),
        out_shape=[jax.ShapeDtypeStruct((steps, LANE), BF16)] * lanes,
        in_specs=[SMEM, pl.BlockSpec((steps, lanes, LANE), lambda i: (0, 0, chunk))],
        out_specs=[spec((steps, LANE))] * lanes,
        compiler_params=pltpu.CompilerParams(vmem_limit_bytes=16 * 2**20),
    )(owner, snapshots)


def gram_kernel(lanes, scale, first, last, *refs):
    order_ref, offsets_ref, w_ref, f_ref, pick_ref = refs[:5]
    pieces = refs[5 : 5 + lanes]
    rest = refs[5 + lanes :]
    if not first:
        before_ref, *rest = rest
    s_ref, packed_ref, record, masked = rest
    steps = pieces[0].shape[0]
    me = lax.axis_index("tm")
    for d in range(lanes):
        start = pl.multiple_of(order_ref[me ^ d] * steps, steps)
        record[pl.ds(start, steps), :] = pieces[d][...].astype(F32)
    for b in range(0, NBLK, 2):
        pair = range(b, min(b + 2, NBLK))
        x = [record[pl.ds(offsets_ref[i], NFFT), :].astype(BF16) for i in pair]
        x = jnp.concatenate(x, axis=1) if len(x) > 1 else x[0]
        y = dot(f_ref[0], x) + dot(f_ref[1], x)
        for at, i in enumerate(pair):
            cols = slice(at * LANE, (at + 1) * LANE)
            s_ref[i] = y[:NFREQ, cols]
            s_ref[NBLK + i] = y[NFREQ:, cols]
    w = w_ref[...]
    row = lax.broadcasted_iota(jnp.int32, (HALF_ROWS, LANE), 0)
    col = lax.broadcasted_iota(jnp.int32, (HALF_ROWS, LANE), 1)
    same = row % SUB == col % SUB
    pad = jnp.zeros((LANE - HALF_ROWS, LANE), F32)
    for g in range(GROUPS):
        at = slice(g * SUB, (g + 1) * SUB)
        s = s_ref[:, at, :].reshape(2 * HALF_ROWS, LANE)
        other = jnp.concatenate([s[:HALF_ROWS], pad, s[HALF_ROWS:], pad], axis=0)
        full = dot_nt((s * w).astype(BF16), other.astype(BF16))
        real = full[:HALF_ROWS, :LANE] + full[HALF_ROWS:, LANE:]
        imag = full[:HALF_ROWS, LANE:] - full[HALF_ROWS:, :LANE]
        masked[:, at, :LANE] = jnp.where(same, real, 0.0).reshape(NBLK, SUB, LANE)
        masked[:, at, LANE:] = jnp.where(same, imag, 0.0).reshape(NBLK, SUB, LANE)
    for pair in range(PAIRS):
        total = jnp.zeros((PAIR_ROWS, NFREQ), F32)
        for a in sorted({pair, NBLK - 1 - pair}):
            high, low = split(masked[a])
            total = total + dot_nt(pick_ref[a], high) + dot_nt(pick_ref[a], low)
        rows = slice(pair * PAIR_ROWS, (pair + 1) * PAIR_ROWS)
        total = total * scale
        if not first:
            total = total + before_ref[rows, :]
        packed_ref[rows, :] = total.astype(packed_ref.dtype)


def gram_part(order, offsets, weights, tables, pieces, before, chunk, scale, last):
    lanes = len(pieces)
    steps = pieces[0].shape[0]
    first = before is None
    args = [order, offsets, weights, *tables, *pieces] + ([] if first else [before])
    in_specs = [SMEM, SMEM, pl.BlockSpec((1, LANE), lambda i: (0, chunk))]
    in_specs += [spec(a.shape) for a in args[3:]]
    return pl.pallas_call(
        functools.partial(gram_kernel, lanes, scale, first, last),
        grid=(1,),
        out_shape=[
            jax.ShapeDtypeStruct((2 * NBLK, NFREQ, LANE), F32),
            jax.ShapeDtypeStruct((PACKED, NFREQ), BF16 if last else F32),
        ],
        in_specs=in_specs,
        out_specs=[spec((2 * NBLK, NFREQ, LANE)), spec((PACKED, NFREQ))],
        scratch_shapes=[
            pltpu.VMEM((lanes * steps, LANE), F32),
            pltpu.VMEM((NBLK, NFREQ, 2 * LANE), F32),
        ],
        compiler_params=pltpu.CompilerParams(vmem_limit_bytes=24 * 2**20),
        cost_estimate=pl.CostEstimate(
            flops=2 * 10**9, bytes_accessed=6 * 10**6, transcendentals=0
        ),
    )(*args)


def product(x, y, store):
    xr, xi = x
    yr, yi = y

    @pl.loop(0, NBLK)
    def _(a):
        real = jnp.zeros((16, NFREQ), F32)
        imag = jnp.zeros((16, NFREQ), F32)
        for b in range(NBLK):
            pr = xr[a, pl.ds(b, 1), :]
            pi = xi[a, pl.ds(b, 1), :]
            qr = yr[b]
            qi = yi[b]
            real = real + (pr * qr - pi * qi)
            imag = imag + (pr * qi + pi * qr)
        store(a, real, imag)


def inverse_root(y, z, p, y2, z2):
    sub = lax.broadcasted_iota(jnp.int32, (16, NFREQ), 0)

    def to(dst):
        def store(a, real, imag):
            dst[0][a] = real
            dst[1][a] = imag

        return store

    def factor(a, real, imag):
        p[0][a] = jnp.where(sub == a, 1.5, 0.0) - 0.5 * real
        p[1][a] = -0.5 * imag

    for step in range(ROOT_STEPS):
        if step == 0:
            for a in range(NBLK):
                real = jnp.where(sub == a, 1.5, 0.0) - 0.5 * y[0][a]
                imag = -0.5 * y[1][a]
                p[0][a] = real
                p[1][a] = imag
                z2[0][a] = real
                z2[1][a] = imag
        else:
            product(z, y, factor)
            product(p, z, to(z2))
        if step < ROOT_STEPS - 1:
            product(y, p, to(y2))
        y, y2 = y2, y
        z, z2 = z2, z
    return z


def mode_kernel(parts, chunks, share, *refs):
    part_refs = refs[:parts]
    spread_ref = refs[parts]
    s_refs = refs[parts + 1 : parts + 1 + chunks]
    out_ref, gram_ref, packed, v, *mats = refs[parts + 1 + chunks :]
    step = pl.program_id(0)

    @pl.when(step == 0)
    def _():
        terms = [r[...].astype(F32) for r in part_refs]
        while len(terms) > 1:
            terms = [a + b for a, b in zip(terms[::2], terms[1::2])]
        packed[...] = terms[0]
        y, z, p, y2, z2 = [(mats[2 * i], mats[2 * i + 1]) for i in range(5)]
        for ref in mats:
            ref[:, 8:, :] = jnp.zeros((NBLK, 8, NFREQ), F32)
        trace = jnp.zeros((1, NFREQ), F32)
        rows = packed_rows()
        for a in range(NBLK):
            line = packed[pl.ds(rows[0, a, a], 1), :]
            trace = trace + line
            y[0][a, pl.ds(a, 1), :] = line
            y[1][a, pl.ds(a, 1), :] = jnp.zeros_like(line)
            for e in range(a + 1, NBLK):
                line = packed[pl.ds(rows[0, a, e], 1), :]
                y[0][a, pl.ds(e, 1), :] = line
                y[0][e, pl.ds(a, 1), :] = line
                line = packed[pl.ds(rows[1, a, e], 1), :]
                y[1][a, pl.ds(e, 1), :] = line
                y[1][e, pl.ds(a, 1), :] = -line
        trace = 2.0 * trace
        at = lax.axis_index("sx") * lax.axis_size("sy") + lax.axis_index("sy")
        back = (NFREQ - at * share) % NFREQ
        for c in range(2):
            for a in range(NBLK):
                gram_ref[c, a] = pltpu.roll(y[c][a], back, 1)
                y[c][a] = y[c][a] / trace
        root = inverse_root(y, z, p, y2, z2)
        norm = 1.0 / jnp.sqrt(trace)
        row = lax.broadcasted_iota(jnp.int32, (NFREQ, 2 * HALF_ROWS), 0)
        col = lax.broadcasted_iota(jnp.int32, (NFREQ, 2 * HALF_ROWS), 1)
        same = row % SUB == col % SUB
        for m0 in range(0, NBLK, STACK):
            modes = range(m0, min(m0 + STACK, NBLK))
            stack = [root[c][m] * norm for m in modes for c in range(2)]
            stack += [jnp.zeros((16, NFREQ), F32)] * (2 * STACK - len(stack))
            high, low = split(jnp.concatenate(stack, axis=0).T)
            for m in modes:
                for c in range(2):
                    table = spread_ref[(m - m0) * 2 + c]
                    wide = dot(high, table) + dot(low, table)
                    v[c * NBLK + m] = jnp.where(same, wide, 0.0)

    fields = []
    for h in range(2):
        start = pl.multiple_of(step * 16 + h * SUB, SUB)
        v_high, v_low = split(v[:, pl.ds(start, SUB), :].reshape(2 * HALF_ROWS, 2 * HALF_ROWS))
        s = jnp.concatenate(
            [r[:, h * SUB : (h + 1) * SUB, :].reshape(2 * HALF_ROWS, LANE) for r in s_refs], axis=1
        )
        s_high, s_low = split(s)
        field = dot(v_high, s_high) + (dot(v_high, s_low) + dot(v_low, s_high))
        fields.append(field.reshape(2 * NBLK, SUB, chunks * LANE))
    both = jnp.concatenate(fields, axis=1).astype(BF16)
    out_ref[...] = both.reshape(2, NBLK, 16, chunks * LANE)


def mode_fields(parts, spread, spectra, share):
    chunks = len(spectra)
    width = chunks * LANE
    mat = pltpu.VMEM((NBLK, 16, NFREQ), F32)
    return pl.pallas_call(
        functools.partial(mode_kernel, len(parts), chunks, share),
        grid=(NFREQ // 16,),
        out_shape=[
            jax.ShapeDtypeStruct((2, NBLK, NFREQ, width), BF16),
            jax.ShapeDtypeStruct((2, NBLK, 16, NFREQ), F32),
        ],
        in_specs=[spec(a.shape) for a in parts]
        + [spec(spread.shape)]
        + [pl.BlockSpec((2 * NBLK, 16, LANE), lambda i: (0, i, 0))] * chunks,
        out_specs=[
            pl.BlockSpec((2, NBLK, 16, width), lambda i: (0, 0, i, 0)),
            spec((2, NBLK, 16, NFREQ)),
        ],
        scratch_shapes=[
            pltpu.VMEM((PACKED, NFREQ), F32),
            pltpu.VMEM((2 * NBLK, NFREQ, 2 * HALF_ROWS), F32),
        ]
        + [mat] * 10,
        compiler_params=pltpu.CompilerParams(vmem_limit_bytes=24 * 2**20),
    )(*parts, spread, *spectra)


def swap(x, axes, mask, size):
    return lax.ppermute(x, axes, [(i, i ^ mask) for i in range(size)])


def body(snapshots, weights, block_order, owner, offsets):
    lanes = lax.axis_size("tm")
    sx = lax.axis_size("sx")
    sy = lax.axis_size("sy")
    groups = sx * sy
    chunks = snapshots.shape[2] // LANE
    scale = 1.0 / (lanes * groups * weights.shape[0])
    tables = (jnp.asarray(fourier_tables()), jnp.asarray(pick_table()))
    weights = weights.reshape(1, -1)

    arrived = []
    for q in range(chunks):
        packed = pack(owner, snapshots, q)
        pieces = [packed[0]]
        for d in range(1, lanes):
            pieces.append(swap(packed[d], "tm", d, lanes))
        arrived.append(pieces)

    spectra = []
    total = None
    for q in range(chunks):
        s, total = gram_part(
            block_order, offsets, weights, tables, arrived[q], total, q, scale, q == chunks - 1
        )
        spectra.append(s)

    bits = [b * groups for b in powers(lanes)] + powers(groups)
    size = lanes * groups
    terms = [total]
    for at in range(0, len(bits), 2):
        here = bits[at : at + 2]
        masks = [0, here[0]] + ([here[1], here[0] + here[1]] if len(here) > 1 else [])
        own = total_of(terms)
        terms = [own] + [swap(own, ("tm", "sx", "sy"), m, size) for m in masks[1:]]

    share = NFREQ // groups
    modes, gram = mode_fields(terms, jnp.asarray(spread_table()), spectra, share)
    modes = jnp.transpose(modes, (0, 2, 1, 3))[:, :, :, None, :]
    gram = jnp.transpose(gram[:, :, :NBLK, :share], (0, 3, 1, 2))
    return modes, gram


def powers(size):
    return [1 << i for i in range(size.bit_length() - 1)]


def total_of(terms):
    if len(terms) == 1:
        return terms[0]
    terms = [t.astype(F32) for t in terms]
    while len(terms) > 1:
        terms = [a + b for a, b in zip(terms[::2], terms[1::2])]
    return terms[0].astype(BF16)


def solution(mesh):
    placed = (P("tm", None, ("sx", "sy")), P(("sx", "sy")), P(), P(("sx", "sy"), None), P())
    return jax.shard_map(
        body,
        mesh=mesh,
        in_specs=placed,
        out_specs=(P(None, None, None, "tm", ("sx", "sy")), P(None, ("sx", "sy"), None, None)),
        check_vma=False,
    )
```

```python
import functools
import math

import jax
import jax.numpy as jnp
import numpy as np
from jax import lax
from jax.experimental import pallas as pl
from jax.experimental.pallas import tpu as pltpu
from jax.sharding import PartitionSpec as P

NFFT = 256
ROOT_STEPS = 5
NFREQ = 128
NBLK = 11
LANE = 128
SUB = 8
HALF_ROWS = NBLK * SUB
GROUPS = NFREQ // SUB
PAIRS = (NBLK + 1) // 2
PAIR_ROWS = 24
PACKED = PAIRS * PAIR_ROWS
STACK = 4
FIRST_LIMIT = 64 * 2**20
BF16 = jnp.bfloat16
F32 = jnp.float32


def fourier_tables():
    n = np.arange(NFFT)
    k = np.arange(NFREQ)
    angles = 2.0 * np.pi * ((k[:, None] * n[None, :]) % NFFT) / NFFT
    scaled = (0.5 - 0.5 * np.cos(2.0 * np.pi * n / NFFT)) / math.sqrt(0.375 * NFFT)
    table = np.concatenate([np.cos(angles) * scaled, -np.sin(angles) * scaled], axis=0)
    high = table.astype(jnp.bfloat16)
    low = (table - high.astype(np.float64)).astype(jnp.bfloat16)
    return np.stack([high, low])


def packed_rows():
    rows = {}
    for pair in range(PAIRS):
        row = pair * PAIR_ROWS
        for a in sorted({pair, NBLK - 1 - pair}):
            for e in range(a, NBLK):
                rows[0, a, e] = row
                row += 1
            for e in range(a + 1, NBLK):
                rows[1, a, e] = row
                row += 1
    return rows


def pick_table():
    pick = np.zeros((NBLK, PAIR_ROWS, 2 * LANE), np.float32)
    for (part, a, e), row in packed_rows().items():
        start = part * LANE + e * SUB
        pick[a, row % PAIR_ROWS, start : start + SUB] = 1.0
    return pick.astype(jnp.bfloat16)


def spread_table():
    spread = np.zeros((STACK, 2, LANE, 2 * HALF_ROWS), np.float32)
    for m in range(STACK):
        for b in range(NBLK):
            real = m * 32 + b
            imag = m * 32 + 16 + b
            first = slice(b * SUB, b * SUB + SUB)
            second = slice(HALF_ROWS + b * SUB, HALF_ROWS + b * SUB + SUB)
            spread[m, 0, real, first] = 1.0
            spread[m, 0, imag, second] = 1.0
            spread[m, 1, imag, first] = -1.0
            spread[m, 1, real, second] = 1.0
    return spread.reshape(STACK * 2, LANE, 2 * HALF_ROWS).astype(jnp.bfloat16)


def split(x):
    high = x.astype(BF16)
    return high, (x - high.astype(F32)).astype(BF16)


def dot(a, b):
    return jnp.dot(a, b, preferred_element_type=F32)


def dot_nt(a, b):
    return lax.dot_general(a, b, (((1,), (1,)), ((), ())), preferred_element_type=F32)


def spec(shape):
    return pl.BlockSpec(shape, lambda *_: (0,) * len(shape))


SMEM = pl.BlockSpec(memory_space=pltpu.SMEM)


def pack_kernel(base, follows, owner_hbm, x_hbm, *refs):
    lanes = x_hbm.shape[1]
    refs = refs[follows:]
    out_refs = refs[:lanes]
    owner, x_ref, owner_sem, x_sem = refs[lanes:]
    steps, _, width = x_ref.shape
    copies = []
    for i, at in enumerate(range(0, width, LANE)):
        copies.append(
            pltpu.make_async_copy(
                x_hbm.at[:, :, base + at : base + at + LANE],
                x_ref.at[:, :, at : at + LANE],
                x_sem.at[i],
            )
        )
    owner_copy = pltpu.make_async_copy(owner_hbm, owner, owner_sem)
    owner_copy.start()
    for copy in copies:
        copy.start()
    me = lax.axis_index("tm")
    rows = 2 * LANE // lanes
    out_row = lax.broadcasted_iota(jnp.int32, (2 * LANE, 2 * LANE), 0)
    in_row = lax.broadcasted_iota(jnp.int32, (2 * LANE, 2 * LANE), 1)
    want = jnp.zeros_like(out_row)
    owner_copy.wait()
    for d in range(lanes):
        slot = me ^ d
        source = jnp.int32(0)
        for lane in range(lanes):
            source = source + jnp.where(owner[0, lane] == slot, lane, 0)
        want = jnp.where(out_row // rows == d, source, want)
    pick = jnp.where(in_row == (out_row % rows) * lanes + want, 1.0, 0.0).astype(BF16)
    for c, copy in enumerate(copies):
        copy.wait()
        cols = slice(c * LANE, (c + 1) * LANE)
        x = x_ref[:, :, cols].reshape(steps * lanes, LANE)
        for i in range(steps // rows):
            y = dot(pick, x[i * 2 * LANE : (i + 1) * 2 * LANE]).astype(BF16)
            for d in range(lanes):
                out_refs[d][i * rows : (i + 1) * rows, cols] = y[d * rows : (d + 1) * rows]


def pack(owner, snapshots, base, width, after):
    steps, lanes, _ = snapshots.shape
    limit = 24 * 2**20 if after else FIRST_LIMIT
    return pl.pallas_call(
        functools.partial(pack_kernel, base, len(after)),
        out_shape=[jax.ShapeDtypeStruct((steps, width), BF16)] * lanes,
        in_specs=[pl.BlockSpec(memory_space=pltpu.HBM)] * (2 + len(after)),
        out_specs=[pl.BlockSpec(memory_space=pltpu.VMEM)] * lanes,
        scratch_shapes=[
            pltpu.SMEM(owner.shape, jnp.int32),
            pltpu.VMEM((steps, lanes, width), BF16),
            pltpu.SemaphoreType.DMA,
            pltpu.SemaphoreType.DMA((width // LANE,)),
        ],
        compiler_params=pltpu.CompilerParams(vmem_limit_bytes=limit),
        cost_estimate=pl.CostEstimate(
            flops=2 * 256 * steps * lanes * width,
            bytes_accessed=4 * steps * lanes * width,
            transcendentals=0,
        ),
    )(owner, snapshots, *after)


def gram_kernel(lanes, scale, first, *refs):
    order_ref, offsets_ref, w_ref, f_ref, pick_ref = refs[:5]
    pieces = refs[5 : 5 + lanes]
    rest = refs[5 + lanes :]
    if not first:
        before_ref, *rest = rest
    high_ref, low_ref, packed_ref, record, s_ref, masked = rest
    steps, width = pieces[0].shape
    me = lax.axis_index("tm")
    for d in range(lanes):
        start = pl.multiple_of(order_ref[me ^ d] * steps, steps)
        for c in range(width // LANE):
            cols = slice(c * LANE, (c + 1) * LANE)
            record[c, pl.ds(start, steps), :] = pieces[d][:, cols].astype(F32)
    wanted = [(i, c) for i in range(NBLK) for c in range(width // LANE)]
    for at in range(0, len(wanted), 2):
        pair = wanted[at : at + 2]
        x = [record[c, pl.ds(offsets_ref[i], NFFT), :].astype(BF16) for i, c in pair]
        x = jnp.concatenate(x, axis=1) if len(x) > 1 else x[0]
        y = dot(f_ref[0], x) + dot(f_ref[1], x)
        for j, (i, c) in enumerate(pair):
            cols = slice(j * LANE, (j + 1) * LANE)
            out = slice(c * LANE, (c + 1) * LANE)
            s_ref[i, :, out] = y[:NFREQ, cols]
            s_ref[NBLK + i, :, out] = y[NFREQ:, cols]
    w = w_ref[...]
    row = lax.broadcasted_iota(jnp.int32, (HALF_ROWS, LANE), 0)
    col = lax.broadcasted_iota(jnp.int32, (HALF_ROWS, LANE), 1)
    same = row % SUB == col % SUB
    pad = jnp.zeros((LANE - HALF_ROWS, width), F32)
    for g in range(GROUPS):
        at = slice(g * SUB, (g + 1) * SUB)
        s = s_ref[:, at, :].reshape(2 * HALF_ROWS, width)
        high, low = split(s)
        high_ref[g] = high
        low_ref[g] = low
        other = jnp.concatenate([s[:HALF_ROWS], pad, s[HALF_ROWS:], pad], axis=0)
        full = dot_nt((s * w).astype(BF16), other.astype(BF16))
        real = full[:HALF_ROWS, :LANE] + full[HALF_ROWS:, LANE:]
        imag = full[:HALF_ROWS, LANE:] - full[HALF_ROWS:, :LANE]
        masked[:, at, :LANE] = jnp.where(same, real, 0.0).reshape(NBLK, SUB, LANE)
        masked[:, at, LANE:] = jnp.where(same, imag, 0.0).reshape(NBLK, SUB, LANE)
    for pair in range(PAIRS):
        total = jnp.zeros((PAIR_ROWS, NFREQ), F32)
        for a in sorted({pair, NBLK - 1 - pair}):
            high, low = split(masked[a])
            total = total + dot_nt(pick_ref[a], high) + dot_nt(pick_ref[a], low)
        rows = slice(pair * PAIR_ROWS, (pair + 1) * PAIR_ROWS)
        total = total * scale
        if not first:
            total = total + before_ref[rows, :]
        packed_ref[rows, :] = total


def gram_part(order, offsets, weights, tables, pieces, before, base, scale):
    lanes = len(pieces)
    steps, width = pieces[0].shape
    first = before is None
    args = [order, offsets, weights[:, base : base + width], *tables, *pieces]
    args += [] if first else [before]
    vmem = pl.BlockSpec(memory_space=pltpu.VMEM)
    return pl.pallas_call(
        functools.partial(gram_kernel, lanes, scale, first),
        out_shape=[
            jax.ShapeDtypeStruct((GROUPS, 2 * HALF_ROWS, width), BF16),
            jax.ShapeDtypeStruct((GROUPS, 2 * HALF_ROWS, width), BF16),
            jax.ShapeDtypeStruct((PACKED, NFREQ), F32),
        ],
        in_specs=[SMEM, SMEM] + [vmem] * (len(args) - 2),
        out_specs=[vmem] * 3,
        scratch_shapes=[
            pltpu.VMEM((width // LANE, lanes * steps, LANE), F32),
            pltpu.VMEM((2 * NBLK, NFREQ, width), F32),
            pltpu.VMEM((NBLK, NFREQ, 2 * LANE), F32),
        ],
        compiler_params=pltpu.CompilerParams(vmem_limit_bytes=24 * 2**20),
        cost_estimate=pl.CostEstimate(
            flops=10**10 * width // LANE // 4, bytes_accessed=6 * 10**6, transcendentals=0
        ),
    )(*args)


def product(x, y, store):
    xr, xi = x
    yr, yi = y

    @pl.loop(0, NBLK)
    def _(a):
        real = jnp.zeros((16, NFREQ), F32)
        imag = jnp.zeros((16, NFREQ), F32)
        for b in range(NBLK):
            pr = xr[a, pl.ds(b, 1), :]
            pi = xi[a, pl.ds(b, 1), :]
            qr = yr[b]
            qi = yi[b]
            real = real + (pr * qr - pi * qi)
            imag = imag + (pr * qi + pi * qr)
        store(a, real, imag)


def inverse_root(y, z, p, y2, z2):
    sub = lax.broadcasted_iota(jnp.int32, (16, NFREQ), 0)

    def to(dst):
        def store(a, real, imag):
            dst[0][a] = real
            dst[1][a] = imag

        return store

    def factor(a, real, imag):
        p[0][a] = jnp.where(sub == a, 1.5, 0.0) - 0.5 * real
        p[1][a] = -0.5 * imag

    for step in range(ROOT_STEPS):
        if step == 0:
            for a in range(NBLK):
                real = jnp.where(sub == a, 1.5, 0.0) - 0.5 * y[0][a]
                imag = -0.5 * y[1][a]
                p[0][a] = real
                p[1][a] = imag
                z2[0][a] = real
                z2[1][a] = imag
        else:
            product(z, y, factor)
            product(p, z, to(z2))
        if step < ROOT_STEPS - 1:
            product(y, p, to(y2))
        y, y2 = y2, y
        z, z2 = z2, z
    return z


def root_kernel(parts, share, *refs):
    part_refs = refs[:parts]
    stack_ref, gram_ref, packed, *mats = refs[parts:]
    terms = [r[...].astype(F32) for r in part_refs]
    while len(terms) > 1:
        terms = [a + b for a, b in zip(terms[::2], terms[1::2])]
    packed[...] = terms[0]
    y, z, p, y2, z2 = [(mats[2 * i], mats[2 * i + 1]) for i in range(5)]
    for ref in mats:
        ref[:, 8:, :] = jnp.zeros((NBLK, 8, NFREQ), F32)
    trace = jnp.zeros((1, NFREQ), F32)
    rows = packed_rows()
    for a in range(NBLK):
        line = packed[pl.ds(rows[0, a, a], 1), :]
        trace = trace + line
        y[0][a, pl.ds(a, 1), :] = line
        y[1][a, pl.ds(a, 1), :] = jnp.zeros_like(line)
        for e in range(a + 1, NBLK):
            line = packed[pl.ds(rows[0, a, e], 1), :]
            y[0][a, pl.ds(e, 1), :] = line
            y[0][e, pl.ds(a, 1), :] = line
            line = packed[pl.ds(rows[1, a, e], 1), :]
            y[1][a, pl.ds(e, 1), :] = line
            y[1][e, pl.ds(a, 1), :] = -line
    trace = 2.0 * trace
    at = lax.axis_index("sx") * lax.axis_size("sy") + lax.axis_index("sy")
    back = (NFREQ - at * share) % NFREQ
    for c in range(2):
        for a in range(NBLK):
            gram_ref[a, :, c, :] = pltpu.roll(y[c][a], back, 1)[:NBLK, :share]
            y[c][a] = y[c][a] / trace
    root = inverse_root(y, z, p, y2, z2)
    norm = 1.0 / jnp.sqrt(trace)
    for at, m0 in enumerate(range(0, NBLK, STACK)):
        modes = range(m0, min(m0 + STACK, NBLK))
        stack = [root[c][m] * norm for m in modes for c in range(2)]
        stack += [jnp.zeros((16, NFREQ), F32)] * (2 * STACK - len(stack))
        stack_ref[at] = jnp.concatenate(stack, axis=0).T


def roots(parts, share):
    stacks = -(-NBLK // STACK)
    vmem = pl.BlockSpec(memory_space=pltpu.VMEM)
    return pl.pallas_call(
        functools.partial(root_kernel, len(parts), share),
        out_shape=[
            jax.ShapeDtypeStruct((stacks, NFREQ, LANE), F32),
            jax.ShapeDtypeStruct((NBLK, NBLK, 2, share), F32),
        ],
        in_specs=[vmem] * len(parts),
        out_specs=[vmem] * 2,
        scratch_shapes=[pltpu.VMEM((PACKED, NFREQ), F32)]
        + [pltpu.VMEM((NBLK, 16, NFREQ), F32)] * 10,
        compiler_params=pltpu.CompilerParams(vmem_limit_bytes=24 * 2**20),
    )(*parts)


def mode_kernel(chunks, stack_ref, spread_ref, *refs):
    high_refs = refs[:chunks]
    low_refs = refs[chunks : 2 * chunks]
    out_ref, v = refs[2 * chunks :]
    step = pl.program_id(0)

    @pl.when(step == 0)
    def _():
        row = lax.broadcasted_iota(jnp.int32, (NFREQ, 2 * HALF_ROWS), 0)
        col = lax.broadcasted_iota(jnp.int32, (NFREQ, 2 * HALF_ROWS), 1)
        same = row % SUB == col % SUB
        for at, m0 in enumerate(range(0, NBLK, STACK)):
            high, low = split(stack_ref[at])
            for m in range(m0, min(m0 + STACK, NBLK)):
                for c in range(2):
                    table = spread_ref[(m - m0) * 2 + c]
                    wide = dot(high, table) + dot(low, table)
                    v[c * NBLK + m] = jnp.where(same, wide, 0.0)

    fields = []
    for h in range(2):
        start = pl.multiple_of(step * 16 + h * SUB, SUB)
        v_high, v_low = split(v[:, pl.ds(start, SUB), :].reshape(2 * HALF_ROWS, 2 * HALF_ROWS))
        s_high = jnp.concatenate([r[h] for r in high_refs], axis=1)
        s_low = jnp.concatenate([r[h] for r in low_refs], axis=1)
        field = dot(v_high, s_high) + (dot(v_high, s_low) + dot(v_low, s_high))
        fields.append(field.reshape(2 * NBLK, SUB, -1))
    both = jnp.concatenate(fields, axis=1).astype(BF16)
    out_ref[...] = both.reshape(out_ref.shape)


def mode_fields(stacks, spread, highs, lows):
    width = sum(s.shape[2] for s in highs)
    return pl.pallas_call(
        functools.partial(mode_kernel, len(highs)),
        grid=(NFREQ // 16,),
        out_shape=jax.ShapeDtypeStruct((2, NBLK, NFREQ, width), BF16),
        in_specs=[spec(stacks.shape), spec(spread.shape)]
        + [
            pl.BlockSpec((2, 2 * HALF_ROWS, s.shape[2]), lambda i: (i, 0, 0))
            for s in highs + lows
        ],
        out_specs=pl.BlockSpec((2, NBLK, 16, width), lambda i: (0, 0, i, 0)),
        scratch_shapes=[pltpu.VMEM((2 * NBLK, NFREQ, 2 * HALF_ROWS), F32)],
        compiler_params=pltpu.CompilerParams(vmem_limit_bytes=24 * 2**20),
    )(stacks, spread, *highs, *lows)


def swap(x, axes, mask, size):
    return lax.ppermute(x, axes, [(i, i ^ mask) for i in range(size)])


def body(snapshots, weights, block_order, owner, offsets):
    lanes = lax.axis_size("tm")
    groups = lax.axis_size("sx") * lax.axis_size("sy")
    points = snapshots.shape[2]
    widths = [points // 2, points // 4, points // 4]
    scale = 1.0 / (lanes * groups * points)
    tables = (jnp.asarray(fourier_tables()), jnp.asarray(pick_table()))
    weights = weights.reshape(1, -1)

    arrived = []
    base = 0
    for width in widths:
        packed = pack(owner, snapshots, base, width, [p[0] for _, p in arrived[-1:]])
        moved = [swap(packed[d], "tm", d, lanes) for d in reversed(range(1, lanes))]
        pieces = [packed[0]] + moved[::-1]
        arrived.append((base, pieces))
        base += width

    highs, lows = [], []
    total = None
    for base, pieces in arrived:
        high, low, total = gram_part(
            block_order, offsets, weights, tables, pieces, total, base, scale
        )
        highs.append(high)
        lows.append(low)

    total = lax.psum(total, ("tm", "sx", "sy"))
    stacks, gram = roots([total], NFREQ // groups)
    modes = mode_fields(stacks, jnp.asarray(spread_table()), highs, lows)
    modes = jnp.transpose(modes, (0, 2, 1, 3))[:, :, :, None, :]
    return modes, jnp.transpose(gram, (2, 3, 0, 1))


def solution(mesh):
    placed = (P("tm", None, ("sx", "sy")), P(("sx", "sy")), P(), P(("sx", "sy"), None), P())
    return jax.shard_map(
        body,
        mesh=mesh,
        in_specs=placed,
        out_specs=(P(None, None, None, "tm", ("sx", "sy")), P(None, ("sx", "sy"), None, None)),
        check_vma=False,
    )
```

```python
import functools
import math

import jax
import jax.numpy as jnp
import numpy as np
from jax import lax
from jax.experimental import pallas as pl
from jax.experimental.pallas import tpu as pltpu
from jax.sharding import PartitionSpec as P

NFFT = 256
ROOT_STEPS = 5
NFREQ = 128
NBLK = 11
LANE = 128
SUB = 8
HALF_ROWS = NBLK * SUB
GROUPS = NFREQ // SUB
PACKED = 128
STACK = 4
FIRST_LIMIT = 64 * 2**20
BF16 = jnp.bfloat16
F32 = jnp.float32


def fourier_tables():
    n = np.arange(NFFT)
    k = np.arange(NFREQ)
    angles = 2.0 * np.pi * ((k[:, None] * n[None, :]) % NFFT) / NFFT
    scaled = (0.5 - 0.5 * np.cos(2.0 * np.pi * n / NFFT)) / math.sqrt(0.375 * NFFT)
    table = np.concatenate([np.cos(angles) * scaled, -np.sin(angles) * scaled], axis=0)
    high = table.astype(jnp.bfloat16)
    low = (table - high.astype(np.float64)).astype(jnp.bfloat16)
    return np.stack([high, low])


def packed_rows():
    rows = {}
    for a in range(NBLK):
        for e in range(a, NBLK):
            rows[0, a, e] = len(rows)
        for e in range(a + 1, NBLK):
            rows[1, a, e] = len(rows)
    return rows


def pick_table():
    pick = np.zeros((NBLK, PACKED, 2 * LANE), np.float32)
    for (part, a, e), row in packed_rows().items():
        start = part * LANE + e * SUB
        pick[a, row, start : start + SUB] = 1.0
    return pick.astype(jnp.bfloat16)


def spread_table():
    spread = np.zeros((STACK, 2, LANE, 2 * HALF_ROWS), np.float32)
    for m in range(STACK):
        for b in range(NBLK):
            real = m * 32 + b
            imag = m * 32 + 16 + b
            first = slice(b * SUB, b * SUB + SUB)
            second = slice(HALF_ROWS + b * SUB, HALF_ROWS + b * SUB + SUB)
            spread[m, 0, real, first] = 1.0
            spread[m, 0, imag, second] = 1.0
            spread[m, 1, imag, first] = -1.0
            spread[m, 1, real, second] = 1.0
    return spread.reshape(STACK * 2, LANE, 2 * HALF_ROWS).astype(jnp.bfloat16)


def split(x):
    high = x.astype(BF16)
    return high, (x - high.astype(F32)).astype(BF16)


def dot(a, b):
    return jnp.dot(a, b, preferred_element_type=F32)


def dot_nt(a, b):
    return lax.dot_general(a, b, (((1,), (1,)), ((), ())), preferred_element_type=F32)


def spec(shape):
    return pl.BlockSpec(shape, lambda *_: (0,) * len(shape))


SMEM = pl.BlockSpec(memory_space=pltpu.SMEM)


def pack_kernel(base, follows, owner_hbm, x_hbm, *refs):
    lanes = x_hbm.shape[1]
    refs = refs[follows:]
    out_refs = refs[:lanes]
    owner, x_ref, owner_sem, x_sem = refs[lanes:]
    steps, _, width = x_ref.shape
    copies = []
    for i, at in enumerate(range(0, width, LANE)):
        copies.append(
            pltpu.make_async_copy(
                x_hbm.at[:, :, base + at : base + at + LANE],
                x_ref.at[:, :, at : at + LANE],
                x_sem.at[i],
            )
        )
    owner_copy = pltpu.make_async_copy(owner_hbm, owner, owner_sem)
    owner_copy.start()
    for copy in copies:
        copy.start()
    me = lax.axis_index("tm")
    rows = 2 * LANE // lanes
    out_row = lax.broadcasted_iota(jnp.int32, (2 * LANE, 2 * LANE), 0)
    in_row = lax.broadcasted_iota(jnp.int32, (2 * LANE, 2 * LANE), 1)
    want = jnp.zeros_like(out_row)
    owner_copy.wait()
    for d in range(lanes):
        slot = me ^ d
        source = jnp.int32(0)
        for lane in range(lanes):
            source = source + jnp.where(owner[0, lane] == slot, lane, 0)
        want = jnp.where(out_row // rows == d, source, want)
    pick = jnp.where(in_row == (out_row % rows) * lanes + want, 1.0, 0.0).astype(BF16)
    for c, copy in enumerate(copies):
        copy.wait()
        cols = slice(c * LANE, (c + 1) * LANE)
        x = x_ref[:, :, cols].reshape(steps * lanes, LANE)
        for i in range(steps // rows):
            y = dot(pick, x[i * 2 * LANE : (i + 1) * 2 * LANE]).astype(BF16)
            for d in range(lanes):
                out_refs[d][i * rows : (i + 1) * rows, cols] = y[d * rows : (d + 1) * rows]


def pack(owner, snapshots, base, width, after):
    steps, lanes, _ = snapshots.shape
    limit = 24 * 2**20 if after else FIRST_LIMIT
    return pl.pallas_call(
        functools.partial(pack_kernel, base, len(after)),
        out_shape=[jax.ShapeDtypeStruct((steps, width), BF16)] * lanes,
        in_specs=[pl.BlockSpec(memory_space=pltpu.HBM)] * (2 + len(after)),
        out_specs=[pl.BlockSpec(memory_space=pltpu.VMEM)] * lanes,
        scratch_shapes=[
            pltpu.SMEM(owner.shape, jnp.int32),
            pltpu.VMEM((steps, lanes, width), BF16),
            pltpu.SemaphoreType.DMA,
            pltpu.SemaphoreType.DMA((width // LANE,)),
        ],
        compiler_params=pltpu.CompilerParams(vmem_limit_bytes=limit),
        cost_estimate=pl.CostEstimate(
            flops=2 * 256 * steps * lanes * width,
            bytes_accessed=4 * steps * lanes * width,
            transcendentals=0,
        ),
    )(owner, snapshots, *after)


def gram_kernel(lanes, scale, first, *refs):
    order_ref, offsets_ref, w_ref, f_ref, pick_ref = refs[:5]
    pieces = refs[5 : 5 + lanes]
    rest = refs[5 + lanes :]
    if not first:
        before_ref, *rest = rest
    high_ref, low_ref, packed_ref, record, s_ref, masked = rest
    steps, width = pieces[0].shape
    me = lax.axis_index("tm")
    for d in range(lanes):
        start = pl.multiple_of(order_ref[me ^ d] * steps, steps)
        for c in range(width // LANE):
            cols = slice(c * LANE, (c + 1) * LANE)
            record[c, pl.ds(start, steps), :] = pieces[d][:, cols].astype(F32)
    wanted = [(i, c) for i in range(NBLK) for c in range(width // LANE)]
    for at in range(0, len(wanted), 2):
        pair = wanted[at : at + 2]
        x = [record[c, pl.ds(offsets_ref[i], NFFT), :].astype(BF16) for i, c in pair]
        x = jnp.concatenate(x, axis=1) if len(x) > 1 else x[0]
        y = dot(f_ref[0], x) + dot(f_ref[1], x)
        for j, (i, c) in enumerate(pair):
            cols = slice(j * LANE, (j + 1) * LANE)
            out = slice(c * LANE, (c + 1) * LANE)
            s_ref[i, :, out] = y[:NFREQ, cols]
            s_ref[NBLK + i, :, out] = y[NFREQ:, cols]
    w = w_ref[...]
    row = lax.broadcasted_iota(jnp.int32, (HALF_ROWS, LANE), 0)
    col = lax.broadcasted_iota(jnp.int32, (HALF_ROWS, LANE), 1)
    same = row % SUB == col % SUB
    pad = jnp.zeros((LANE - HALF_ROWS, width), F32)
    for g in range(GROUPS):
        at = slice(g * SUB, (g + 1) * SUB)
        s = s_ref[:, at, :].reshape(2 * HALF_ROWS, width)
        high, low = split(s)
        high_ref[g] = high
        low_ref[g] = low
        other = jnp.concatenate([s[:HALF_ROWS], pad, s[HALF_ROWS:], pad], axis=0)
        full = dot_nt((s * w).astype(BF16), other.astype(BF16))
        real = full[:HALF_ROWS, :LANE] + full[HALF_ROWS:, LANE:]
        imag = full[:HALF_ROWS, LANE:] - full[HALF_ROWS:, :LANE]
        masked[:, at, :LANE] = jnp.where(same, real, 0.0).reshape(NBLK, SUB, LANE)
        masked[:, at, LANE:] = jnp.where(same, imag, 0.0).reshape(NBLK, SUB, LANE)
    total = jnp.zeros((PACKED, NFREQ), F32)
    for a in range(NBLK):
        total = total + dot_nt(pick_ref[a], masked[a].astype(BF16))
    total = total * scale
    if not first:
        total = total + before_ref[...]
    packed_ref[...] = total


def gram_part(order, offsets, weights, tables, pieces, before, base, scale):
    lanes = len(pieces)
    steps, width = pieces[0].shape
    first = before is None
    args = [order, offsets, weights[:, base : base + width], *tables, *pieces]
    args += [] if first else [before]
    vmem = pl.BlockSpec(memory_space=pltpu.VMEM)
    return pl.pallas_call(
        functools.partial(gram_kernel, lanes, scale, first),
        out_shape=[
            jax.ShapeDtypeStruct((GROUPS, 2 * HALF_ROWS, width), BF16),
            jax.ShapeDtypeStruct((GROUPS, 2 * HALF_ROWS, width), BF16),
            jax.ShapeDtypeStruct((PACKED, NFREQ), F32),
        ],
        in_specs=[SMEM, SMEM] + [vmem] * (len(args) - 2),
        out_specs=[vmem] * 3,
        scratch_shapes=[
            pltpu.VMEM((width // LANE, lanes * steps, LANE), F32),
            pltpu.VMEM((2 * NBLK, NFREQ, width), F32),
            pltpu.VMEM((NBLK, NFREQ, 2 * LANE), F32),
        ],
        compiler_params=pltpu.CompilerParams(vmem_limit_bytes=24 * 2**20),
        cost_estimate=pl.CostEstimate(
            flops=10**10 * width // LANE // 4, bytes_accessed=6 * 10**6, transcendentals=0
        ),
    )(*args)


def product(x, y, store):
    xr, xi = x
    yr, yi = y

    @pl.loop(0, NBLK)
    def _(a):
        real = jnp.zeros((16, NFREQ), F32)
        imag = jnp.zeros((16, NFREQ), F32)
        for b in range(NBLK):
            pr = xr[a, pl.ds(b, 1), :]
            pi = xi[a, pl.ds(b, 1), :]
            qr = yr[b]
            qi = yi[b]
            real = real + (pr * qr - pi * qi)
            imag = imag + (pr * qi + pi * qr)
        store(a, real, imag)


def inverse_root(y, z, p, y2, z2):
    sub = lax.broadcasted_iota(jnp.int32, (16, NFREQ), 0)

    def to(dst):
        def store(a, real, imag):
            dst[0][a] = real
            dst[1][a] = imag

        return store

    def factor(a, real, imag):
        p[0][a] = jnp.where(sub == a, 1.5, 0.0) - 0.5 * real
        p[1][a] = -0.5 * imag

    for step in range(ROOT_STEPS):
        if step == 0:
            for a in range(NBLK):
                real = jnp.where(sub == a, 1.5, 0.0) - 0.5 * y[0][a]
                imag = -0.5 * y[1][a]
                p[0][a] = real
                p[1][a] = imag
                z2[0][a] = real
                z2[1][a] = imag
        else:
            product(z, y, factor)
            product(p, z, to(z2))
        if step < ROOT_STEPS - 1:
            product(y, p, to(y2))
        y, y2 = y2, y
        z, z2 = z2, z
    return z


def root_kernel(parts, share, *refs):
    part_refs = refs[:parts]
    stack_ref, gram_ref, packed, *mats = refs[parts:]
    terms = [r[...].astype(F32) for r in part_refs]
    while len(terms) > 1:
        terms = [a + b for a, b in zip(terms[::2], terms[1::2])]
    packed[...] = terms[0]
    y, z, p, y2, z2 = [(mats[2 * i], mats[2 * i + 1]) for i in range(5)]
    for ref in mats:
        ref[:, 8:, :] = jnp.zeros((NBLK, 8, NFREQ), F32)
    trace = jnp.zeros((1, NFREQ), F32)
    rows = packed_rows()
    for a in range(NBLK):
        line = packed[pl.ds(rows[0, a, a], 1), :]
        trace = trace + line
        y[0][a, pl.ds(a, 1), :] = line
        y[1][a, pl.ds(a, 1), :] = jnp.zeros_like(line)
        for e in range(a + 1, NBLK):
            line = packed[pl.ds(rows[0, a, e], 1), :]
            y[0][a, pl.ds(e, 1), :] = line
            y[0][e, pl.ds(a, 1), :] = line
            line = packed[pl.ds(rows[1, a, e], 1), :]
            y[1][a, pl.ds(e, 1), :] = line
            y[1][e, pl.ds(a, 1), :] = -line
    trace = 2.0 * trace
    at = lax.axis_index("sx") * lax.axis_size("sy") + lax.axis_index("sy")
    back = (NFREQ - at * share) % NFREQ
    for c in range(2):
        for a in range(NBLK):
            gram_ref[a, :, c, :] = pltpu.roll(y[c][a], back, 1)[:NBLK, :share]
            y[c][a] = y[c][a] / trace
    root = inverse_root(y, z, p, y2, z2)
    norm = 1.0 / jnp.sqrt(trace)
    for at, m0 in enumerate(range(0, NBLK, STACK)):
        modes = range(m0, min(m0 + STACK, NBLK))
        stack = [root[c][m] * norm for m in modes for c in range(2)]
        stack += [jnp.zeros((16, NFREQ), F32)] * (2 * STACK - len(stack))
        stack_ref[at] = jnp.concatenate(stack, axis=0).T


def roots(parts, share):
    stacks = -(-NBLK // STACK)
    vmem = pl.BlockSpec(memory_space=pltpu.VMEM)
    return pl.pallas_call(
        functools.partial(root_kernel, len(parts), share),
        out_shape=[
            jax.ShapeDtypeStruct((stacks, NFREQ, LANE), F32),
            jax.ShapeDtypeStruct((NBLK, NBLK, 2, share), F32),
        ],
        in_specs=[vmem] * len(parts),
        out_specs=[vmem] * 2,
        scratch_shapes=[pltpu.VMEM((PACKED, NFREQ), F32)]
        + [pltpu.VMEM((NBLK, 16, NFREQ), F32)] * 10,
        compiler_params=pltpu.CompilerParams(vmem_limit_bytes=24 * 2**20),
    )(*parts)


def mode_kernel(chunks, stack_ref, spread_ref, *refs):
    high_refs = refs[:chunks]
    low_refs = refs[chunks : 2 * chunks]
    out_ref, v = refs[2 * chunks :]
    step = pl.program_id(0)

    @pl.when(step == 0)
    def _():
        row = lax.broadcasted_iota(jnp.int32, (NFREQ, 2 * HALF_ROWS), 0)
        col = lax.broadcasted_iota(jnp.int32, (NFREQ, 2 * HALF_ROWS), 1)
        same = row % SUB == col % SUB
        for at, m0 in enumerate(range(0, NBLK, STACK)):
            high, low = split(stack_ref[at])
            for m in range(m0, min(m0 + STACK, NBLK)):
                for c in range(2):
                    table = spread_ref[(m - m0) * 2 + c]
                    wide = dot(high, table) + dot(low, table)
                    v[c * NBLK + m] = jnp.where(same, wide, 0.0)

    fields = []
    for h in range(2):
        start = pl.multiple_of(step * 16 + h * SUB, SUB)
        v_high, v_low = split(v[:, pl.ds(start, SUB), :].reshape(2 * HALF_ROWS, 2 * HALF_ROWS))
        s_high = jnp.concatenate([r[h] for r in high_refs], axis=1)
        s_low = jnp.concatenate([r[h] for r in low_refs], axis=1)
        field = dot(v_high, s_high) + (dot(v_high, s_low) + dot(v_low, s_high))
        fields.append(field.reshape(2 * NBLK, SUB, -1))
    both = jnp.concatenate(fields, axis=1).astype(BF16)
    out_ref[...] = both.reshape(out_ref.shape)


def mode_fields(stacks, spread, highs, lows):
    width = sum(s.shape[2] for s in highs)
    return pl.pallas_call(
        functools.partial(mode_kernel, len(highs)),
        grid=(NFREQ // 16,),
        out_shape=jax.ShapeDtypeStruct((2, NBLK, NFREQ, width), BF16),
        in_specs=[spec(stacks.shape), spec(spread.shape)]
        + [
            pl.BlockSpec((2, 2 * HALF_ROWS, s.shape[2]), lambda i: (i, 0, 0))
            for s in highs + lows
        ],
        out_specs=pl.BlockSpec((2, NBLK, 16, width), lambda i: (0, 0, i, 0)),
        scratch_shapes=[pltpu.VMEM((2 * NBLK, NFREQ, 2 * HALF_ROWS), F32)],
        compiler_params=pltpu.CompilerParams(vmem_limit_bytes=24 * 2**20),
    )(stacks, spread, *highs, *lows)


def swap(x, axes, mask, size):
    return lax.ppermute(x, axes, [(i, i ^ mask) for i in range(size)])


def body(snapshots, weights, block_order, owner, offsets):
    lanes = lax.axis_size("tm")
    groups = lax.axis_size("sx") * lax.axis_size("sy")
    points = snapshots.shape[2]
    widths = [points // 2, points // 4, points // 4]
    scale = 1.0 / (lanes * groups * points)
    tables = (jnp.asarray(fourier_tables()), jnp.asarray(pick_table()))
    weights = weights.reshape(1, -1)

    arrived = []
    base = 0
    for width in widths:
        packed = pack(owner, snapshots, base, width, [p[0] for _, p in arrived[-1:]])
        moved = [swap(packed[d], "tm", d, lanes) for d in reversed(range(1, lanes))]
        pieces = [packed[0]] + moved[::-1]
        arrived.append((base, pieces))
        base += width

    highs, lows = [], []
    total = None
    for base, pieces in arrived:
        high, low, total = gram_part(
            block_order, offsets, weights, tables, pieces, total, base, scale
        )
        highs.append(high)
        lows.append(low)

    axes = ("tm", "sx", "sy")
    size = lanes * groups
    total = total.reshape(size, -1, min(LANE, PACKED * NFREQ // size))
    total = lax.all_to_all(total, axes, split_axis=0, concat_axis=0, tiled=True)
    total = jnp.broadcast_to(jnp.sum(total, axis=0, keepdims=True), total.shape)
    total = lax.all_to_all(total, axes, split_axis=0, concat_axis=0, tiled=True)
    total = total.reshape(PACKED, NFREQ)
    stacks, gram = roots([total], NFREQ // groups)
    modes = mode_fields(stacks, jnp.asarray(spread_table()), highs, lows)
    modes = jnp.transpose(modes, (0, 2, 1, 3))[:, :, :, None, :]
    return modes, jnp.transpose(gram, (2, 3, 0, 1))


def solution(mesh):
    placed = (P("tm", None, ("sx", "sy")), P(("sx", "sy")), P(), P(("sx", "sy"), None), P())
    return jax.shard_map(
        body,
        mesh=mesh,
        in_specs=placed,
        out_specs=(P(None, None, None, "tm", ("sx", "sy")), P(None, ("sx", "sy"), None, None)),
        check_vma=False,
    )
```

```python
import functools
import math

import jax
import jax.numpy as jnp
import numpy as np
from jax import lax
from jax.experimental import pallas as pl
from jax.experimental.pallas import tpu as pltpu
from jax.sharding import PartitionSpec as P

NFFT = 256
ROOT_STEPS = 5
NFREQ = 128
NBLK = 11
LANE = 128
SUB = 8
HALF_ROWS = NBLK * SUB
GROUPS = NFREQ // SUB
PACKED = 128
STACK = 4
CORNER = NBLK - SUB
WIDE = 2 * LANE
FIRST_LIMIT = 64 * 2**20
SECOND_LIMIT = FIRST_LIMIT - 1450 * 2**10
BF16 = jnp.bfloat16
F32 = jnp.float32


def fourier_tables():
    n = np.arange(NFFT)
    k = np.arange(NFREQ)
    angles = 2.0 * np.pi * ((k[:, None] * n[None, :]) % NFFT) / NFFT
    scaled = (0.5 - 0.5 * np.cos(2.0 * np.pi * n / NFFT)) / math.sqrt(0.375 * NFFT)
    table = np.concatenate([np.cos(angles) * scaled, -np.sin(angles) * scaled], axis=0)
    high = table.astype(jnp.bfloat16)
    low = (table - high.astype(np.float64)).astype(jnp.bfloat16)
    return np.stack([high, low])


def packed_rows():
    rows = {}
    for a in range(NBLK):
        for e in range(a, NBLK):
            rows[0, a, e] = len(rows)
        for e in range(a + 1, NBLK):
            rows[1, a, e] = len(rows)
    return rows


ROWS = packed_rows()


def pick_table():
    pick = np.zeros((NBLK, 2, LANE, PACKED), np.float32)
    for (part, a, e), row in ROWS.items():
        pick[a, part, e * SUB : (e + 1) * SUB, row] = 1.0
    return pick.reshape(NBLK * WIDE, PACKED).astype(jnp.bfloat16)


def spread_table():
    spread = np.zeros((STACK, 2, LANE, 2 * HALF_ROWS), np.float32)
    for m in range(STACK):
        for b in range(NBLK):
            real = m * 32 + b
            imag = m * 32 + 16 + b
            first = slice(b * SUB, b * SUB + SUB)
            second = slice(HALF_ROWS + b * SUB, HALF_ROWS + b * SUB + SUB)
            spread[m, 0, real, first] = 1.0
            spread[m, 0, imag, second] = 1.0
            spread[m, 1, imag, first] = -1.0
            spread[m, 1, real, second] = 1.0
    spread = np.concatenate([spread, spread], axis=2)
    return spread.reshape(STACK * 2, WIDE, 2 * HALF_ROWS).astype(jnp.bfloat16)


def split(x):
    high = x.astype(BF16)
    return high, (x - high.astype(F32)).astype(BF16)


def dot(a, b):
    return jnp.dot(a, b, preferred_element_type=F32)


def dot_nt(a, b):
    return lax.dot_general(a, b, (((1,), (1,)), ((), ())), preferred_element_type=F32)


def spec(shape):
    return pl.BlockSpec(shape, lambda *_: (0,) * len(shape))


SMEM = pl.BlockSpec(memory_space=pltpu.SMEM)
VMEM = pl.BlockSpec(memory_space=pltpu.VMEM)
HBM = pl.BlockSpec(memory_space=pltpu.HBM)


def lane_pick(owner, lanes):
    me = lax.axis_index("tm")
    rows = WIDE // lanes
    out_row = lax.broadcasted_iota(jnp.int32, (WIDE, WIDE), 0)
    in_row = lax.broadcasted_iota(jnp.int32, (WIDE, WIDE), 1)
    row_of = (out_row % rows) * lanes
    for d in range(lanes):
        slot = me ^ d
        source = jnp.int32(0)
        for lane in range(lanes):
            source = source + jnp.where(owner[0, lane] == slot, lane, 0)
        row_of = jnp.where(out_row // rows == d, row_of + source, row_of)
    return jnp.where(in_row == row_of, 1.0, 0.0).astype(BF16)


def pack_kernel(base, parts, first, table_hbm, x_hbm, *refs):
    lanes = x_hbm.shape[1]
    out_refs = refs[:lanes]
    if first:
        pick, table, x_ref, table_sem, x_sem = refs[lanes:]
    else:
        pick, x_ref, table_sem, x_sem = refs[lanes:]
        table = pick
    steps, _, width = x_ref.shape
    part = steps // parts
    table_copy = pltpu.make_async_copy(table_hbm, table, table_sem)
    table_copy.start()
    copies = []
    for i in range(parts):
        at = slice(i * part, (i + 1) * part)
        source = x_hbm.at[at, :, base : base + width]
        copies.append(pltpu.make_async_copy(source, x_ref.at[at], x_sem.at[i]))
        copies[-1].start()
    table_copy.wait()
    if first:
        pick[...] = lane_pick(table, lanes)
    rows = WIDE // lanes
    for i in range(steps // rows):
        if i * rows % part == 0:
            copies[i * rows // part].wait()
        at = slice(i * rows, (i + 1) * rows)
        y = dot(pick[...], x_ref[at].reshape(WIDE, width)).astype(BF16)
        for d in range(lanes):
            out_refs[d][at, :] = y[d * rows : (d + 1) * rows]


def pack(table, snapshots, base, width, first):
    steps, lanes, _ = snapshots.shape
    parts = math.gcd(steps * lanes // WIDE, 3)
    outs = [jax.ShapeDtypeStruct((steps, width), BF16)] * lanes
    scratch = [
        pltpu.VMEM((steps, lanes, width), BF16),
        pltpu.SemaphoreType.DMA,
        pltpu.SemaphoreType.DMA((parts,)),
    ]
    if first:
        outs.append(jax.ShapeDtypeStruct((WIDE, WIDE), BF16))
        scratch = [pltpu.SMEM(table.shape, jnp.int32)] + scratch
    else:
        scratch = [pltpu.VMEM(table.shape, BF16)] + scratch
    return pl.pallas_call(
        functools.partial(pack_kernel, base, parts, first),
        out_shape=outs,
        in_specs=[HBM] * 2,
        out_specs=[VMEM] * len(outs),
        scratch_shapes=scratch,
        compiler_params=pltpu.CompilerParams(
            vmem_limit_bytes=FIRST_LIMIT if first else SECOND_LIMIT
        ),
        cost_estimate=pl.CostEstimate(
            flops=2 * WIDE * steps * lanes * width,
            bytes_accessed=4 * steps * lanes * width,
            transcendentals=0,
        ),
    )(table, snapshots)


def fill_record(order_ref, pieces, record, factor):
    steps, width = pieces[0].shape
    me = lax.axis_index("tm")
    for d, piece in enumerate(pieces):
        partner = me ^ (len(pieces) - d if d else 0)
        start = pl.multiple_of(order_ref[partner] * steps, steps)
        for c in range(width // LANE):
            cols = slice(c * LANE, (c + 1) * LANE)
            part = piece[:, cols].astype(F32)
            record[c, pl.ds(start, steps), :] = part if factor is None else part * factor[:, cols]


def transform(offsets_ref, f_ref, record, s_ref):
    for i in range(NBLK):
        x = [record[c, pl.ds(offsets_ref[i], NFFT), :].astype(BF16) for c in range(record.shape[0])]
        x = jnp.concatenate(x, axis=1)
        y = dot(f_ref[0], x) + dot(f_ref[1], x)
        s_ref[i] = y[:NFREQ]
        s_ref[NBLK + i] = y[NFREQ:]


def gram_kernel(lanes, scale, first, order_ref, offsets_ref, w_ref, f_ref, pick_ref, *refs):
    pieces = refs[:lanes]
    rest = refs[lanes:]
    if not first:
        before_ref, _, *rest = rest
    packed_ref, record, s_ref, masked = rest
    fill_record(order_ref, pieces, record, jnp.sqrt(w_ref[...]))
    transform(offsets_ref, f_ref, record, s_ref)
    row = lax.broadcasted_iota(jnp.int32, (HALF_ROWS, LANE), 0)
    col = lax.broadcasted_iota(jnp.int32, (HALF_ROWS, LANE), 1)
    same = row % SUB == col % SUB
    pad = jnp.zeros((LANE - HALF_ROWS, s_ref.shape[2]), F32)
    for g in range(GROUPS):
        at = slice(g * SUB, (g + 1) * SUB)
        s = s_ref[:, at, :].reshape(2 * HALF_ROWS, -1)
        other = jnp.concatenate([s[:HALF_ROWS], pad, s[HALF_ROWS:], pad], axis=0)
        full = dot_nt(s.astype(BF16), other.astype(BF16))
        real = full[:HALF_ROWS, :LANE] + full[HALF_ROWS:, LANE:]
        imag = full[:HALF_ROWS, LANE:] - full[HALF_ROWS:, :LANE]
        real = jnp.where(same, real, 0.0)
        imag = jnp.where(same, imag, 0.0)
        for a in range(NBLK):
            rows = slice(a * SUB, (a + 1) * SUB)
            masked[at, a * WIDE : a * WIDE + LANE] = real[rows]
            masked[at, a * WIDE + LANE : (a + 1) * WIDE] = imag[rows]
    total = dot(masked[...].astype(BF16), pick_ref[...]).T * scale
    if not first:
        total = total + before_ref[...]
    packed_ref[...] = total.astype(packed_ref.dtype)


def gram_part(order, offsets, weights, tables, pieces, before, scale):
    lanes = len(pieces)
    steps, width = pieces[0].shape
    first = not before
    args = [order, offsets, weights, *tables, *pieces, *before]
    return pl.pallas_call(
        functools.partial(gram_kernel, lanes, scale, first),
        out_shape=jax.ShapeDtypeStruct((PACKED, NFREQ), F32 if first else BF16),
        in_specs=[SMEM, SMEM] + [VMEM] * (len(args) - 2),
        out_specs=VMEM,
        scratch_shapes=[
            pltpu.VMEM((width // LANE, lanes * steps, LANE), F32),
            pltpu.VMEM((2 * NBLK, NFREQ, width), F32),
            pltpu.VMEM((NFREQ, NBLK * WIDE), F32),
        ],
        compiler_params=pltpu.CompilerParams(vmem_limit_bytes=32 * 2**20),
        cost_estimate=pl.CostEstimate(
            flops=25 * 10**8, bytes_accessed=3 * 10**6, transcendentals=0
        ),
    )(*args)


def spectrum_kernel(lanes, order_ref, offsets_ref, f_ref, *refs):
    high_ref, low_ref, record, s_ref = refs[-4:]
    fill_record(order_ref, refs[:lanes], record, None)
    transform(offsets_ref, f_ref, record, s_ref)
    for g in range(GROUPS):
        s = s_ref[:, g * SUB : (g + 1) * SUB, :].reshape(2 * HALF_ROWS, -1)
        high_ref[g], low_ref[g] = split(s)


def spectrum(order, offsets, fourier, pieces, after):
    lanes = len(pieces)
    steps, width = pieces[0].shape
    args = [order, offsets, fourier, *pieces, *after]
    part = jax.ShapeDtypeStruct((GROUPS, 2 * HALF_ROWS, width), BF16)
    return pl.pallas_call(
        functools.partial(spectrum_kernel, lanes),
        out_shape=[part, part],
        in_specs=[SMEM, SMEM] + [VMEM] * (len(args) - 2),
        out_specs=[VMEM, VMEM],
        scratch_shapes=[
            pltpu.VMEM((width // LANE, lanes * steps, LANE), F32),
            pltpu.VMEM((2 * NBLK, NFREQ, width), F32),
        ],
        compiler_params=pltpu.CompilerParams(vmem_limit_bytes=32 * 2**20),
        cost_estimate=pl.CostEstimate(
            flops=25 * 10**8, bytes_accessed=3 * 10**6, transcendentals=0
        ),
    )(*args)


class Hermitian:
    def __init__(self, main, corner):
        self.main = main
        self.corner = corner

    def entry(self, a, e):
        if e < SUB:
            return self.main[0, a, pl.ds(e, 1), :], self.main[1, a, pl.ds(e, 1), :], 1
        if a < SUB:
            return self.main[0, e, pl.ds(a, 1), :], self.main[1, e, pl.ds(a, 1), :], -1
        at = pl.ds(e - SUB, 1)
        return self.corner[0, a - SUB, at, :], self.corner[1, a - SUB, at, :], 1

    def put(self, a, e, real, imag):
        if e < SUB:
            self.main[0, a, pl.ds(e, 1), :] = real
            self.main[1, a, pl.ds(e, 1), :] = imag
        elif a >= SUB:
            at = pl.ds(e - SUB, 1)
            self.corner[0, a - SUB, at, :] = real
            self.corner[1, a - SUB, at, :] = imag


def product(x, y, out, diagonal=0.0, factor=1.0):
    sub = lax.broadcasted_iota(jnp.int32, (SUB, NFREQ), 0)
    yr = [y.main[0, b] for b in range(NBLK)]
    yi = [y.main[1, b] for b in range(NBLK)]
    for a in range(NBLK):
        real = imag = None
        for b in range(NBLK):
            pr, pi, sign = x.entry(a, b)
            tr, ti = pi * yi[b], pi * yr[b]
            if sign > 0:
                tr, ti = pr * yr[b] - tr, pr * yi[b] + ti
            else:
                tr, ti = pr * yr[b] + tr, pr * yi[b] - ti
            real = tr if real is None else real + tr
            imag = ti if imag is None else imag + ti
        if factor != 1.0:
            real, imag = factor * real, factor * imag
        if diagonal and a < SUB:
            real = real + jnp.where(sub == a, diagonal, 0.0)
        out.main[0, a] = real
        out.main[1, a] = imag
    ar = [[x.main[0, SUB + a], x.corner[0, a]] for a in range(CORNER)]
    ai = [[x.main[1, SUB + a], x.corner[1, a]] for a in range(CORNER)]
    er = [[yr[SUB + e], y.corner[0, e]] for e in range(CORNER)]
    ei = [[yi[SUB + e], y.corner[1, e]] for e in range(CORNER)]
    for a in range(CORNER):
        for e in range(a, CORNER):
            real = sum(ar[a][h] * er[e][h] + ai[a][h] * ei[e][h] for h in range(2))
            real = factor * jnp.sum(real, axis=0, keepdims=True)
            if a == e:
                real = real + diagonal
                out.put(SUB + a, SUB + a, real, jnp.zeros_like(real))
            else:
                imag = sum(ai[a][h] * er[e][h] - ar[a][h] * ei[e][h] for h in range(2))
                imag = factor * jnp.sum(imag, axis=0, keepdims=True)
                out.put(SUB + a, SUB + e, real, imag)
                out.put(SUB + e, SUB + a, real, -imag)


def affine(x, outs):
    sub = lax.broadcasted_iota(jnp.int32, (SUB, NFREQ), 0)
    for a in range(NBLK):
        real = -0.5 * x.main[0, a]
        imag = -0.5 * x.main[1, a]
        if a < SUB:
            real = real + jnp.where(sub == a, 1.5, 0.0)
        for out in outs:
            out.main[0, a] = real
            out.main[1, a] = imag
    for a in range(CORNER):
        real = jnp.where(sub == a, 1.5, 0.0) - 0.5 * x.corner[0, a]
        imag = -0.5 * x.corner[1, a]
        for out in outs:
            out.corner[0, a] = real
            out.corner[1, a] = imag


def root_kernel(parts, share, *refs):
    part_refs = refs[:parts]
    stack_ref, gram_ref, packed, rolled, *mats = refs[parts:]
    terms = [r[...].astype(F32) for r in part_refs]
    packed[...] = terms[0] + terms[1]
    at = lax.axis_index("sx") * lax.axis_size("sy") + lax.axis_index("sy")
    rolled[...] = pltpu.roll(packed[...], (NFREQ - at * share) % NFREQ, 1)
    y, z, p, y2, z2 = [Hermitian(mats[2 * i], mats[2 * i + 1]) for i in range(5)]
    for ref in mats[1::2]:
        ref[...] = jnp.zeros_like(ref)

    def row(ref, part, a, e):
        return ref[pl.ds(ROWS[part, a, e], 1), :]

    trace = 2.0 * sum(row(packed, 0, a, a) for a in range(NBLK))
    norm = 1.0 / jnp.sqrt(trace)
    packed[...] = packed[...] / trace
    zero = jnp.zeros((1, NFREQ), F32)
    for a in range(NBLK):
        y.put(a, a, row(packed, 0, a, a), zero)
        gram_ref[a, a, 0:1, :] = row(rolled, 0, a, a)[:, :share]
        gram_ref[a, a, 1:2, :] = zero[:, :share]
        for e in range(a + 1, NBLK):
            real, imag = row(packed, 0, a, e), row(packed, 1, a, e)
            y.put(a, e, real, imag)
            y.put(e, a, real, -imag)
            real, imag = row(rolled, 0, a, e)[:, :share], row(rolled, 1, a, e)[:, :share]
            gram_ref[a, e, 0:1, :] = real
            gram_ref[e, a, 0:1, :] = real
            gram_ref[a, e, 1:2, :] = imag
            gram_ref[e, a, 1:2, :] = -imag
    for step in range(ROOT_STEPS):
        if step == 0:
            affine(y, [p, z2])
        else:
            product(z, y, p, 1.5, -0.5)
            product(p, z, z2)
        if step < ROOT_STEPS - 1:
            product(y, p, y2)
        y, y2 = y2, y
        z, z2 = z2, z
    none = jnp.zeros((SUB - CORNER, NFREQ), F32)
    for at, m0 in enumerate(range(0, NBLK, STACK)):
        modes = range(m0, min(m0 + STACK, NBLK))
        stack = []
        for m in modes:
            for c in range(2):
                stack.append(z.main[c, m] * norm)
                for b in range(SUB, NBLK):
                    real, imag, sign = z.entry(m, b)
                    stack.append((imag * sign if c else real) * norm)
                stack.append(none)
        stack += [jnp.zeros((32, NFREQ), F32)] * (STACK - len(modes))
        stack_ref[at] = jnp.concatenate(stack, axis=0).T


def roots(parts, share):
    stacks = -(-NBLK // STACK)
    return pl.pallas_call(
        functools.partial(root_kernel, len(parts), share),
        out_shape=[
            jax.ShapeDtypeStruct((stacks, NFREQ, LANE), F32),
            jax.ShapeDtypeStruct((NBLK, NBLK, 2, share), F32),
        ],
        in_specs=[VMEM] * len(parts),
        out_specs=[VMEM] * 2,
        scratch_shapes=[pltpu.VMEM((PACKED, NFREQ), F32)] * 2
        + [
            pltpu.VMEM((2, NBLK, SUB, NFREQ), F32),
            pltpu.VMEM((2, CORNER, SUB, NFREQ), F32),
        ]
        * 5,
        compiler_params=pltpu.CompilerParams(vmem_limit_bytes=32 * 2**20),
    )(*parts)


def mode_kernel(chunks, stack_ref, spread_ref, *refs):
    high_refs = refs[:chunks]
    low_refs = refs[chunks : 2 * chunks]
    out_ref, v = refs[2 * chunks :]
    step = pl.program_id(0)

    @pl.when(step == 0)
    def _():
        row = lax.broadcasted_iota(jnp.int32, (NFREQ, 2 * HALF_ROWS), 0)
        col = lax.broadcasted_iota(jnp.int32, (NFREQ, 2 * HALF_ROWS), 1)
        same = row % SUB == col % SUB
        for at, m0 in enumerate(range(0, NBLK, STACK)):
            both = jnp.concatenate(split(stack_ref[at]), axis=1)
            for m in range(m0, min(m0 + STACK, NBLK)):
                for c in range(2):
                    wide = dot(both, spread_ref[(m - m0) * 2 + c])
                    v[c * NBLK + m] = jnp.where(same, wide, 0.0)

    fields = []
    for h in range(2):
        g = step * 2 + h
        start = pl.multiple_of(g * SUB, SUB)
        v_high, v_low = split(v[:, pl.ds(start, SUB), :].reshape(2 * HALF_ROWS, 2 * HALF_ROWS))
        s_high = jnp.concatenate([r[g] for r in high_refs], axis=1)
        s_low = jnp.concatenate([r[g] for r in low_refs], axis=1)
        field = dot(jnp.concatenate([v_high, v_low], axis=0), s_high)
        field = field[: 2 * HALF_ROWS] + (field[2 * HALF_ROWS :] + dot(v_high, s_low))
        fields.append(field.reshape(2 * NBLK, SUB, -1))
    both = jnp.concatenate(fields, axis=1).astype(BF16)
    out_ref[...] = both.reshape(out_ref.shape)


def mode_fields(stacks, spread, highs, lows):
    width = sum(s.shape[2] for s in highs)
    return pl.pallas_call(
        functools.partial(mode_kernel, len(highs)),
        grid=(NFREQ // 16,),
        out_shape=jax.ShapeDtypeStruct((2, NBLK, NFREQ, width), BF16),
        in_specs=[VMEM] * (2 + 2 * len(highs)),
        out_specs=pl.BlockSpec((2, NBLK, 16, width), lambda i: (0, 0, i, 0)),
        scratch_shapes=[pltpu.VMEM((2 * NBLK, NFREQ, 2 * HALF_ROWS), F32)],
        compiler_params=pltpu.CompilerParams(vmem_limit_bytes=32 * 2**20),
    )(stacks, spread, *highs, *lows)


def swap(x, axes, mask, size):
    return lax.ppermute(x, axes, [(i, i ^ mask) for i in range(size)])


def powers(size):
    return [1 << i for i in range(size.bit_length() - 1)]


def body(snapshots, weights, block_order, owner, offsets):
    lanes = lax.axis_size("tm")
    groups = lax.axis_size("sx") * lax.axis_size("sy")
    points = snapshots.shape[2]
    width = points // 2
    scale = 1.0 / (lanes * groups * points)
    tables = (jnp.asarray(fourier_tables()), jnp.asarray(pick_table()))
    weights = weights.reshape(1, -1)

    arrived = []
    table = owner
    for base in range(0, points, width):
        packed = pack(table, snapshots, base, width, base == 0)
        table = packed[lanes] if base == 0 else table
        moved = [swap(packed[d], "tm", d, lanes) for d in reversed(range(1, lanes))]
        arrived.append([packed[0]] + moved)

    highs, lows = [], []
    before = []
    for at, pieces in enumerate(arrived):
        here = weights[:, at * width : (at + 1) * width]
        total = gram_part(block_order, offsets, here, tables, pieces, before, scale)
        after = [total] if at == len(arrived) - 1 else []
        high, low = spectrum(block_order, offsets, tables[0], pieces, after)
        highs.append(high)
        lows.append(low)
        before = [total, high]

    axes = ("tm", "sx", "sy")
    size = lanes * groups
    masks = [b * groups for b in powers(lanes)] + powers(groups)
    other = swap(total, axes, masks[0], size)
    for mask in masks[1:]:
        total = (total.astype(F32) + other.astype(F32)).astype(BF16)
        other = swap(total, axes, mask, size)

    stacks, gram = roots([total, other], NFREQ // groups)
    modes = mode_fields(stacks, jnp.asarray(spread_table()), highs, lows)
    modes = jnp.transpose(modes, (0, 2, 1, 3))[:, :, :, None, :]
    return modes, jnp.transpose(gram, (2, 3, 0, 1))


def solution(mesh):
    placed = (P("tm", None, ("sx", "sy")), P(("sx", "sy")), P(), P(("sx", "sy"), None), P())
    return jax.shard_map(
        body,
        mesh=mesh,
        in_specs=placed,
        out_specs=(P(None, None, None, "tm", ("sx", "sy")), P(None, ("sx", "sy"), None, None)),
        check_vma=False,
    )
```

```python
import functools
import math

import jax
import jax.numpy as jnp
import numpy as np
from jax import lax
from jax.experimental import pallas as pl
from jax.experimental.pallas import tpu as pltpu
from jax.sharding import PartitionSpec as P

NFFT = 256
ROOT_STEPS = 5
NFREQ = 128
NBLK = 11
LANE = 128
SUB = 8
HALF_ROWS = NBLK * SUB
GROUPS = NFREQ // SUB
STEP_GROUPS = 4
PACKED = 128
HALF = PACKED // 2
STACK = 4
CORNER = NBLK - SUB
WIDE = 2 * LANE
FIRST_LIMIT = 64 * 2**20
SECOND_LIMIT = FIRST_LIMIT - 1450 * 2**10
BF16 = jnp.bfloat16
F32 = jnp.float32


def fourier_tables():
    n = np.arange(NFFT)
    k = np.arange(NFREQ)
    angles = 2.0 * np.pi * ((k[:, None] * n[None, :]) % NFFT) / NFFT
    scaled = (0.5 - 0.5 * np.cos(2.0 * np.pi * n / NFFT)) / math.sqrt(0.375 * NFFT)
    table = np.concatenate([np.cos(angles) * scaled, -np.sin(angles) * scaled], axis=0)
    high = table.astype(jnp.bfloat16)
    low = (table - high.astype(np.float64)).astype(jnp.bfloat16)
    return np.concatenate([high, low], axis=1)


def packed_rows():
    rows = {}
    for a in range(NBLK):
        for e in range(a, NBLK):
            rows[0, a, e] = len(rows)
        for e in range(a + 1, NBLK):
            rows[1, a, e] = len(rows)
    return rows


ROWS = packed_rows()


def pick_table():
    pick = np.zeros((NBLK, 2, LANE, PACKED), np.float32)
    for (part, a, e), row in ROWS.items():
        pick[a, part, e * SUB : (e + 1) * SUB, row] = 1.0
    return pick.reshape(NBLK * WIDE, PACKED).astype(jnp.bfloat16)


def spread_table():
    spread = np.zeros((STACK, 2, LANE, 2 * HALF_ROWS), np.float32)
    for m in range(STACK):
        for b in range(NBLK):
            real = m * 32 + b
            imag = m * 32 + 16 + b
            first = slice(b * SUB, b * SUB + SUB)
            second = slice(HALF_ROWS + b * SUB, HALF_ROWS + b * SUB + SUB)
            spread[m, 0, real, first] = 1.0
            spread[m, 0, imag, second] = 1.0
            spread[m, 1, imag, first] = -1.0
            spread[m, 1, real, second] = 1.0
    spread = np.concatenate([spread, spread], axis=2)
    return spread.reshape(STACK * 2, WIDE, 2 * HALF_ROWS).astype(jnp.bfloat16)


def split(x):
    high = x.astype(BF16)
    return high, (x - high.astype(F32)).astype(BF16)


def dot(a, b):
    return jnp.dot(a, b, preferred_element_type=F32)


def dot_nt(a, b):
    return lax.dot_general(a, b, (((1,), (1,)), ((), ())), preferred_element_type=F32)


def spec(shape):
    return pl.BlockSpec(shape, lambda *_: (0,) * len(shape))


SMEM = pl.BlockSpec(memory_space=pltpu.SMEM)
VMEM = pl.BlockSpec(memory_space=pltpu.VMEM)
HBM = pl.BlockSpec(memory_space=pltpu.HBM)


def lane_pick(owner, lanes):
    me = lax.axis_index("tm")
    rows = WIDE // lanes
    out_row = lax.broadcasted_iota(jnp.int32, (WIDE, WIDE), 0)
    in_row = lax.broadcasted_iota(jnp.int32, (WIDE, WIDE), 1)
    row_of = (out_row % rows) * lanes
    for d in range(lanes):
        slot = me ^ d
        source = jnp.int32(0)
        for lane in range(lanes):
            source = source + jnp.where(owner[0, lane] == slot, lane, 0)
        row_of = jnp.where(out_row // rows == d, row_of + source, row_of)
    return jnp.where(in_row == row_of, 1.0, 0.0).astype(BF16)


def pack_kernel(base, parts, first, table_hbm, x_hbm, *refs):
    lanes = x_hbm.shape[1]
    out_refs = refs[:lanes]
    if first:
        pick, table, x_ref, table_sem, x_sem = refs[lanes:]
    else:
        pick, x_ref, table_sem, x_sem = refs[lanes:]
        table = pick
    steps, _, width = x_ref.shape
    part = steps // parts
    table_copy = pltpu.make_async_copy(table_hbm, table, table_sem)
    table_copy.start()
    copies = []
    for i in range(parts):
        at = slice(i * part, (i + 1) * part)
        source = x_hbm.at[at, :, base : base + width]
        copies.append(pltpu.make_async_copy(source, x_ref.at[at], x_sem.at[i]))
        copies[-1].start()
    table_copy.wait()
    if first:
        pick[...] = lane_pick(table, lanes)
    rows = WIDE // lanes
    for i in range(steps // rows):
        if i * rows % part == 0:
            copies[i * rows // part].wait()
        at = slice(i * rows, (i + 1) * rows)
        y = dot(pick[...], x_ref[at].reshape(WIDE, width)).astype(BF16)
        for d in range(lanes):
            out_refs[d][at, :] = y[d * rows : (d + 1) * rows]


def pack(table, snapshots, base, width, first):
    steps, lanes, _ = snapshots.shape
    parts = math.gcd(steps * lanes // WIDE, 3)
    outs = [jax.ShapeDtypeStruct((steps, width), BF16)] * lanes
    scratch = [
        pltpu.VMEM((steps, lanes, width), BF16),
        pltpu.SemaphoreType.DMA,
        pltpu.SemaphoreType.DMA((parts,)),
    ]
    if first:
        outs.append(jax.ShapeDtypeStruct((WIDE, WIDE), BF16))
        scratch = [pltpu.SMEM(table.shape, jnp.int32)] + scratch
    else:
        scratch = [pltpu.VMEM(table.shape, BF16)] + scratch
    return pl.pallas_call(
        functools.partial(pack_kernel, base, parts, first),
        out_shape=outs,
        in_specs=[HBM] * 2,
        out_specs=[VMEM] * len(outs),
        scratch_shapes=scratch,
        compiler_params=pltpu.CompilerParams(
            vmem_limit_bytes=FIRST_LIMIT if first else SECOND_LIMIT
        ),
        cost_estimate=pl.CostEstimate(
            flops=2 * WIDE * steps * lanes * width,
            bytes_accessed=4 * steps * lanes * width,
            transcendentals=0,
        ),
    )(table, snapshots)


def fill_record(order_ref, pieces, record, factor):
    steps, width = pieces[0].shape
    me = lax.axis_index("tm")
    for d, piece in enumerate(pieces):
        partner = me ^ (len(pieces) - d if d else 0)
        start = pl.multiple_of(order_ref[partner] * steps, steps)
        for c in range(width // LANE):
            cols = slice(c * LANE, (c + 1) * LANE)
            part = piece[:, cols].astype(F32)
            record[c, pl.ds(start, steps), :] = part if factor is None else part * factor[:, cols]


def transform(offsets_ref, f_ref, record, s_ref):
    for i in range(NBLK):
        x = [record[c, pl.ds(offsets_ref[i], NFFT), :].astype(BF16) for c in range(record.shape[0])]
        x = jnp.concatenate(x, axis=1)
        y = dot(f_ref[...], jnp.concatenate([x, x], axis=0))
        s_ref[i] = y[:NFREQ]
        s_ref[NBLK + i] = y[NFREQ:]


def gram_kernel(lanes, scale, first, order_ref, offsets_ref, w_ref, f_ref, pick_ref, *refs):
    pieces = refs[:lanes]
    rest = refs[lanes:]
    if not first:
        before_ref, _, *rest = rest
    *packed_refs, record, s_ref, masked = rest
    fill_record(order_ref, pieces, record, jnp.sqrt(w_ref[...]))
    transform(offsets_ref, f_ref, record, s_ref)
    row = lax.broadcasted_iota(jnp.int32, (HALF_ROWS, LANE), 0)
    col = lax.broadcasted_iota(jnp.int32, (HALF_ROWS, LANE), 1)
    same = row % SUB == col % SUB
    pad = jnp.zeros((LANE - HALF_ROWS, s_ref.shape[2]), F32)
    for g in range(GROUPS):
        at = slice(g * SUB, (g + 1) * SUB)
        s = s_ref[:, at, :].reshape(2 * HALF_ROWS, -1)
        other = jnp.concatenate([s[:HALF_ROWS], pad, s[HALF_ROWS:], pad], axis=0)
        full = dot_nt(s.astype(BF16), other.astype(BF16))
        real = full[:HALF_ROWS, :LANE] + full[HALF_ROWS:, LANE:]
        imag = full[:HALF_ROWS, LANE:] - full[HALF_ROWS:, :LANE]
        real = jnp.where(same, real, 0.0)
        imag = jnp.where(same, imag, 0.0)
        for a in range(NBLK):
            rows = slice(a * SUB, (a + 1) * SUB)
            masked[at, a * WIDE : a * WIDE + LANE] = real[rows]
            masked[at, a * WIDE + LANE : (a + 1) * WIDE] = imag[rows]
    total = dot(masked[...].astype(BF16), pick_ref[...]).T * scale
    if first:
        packed_refs[0][...] = total
        return
    keep_ref, send_ref = packed_refs
    total = total + before_ref[...]
    other = lax.axis_index("tm") % 2 == 1
    keep_ref[...] = jnp.where(other, total[HALF:], total[:HALF]).astype(BF16)
    send_ref[...] = jnp.where(other, total[:HALF], total[HALF:]).astype(BF16)


def gram_part(order, offsets, weights, tables, pieces, before, scale):
    lanes = len(pieces)
    steps, width = pieces[0].shape
    first = not before
    args = [order, offsets, weights, *tables, *pieces, *before]
    return pl.pallas_call(
        functools.partial(gram_kernel, lanes, scale, first),
        out_shape=[jax.ShapeDtypeStruct((PACKED, NFREQ), F32)]
        if first
        else [jax.ShapeDtypeStruct((HALF, NFREQ), BF16)] * 2,
        in_specs=[SMEM, SMEM] + [VMEM] * (len(args) - 2),
        out_specs=[VMEM] * (1 if first else 2),
        scratch_shapes=[
            pltpu.VMEM((width // LANE, lanes * steps, LANE), F32),
            pltpu.VMEM((2 * NBLK, NFREQ, width), F32),
            pltpu.VMEM((NFREQ, NBLK * WIDE), F32),
        ],
        compiler_params=pltpu.CompilerParams(vmem_limit_bytes=32 * 2**20),
        cost_estimate=pl.CostEstimate(
            flops=25 * 10**8, bytes_accessed=3 * 10**6, transcendentals=0
        ),
    )(*args)


def spectrum_kernel(lanes, order_ref, offsets_ref, f_ref, *refs):
    high_ref, low_ref, record, s_ref = refs[-4:]
    fill_record(order_ref, refs[:lanes], record, None)
    transform(offsets_ref, f_ref, record, s_ref)
    for g in range(GROUPS):
        s = s_ref[:, g * SUB : (g + 1) * SUB, :].reshape(2 * HALF_ROWS, -1)
        high_ref[g], low_ref[g] = split(s)


def spectrum(order, offsets, fourier, pieces, after):
    lanes = len(pieces)
    steps, width = pieces[0].shape
    args = [order, offsets, fourier, *pieces, *after]
    part = jax.ShapeDtypeStruct((GROUPS, 2 * HALF_ROWS, width), BF16)
    return pl.pallas_call(
        functools.partial(spectrum_kernel, lanes),
        out_shape=[part, part],
        in_specs=[SMEM, SMEM] + [VMEM] * (len(args) - 2),
        out_specs=[VMEM, VMEM],
        scratch_shapes=[
            pltpu.VMEM((width // LANE, lanes * steps, LANE), F32),
            pltpu.VMEM((2 * NBLK, NFREQ, width), F32),
        ],
        compiler_params=pltpu.CompilerParams(vmem_limit_bytes=32 * 2**20),
        cost_estimate=pl.CostEstimate(
            flops=25 * 10**8, bytes_accessed=3 * 10**6, transcendentals=0
        ),
    )(*args)


class Hermitian:
    def __init__(self, main, corner):
        self.main = main
        self.corner = corner

    def entry(self, a, e):
        if e < SUB:
            return self.main[0, a, pl.ds(e, 1), :], self.main[1, a, pl.ds(e, 1), :], 1
        if a < SUB:
            return self.main[0, e, pl.ds(a, 1), :], self.main[1, e, pl.ds(a, 1), :], -1
        at = pl.ds(e - SUB, 1)
        return self.corner[0, a - SUB, at, :], self.corner[1, a - SUB, at, :], 1

    def put(self, a, e, real, imag):
        if e < SUB:
            self.main[0, a, pl.ds(e, 1), :] = real
            self.main[1, a, pl.ds(e, 1), :] = imag
        elif a >= SUB:
            at = pl.ds(e - SUB, 1)
            self.corner[0, a - SUB, at, :] = real
            self.corner[1, a - SUB, at, :] = imag


def product(x, y, out, diagonal=0.0, factor=1.0):
    sub = lax.broadcasted_iota(jnp.int32, (SUB, NFREQ), 0)
    yr = [y.main[0, b] for b in range(NBLK)]
    yi = [y.main[1, b] for b in range(NBLK)]
    for a in range(NBLK):
        real = imag = None
        for b in range(NBLK):
            pr, pi, sign = x.entry(a, b)
            tr, ti = pi * yi[b], pi * yr[b]
            if sign > 0:
                tr, ti = pr * yr[b] - tr, pr * yi[b] + ti
            else:
                tr, ti = pr * yr[b] + tr, pr * yi[b] - ti
            real = tr if real is None else real + tr
            imag = ti if imag is None else imag + ti
        if factor != 1.0:
            real, imag = factor * real, factor * imag
        if diagonal and a < SUB:
            real = real + jnp.where(sub == a, diagonal, 0.0)
        out.main[0, a] = real
        out.main[1, a] = imag
    ar = [[x.main[0, SUB + a], x.corner[0, a]] for a in range(CORNER)]
    ai = [[x.main[1, SUB + a], x.corner[1, a]] for a in range(CORNER)]
    er = [[yr[SUB + e], y.corner[0, e]] for e in range(CORNER)]
    ei = [[yi[SUB + e], y.corner[1, e]] for e in range(CORNER)]
    for a in range(CORNER):
        for e in range(a, CORNER):
            real = sum(ar[a][h] * er[e][h] + ai[a][h] * ei[e][h] for h in range(2))
            real = factor * jnp.sum(real, axis=0, keepdims=True)
            if a == e:
                real = real + diagonal
                out.put(SUB + a, SUB + a, real, jnp.zeros_like(real))
            else:
                imag = sum(ai[a][h] * er[e][h] - ar[a][h] * ei[e][h] for h in range(2))
                imag = factor * jnp.sum(imag, axis=0, keepdims=True)
                out.put(SUB + a, SUB + e, real, imag)
                out.put(SUB + e, SUB + a, real, -imag)


def affine(x, outs):
    sub = lax.broadcasted_iota(jnp.int32, (SUB, NFREQ), 0)
    for a in range(NBLK):
        real = -0.5 * x.main[0, a]
        imag = -0.5 * x.main[1, a]
        if a < SUB:
            real = real + jnp.where(sub == a, 1.5, 0.0)
        for out in outs:
            out.main[0, a] = real
            out.main[1, a] = imag
    for a in range(CORNER):
        real = jnp.where(sub == a, 1.5, 0.0) - 0.5 * x.corner[0, a]
        imag = -0.5 * x.corner[1, a]
        for out in outs:
            out.corner[0, a] = real
            out.corner[1, a] = imag


def root_kernel(share, half_ref, other_ref, stack_ref, gram_ref, packed, rolled, *mats):
    core = lax.axis_index("tm") % 2
    packed[pl.ds(pl.multiple_of(core * HALF, HALF), HALF), :] = half_ref[...]
    packed[pl.ds(pl.multiple_of((1 - core) * HALF, HALF), HALF), :] = other_ref[...]
    at = lax.axis_index("sx") * lax.axis_size("sy") + lax.axis_index("sy")
    rolled[...] = pltpu.roll(packed[...], (NFREQ - at * share) % NFREQ, 1)
    y, z, p, y2, z2 = [Hermitian(mats[2 * i], mats[2 * i + 1]) for i in range(5)]
    for ref in mats[1::2]:
        ref[...] = jnp.zeros_like(ref)

    def row(ref, part, a, e):
        return ref[pl.ds(ROWS[part, a, e], 1), :]

    trace = 2.0 * sum(row(packed, 0, a, a) for a in range(NBLK))
    norm = 1.0 / jnp.sqrt(trace)
    packed[...] = packed[...] / trace
    zero = jnp.zeros((1, NFREQ), F32)
    for a in range(NBLK):
        y.put(a, a, row(packed, 0, a, a), zero)
        gram_ref[a, a, 0:1, :] = row(rolled, 0, a, a)[:, :share]
        gram_ref[a, a, 1:2, :] = zero[:, :share]
        for e in range(a + 1, NBLK):
            real, imag = row(packed, 0, a, e), row(packed, 1, a, e)
            y.put(a, e, real, imag)
            y.put(e, a, real, -imag)
            real, imag = row(rolled, 0, a, e)[:, :share], row(rolled, 1, a, e)[:, :share]
            gram_ref[a, e, 0:1, :] = real
            gram_ref[e, a, 0:1, :] = real
            gram_ref[a, e, 1:2, :] = imag
            gram_ref[e, a, 1:2, :] = -imag
    for step in range(ROOT_STEPS):
        if step == 0:
            affine(y, [p, z2])
        else:
            product(z, y, p, 1.5, -0.5)
            product(p, z, z2)
        if step < ROOT_STEPS - 1:
            product(y, p, y2)
        y, y2 = y2, y
        z, z2 = z2, z
    none = jnp.zeros((SUB - CORNER, NFREQ), F32)
    for at, m0 in enumerate(range(0, NBLK, STACK)):
        modes = range(m0, min(m0 + STACK, NBLK))
        stack = []
        for m in modes:
            for c in range(2):
                stack.append(z.main[c, m] * norm)
                for b in range(SUB, NBLK):
                    real, imag, sign = z.entry(m, b)
                    stack.append((imag * sign if c else real) * norm)
                stack.append(none)
        stack += [jnp.zeros((32, NFREQ), F32)] * (STACK - len(modes))
        stack_ref[at] = jnp.concatenate(stack, axis=0).T


def roots(half, other, share):
    stacks = -(-NBLK // STACK)
    return pl.pallas_call(
        functools.partial(root_kernel, share),
        out_shape=[
            jax.ShapeDtypeStruct((stacks, NFREQ, LANE), F32),
            jax.ShapeDtypeStruct((NBLK, NBLK, 2, share), F32),
        ],
        in_specs=[VMEM] * 2,
        out_specs=[VMEM] * 2,
        scratch_shapes=[pltpu.VMEM((PACKED, NFREQ), F32)] * 2
        + [
            pltpu.VMEM((2, NBLK, SUB, NFREQ), F32),
            pltpu.VMEM((2, CORNER, SUB, NFREQ), F32),
        ]
        * 5,
        compiler_params=pltpu.CompilerParams(vmem_limit_bytes=32 * 2**20),
    )(half, other)


def mode_kernel(chunks, stack_ref, spread_ref, *refs):
    high_refs = refs[:chunks]
    low_refs = refs[chunks : 2 * chunks]
    out_ref, v = refs[2 * chunks :]
    step = pl.program_id(0)

    @pl.when(step == 0)
    def _():
        row = lax.broadcasted_iota(jnp.int32, (NFREQ, 2 * HALF_ROWS), 0)
        col = lax.broadcasted_iota(jnp.int32, (NFREQ, 2 * HALF_ROWS), 1)
        same = row % SUB == col % SUB
        for at, m0 in enumerate(range(0, NBLK, STACK)):
            both = jnp.concatenate(split(stack_ref[at]), axis=1)
            for m in range(m0, min(m0 + STACK, NBLK)):
                for c in range(2):
                    wide = dot(both, spread_ref[(m - m0) * 2 + c])
                    v[c * NBLK + m] = jnp.where(same, wide, 0.0)

    fields = []
    for h in range(STEP_GROUPS):
        g = step * STEP_GROUPS + h
        start = pl.multiple_of(g * SUB, SUB)
        v_high, v_low = split(v[:, pl.ds(start, SUB), :].reshape(2 * HALF_ROWS, 2 * HALF_ROWS))
        s_high = jnp.concatenate([r[g] for r in high_refs], axis=1)
        s_low = jnp.concatenate([r[g] for r in low_refs], axis=1)
        field = dot(jnp.concatenate([v_high, v_low], axis=0), s_high)
        field = field[: 2 * HALF_ROWS] + (field[2 * HALF_ROWS :] + dot(v_high, s_low))
        fields.append(field.reshape(2 * NBLK, SUB, -1))
    both = jnp.concatenate(fields, axis=1).astype(BF16)
    out_ref[...] = both.reshape(out_ref.shape)


def mode_fields(stacks, spread, highs, lows):
    width = sum(s.shape[2] for s in highs)
    return pl.pallas_call(
        functools.partial(mode_kernel, len(highs)),
        grid=(GROUPS // STEP_GROUPS,),
        out_shape=jax.ShapeDtypeStruct((2, NBLK, NFREQ, width), BF16),
        in_specs=[VMEM] * (2 + 2 * len(highs)),
        out_specs=pl.BlockSpec(
            (2, NBLK, STEP_GROUPS * SUB, width), lambda i: (0, 0, i, 0)
        ),
        scratch_shapes=[pltpu.VMEM((2 * NBLK, NFREQ, 2 * HALF_ROWS), F32)],
        compiler_params=pltpu.CompilerParams(vmem_limit_bytes=32 * 2**20),
    )(stacks, spread, *highs, *lows)


def swap(x, axes, mask, size):
    return lax.ppermute(x, axes, [(i, i ^ mask) for i in range(size)])


def powers(size):
    return [1 << i for i in range(size.bit_length() - 1)]


def body(snapshots, weights, block_order, owner, offsets):
    lanes = lax.axis_size("tm")
    groups = lax.axis_size("sx") * lax.axis_size("sy")
    points = snapshots.shape[2]
    width = points // 2
    scale = 1.0 / (lanes * groups * points)
    tables = (jnp.asarray(fourier_tables()), jnp.asarray(pick_table()))
    weights = weights.reshape(1, -1)

    arrived = []
    table = owner
    for base in range(0, points, width):
        packed = pack(table, snapshots, base, width, base == 0)
        table = packed[lanes] if base == 0 else table
        moved = [swap(packed[d], "tm", d, lanes) for d in reversed(range(1, lanes))]
        arrived.append([packed[0]] + moved)

    highs, lows = [], []
    before = []
    for at, pieces in enumerate(arrived):
        here = weights[:, at * width : (at + 1) * width]
        total = gram_part(block_order, offsets, here, tables, pieces, before, scale)
        after = total if at == len(arrived) - 1 else []
        high, low = spectrum(block_order, offsets, tables[0], pieces, after)
        highs.append(high)
        lows.append(low)
        before = [total[0], high]

    axes = ("tm", "sx", "sy")
    size = lanes * groups
    bits = [b * groups for b in powers(lanes)] + powers(groups)
    keep, send = total
    half = keep.astype(F32) + swap(send, axes, bits[0], size).astype(F32)
    for at in range(1, len(bits), 2):
        masks = bits[at : at + 2]
        if len(masks) == 2:
            masks.append(masks[0] ^ masks[1])
        half = half.astype(BF16)
        terms = [half] + [swap(half, axes, mask, size) for mask in masks]
        terms = [t.astype(F32) for t in terms]
        while len(terms) > 1:
            terms = [a + b for a, b in zip(terms[::2], terms[1::2])]
        half = terms[0]
    other = swap(half, axes, bits[0], size)

    stacks, gram = roots(half, other, NFREQ // groups)
    modes = mode_fields(stacks, jnp.asarray(spread_table()), highs, lows)
    modes = jnp.transpose(modes, (0, 2, 1, 3))[:, :, :, None, :]
    return modes, jnp.transpose(gram, (2, 3, 0, 1))


def solution(mesh):
    placed = (P("tm", None, ("sx", "sy")), P(("sx", "sy")), P(), P(("sx", "sy"), None), P())
    return jax.shard_map(
        body,
        mesh=mesh,
        in_specs=placed,
        out_specs=(P(None, None, None, "tm", ("sx", "sy")), P(None, ("sx", "sy"), None, None)),
        check_vma=False,
    )
```

```python
import functools
import math

import jax
import jax.numpy as jnp
import numpy as np
from jax import lax
from jax.experimental import pallas as pl
from jax.experimental.pallas import tpu as pltpu
from jax.sharding import PartitionSpec as P

NFFT = 256
ROOT_STEPS = 5
NFREQ = 128
NBLK = 11
LANE = 128
SUB = 8
HALF_ROWS = NBLK * SUB
GROUPS = NFREQ // SUB
STEP_GROUPS = 4
PACKED = 128
HALF = PACKED // 2
STACK = 4
CORNER = NBLK - SUB
WIDE = 2 * LANE
FIRST_LIMIT = 64 * 2**20
SECOND_LIMIT = FIRST_LIMIT - 1450 * 2**10
BF16 = jnp.bfloat16
F32 = jnp.float32


def fourier_tables():
    n = np.arange(NFFT)
    k = np.arange(NFREQ)
    angles = 2.0 * np.pi * ((k[:, None] * n[None, :]) % NFFT) / NFFT
    scaled = (0.5 - 0.5 * np.cos(2.0 * np.pi * n / NFFT)) / math.sqrt(0.375 * NFFT)
    table = np.concatenate([np.cos(angles) * scaled, -np.sin(angles) * scaled], axis=0)
    high = table.astype(jnp.bfloat16)
    low = (table - high.astype(np.float64)).astype(jnp.bfloat16)
    return np.concatenate([high, low], axis=1)


def packed_rows():
    rows = {}
    for a in range(NBLK):
        for e in range(a, NBLK):
            rows[0, a, e] = len(rows)
        for e in range(a + 1, NBLK):
            rows[1, a, e] = len(rows)
    return rows


ROWS = packed_rows()


def pick_table():
    pick = np.zeros((NBLK, 2, LANE, PACKED), np.float32)
    for (part, a, e), row in ROWS.items():
        pick[a, part, e * SUB : (e + 1) * SUB, row] = 1.0
    return pick.reshape(NBLK * WIDE, PACKED).astype(jnp.bfloat16)


def spread_table():
    spread = np.zeros((STACK, 2, LANE, WIDE), np.float32)
    for m in range(STACK):
        for b in range(NBLK):
            real = m * 32 + b
            imag = m * 32 + 16 + b
            first = slice(b * SUB, b * SUB + SUB)
            second = slice(LANE + b * SUB, LANE + b * SUB + SUB)
            spread[m, 0, real, first] = 1.0
            spread[m, 0, imag, second] = 1.0
            spread[m, 1, imag, first] = -1.0
            spread[m, 1, real, second] = 1.0
    spread = np.concatenate([spread, spread], axis=2)
    return spread.reshape(STACK * 2, WIDE, WIDE).astype(jnp.bfloat16)


def split(x):
    high = x.astype(BF16)
    return high, (x - high.astype(F32)).astype(BF16)


def dot(a, b):
    return jnp.dot(a, b, preferred_element_type=F32)


def dot_nt(a, b):
    return lax.dot_general(a, b, (((1,), (1,)), ((), ())), preferred_element_type=F32)


def spec(shape):
    return pl.BlockSpec(shape, lambda *_: (0,) * len(shape))


SMEM = pl.BlockSpec(memory_space=pltpu.SMEM)
VMEM = pl.BlockSpec(memory_space=pltpu.VMEM)
HBM = pl.BlockSpec(memory_space=pltpu.HBM)


def lane_pick(owner, lanes):
    me = lax.axis_index("tm")
    rows = WIDE // lanes
    out_row = lax.broadcasted_iota(jnp.int32, (WIDE, WIDE), 0)
    in_row = lax.broadcasted_iota(jnp.int32, (WIDE, WIDE), 1)
    row_of = (out_row % rows) * lanes
    for d in range(lanes):
        slot = me ^ d
        source = jnp.int32(0)
        for lane in range(lanes):
            source = source + jnp.where(owner[0, lane] == slot, lane, 0)
        row_of = jnp.where(out_row // rows == d, row_of + source, row_of)
    return jnp.where(in_row == row_of, 1.0, 0.0).astype(BF16)


def pack_kernel(base, parts, first, table_hbm, x_hbm, *refs):
    lanes = x_hbm.shape[1]
    out_refs = refs[:lanes]
    pick, table, x_ref, table_sem, x_sem = refs[lanes:]
    steps, _, width = x_ref.shape
    part = steps // parts
    table_copy = pltpu.make_async_copy(table_hbm, table, table_sem)
    table_copy.start()
    copies = []
    for i in range(parts):
        at = slice(i * part, (i + 1) * part)
        source = x_hbm.at[at, :, base : base + width]
        copies.append(pltpu.make_async_copy(source, x_ref.at[at], x_sem.at[i]))
        copies[-1].start()
    table_copy.wait()
    pick[...] = lane_pick(table, lanes) if first else table[...]
    rows = WIDE // lanes
    for i in range(steps // rows):
        if i * rows % part == 0:
            copies[i * rows // part].wait()
        at = slice(i * rows, (i + 1) * rows)
        y = dot(pick[...], x_ref[at].reshape(WIDE, width)).astype(BF16)
        for d in range(lanes):
            out_refs[d][at, :] = y[d * rows : (d + 1) * rows]


def pack(table, snapshots, base, width, first):
    steps, lanes, _ = snapshots.shape
    parts = math.gcd(steps * lanes // WIDE, 3)
    outs = [jax.ShapeDtypeStruct((steps, width), BF16)] * lanes
    outs.append(jax.ShapeDtypeStruct((WIDE, WIDE), BF16))
    scratch = [
        pltpu.SMEM(table.shape, jnp.int32) if first else pltpu.VMEM(table.shape, BF16),
        pltpu.VMEM((steps, lanes, width), BF16),
        pltpu.SemaphoreType.DMA,
        pltpu.SemaphoreType.DMA((parts,)),
    ]
    return pl.pallas_call(
        functools.partial(pack_kernel, base, parts, first),
        out_shape=outs,
        in_specs=[HBM] * 2,
        out_specs=[VMEM] * len(outs),
        scratch_shapes=scratch,
        compiler_params=pltpu.CompilerParams(
            vmem_limit_bytes=FIRST_LIMIT if first else SECOND_LIMIT
        ),
        cost_estimate=pl.CostEstimate(
            flops=2 * WIDE * steps * lanes * width,
            bytes_accessed=4 * steps * lanes * width,
            transcendentals=0,
        ),
    )(table, snapshots)


def fill_record(order_ref, pieces, record, factor):
    steps, width = pieces[0].shape
    me = lax.axis_index("tm")
    for d, piece in enumerate(pieces):
        partner = me ^ (len(pieces) - d if d else 0)
        start = pl.multiple_of(order_ref[partner] * steps, steps)
        for c in range(width // LANE):
            cols = slice(c * LANE, (c + 1) * LANE)
            part = piece[:, cols].astype(F32)
            record[c, pl.ds(start, steps), :] = part if factor is None else part * factor[:, cols]


def transform(offsets_ref, f_ref, record, s_ref):
    wanted = [(i, c) for i in range(NBLK) for c in range(record.shape[0])]
    for first in range(0, len(wanted), 2):
        pair = wanted[first : first + 2]
        x = [record[c, pl.ds(offsets_ref[i], NFFT), :].astype(BF16) for i, c in pair]
        x = jnp.concatenate(x, axis=1) if len(x) > 1 else x[0]
        y = dot(f_ref[...], jnp.concatenate([x, x], axis=0))
        for at, (i, c) in enumerate(pair):
            cols = slice(c * LANE, (c + 1) * LANE)
            s_ref[i, :, cols] = y[:NFREQ, at * LANE : (at + 1) * LANE]
            s_ref[NBLK + i, :, cols] = y[NFREQ:, at * LANE : (at + 1) * LANE]


def padded(s):
    width = s.shape[2]
    pad = jnp.zeros((LANE - HALF_ROWS, width), F32)
    real = s[:NBLK].reshape(HALF_ROWS, width)
    imag = s[NBLK:].reshape(HALF_ROWS, width)
    return jnp.concatenate([real, pad, imag, pad], axis=0)


def gram_kernel(lanes, scale, first, last, order_ref, offsets_ref, w_ref, f_ref, pick_ref, *refs):
    pieces = refs[:lanes]
    rest = refs[lanes:]
    if not first:
        before_ref, _, *rest = rest
    *packed_refs, record, s_ref, masked = rest
    fill_record(order_ref, pieces, record, jnp.sqrt(w_ref[...]))
    transform(offsets_ref, f_ref, record, s_ref)
    row = lax.broadcasted_iota(jnp.int32, (HALF_ROWS, LANE), 0)
    col = lax.broadcasted_iota(jnp.int32, (HALF_ROWS, LANE), 1)
    same = row % SUB == col % SUB
    for g in range(GROUPS):
        at = slice(g * SUB, (g + 1) * SUB)
        s = s_ref[:, at, :]
        full = dot_nt(s.reshape(2 * HALF_ROWS, -1).astype(BF16), padded(s).astype(BF16))
        real = full[:HALF_ROWS, :LANE] + full[HALF_ROWS:, LANE:]
        imag = full[:HALF_ROWS, LANE:] - full[HALF_ROWS:, :LANE]
        real = jnp.where(same, real, 0.0)
        imag = jnp.where(same, imag, 0.0)
        for a in range(NBLK):
            rows = slice(a * SUB, (a + 1) * SUB)
            masked[at, a * WIDE : a * WIDE + LANE] = real[rows]
            masked[at, a * WIDE + LANE : (a + 1) * WIDE] = imag[rows]
    total = dot(masked[...].astype(BF16), pick_ref[...]).T * scale
    if not first:
        total = total + before_ref[...]
    if not last:
        packed_refs[0][...] = total
        return
    keep_ref, send_ref = packed_refs
    other = lax.axis_index("tm") % 2 == 1
    keep_ref[...] = jnp.where(other, total[HALF:], total[:HALF]).astype(BF16)
    send_ref[...] = jnp.where(other, total[:HALF], total[HALF:]).astype(BF16)


def gram_part(order, offsets, weights, tables, pieces, before, last, scale):
    lanes = len(pieces)
    steps, width = pieces[0].shape
    first = not before
    args = [order, offsets, weights, *tables, *pieces, *before]
    return pl.pallas_call(
        functools.partial(gram_kernel, lanes, scale, first, last),
        out_shape=[jax.ShapeDtypeStruct((HALF, NFREQ), BF16)] * 2
        if last
        else [jax.ShapeDtypeStruct((PACKED, NFREQ), F32)],
        in_specs=[SMEM, SMEM] + [VMEM] * (len(args) - 2),
        out_specs=[VMEM] * (2 if last else 1),
        scratch_shapes=[
            pltpu.VMEM((width // LANE, lanes * steps, LANE), F32),
            pltpu.VMEM((2 * NBLK, NFREQ, width), F32),
            pltpu.VMEM((NFREQ, NBLK * WIDE), F32),
        ],
        compiler_params=pltpu.CompilerParams(vmem_limit_bytes=32 * 2**20),
        cost_estimate=pl.CostEstimate(
            flops=width * 10**7, bytes_accessed=3 * 10**6, transcendentals=0
        ),
    )(*args)


def spectrum_kernel(lanes, order_ref, offsets_ref, f_ref, *refs):
    high_ref, low_ref, record, s_ref = refs[-4:]
    fill_record(order_ref, refs[:lanes], record, None)
    transform(offsets_ref, f_ref, record, s_ref)
    for g in range(GROUPS):
        high_ref[g], low_ref[g] = split(padded(s_ref[:, g * SUB : (g + 1) * SUB, :]))


def spectrum(order, offsets, fourier, pieces, after):
    lanes = len(pieces)
    steps, width = pieces[0].shape
    args = [order, offsets, fourier, *pieces, *after]
    part = jax.ShapeDtypeStruct((GROUPS, WIDE, width), BF16)
    return pl.pallas_call(
        functools.partial(spectrum_kernel, lanes),
        out_shape=[part, part],
        in_specs=[SMEM, SMEM] + [VMEM] * (len(args) - 2),
        out_specs=[VMEM, VMEM],
        scratch_shapes=[
            pltpu.VMEM((width // LANE, lanes * steps, LANE), F32),
            pltpu.VMEM((2 * NBLK, NFREQ, width), F32),
        ],
        compiler_params=pltpu.CompilerParams(vmem_limit_bytes=32 * 2**20),
        cost_estimate=pl.CostEstimate(
            flops=width * 10**7, bytes_accessed=3 * 10**6, transcendentals=0
        ),
    )(*args)


class Hermitian:
    def __init__(self, main, corner):
        self.main = main
        self.corner = corner

    def entry(self, a, e):
        if e < SUB:
            return self.main[0, a, pl.ds(e, 1), :], self.main[1, a, pl.ds(e, 1), :], 1
        if a < SUB:
            return self.main[0, e, pl.ds(a, 1), :], self.main[1, e, pl.ds(a, 1), :], -1
        at = pl.ds(e - SUB, 1)
        return self.corner[0, a - SUB, at, :], self.corner[1, a - SUB, at, :], 1

    def put(self, a, e, real, imag):
        if e < SUB:
            self.main[0, a, pl.ds(e, 1), :] = real
            self.main[1, a, pl.ds(e, 1), :] = imag
        elif a >= SUB:
            at = pl.ds(e - SUB, 1)
            self.corner[0, a - SUB, at, :] = real
            self.corner[1, a - SUB, at, :] = imag


def product(x, y, out, diagonal=0.0, factor=1.0):
    sub = lax.broadcasted_iota(jnp.int32, (SUB, NFREQ), 0)
    yr = [y.main[0, b] for b in range(NBLK)]
    yi = [y.main[1, b] for b in range(NBLK)]
    for a in range(NBLK):
        real = imag = None
        for b in range(NBLK):
            pr, pi, sign = x.entry(a, b)
            tr, ti = pi * yi[b], pi * yr[b]
            if sign > 0:
                tr, ti = pr * yr[b] - tr, pr * yi[b] + ti
            else:
                tr, ti = pr * yr[b] + tr, pr * yi[b] - ti
            real = tr if real is None else real + tr
            imag = ti if imag is None else imag + ti
        if factor != 1.0:
            real, imag = factor * real, factor * imag
        if diagonal and a < SUB:
            real = real + jnp.where(sub == a, diagonal, 0.0)
        out.main[0, a] = real
        out.main[1, a] = imag
    ar = [[x.main[0, SUB + a], x.corner[0, a]] for a in range(CORNER)]
    ai = [[x.main[1, SUB + a], x.corner[1, a]] for a in range(CORNER)]
    er = [[yr[SUB + e], y.corner[0, e]] for e in range(CORNER)]
    ei = [[yi[SUB + e], y.corner[1, e]] for e in range(CORNER)]
    for a in range(CORNER):
        for e in range(a, CORNER):
            real = sum(ar[a][h] * er[e][h] + ai[a][h] * ei[e][h] for h in range(2))
            real = factor * jnp.sum(real, axis=0, keepdims=True)
            if a == e:
                real = real + diagonal
                out.put(SUB + a, SUB + a, real, jnp.zeros_like(real))
            else:
                imag = sum(ai[a][h] * er[e][h] - ar[a][h] * ei[e][h] for h in range(2))
                imag = factor * jnp.sum(imag, axis=0, keepdims=True)
                out.put(SUB + a, SUB + e, real, imag)
                out.put(SUB + e, SUB + a, real, -imag)


def affine(x, outs):
    sub = lax.broadcasted_iota(jnp.int32, (SUB, NFREQ), 0)
    for a in range(NBLK):
        real = -0.5 * x.main[0, a]
        imag = -0.5 * x.main[1, a]
        if a < SUB:
            real = real + jnp.where(sub == a, 1.5, 0.0)
        for out in outs:
            out.main[0, a] = real
            out.main[1, a] = imag
    for a in range(CORNER):
        real = jnp.where(sub == a, 1.5, 0.0) - 0.5 * x.corner[0, a]
        imag = -0.5 * x.corner[1, a]
        for out in outs:
            out.corner[0, a] = real
            out.corner[1, a] = imag


def root_kernel(share, half_ref, other_ref, stack_ref, gram_ref, packed, rolled, *mats):
    core = lax.axis_index("tm") % 2
    packed[pl.ds(pl.multiple_of(core * HALF, HALF), HALF), :] = half_ref[...]
    packed[pl.ds(pl.multiple_of((1 - core) * HALF, HALF), HALF), :] = other_ref[...]
    at = lax.axis_index("sx") * lax.axis_size("sy") + lax.axis_index("sy")
    rolled[...] = pltpu.roll(packed[...], (NFREQ - at * share) % NFREQ, 1)
    y, z, p, y2, z2 = [Hermitian(mats[2 * i], mats[2 * i + 1]) for i in range(5)]
    for ref in mats[1::2]:
        ref[...] = jnp.zeros_like(ref)

    def row(ref, part, a, e):
        return ref[pl.ds(ROWS[part, a, e], 1), :]

    trace = 2.0 * sum(row(packed, 0, a, a) for a in range(NBLK))
    norm = 1.0 / jnp.sqrt(trace)
    packed[...] = packed[...] / trace
    zero = jnp.zeros((1, NFREQ), F32)
    for a in range(NBLK):
        y.put(a, a, row(packed, 0, a, a), zero)
        gram_ref[a, a, 0:1, :] = row(rolled, 0, a, a)[:, :share]
        gram_ref[a, a, 1:2, :] = zero[:, :share]
        for e in range(a + 1, NBLK):
            real, imag = row(packed, 0, a, e), row(packed, 1, a, e)
            y.put(a, e, real, imag)
            y.put(e, a, real, -imag)
            real, imag = row(rolled, 0, a, e)[:, :share], row(rolled, 1, a, e)[:, :share]
            gram_ref[a, e, 0:1, :] = real
            gram_ref[e, a, 0:1, :] = real
            gram_ref[a, e, 1:2, :] = imag
            gram_ref[e, a, 1:2, :] = -imag
    for step in range(ROOT_STEPS):
        if step == 0:
            affine(y, [p, z2])
        else:
            product(z, y, p, 1.5, -0.5)
            product(p, z, z2)
        if step < ROOT_STEPS - 1:
            product(y, p, y2)
        y, y2 = y2, y
        z, z2 = z2, z
    none = jnp.zeros((SUB - CORNER, NFREQ), F32)
    for at, m0 in enumerate(range(0, NBLK, STACK)):
        modes = range(m0, min(m0 + STACK, NBLK))
        stack = []
        for m in modes:
            for c in range(2):
                stack.append(z.main[c, m] * norm)
                for b in range(SUB, NBLK):
                    real, imag, sign = z.entry(m, b)
                    stack.append((imag * sign if c else real) * norm)
                stack.append(none)
        stack += [jnp.zeros((32, NFREQ), F32)] * (STACK - len(modes))
        stack_ref[at] = jnp.concatenate(stack, axis=0).T


def roots(half, other, share):
    stacks = -(-NBLK // STACK)
    return pl.pallas_call(
        functools.partial(root_kernel, share),
        out_shape=[
            jax.ShapeDtypeStruct((stacks, NFREQ, LANE), F32),
            jax.ShapeDtypeStruct((NBLK, NBLK, 2, share), F32),
        ],
        in_specs=[VMEM] * 2,
        out_specs=[VMEM] * 2,
        scratch_shapes=[pltpu.VMEM((PACKED, NFREQ), F32)] * 2
        + [
            pltpu.VMEM((2, NBLK, SUB, NFREQ), F32),
            pltpu.VMEM((2, CORNER, SUB, NFREQ), F32),
        ]
        * 5,
        compiler_params=pltpu.CompilerParams(vmem_limit_bytes=32 * 2**20),
    )(half, other)


def mode_kernel(chunks, stack_ref, spread_ref, *refs):
    high_refs = refs[:chunks]
    low_refs = refs[chunks : 2 * chunks]
    out_ref, v = refs[2 * chunks :]
    step = pl.program_id(0)

    @pl.when(step == 0)
    def _():
        row = lax.broadcasted_iota(jnp.int32, (NFREQ, WIDE), 0)
        col = lax.broadcasted_iota(jnp.int32, (NFREQ, WIDE), 1)
        same = row % SUB == col % SUB
        for at, m0 in enumerate(range(0, NBLK, STACK)):
            both = jnp.concatenate(split(stack_ref[at]), axis=1)
            for m in range(m0, min(m0 + STACK, NBLK)):
                for c in range(2):
                    wide = dot(both, spread_ref[(m - m0) * 2 + c])
                    v[c * NBLK + m] = jnp.where(same, wide, 0.0)

    fields = []
    for h in range(STEP_GROUPS):
        g = step * STEP_GROUPS + h
        start = pl.multiple_of(g * SUB, SUB)
        v_high, v_low = split(v[:, pl.ds(start, SUB), :].reshape(2 * HALF_ROWS, WIDE))
        s_high = jnp.concatenate([r[g] for r in high_refs], axis=1)
        s_low = jnp.concatenate([r[g] for r in low_refs], axis=1)
        field = dot(
            jnp.concatenate([v_high, v_high, v_low], axis=1),
            jnp.concatenate([s_high, s_low, s_high], axis=0),
        )
        fields.append(field.reshape(2 * NBLK, SUB, -1))
    both = jnp.concatenate(fields, axis=1).astype(BF16)
    out_ref[...] = both.reshape(out_ref.shape)


def mode_fields(stacks, spread, highs, lows):
    width = sum(s.shape[2] for s in highs)
    return pl.pallas_call(
        functools.partial(mode_kernel, len(highs)),
        grid=(GROUPS // STEP_GROUPS,),
        out_shape=jax.ShapeDtypeStruct((2, NBLK, NFREQ, width), BF16),
        in_specs=[VMEM] * (2 + 2 * len(highs)),
        out_specs=pl.BlockSpec(
            (2, NBLK, STEP_GROUPS * SUB, width), lambda i: (0, 0, i, 0)
        ),
        scratch_shapes=[pltpu.VMEM((2 * NBLK, NFREQ, WIDE), F32)],
        compiler_params=pltpu.CompilerParams(vmem_limit_bytes=32 * 2**20),
    )(stacks, spread, *highs, *lows)


def swap(x, axes, mask, size):
    return lax.ppermute(x, axes, [(i, i ^ mask) for i in range(size)])


def powers(size):
    return [1 << i for i in range(size.bit_length() - 1)]


def body(snapshots, weights, block_order, owner, offsets):
    lanes = lax.axis_size("tm")
    groups = lax.axis_size("sx") * lax.axis_size("sy")
    points = snapshots.shape[2]
    chunks = [(0, points // 2), (points // 2, points // 2)]
    scale = 1.0 / (lanes * groups * points)
    tables = (jnp.asarray(fourier_tables()), jnp.asarray(pick_table()))
    weights = weights.reshape(1, -1)

    arrived = []
    table = owner
    for base, width in chunks:
        packed = pack(table, snapshots, base, width, base == 0)
        table = packed[lanes]
        moved = [swap(packed[d], "tm", d, lanes) for d in reversed(range(1, lanes))]
        arrived.append([packed[0]] + moved)

    highs, lows = [], []
    before = []
    for at, pieces in enumerate(arrived):
        base, width = chunks[at]
        here = weights[:, base : base + width]
        last = at == len(arrived) - 1
        total = gram_part(block_order, offsets, here, tables, pieces, before, last, scale)
        after = total if last else []
        high, low = spectrum(block_order, offsets, tables[0], pieces, after)
        highs.append(high)
        lows.append(low)
        before = [total[0], high]

    axes = ("tm", "sx", "sy")
    size = lanes * groups
    bits = [b * groups for b in powers(lanes)] + powers(groups)
    keep, send = total
    half = keep.astype(F32) + swap(send, axes, bits[0], size).astype(F32)
    for at in range(1, len(bits), 2):
        masks = bits[at : at + 2]
        if len(masks) == 2:
            masks.append(masks[0] ^ masks[1])
        half = half.astype(BF16)
        terms = [half] + [swap(half, axes, mask, size) for mask in masks]
        terms = [t.astype(F32) for t in terms]
        while len(terms) > 1:
            terms = [a + b for a, b in zip(terms[::2], terms[1::2])]
        half = terms[0]
    half, highs[-1] = lax.optimization_barrier((half, highs[-1]))
    other = swap(half, axes, bits[0], size)

    stacks, gram = roots(half, other, NFREQ // groups)
    modes = mode_fields(stacks, jnp.asarray(spread_table()), highs, lows)
    modes = jnp.transpose(modes, (0, 2, 1, 3))[:, :, :, None, :]
    return modes, jnp.transpose(gram, (2, 3, 0, 1))


def solution(mesh):
    placed = (P("tm", None, ("sx", "sy")), P(("sx", "sy")), P(), P(("sx", "sy"), None), P())
    return jax.shard_map(
        body,
        mesh=mesh,
        in_specs=placed,
        out_specs=(P(None, None, None, "tm", ("sx", "sy")), P(None, ("sx", "sy"), None, None)),
        check_vma=False,
    )
```

```python
import functools
import math

import jax
import jax.numpy as jnp
import numpy as np
from jax import lax
from jax.experimental import pallas as pl
from jax.experimental.pallas import tpu as pltpu
from jax.sharding import PartitionSpec as P

NFFT = 256
ROOT_STEPS = 5
NFREQ = 128
NBLK = 11
LANE = 128
SUB = 8
HALF_ROWS = NBLK * SUB
GROUPS = NFREQ // SUB
STEP_GROUPS = 4
PACKED = 128
HALF = PACKED // 2
STACK = 4
CORNER = NBLK - SUB
WIDE = 2 * LANE
FIRST_LIMIT = 64 * 2**20
SECOND_LIMIT = FIRST_LIMIT - 1450 * 2**10
BF16 = jnp.bfloat16
F32 = jnp.float32


def fourier_tables():
    n = np.arange(NFFT)
    k = np.arange(NFREQ)
    angles = 2.0 * np.pi * ((k[:, None] * n[None, :]) % NFFT) / NFFT
    scaled = (0.5 - 0.5 * np.cos(2.0 * np.pi * n / NFFT)) / math.sqrt(0.375 * NFFT)
    table = np.concatenate([np.cos(angles) * scaled, -np.sin(angles) * scaled], axis=0)
    high = table.astype(jnp.bfloat16)
    low = (table - high.astype(np.float64)).astype(jnp.bfloat16)
    return np.concatenate([high, low], axis=0)


def packed_rows():
    rows = {}
    for a in range(NBLK):
        for e in range(a, NBLK):
            rows[0, a, e] = len(rows)
        for e in range(a + 1, NBLK):
            rows[1, a, e] = len(rows)
    return rows


ROWS = packed_rows()


def pick_table():
    pick = np.zeros((NBLK, 2, LANE, PACKED), np.float32)
    for (part, a, e), row in ROWS.items():
        pick[a, part, e * SUB : (e + 1) * SUB, row] = 1.0
    return pick.reshape(NBLK * WIDE, PACKED).astype(jnp.bfloat16)


def spread_table():
    spread = np.zeros((STACK, 2, LANE, 2 * HALF_ROWS), np.float32)
    for m in range(STACK):
        for b in range(NBLK):
            real = m * 32 + b
            imag = m * 32 + 16 + b
            first = slice(b * SUB, b * SUB + SUB)
            second = slice(HALF_ROWS + b * SUB, HALF_ROWS + b * SUB + SUB)
            spread[m, 0, real, first] = 1.0
            spread[m, 0, imag, second] = 1.0
            spread[m, 1, imag, first] = -1.0
            spread[m, 1, real, second] = 1.0
    spread = np.concatenate([spread, spread], axis=2)
    return spread.reshape(STACK * 2, WIDE, 2 * HALF_ROWS).astype(jnp.bfloat16)


def split(x):
    high = x.astype(BF16)
    return high, (x - high.astype(F32)).astype(BF16)


def dot(a, b):
    return jnp.dot(a, b, preferred_element_type=F32)


def dot_nt(a, b):
    return lax.dot_general(a, b, (((1,), (1,)), ((), ())), preferred_element_type=F32)


def spec(shape):
    return pl.BlockSpec(shape, lambda *_: (0,) * len(shape))


SMEM = pl.BlockSpec(memory_space=pltpu.SMEM)
VMEM = pl.BlockSpec(memory_space=pltpu.VMEM)
HBM = pl.BlockSpec(memory_space=pltpu.HBM)


def lane_pick(owner, lanes):
    me = lax.axis_index("tm")
    rows = WIDE // lanes
    out_row = lax.broadcasted_iota(jnp.int32, (WIDE, WIDE), 0)
    in_row = lax.broadcasted_iota(jnp.int32, (WIDE, WIDE), 1)
    row_of = (out_row % rows) * lanes
    for d in range(lanes):
        slot = me ^ d
        source = jnp.int32(0)
        for lane in range(lanes):
            source = source + jnp.where(owner[0, lane] == slot, lane, 0)
        row_of = jnp.where(out_row // rows == d, row_of + source, row_of)
    return jnp.where(in_row == row_of, 1.0, 0.0).astype(BF16)


def pack_kernel(base, parts, first, table_hbm, x_hbm, *refs):
    lanes = x_hbm.shape[1]
    out_refs = refs[:lanes]
    pick, table, x_ref, staged, table_sem, x_sem, out_sem = refs[lanes:]
    steps, _, width = x_ref.shape
    part = steps // parts
    table_copy = pltpu.make_async_copy(table_hbm, table, table_sem)
    table_copy.start()
    copies = []
    for i in range(parts):
        at = slice(i * part, (i + 1) * part)
        source = x_hbm.at[at, :, base : base + width]
        copies.append(pltpu.make_async_copy(source, x_ref.at[at], x_sem.at[i]))
        copies[-1].start()
    table_copy.wait()
    pick[...] = lane_pick(table, lanes) if first else table[...]
    rows = WIDE // lanes
    stores = []
    for i in range(parts):
        copies[i].wait()
        for start in range(i * part, (i + 1) * part, rows):
            at = slice(start, start + rows)
            y = dot(pick[...], x_ref[at].reshape(WIDE, width)).astype(BF16)
            for d in range(lanes):
                staged[d, at, :] = y[d * rows : (d + 1) * rows]
        at = slice(i * part, (i + 1) * part)
        for d in range(lanes):
            store = pltpu.make_async_copy(
                staged.at[d, at], out_refs[d].at[at], out_sem.at[i * lanes + d]
            )
            store.start()
            stores.append(store)
    for store in stores:
        store.wait()


def pack(table, snapshots, base, width, first):
    steps, lanes, _ = snapshots.shape
    parts = math.gcd(steps * lanes // WIDE, 3)
    outs = [jax.ShapeDtypeStruct((steps, width), BF16)] * lanes
    outs.append(jax.ShapeDtypeStruct((WIDE, WIDE), BF16))
    return pl.pallas_call(
        functools.partial(pack_kernel, base, parts, first),
        out_shape=outs,
        in_specs=[HBM] * 2,
        out_specs=[HBM] * lanes + [VMEM],
        scratch_shapes=[
            pltpu.SMEM(table.shape, jnp.int32) if first else pltpu.VMEM(table.shape, BF16),
            pltpu.VMEM((steps, lanes, width), BF16),
            pltpu.VMEM((lanes, steps, width), BF16),
            pltpu.SemaphoreType.DMA,
            pltpu.SemaphoreType.DMA((parts,)),
            pltpu.SemaphoreType.DMA((parts * lanes,)),
        ],
        compiler_params=pltpu.CompilerParams(
            vmem_limit_bytes=FIRST_LIMIT if first else SECOND_LIMIT
        ),
        cost_estimate=pl.CostEstimate(
            flops=2 * WIDE * steps * lanes * width,
            bytes_accessed=4 * steps * lanes * width,
            transcendentals=0,
        ),
    )(table, snapshots)


def fill_record(order_ref, pieces, record, factor):
    steps, width = pieces[0].shape
    me = lax.axis_index("tm")
    for d, piece in enumerate(pieces):
        partner = me ^ (len(pieces) - d if d else 0)
        start = pl.multiple_of(order_ref[partner] * steps, steps)
        for c in range(width // LANE):
            cols = slice(c * LANE, (c + 1) * LANE)
            part = piece[:, cols].astype(F32)
            record[c, pl.ds(start, steps), :] = part if factor is None else part * factor[:, cols]


def transform(offsets_ref, f_ref, record, s_ref):
    wanted = [(i, c) for i in range(NBLK) for c in range(record.shape[0])]
    for first in range(0, len(wanted), 2):
        pair = wanted[first : first + 2]
        x = [record[c, pl.ds(offsets_ref[i], NFFT), :].astype(BF16) for i, c in pair]
        x = jnp.concatenate(x, axis=1) if len(x) > 1 else x[0]
        y = dot(f_ref[...], x)
        y = y[:NFFT] + y[NFFT:]
        for at, (i, c) in enumerate(pair):
            cols = slice(c * LANE, (c + 1) * LANE)
            s_ref[i, :, cols] = y[:NFREQ, at * LANE : (at + 1) * LANE]
            s_ref[NBLK + i, :, cols] = y[NFREQ:, at * LANE : (at + 1) * LANE]


def padded(s):
    width = s.shape[2]
    pad = jnp.zeros((LANE - HALF_ROWS, width), F32)
    real = s[:NBLK].reshape(HALF_ROWS, width)
    imag = s[NBLK:].reshape(HALF_ROWS, width)
    return jnp.concatenate([real, pad, imag, pad], axis=0)


def gram_kernel(lanes, scale, first, last, order_ref, offsets_ref, w_ref, f_ref, pick_ref, *refs):
    pieces = refs[:lanes]
    rest = refs[lanes:]
    if not first:
        before_ref, _, *rest = rest
    *packed_refs, record, s_ref, masked = rest
    fill_record(order_ref, pieces, record, jnp.sqrt(w_ref[...]))
    transform(offsets_ref, f_ref, record, s_ref)
    row = lax.broadcasted_iota(jnp.int32, (HALF_ROWS, LANE), 0)
    col = lax.broadcasted_iota(jnp.int32, (HALF_ROWS, LANE), 1)
    same = row % SUB == col % SUB
    for g in range(GROUPS):
        at = slice(g * SUB, (g + 1) * SUB)
        s = s_ref[:, at, :]
        full = dot_nt(s.reshape(2 * HALF_ROWS, -1).astype(BF16), padded(s).astype(BF16))
        real = full[:HALF_ROWS, :LANE] + full[HALF_ROWS:, LANE:]
        imag = full[:HALF_ROWS, LANE:] - full[HALF_ROWS:, :LANE]
        real = jnp.where(same, real, 0.0)
        imag = jnp.where(same, imag, 0.0)
        for a in range(NBLK):
            rows = slice(a * SUB, (a + 1) * SUB)
            masked[at, a * WIDE : a * WIDE + LANE] = real[rows]
            masked[at, a * WIDE + LANE : (a + 1) * WIDE] = imag[rows]
    total = dot(masked[...].astype(BF16), pick_ref[...]).T * scale
    if not first:
        total = total + before_ref[...]
    if not last:
        packed_refs[0][...] = total
        return
    keep_ref, send_ref = packed_refs
    other = lax.axis_index("tm") % 2 == 1
    keep_ref[...] = jnp.where(other, total[HALF:], total[:HALF]).astype(BF16)
    send_ref[...] = jnp.where(other, total[:HALF], total[HALF:]).astype(BF16)


def gram_part(order, offsets, weights, tables, pieces, before, last, scale):
    lanes = len(pieces)
    steps, width = pieces[0].shape
    first = not before
    args = [order, offsets, weights, *tables, *pieces, *before]
    return pl.pallas_call(
        functools.partial(gram_kernel, lanes, scale, first, last),
        out_shape=[jax.ShapeDtypeStruct((HALF, NFREQ), BF16)] * 2
        if last
        else [jax.ShapeDtypeStruct((PACKED, NFREQ), F32)],
        in_specs=[SMEM, SMEM] + [VMEM] * (len(args) - 2),
        out_specs=[VMEM] * (2 if last else 1),
        scratch_shapes=[
            pltpu.VMEM((width // LANE, lanes * steps, LANE), F32),
            pltpu.VMEM((2 * NBLK, NFREQ, width), F32),
            pltpu.VMEM((NFREQ, NBLK * WIDE), F32),
        ],
        compiler_params=pltpu.CompilerParams(vmem_limit_bytes=32 * 2**20),
        cost_estimate=pl.CostEstimate(
            flops=width * 10**7, bytes_accessed=3 * 10**6, transcendentals=0
        ),
    )(*args)


def spectrum_kernel(lanes, order_ref, offsets_ref, f_ref, *refs):
    high_ref, low_ref, record, s_ref = refs[-4:]
    fill_record(order_ref, refs[:lanes], record, None)
    transform(offsets_ref, f_ref, record, s_ref)
    for g in range(GROUPS):
        s = s_ref[:, g * SUB : (g + 1) * SUB, :].reshape(2 * HALF_ROWS, -1)
        high_ref[g], low_ref[g] = split(s)


def spectrum(order, offsets, fourier, pieces, after):
    lanes = len(pieces)
    steps, width = pieces[0].shape
    args = [order, offsets, fourier, *pieces, *after]
    part = jax.ShapeDtypeStruct((GROUPS, 2 * HALF_ROWS, width), BF16)
    return pl.pallas_call(
        functools.partial(spectrum_kernel, lanes),
        out_shape=[part, part],
        in_specs=[SMEM, SMEM] + [VMEM] * (len(args) - 2),
        out_specs=[VMEM, VMEM],
        scratch_shapes=[
            pltpu.VMEM((width // LANE, lanes * steps, LANE), F32),
            pltpu.VMEM((2 * NBLK, NFREQ, width), F32),
        ],
        compiler_params=pltpu.CompilerParams(vmem_limit_bytes=32 * 2**20),
        cost_estimate=pl.CostEstimate(
            flops=width * 10**7, bytes_accessed=3 * 10**6, transcendentals=0
        ),
    )(*args)


class Hermitian:
    def __init__(self, main, corner):
        self.main = main
        self.corner = corner

    def entry(self, a, e):
        if e < SUB:
            return self.main[0, a, pl.ds(e, 1), :], self.main[1, a, pl.ds(e, 1), :], 1
        if a < SUB:
            return self.main[0, e, pl.ds(a, 1), :], self.main[1, e, pl.ds(a, 1), :], -1
        at = pl.ds(e - SUB, 1)
        return self.corner[0, a - SUB, at, :], self.corner[1, a - SUB, at, :], 1

    def put(self, a, e, real, imag):
        if e < SUB:
            self.main[0, a, pl.ds(e, 1), :] = real
            self.main[1, a, pl.ds(e, 1), :] = imag
        elif a >= SUB:
            at = pl.ds(e - SUB, 1)
            self.corner[0, a - SUB, at, :] = real
            self.corner[1, a - SUB, at, :] = imag


def product(x, y, out, diagonal=0.0, factor=1.0):
    sub = lax.broadcasted_iota(jnp.int32, (SUB, NFREQ), 0)
    yr = [y.main[0, b] for b in range(NBLK)]
    yi = [y.main[1, b] for b in range(NBLK)]
    for a in range(NBLK):
        real = imag = None
        for b in range(NBLK):
            pr, pi, sign = x.entry(a, b)
            tr, ti = pi * yi[b], pi * yr[b]
            if sign > 0:
                tr, ti = pr * yr[b] - tr, pr * yi[b] + ti
            else:
                tr, ti = pr * yr[b] + tr, pr * yi[b] - ti
            real = tr if real is None else real + tr
            imag = ti if imag is None else imag + ti
        if factor != 1.0:
            real, imag = factor * real, factor * imag
        if diagonal and a < SUB:
            real = real + jnp.where(sub == a, diagonal, 0.0)
        out.main[0, a] = real
        out.main[1, a] = imag
    ar = [[x.main[0, SUB + a], x.corner[0, a]] for a in range(CORNER)]
    ai = [[x.main[1, SUB + a], x.corner[1, a]] for a in range(CORNER)]
    er = [[yr[SUB + e], y.corner[0, e]] for e in range(CORNER)]
    ei = [[yi[SUB + e], y.corner[1, e]] for e in range(CORNER)]
    for a in range(CORNER):
        for e in range(a, CORNER):
            real = sum(ar[a][h] * er[e][h] + ai[a][h] * ei[e][h] for h in range(2))
            real = factor * jnp.sum(real, axis=0, keepdims=True)
            if a == e:
                real = real + diagonal
                out.put(SUB + a, SUB + a, real, jnp.zeros_like(real))
            else:
                imag = sum(ai[a][h] * er[e][h] - ar[a][h] * ei[e][h] for h in range(2))
                imag = factor * jnp.sum(imag, axis=0, keepdims=True)
                out.put(SUB + a, SUB + e, real, imag)
                out.put(SUB + e, SUB + a, real, -imag)


def affine(x, outs):
    sub = lax.broadcasted_iota(jnp.int32, (SUB, NFREQ), 0)
    for a in range(NBLK):
        real = -0.5 * x.main[0, a]
        imag = -0.5 * x.main[1, a]
        if a < SUB:
            real = real + jnp.where(sub == a, 1.5, 0.0)
        for out in outs:
            out.main[0, a] = real
            out.main[1, a] = imag
    for a in range(CORNER):
        real = jnp.where(sub == a, 1.5, 0.0) - 0.5 * x.corner[0, a]
        imag = -0.5 * x.corner[1, a]
        for out in outs:
            out.corner[0, a] = real
            out.corner[1, a] = imag


def make_roots(share, half_ref, other_ref, gram_ref, packed, rolled, mats):
    core = lax.axis_index("tm") % 2
    packed[pl.ds(pl.multiple_of(core * HALF, HALF), HALF), :] = half_ref[...]
    packed[pl.ds(pl.multiple_of((1 - core) * HALF, HALF), HALF), :] = other_ref[...]
    at = lax.axis_index("sx") * lax.axis_size("sy") + lax.axis_index("sy")
    rolled[...] = pltpu.roll(packed[...], (NFREQ - at * share) % NFREQ, 1)
    y, z, p, y2, z2 = [Hermitian(mats[2 * i], mats[2 * i + 1]) for i in range(5)]
    for ref in mats[1::2]:
        ref[...] = jnp.zeros_like(ref)

    def row(ref, part, a, e):
        return ref[pl.ds(ROWS[part, a, e], 1), :]

    trace = 2.0 * sum(row(packed, 0, a, a) for a in range(NBLK))
    norm = 1.0 / jnp.sqrt(trace)
    packed[...] = packed[...] / trace
    zero = jnp.zeros((1, NFREQ), F32)
    for a in range(NBLK):
        y.put(a, a, row(packed, 0, a, a), zero)
        gram_ref[a, a, 0:1, :] = row(rolled, 0, a, a)[:, :share]
        gram_ref[a, a, 1:2, :] = zero[:, :share]
        for e in range(a + 1, NBLK):
            real, imag = row(packed, 0, a, e), row(packed, 1, a, e)
            y.put(a, e, real, imag)
            y.put(e, a, real, -imag)
            real, imag = row(rolled, 0, a, e)[:, :share], row(rolled, 1, a, e)[:, :share]
            gram_ref[a, e, 0:1, :] = real
            gram_ref[e, a, 0:1, :] = real
            gram_ref[a, e, 1:2, :] = imag
            gram_ref[e, a, 1:2, :] = -imag
    for step in range(ROOT_STEPS):
        if step == 0:
            affine(y, [p, z2])
        else:
            product(z, y, p, 1.5, -0.5)
            product(p, z, z2)
        if step < ROOT_STEPS - 1:
            product(y, p, y2)
        y, y2 = y2, y
        z, z2 = z2, z
    none = jnp.zeros((SUB - CORNER, NFREQ), F32)
    stacks = []
    for m0 in range(0, NBLK, STACK):
        modes = range(m0, min(m0 + STACK, NBLK))
        stack = []
        for m in modes:
            for c in range(2):
                stack.append(z.main[c, m] * norm)
                for b in range(SUB, NBLK):
                    real, imag, sign = z.entry(m, b)
                    stack.append((imag * sign if c else real) * norm)
                stack.append(none)
        stack += [jnp.zeros((32, NFREQ), F32)] * (STACK - len(modes))
        stacks.append(jnp.concatenate(stack, axis=0).T)
    return stacks


def mode_kernel(chunks, share, half_ref, other_ref, spread_ref, *refs):
    high_refs = refs[:chunks]
    low_refs = refs[chunks : 2 * chunks]
    out_ref, gram_ref, v, packed, rolled, *mats = refs[2 * chunks :]
    step = pl.program_id(0)

    @pl.when(step == 0)
    def _():
        stacks = make_roots(share, half_ref, other_ref, gram_ref, packed, rolled, mats)
        row = lax.broadcasted_iota(jnp.int32, (NFREQ, 2 * HALF_ROWS), 0)
        col = lax.broadcasted_iota(jnp.int32, (NFREQ, 2 * HALF_ROWS), 1)
        same = row % SUB == col % SUB
        for at, stack in enumerate(stacks):
            both = jnp.concatenate(split(stack), axis=1)
            for m in range(at * STACK, min((at + 1) * STACK, NBLK)):
                for c in range(2):
                    wide = dot(both, spread_ref[(m - at * STACK) * 2 + c])
                    v[c * NBLK + m] = jnp.where(same, wide, 0.0)

    fields = []
    for h in range(STEP_GROUPS):
        g = step * STEP_GROUPS + h
        start = pl.multiple_of(g * SUB, SUB)
        v_high, v_low = split(v[:, pl.ds(start, SUB), :].reshape(2 * HALF_ROWS, 2 * HALF_ROWS))
        s_high = jnp.concatenate([r[g] for r in high_refs], axis=1)
        s_low = jnp.concatenate([r[g] for r in low_refs], axis=1)
        field = dot(jnp.concatenate([v_high, v_low], axis=0), s_high)
        field = field[: 2 * HALF_ROWS] + (field[2 * HALF_ROWS :] + dot(v_high, s_low))
        fields.append(field.reshape(2 * NBLK, SUB, -1))
    both = jnp.concatenate(fields, axis=1).astype(BF16)
    out_ref[...] = both.reshape(out_ref.shape)


def mode_fields(half, other, spread, highs, lows, share):
    width = sum(s.shape[2] for s in highs)
    return pl.pallas_call(
        functools.partial(mode_kernel, len(highs), share),
        grid=(GROUPS // STEP_GROUPS,),
        out_shape=[
            jax.ShapeDtypeStruct((2, NBLK, NFREQ, width), BF16),
            jax.ShapeDtypeStruct((NBLK, NBLK, 2, share), F32),
        ],
        in_specs=[VMEM] * (3 + 2 * len(highs)),
        out_specs=[
            pl.BlockSpec((2, NBLK, STEP_GROUPS * SUB, width), lambda i: (0, 0, i, 0)),
            spec((NBLK, NBLK, 2, share)),
        ],
        scratch_shapes=[
            pltpu.VMEM((2 * NBLK, NFREQ, 2 * HALF_ROWS), F32),
            pltpu.VMEM((PACKED, NFREQ), F32),
            pltpu.VMEM((PACKED, NFREQ), F32),
        ]
        + [
            pltpu.VMEM((2, NBLK, SUB, NFREQ), F32),
            pltpu.VMEM((2, CORNER, SUB, NFREQ), F32),
        ]
        * 5,
        compiler_params=pltpu.CompilerParams(vmem_limit_bytes=32 * 2**20),
    )(half, other, spread, *highs, *lows)


def swap(x, axes, mask, size):
    return lax.ppermute(x, axes, [(i, i ^ mask) for i in range(size)])


def powers(size):
    return [1 << i for i in range(size.bit_length() - 1)]


def body(snapshots, weights, block_order, owner, offsets):
    lanes = lax.axis_size("tm")
    groups = lax.axis_size("sx") * lax.axis_size("sy")
    points = snapshots.shape[2]
    chunks = [(0, points // 2), (points // 2, points // 2)]
    scale = 1.0 / (lanes * groups * points)
    tables = (jnp.asarray(fourier_tables()), jnp.asarray(pick_table()))
    weights = weights.reshape(1, -1)

    arrived = []
    table = owner
    for base, width in chunks:
        packed = pack(table, snapshots, base, width, base == 0)
        table = packed[lanes]
        moved = [swap(packed[d], "tm", d, lanes) for d in reversed(range(1, lanes))]
        arrived.append([packed[0]] + moved)

    highs, lows = [], []
    before = []
    for at, pieces in enumerate(arrived):
        base, width = chunks[at]
        here = weights[:, base : base + width]
        last = at == len(arrived) - 1
        total = gram_part(block_order, offsets, here, tables, pieces, before, last, scale)
        after = total if last else []
        high, low = spectrum(block_order, offsets, tables[0], pieces, after)
        highs.append(high)
        lows.append(low)
        before = [total[0], high]

    axes = ("tm", "sx", "sy")
    size = lanes * groups
    bits = [b * groups for b in powers(lanes)] + powers(groups)
    keep, send = total
    half = keep.astype(F32) + swap(send, axes, bits[0], size).astype(F32)
    for at in range(1, len(bits), 2):
        masks = bits[at : at + 2]
        if len(masks) == 2:
            masks.append(masks[0] ^ masks[1])
        half = half.astype(BF16)
        terms = [half] + [swap(half, axes, mask, size) for mask in masks]
        terms = [t.astype(F32) for t in terms]
        while len(terms) > 1:
            terms = [a + b for a, b in zip(terms[::2], terms[1::2])]
        half = terms[0]
    half, highs[-1] = lax.optimization_barrier((half, highs[-1]))
    other = swap(half, axes, bits[0], size)

    spread = jnp.asarray(spread_table())
    modes, gram = mode_fields(half, other, spread, highs, lows, NFREQ // groups)
    modes = jnp.transpose(modes, (0, 2, 1, 3))[:, :, :, None, :]
    return modes, jnp.transpose(gram, (2, 3, 0, 1))


def solution(mesh):
    placed = (P("tm", None, ("sx", "sy")), P(("sx", "sy")), P(), P(("sx", "sy"), None), P())
    return jax.shard_map(
        body,
        mesh=mesh,
        in_specs=placed,
        out_specs=(P(None, None, None, "tm", ("sx", "sy")), P(None, ("sx", "sy"), None, None)),
        check_vma=False,
    )
```

```python
import functools
import math

import jax
import jax.numpy as jnp
import numpy as np
from jax import lax
from jax.experimental import pallas as pl
from jax.experimental.pallas import tpu as pltpu
from jax.sharding import PartitionSpec as P

NFFT = 256
ROOT_STEPS = 5
NFREQ = 128
NBLK = 11
LANE = 128
SUB = 8
HALF_ROWS = NBLK * SUB
GROUPS = NFREQ // SUB
STEP_GROUPS = 4
PACKED = 128
HALF = PACKED // 2
STACK = 4
CORNER = NBLK - SUB
WIDE = 2 * LANE
LOW = 10 * SUB
FIRST_LIMIT = 64 * 2**20
SECOND_LIMIT = FIRST_LIMIT - 1450 * 2**10
BF16 = jnp.bfloat16
F32 = jnp.float32


def fourier_tables():
    n = np.arange(NFFT)
    k = np.arange(NFREQ)
    angles = 2.0 * np.pi * ((k[:, None] * n[None, :]) % NFFT) / NFFT
    scaled = (0.5 - 0.5 * np.cos(2.0 * np.pi * n / NFFT)) / math.sqrt(0.375 * NFFT)
    table = np.concatenate([np.cos(angles) * scaled, -np.sin(angles) * scaled], axis=0)
    high = table.astype(jnp.bfloat16)
    low = (table - high.astype(np.float64)).astype(jnp.bfloat16)
    return np.concatenate([high, low], axis=0)


def packed_rows():
    rows = {}
    for a in range(NBLK):
        for e in range(a, NBLK):
            rows[0, a, e] = len(rows)
        for e in range(a + 1, NBLK):
            rows[1, a, e] = len(rows)
    return rows


ROWS = packed_rows()


def pick_table():
    pick = np.zeros((NBLK, 2, LANE, PACKED), np.float32)
    for (part, a, e), row in ROWS.items():
        pick[a, part, e * SUB : (e + 1) * SUB, row] = 1.0
    return pick.reshape(NBLK * WIDE, PACKED).astype(jnp.bfloat16)


def spread_table():
    places = [[(0, q) for q in range(16)]]
    places += [[(0, q) for q in range(16, 22)] + [(1, q) for q in range(at, at + 10)] for at in (0, 10)]
    spread = np.zeros((STACK, 2, LANE, 2, 3, 16, SUB), np.float32)
    for m in range(STACK):
        for tile, inputs in enumerate(places):
            for at, (low, q) in enumerate(inputs):
                part, b = divmod(q, NBLK)
                real = m * 32 + b
                imag = m * 32 + 16 + b
                spread[m, low, imag if part else real, 0, tile, at] = 1.0
                spread[m, low, real if part else imag, 1, tile, at] = 1.0 if part else -1.0
    return spread.reshape(STACK, WIDE, 6 * LANE).astype(jnp.bfloat16)


def split(x):
    high = x.astype(BF16)
    return high, (x - high.astype(F32)).astype(BF16)


def dot(a, b):
    return jnp.dot(a, b, preferred_element_type=F32)


def dot_nt(a, b):
    return lax.dot_general(a, b, (((1,), (1,)), ((), ())), preferred_element_type=F32)


def spec(shape):
    return pl.BlockSpec(shape, lambda *_: (0,) * len(shape))


SMEM = pl.BlockSpec(memory_space=pltpu.SMEM)
VMEM = pl.BlockSpec(memory_space=pltpu.VMEM)
HBM = pl.BlockSpec(memory_space=pltpu.HBM)


def lane_pick(owner, lanes):
    me = lax.axis_index("tm")
    rows = WIDE // lanes
    out_row = lax.broadcasted_iota(jnp.int32, (WIDE, WIDE), 0)
    in_row = lax.broadcasted_iota(jnp.int32, (WIDE, WIDE), 1)
    row_of = (out_row % rows) * lanes
    for d in range(lanes):
        slot = me ^ d
        source = jnp.int32(0)
        for lane in range(lanes):
            source = source + jnp.where(owner[0, lane] == slot, lane, 0)
        row_of = jnp.where(out_row // rows == d, row_of + source, row_of)
    return jnp.where(in_row == row_of, 1.0, 0.0).astype(BF16)


def pack_kernel(jobs, parts, first, table_hbm, x_hbm, *refs):
    steps, lanes, _ = x_hbm.shape
    base = jobs[0][0]
    table, x_ref, table_sem, x_sem = refs[-4:]
    outs = list(refs[:-4])
    part = steps // parts
    table_copy = pltpu.make_async_copy(table_hbm, table, table_sem)
    table_copy.start()
    copies = []
    for i in range(parts):
        at = slice(i * part, (i + 1) * part)
        source = x_hbm.at[at, :, base : base + x_ref.shape[2]]
        copies.append(pltpu.make_async_copy(source, x_ref.at[at], x_sem.at[i]))
        copies[-1].start()
    table_copy.wait()
    pick = table
    if first:
        pick = outs.pop()
        pick[...] = lane_pick(table, lanes)
    rows = WIDE // lanes
    for i in range(parts):
        copies[i].wait()
        for start in range(i * part, (i + 1) * part, rows):
            at = slice(start, start + rows)
            x = x_ref[at].reshape(WIDE, x_ref.shape[2])
            out = iter(outs)
            for job, width, begin, end in jobs:
                here = x[:, job - base : job - base + width]
                y = dot(pick[begin * rows : end * rows, :], here).astype(BF16)
                for d in range(end - begin):
                    next(out)[at, :] = y[d * rows : (d + 1) * rows]


def pack(table, snapshots, jobs, first):
    steps, lanes, _ = snapshots.shape
    parts = math.gcd(steps * lanes // WIDE, 3)
    outs = [
        jax.ShapeDtypeStruct((steps, width), BF16)
        for _, width, begin, end in jobs
        for _ in range(begin, end)
    ]
    if first:
        outs.append(jax.ShapeDtypeStruct((WIDE, WIDE), BF16))
    columns = jobs[-1][0] + jobs[-1][1] - jobs[0][0]
    return pl.pallas_call(
        functools.partial(pack_kernel, jobs, parts, first),
        out_shape=outs,
        in_specs=[HBM] * 2,
        out_specs=[VMEM] * len(outs),
        scratch_shapes=[
            pltpu.SMEM(table.shape, jnp.int32) if first else pltpu.VMEM(table.shape, BF16),
            pltpu.VMEM((steps, lanes, columns), BF16),
            pltpu.SemaphoreType.DMA,
            pltpu.SemaphoreType.DMA((parts,)),
        ],
        compiler_params=pltpu.CompilerParams(
            vmem_limit_bytes=FIRST_LIMIT if first else SECOND_LIMIT
        ),
        cost_estimate=pl.CostEstimate(
            flops=2 * WIDE * steps * lanes * columns,
            bytes_accessed=4 * steps * lanes * columns,
            transcendentals=0,
        ),
    )(table, snapshots)


def fill_record(order_ref, pieces, record, factor):
    steps, width = pieces[0].shape
    me = lax.axis_index("tm")
    for d, piece in enumerate(pieces):
        partner = me ^ (len(pieces) - d if d else 0)
        start = pl.multiple_of(order_ref[partner] * steps, steps)
        for c in range(width // LANE):
            cols = slice(c * LANE, (c + 1) * LANE)
            part = piece[:, cols].astype(F32)
            record[c, pl.ds(start, steps), :] = part if factor is None else part * factor[:, cols]


def transform(offsets_ref, f, record, s_ref):
    wanted = [(i, c) for i in range(NBLK) for c in range(record.shape[0])]
    for first in range(0, len(wanted), 2):
        pair = wanted[first : first + 2]
        x = [record[c, pl.ds(offsets_ref[i], NFFT), :].astype(BF16) for i, c in pair]
        x = jnp.concatenate(x, axis=1) if len(x) > 1 else x[0]
        y = dot(f, x)
        if f.shape[0] > NFFT:
            y = y[:NFFT] + y[NFFT:]
        for at, (i, c) in enumerate(pair):
            cols = slice(c * LANE, (c + 1) * LANE)
            s_ref[i, :, cols] = y[:NFREQ, at * LANE : (at + 1) * LANE]
            s_ref[NBLK + i, :, cols] = y[NFREQ:, at * LANE : (at + 1) * LANE]


def padded(s):
    width = s.shape[2]
    pad = jnp.zeros((LANE - HALF_ROWS, width), F32)
    real = s[:NBLK].reshape(HALF_ROWS, width)
    imag = s[NBLK:].reshape(HALF_ROWS, width)
    return jnp.concatenate([real, pad, imag, pad], axis=0)


def gram_kernel(lanes, scale, first, last, order_ref, offsets_ref, w_ref, f_ref, pick_ref, *refs):
    pieces = refs[:lanes]
    rest = refs[lanes:]
    if not first:
        before_ref, _, *rest = rest
    *packed_refs, record, s_ref, masked = rest
    fill_record(order_ref, pieces, record, jnp.sqrt(w_ref[...]))
    transform(offsets_ref, f_ref[:NFFT] if last else f_ref[...], record, s_ref)
    row = lax.broadcasted_iota(jnp.int32, (HALF_ROWS, LANE), 0)
    col = lax.broadcasted_iota(jnp.int32, (HALF_ROWS, LANE), 1)
    same = row % SUB == col % SUB
    for g in range(GROUPS):
        at = slice(g * SUB, (g + 1) * SUB)
        s = s_ref[:, at, :]
        full = dot_nt(s.reshape(2 * HALF_ROWS, -1).astype(BF16), padded(s).astype(BF16))
        real = full[:HALF_ROWS, :LANE] + full[HALF_ROWS:, LANE:]
        imag = full[:HALF_ROWS, LANE:] - full[HALF_ROWS:, :LANE]
        real = jnp.where(same, real, 0.0)
        imag = jnp.where(same, imag, 0.0)
        for a in range(NBLK):
            rows = slice(a * SUB, (a + 1) * SUB)
            masked[at, a * WIDE : a * WIDE + LANE] = real[rows]
            masked[at, a * WIDE + LANE : (a + 1) * WIDE] = imag[rows]
    total = dot(masked[...].astype(BF16), pick_ref[...]).T * scale
    if not first:
        total = total + before_ref[...]
    if not last:
        packed_refs[0][...] = total
        return
    keep_ref, send_ref = packed_refs
    other = lax.axis_index("tm") % 2 == 1
    keep_ref[...] = jnp.where(other, total[HALF:], total[:HALF]).astype(BF16)
    send_ref[...] = jnp.where(other, total[:HALF], total[HALF:]).astype(BF16)


def gram_part(order, offsets, weights, tables, pieces, before, last, scale):
    lanes = len(pieces)
    steps, width = pieces[0].shape
    first = not before
    args = [order, offsets, weights, *tables, *pieces, *before]
    return pl.pallas_call(
        functools.partial(gram_kernel, lanes, scale, first, last),
        out_shape=[jax.ShapeDtypeStruct((HALF, NFREQ), BF16)] * 2
        if last
        else [jax.ShapeDtypeStruct((PACKED, NFREQ), F32)],
        in_specs=[SMEM, SMEM] + [VMEM] * (len(args) - 2),
        out_specs=[VMEM] * (2 if last else 1),
        scratch_shapes=[
            pltpu.VMEM((width // LANE, lanes * steps, LANE), F32),
            pltpu.VMEM((2 * NBLK, NFREQ, width), F32),
            pltpu.VMEM((NFREQ, NBLK * WIDE), F32),
        ],
        compiler_params=pltpu.CompilerParams(vmem_limit_bytes=32 * 2**20),
        cost_estimate=pl.CostEstimate(
            flops=width * 10**7, bytes_accessed=3 * 10**6, transcendentals=0
        ),
    )(*args)


def spectrum_kernel(lanes, order_ref, offsets_ref, f_ref, *refs):
    high_ref, low_ref, record, s_ref = refs[-4:]
    fill_record(order_ref, refs[:lanes], record, None)
    transform(offsets_ref, f_ref[...], record, s_ref)
    for g in range(GROUPS):
        s = s_ref[:, g * SUB : (g + 1) * SUB, :].reshape(2 * HALF_ROWS, -1)
        high_ref[g], low_ref[g] = split(s)


def spectrum(order, offsets, fourier, pieces, after):
    lanes = len(pieces)
    steps, width = pieces[0].shape
    args = [order, offsets, fourier, *pieces, *after]
    part = jax.ShapeDtypeStruct((GROUPS, 2 * HALF_ROWS, width), BF16)
    return pl.pallas_call(
        functools.partial(spectrum_kernel, lanes),
        out_shape=[part, part],
        in_specs=[SMEM, SMEM] + [VMEM] * (len(args) - 2),
        out_specs=[VMEM, VMEM],
        scratch_shapes=[
            pltpu.VMEM((width // LANE, lanes * steps, LANE), F32),
            pltpu.VMEM((2 * NBLK, NFREQ, width), F32),
        ],
        compiler_params=pltpu.CompilerParams(vmem_limit_bytes=32 * 2**20),
        cost_estimate=pl.CostEstimate(
            flops=width * 10**7, bytes_accessed=3 * 10**6, transcendentals=0
        ),
    )(*args)


class Hermitian:
    def __init__(self, main, corner):
        self.main = main
        self.corner = corner

    def entry(self, a, e):
        if e < SUB:
            return self.main[0, a, pl.ds(e, 1), :], self.main[1, a, pl.ds(e, 1), :], 1
        if a < SUB:
            return self.main[0, e, pl.ds(a, 1), :], self.main[1, e, pl.ds(a, 1), :], -1
        at = pl.ds(e - SUB, 1)
        return self.corner[0, a - SUB, at, :], self.corner[1, a - SUB, at, :], 1

    def put(self, a, e, real, imag):
        if e < SUB:
            self.main[0, a, pl.ds(e, 1), :] = real
            self.main[1, a, pl.ds(e, 1), :] = imag
        elif a >= SUB:
            at = pl.ds(e - SUB, 1)
            self.corner[0, a - SUB, at, :] = real
            self.corner[1, a - SUB, at, :] = imag


def product(x, y, out, diagonal=0.0, factor=1.0):
    sub = lax.broadcasted_iota(jnp.int32, (SUB, NFREQ), 0)
    yr = [y.main[0, b] for b in range(NBLK)]
    yi = [y.main[1, b] for b in range(NBLK)]
    for a in range(NBLK):
        real = imag = None
        for b in range(NBLK):
            pr, pi, sign = x.entry(a, b)
            tr, ti = pi * yi[b], pi * yr[b]
            if sign > 0:
                tr, ti = pr * yr[b] - tr, pr * yi[b] + ti
            else:
                tr, ti = pr * yr[b] + tr, pr * yi[b] - ti
            real = tr if real is None else real + tr
            imag = ti if imag is None else imag + ti
        if factor != 1.0:
            real, imag = factor * real, factor * imag
        if diagonal and a < SUB:
            real = real + jnp.where(sub == a, diagonal, 0.0)
        out.main[0, a] = real
        out.main[1, a] = imag
    ar = [[x.main[0, SUB + a], x.corner[0, a]] for a in range(CORNER)]
    ai = [[x.main[1, SUB + a], x.corner[1, a]] for a in range(CORNER)]
    er = [[yr[SUB + e], y.corner[0, e]] for e in range(CORNER)]
    ei = [[yi[SUB + e], y.corner[1, e]] for e in range(CORNER)]
    for a in range(CORNER):
        for e in range(a, CORNER):
            real = sum(ar[a][h] * er[e][h] + ai[a][h] * ei[e][h] for h in range(2))
            real = factor * jnp.sum(real, axis=0, keepdims=True)
            if a == e:
                real = real + diagonal
                out.put(SUB + a, SUB + a, real, jnp.zeros_like(real))
            else:
                imag = sum(ai[a][h] * er[e][h] - ar[a][h] * ei[e][h] for h in range(2))
                imag = factor * jnp.sum(imag, axis=0, keepdims=True)
                out.put(SUB + a, SUB + e, real, imag)
                out.put(SUB + e, SUB + a, real, -imag)


def affine(x, outs):
    sub = lax.broadcasted_iota(jnp.int32, (SUB, NFREQ), 0)
    for a in range(NBLK):
        real = -0.5 * x.main[0, a]
        imag = -0.5 * x.main[1, a]
        if a < SUB:
            real = real + jnp.where(sub == a, 1.5, 0.0)
        for out in outs:
            out.main[0, a] = real
            out.main[1, a] = imag
    for a in range(CORNER):
        real = jnp.where(sub == a, 1.5, 0.0) - 0.5 * x.corner[0, a]
        imag = -0.5 * x.corner[1, a]
        for out in outs:
            out.corner[0, a] = real
            out.corner[1, a] = imag


def make_roots(share, half_ref, other_ref, gram_ref, packed, rolled, mats):
    core = lax.axis_index("tm") % 2
    packed[pl.ds(pl.multiple_of(core * HALF, HALF), HALF), :] = half_ref[...]
    packed[pl.ds(pl.multiple_of((1 - core) * HALF, HALF), HALF), :] = other_ref[...]
    at = lax.axis_index("sx") * lax.axis_size("sy") + lax.axis_index("sy")
    rolled[...] = pltpu.roll(packed[...], (NFREQ - at * share) % NFREQ, 1)
    y, z, p, y2, z2 = [Hermitian(mats[2 * i], mats[2 * i + 1]) for i in range(5)]
    for ref in mats[1::2]:
        ref[...] = jnp.zeros_like(ref)

    def row(ref, part, a, e):
        return ref[pl.ds(ROWS[part, a, e], 1), :]

    trace = 2.0 * sum(row(packed, 0, a, a) for a in range(NBLK))
    norm = 1.0 / jnp.sqrt(trace)
    packed[...] = packed[...] / trace
    zero = jnp.zeros((1, NFREQ), F32)
    for a in range(NBLK):
        y.put(a, a, row(packed, 0, a, a), zero)
        gram_ref[a, a, 0:1, :] = row(rolled, 0, a, a)[:, :share]
        gram_ref[a, a, 1:2, :] = zero[:, :share]
        for e in range(a + 1, NBLK):
            real, imag = row(packed, 0, a, e), row(packed, 1, a, e)
            y.put(a, e, real, imag)
            y.put(e, a, real, -imag)
            real, imag = row(rolled, 0, a, e)[:, :share], row(rolled, 1, a, e)[:, :share]
            gram_ref[a, e, 0:1, :] = real
            gram_ref[e, a, 0:1, :] = real
            gram_ref[a, e, 1:2, :] = imag
            gram_ref[e, a, 1:2, :] = -imag
    for step in range(ROOT_STEPS):
        if step == 0:
            affine(y, [p, z2])
        else:
            product(z, y, p, 1.5, -0.5)
            product(p, z, z2)
        if step < ROOT_STEPS - 1:
            product(y, p, y2)
        y, y2 = y2, y
        z, z2 = z2, z
    none = jnp.zeros((SUB - CORNER, NFREQ), F32)
    stacks = []
    for m0 in range(0, NBLK, STACK):
        modes = range(m0, min(m0 + STACK, NBLK))
        stack = []
        for m in modes:
            for c in range(2):
                stack.append(z.main[c, m] * norm)
                for b in range(SUB, NBLK):
                    real, imag, sign = z.entry(m, b)
                    stack.append((imag * sign if c else real) * norm)
                stack.append(none)
        stack += [jnp.zeros((32, NFREQ), F32)] * (STACK - len(modes))
        stacks.append(jnp.concatenate(stack, axis=0).T)
    return stacks


def mode_kernel(chunks, share, half_ref, other_ref, spread_ref, *refs):
    high_refs = refs[:chunks]
    low_refs = refs[chunks : 2 * chunks]
    out_ref, gram_ref, v, packed, rolled, *mats = refs[2 * chunks :]
    step = pl.program_id(0)

    @pl.when(step == 0)
    def _():
        stacks = make_roots(share, half_ref, other_ref, gram_ref, packed, rolled, mats)
        row = lax.broadcasted_iota(jnp.int32, (NFREQ, 3 * LANE), 0)
        col = lax.broadcasted_iota(jnp.int32, (NFREQ, 3 * LANE), 1)
        same = row % SUB == col % SUB
        for at, stack in enumerate(stacks):
            both = jnp.concatenate(split(stack), axis=1)
            for m in range(at * STACK, min((at + 1) * STACK, NBLK)):
                wide = dot(both, spread_ref[m - at * STACK])
                for c in range(2):
                    here = wide[:, c * 3 * LANE : (c + 1) * 3 * LANE]
                    v[c * NBLK + m] = jnp.where(same, here, 0.0)

    fields = []
    for h in range(STEP_GROUPS):
        g = step * STEP_GROUPS + h
        start = pl.multiple_of(g * SUB, SUB)
        vg = v[:, pl.ds(start, SUB), :].reshape(2 * HALF_ROWS, 3 * LANE).astype(BF16)
        vg = jnp.concatenate([vg[:, : 2 * LANE], vg[:, :LANE], vg[:, 2 * LANE :]], axis=1)
        high = jnp.concatenate([r[g] for r in high_refs], axis=1)
        low = jnp.concatenate([r[g] for r in low_refs], axis=1)
        inputs = jnp.concatenate([high, high[:LOW], low, high[LOW : 2 * LOW]], axis=0)
        fields.append(dot(vg, inputs).reshape(2 * NBLK, SUB, -1))
    both = jnp.concatenate(fields, axis=1).astype(BF16)
    out_ref[...] = both.reshape(out_ref.shape)


def mode_fields(half, other, spread, highs, lows, share):
    width = sum(s.shape[2] for s in highs)
    return pl.pallas_call(
        functools.partial(mode_kernel, len(highs), share),
        grid=(GROUPS // STEP_GROUPS,),
        out_shape=[
            jax.ShapeDtypeStruct((2, NBLK, NFREQ, width), BF16),
            jax.ShapeDtypeStruct((NBLK, NBLK, 2, share), F32),
        ],
        in_specs=[VMEM] * (3 + 2 * len(highs)),
        out_specs=[
            pl.BlockSpec((2, NBLK, STEP_GROUPS * SUB, width), lambda i: (0, 0, i, 0)),
            spec((NBLK, NBLK, 2, share)),
        ],
        scratch_shapes=[
            pltpu.VMEM((2 * NBLK, NFREQ, 3 * LANE), F32),
            pltpu.VMEM((PACKED, NFREQ), F32),
            pltpu.VMEM((PACKED, NFREQ), F32),
        ]
        + [
            pltpu.VMEM((2, NBLK, SUB, NFREQ), F32),
            pltpu.VMEM((2, CORNER, SUB, NFREQ), F32),
        ]
        * 5,
        compiler_params=pltpu.CompilerParams(vmem_limit_bytes=32 * 2**20),
    )(half, other, spread, *highs, *lows)


def swap(x, axes, mask, size):
    return lax.ppermute(x, axes, [(i, i ^ mask) for i in range(size)])


def powers(size):
    return [1 << i for i in range(size.bit_length() - 1)]


def body(snapshots, weights, block_order, owner, offsets):
    lanes = lax.axis_size("tm")
    groups = lax.axis_size("sx") * lax.axis_size("sy")
    points = snapshots.shape[2]
    chunks = [(0, points // 2), (points // 2, points // 2)]
    scale = 1.0 / (lanes * groups * points)
    tables = (jnp.asarray(fourier_tables()), jnp.asarray(pick_table()))
    weights = weights.reshape(1, -1)

    near = min(2, lanes)
    (base, width), (next_base, next_width) = chunks
    *far, table = pack(owner, snapshots, [(base, width, near, lanes)], True)
    jobs = [(base, width, 0, near), (next_base, next_width, 0, lanes)]
    rest = list(pack(table, snapshots, jobs, False))
    arrived = []
    for packed in (rest[:near] + far, rest[near:]):
        moved = [swap(packed[d], "tm", d, lanes) for d in reversed(range(1, lanes))]
        arrived.append([packed[0]] + moved)

    highs, lows = [], []
    before = []
    for at, pieces in enumerate(arrived):
        base, width = chunks[at]
        here = weights[:, base : base + width]
        last = at == len(arrived) - 1
        total = gram_part(block_order, offsets, here, tables, pieces, before, last, scale)
        after = total if last else []
        high, low = spectrum(block_order, offsets, tables[0], pieces, after)
        highs.append(high)
        lows.append(low)
        before = [total[0], high]

    axes = ("tm", "sx", "sy")
    size = lanes * groups
    bits = [b * groups for b in powers(lanes)] + powers(groups)
    keep, send = total
    half = keep.astype(F32) + swap(send, axes, bits[0], size).astype(F32)
    for at in range(1, len(bits), 2):
        masks = bits[at : at + 2]
        if len(masks) == 2:
            masks.append(masks[0] ^ masks[1])
        half = half.astype(BF16)
        terms = [half] + [swap(half, axes, mask, size) for mask in masks]
        terms = [t.astype(F32) for t in terms]
        while len(terms) > 1:
            terms = [a + b for a, b in zip(terms[::2], terms[1::2])]
        half = terms[0]
    half, highs[-1] = lax.optimization_barrier((half, highs[-1]))
    other = swap(half, axes, bits[0], size)

    spread = jnp.asarray(spread_table())
    modes, gram = mode_fields(half, other, spread, highs, lows, NFREQ // groups)
    modes = jnp.transpose(modes, (0, 2, 1, 3))[:, :, :, None, :]
    return modes, jnp.transpose(gram, (2, 3, 0, 1))


def solution(mesh):
    placed = (P("tm", None, ("sx", "sy")), P(("sx", "sy")), P(), P(("sx", "sy"), None), P())
    return jax.shard_map(
        body,
        mesh=mesh,
        in_specs=placed,
        out_specs=(P(None, None, None, "tm", ("sx", "sy")), P(None, ("sx", "sy"), None, None)),
        check_vma=False,
    )
```

```python
import functools
import math

import jax
import jax.numpy as jnp
import numpy as np
from jax import lax
from jax.experimental import pallas as pl
from jax.experimental.pallas import tpu as pltpu
from jax.sharding import PartitionSpec as P

NFFT = 256
NFREQ = 128
NBLK = 11
LANE = 128
SUB = 8
HALF_ROWS = NBLK * SUB
GROUPS = NFREQ // SUB
STEP_GROUPS = 4
MATS = 7
PACKED = 128
HALF = PACKED // 2
STACK = 4
CORNER = NBLK - SUB
WIDE = 2 * LANE
FIRST_LIMIT = 64 * 2**20
SECOND_LIMIT = FIRST_LIMIT - 1450 * 2**10
BF16 = jnp.bfloat16
F32 = jnp.float32


def fourier_tables():
    n = np.arange(NFFT)
    k = np.arange(NFREQ)
    angles = 2.0 * np.pi * ((k[:, None] * n[None, :]) % NFFT) / NFFT
    scaled = (0.5 - 0.5 * np.cos(2.0 * np.pi * n / NFFT)) / math.sqrt(0.375 * NFFT)
    table = np.concatenate([np.cos(angles) * scaled, -np.sin(angles) * scaled], axis=0)
    high = table.astype(jnp.bfloat16)
    low = (table - high.astype(np.float64)).astype(jnp.bfloat16)
    return np.concatenate([high, low], axis=0)


def packed_rows():
    rows = {}
    for a in range(NBLK):
        for e in range(a, NBLK):
            rows[0, a, e] = len(rows)
        for e in range(a + 1, NBLK):
            rows[1, a, e] = len(rows)
    return rows


ROWS = packed_rows()


def pick_table():
    pick = np.zeros((NBLK, 2, LANE, PACKED), np.float32)
    for (part, a, e), row in ROWS.items():
        pick[a, part, e * SUB : (e + 1) * SUB, row] = 1.0
    return pick.reshape(NBLK * WIDE, PACKED).astype(jnp.bfloat16)


def spread_table():
    spread = np.zeros((2, STACK, 2, 16, WIDE), np.float32)
    for b in range(NBLK):
        first = slice(b * SUB, b * SUB + SUB)
        second = slice(HALF_ROWS + b * SUB, HALF_ROWS + b * SUB + SUB)
        spread[0, :, 0, b, first] = 1.0
        spread[0, :, 1, b, second] = 1.0
        spread[1, :, 1, b, first] = -1.0
        spread[1, :, 0, b, second] = 1.0
    return spread.reshape(2, LANE, WIDE).astype(jnp.bfloat16)


def dot(a, b):
    return jnp.dot(a, b, preferred_element_type=F32)


def dot_nt(a, b):
    return lax.dot_general(a, b, (((1,), (1,)), ((), ())), preferred_element_type=F32)


def spec(shape):
    return pl.BlockSpec(shape, lambda *_: (0,) * len(shape))


SMEM = pl.BlockSpec(memory_space=pltpu.SMEM)
VMEM = pl.BlockSpec(memory_space=pltpu.VMEM)
HBM = pl.BlockSpec(memory_space=pltpu.HBM)


def lane_pick(owner, lanes):
    me = lax.axis_index("tm")
    rows = WIDE // lanes
    out_row = lax.broadcasted_iota(jnp.int32, (WIDE, WIDE), 0)
    in_row = lax.broadcasted_iota(jnp.int32, (WIDE, WIDE), 1)
    row_of = (out_row % rows) * lanes
    for d in range(lanes):
        slot = me ^ d
        source = jnp.int32(0)
        for lane in range(lanes):
            source = source + jnp.where(owner[0, lane] == slot, lane, 0)
        row_of = jnp.where(out_row // rows == d, row_of + source, row_of)
    return jnp.where(in_row == row_of, 1.0, 0.0).astype(BF16)


def pack_kernel(jobs, parts, first, table_hbm, x_hbm, *refs):
    steps, lanes, _ = x_hbm.shape
    base = jobs[0][0]
    table, x_ref, table_sem, x_sem = refs[-4:]
    outs = list(refs[:-4])
    part = steps // parts
    table_copy = pltpu.make_async_copy(table_hbm, table, table_sem)
    table_copy.start()
    copies = []
    for i in range(parts):
        at = slice(i * part, (i + 1) * part)
        source = x_hbm.at[at, :, base : base + x_ref.shape[2]]
        copies.append(pltpu.make_async_copy(source, x_ref.at[at], x_sem.at[i]))
        copies[-1].start()
    table_copy.wait()
    pick = table
    if first:
        pick = outs.pop()
        pick[...] = lane_pick(table, lanes)
    rows = WIDE // lanes
    for i in range(parts):
        copies[i].wait()
        for start in range(i * part, (i + 1) * part, rows):
            at = slice(start, start + rows)
            x = x_ref[at].reshape(WIDE, x_ref.shape[2])
            out = iter(outs)
            for job, width, begin, end in jobs:
                here = x[:, job - base : job - base + width]
                y = dot(pick[begin * rows : end * rows, :], here).astype(BF16)
                for d in range(end - begin):
                    next(out)[at, :] = y[d * rows : (d + 1) * rows]


def pack(table, snapshots, jobs, first):
    steps, lanes, _ = snapshots.shape
    parts = math.gcd(steps * lanes // WIDE, 3)
    outs = [
        jax.ShapeDtypeStruct((steps, width), BF16)
        for _, width, begin, end in jobs
        for _ in range(begin, end)
    ]
    if first:
        outs.append(jax.ShapeDtypeStruct((WIDE, WIDE), BF16))
    columns = jobs[-1][0] + jobs[-1][1] - jobs[0][0]
    return pl.pallas_call(
        functools.partial(pack_kernel, jobs, parts, first),
        out_shape=outs,
        in_specs=[HBM] * 2,
        out_specs=[VMEM] * len(outs),
        scratch_shapes=[
            pltpu.SMEM(table.shape, jnp.int32) if first else pltpu.VMEM(table.shape, BF16),
            pltpu.VMEM((steps, lanes, columns), BF16),
            pltpu.SemaphoreType.DMA,
            pltpu.SemaphoreType.DMA((parts,)),
        ],
        compiler_params=pltpu.CompilerParams(
            vmem_limit_bytes=FIRST_LIMIT if first else SECOND_LIMIT
        ),
        cost_estimate=pl.CostEstimate(
            flops=2 * WIDE * steps * lanes * columns,
            bytes_accessed=4 * steps * lanes * columns,
            transcendentals=0,
        ),
    )(table, snapshots)


def fill_record(order_ref, pieces, record, factor):
    steps, width = pieces[0].shape
    me = lax.axis_index("tm")
    for d, piece in enumerate(pieces):
        partner = me ^ (len(pieces) - d if d else 0)
        start = pl.multiple_of(order_ref[partner] * steps, steps)
        for c in range(width // LANE):
            cols = slice(c * LANE, (c + 1) * LANE)
            part = piece[:, cols].astype(F32)
            record[c, pl.ds(start, steps), :] = part if factor is None else part * factor[:, cols]


def transform(offsets_ref, f, record, s_ref):
    wanted = [(i, c) for i in range(NBLK) for c in range(record.shape[0])]
    for first in range(0, len(wanted), 2):
        pair = wanted[first : first + 2]
        x = [record[c, pl.ds(offsets_ref[i], NFFT), :].astype(BF16) for i, c in pair]
        x = jnp.concatenate(x, axis=1) if len(x) > 1 else x[0]
        y = dot(f, x)
        if f.shape[0] > NFFT:
            y = y[:NFFT] + y[NFFT:]
        for at, (i, c) in enumerate(pair):
            cols = slice(c * LANE, (c + 1) * LANE)
            s_ref[i, :, cols] = y[:NFREQ, at * LANE : (at + 1) * LANE]
            s_ref[NBLK + i, :, cols] = y[NFREQ:, at * LANE : (at + 1) * LANE]


def padded(s):
    width = s.shape[2]
    pad = jnp.zeros((LANE - HALF_ROWS, width), F32)
    real = s[:NBLK].reshape(HALF_ROWS, width)
    imag = s[NBLK:].reshape(HALF_ROWS, width)
    return jnp.concatenate([real, pad, imag, pad], axis=0)


def gram_kernel(lanes, scale, first, last, order_ref, offsets_ref, w_ref, f_ref, pick_ref, *refs):
    pieces = refs[:lanes]
    rest = refs[lanes:]
    if not first:
        before_ref, _, *rest = rest
    *packed_refs, record, s_ref, masked = rest
    fill_record(order_ref, pieces, record, jnp.sqrt(w_ref[...]))
    transform(offsets_ref, f_ref[:NFFT] if last else f_ref[...], record, s_ref)
    row = lax.broadcasted_iota(jnp.int32, (HALF_ROWS, LANE), 0)
    col = lax.broadcasted_iota(jnp.int32, (HALF_ROWS, LANE), 1)
    same = row % SUB == col % SUB
    for g in range(GROUPS):
        at = slice(g * SUB, (g + 1) * SUB)
        s = s_ref[:, at, :]
        full = dot_nt(s.reshape(2 * HALF_ROWS, -1).astype(BF16), padded(s).astype(BF16))
        real = full[:HALF_ROWS, :LANE] + full[HALF_ROWS:, LANE:]
        imag = full[:HALF_ROWS, LANE:] - full[HALF_ROWS:, :LANE]
        real = jnp.where(same, real, 0.0)
        imag = jnp.where(same, imag, 0.0)
        for a in range(NBLK):
            rows = slice(a * SUB, (a + 1) * SUB)
            masked[at, a * WIDE : a * WIDE + LANE] = real[rows]
            masked[at, a * WIDE + LANE : (a + 1) * WIDE] = imag[rows]
    total = dot(masked[...].astype(BF16), pick_ref[...]).T * scale
    if not first:
        total = total + before_ref[...]
    if not last:
        packed_refs[0][...] = total
        return
    keep_ref, send_ref = packed_refs
    other = lax.axis_index("tm") % 2 == 1
    keep_ref[...] = jnp.where(other, total[HALF:], total[:HALF]).astype(BF16)
    send_ref[...] = jnp.where(other, total[:HALF], total[HALF:]).astype(BF16)


def gram_part(order, offsets, weights, tables, pieces, before, last, scale):
    lanes = len(pieces)
    steps, width = pieces[0].shape
    first = not before
    args = [order, offsets, weights, *tables, *pieces, *before]
    return pl.pallas_call(
        functools.partial(gram_kernel, lanes, scale, first, last),
        out_shape=[jax.ShapeDtypeStruct((HALF, NFREQ), BF16)] * 2
        if last
        else [jax.ShapeDtypeStruct((PACKED, NFREQ), F32)],
        in_specs=[SMEM, SMEM] + [VMEM] * (len(args) - 2),
        out_specs=[VMEM] * (2 if last else 1),
        scratch_shapes=[
            pltpu.VMEM((width // LANE, lanes * steps, LANE), F32),
            pltpu.VMEM((2 * NBLK, NFREQ, width), F32),
            pltpu.VMEM((NFREQ, NBLK * WIDE), F32),
        ],
        compiler_params=pltpu.CompilerParams(vmem_limit_bytes=32 * 2**20),
        cost_estimate=pl.CostEstimate(
            flops=width * 10**7, bytes_accessed=3 * 10**6, transcendentals=0
        ),
    )(*args)


def spectrum_kernel(lanes, order_ref, offsets_ref, f_ref, *refs):
    s_ref, record = refs[-2:]
    fill_record(order_ref, refs[:lanes], record, None)
    transform(offsets_ref, f_ref[...], record, s_ref)


def spectrum(order, offsets, fourier, pieces, after):
    lanes = len(pieces)
    steps, width = pieces[0].shape
    args = [order, offsets, fourier, *pieces, *after]
    return pl.pallas_call(
        functools.partial(spectrum_kernel, lanes),
        out_shape=jax.ShapeDtypeStruct((2 * NBLK, NFREQ, width), F32),
        in_specs=[SMEM, SMEM] + [VMEM] * (len(args) - 2),
        out_specs=VMEM,
        scratch_shapes=[pltpu.VMEM((width // LANE, lanes * steps, LANE), F32)],
        compiler_params=pltpu.CompilerParams(vmem_limit_bytes=32 * 2**20),
        cost_estimate=pl.CostEstimate(
            flops=width * 10**7, bytes_accessed=3 * 10**6, transcendentals=0
        ),
    )(*args)


class Hermitian:
    def __init__(self, main, corner):
        self.main = main
        self.corner = corner

    def entry(self, a, e):
        if e < SUB:
            return self.main[0, a, pl.ds(e, 1), :], self.main[1, a, pl.ds(e, 1), :], 1
        if a < SUB:
            return self.main[0, e, pl.ds(a, 1), :], self.main[1, e, pl.ds(a, 1), :], -1
        at = pl.ds(e - SUB, 1)
        return self.corner[0, a - SUB, at, :], self.corner[1, a - SUB, at, :], 1

    def put(self, a, e, real, imag):
        if e < SUB:
            self.main[0, a, pl.ds(e, 1), :] = real
            self.main[1, a, pl.ds(e, 1), :] = imag
        elif a >= SUB:
            at = pl.ds(e - SUB, 1)
            self.corner[0, a - SUB, at, :] = real
            self.corner[1, a - SUB, at, :] = imag


def product(x, y, out, diagonal=0.0, terms=()):
    sub = lax.broadcasted_iota(jnp.int32, (SUB, NFREQ), 0)
    yr = [y.main[0, b] for b in range(NBLK)]
    yi = [y.main[1, b] for b in range(NBLK)]
    for a in range(NBLK):
        real = imag = None
        for b in range(NBLK):
            pr, pi, sign = x.entry(a, b)
            tr, ti = pi * yi[b], pi * yr[b]
            if sign > 0:
                tr, ti = pr * yr[b] - tr, pr * yi[b] + ti
            else:
                tr, ti = pr * yr[b] + tr, pr * yi[b] - ti
            real = tr if real is None else real + tr
            imag = ti if imag is None else imag + ti
        for factor, term in terms:
            real = real + factor * term.main[0, a]
            imag = imag + factor * term.main[1, a]
        if diagonal and a < SUB:
            real = real + jnp.where(sub == a, diagonal, 0.0)
        out.main[0, a] = real
        out.main[1, a] = imag
    ar = [[x.main[0, SUB + a], x.corner[0, a]] for a in range(CORNER)]
    ai = [[x.main[1, SUB + a], x.corner[1, a]] for a in range(CORNER)]
    er = [[yr[SUB + e], y.corner[0, e]] for e in range(CORNER)]
    ei = [[yi[SUB + e], y.corner[1, e]] for e in range(CORNER)]
    for a in range(CORNER):
        for e in range(a, CORNER):
            real = sum(ar[a][h] * er[e][h] + ai[a][h] * ei[e][h] for h in range(2))
            real = jnp.sum(real, axis=0, keepdims=True)
            imag = jnp.zeros_like(real)
            if a != e:
                imag = sum(ai[a][h] * er[e][h] - ar[a][h] * ei[e][h] for h in range(2))
                imag = jnp.sum(imag, axis=0, keepdims=True)
            for factor, term in terms:
                r, i, _ = term.entry(SUB + a, SUB + e)
                real, imag = real + factor * r, imag + factor * i
            if a == e:
                out.put(SUB + a, SUB + a, real + diagonal, jnp.zeros_like(real))
            else:
                out.put(SUB + a, SUB + e, real, imag)
                out.put(SUB + e, SUB + a, real, -imag)


def combine(out, diagonal, terms):
    sub = lax.broadcasted_iota(jnp.int32, (SUB, NFREQ), 0)
    for name, rows in (("main", NBLK), ("corner", CORNER)):
        target = getattr(out, name)
        for a in range(rows):
            real = sum(factor * getattr(term, name)[0, a] for factor, term in terms)
            imag = sum(factor * getattr(term, name)[1, a] for factor, term in terms)
            if diagonal and (name == "corner" or a < SUB):
                real = real + jnp.where(sub == a, diagonal, 0.0)
            target[0, a] = real
            target[1, a] = imag


TWO_STEPS = (2.25, -2.4375, 1.6875, -0.5625, 0.0625)


def inverse_root(w, mats):
    q, u, r, t, w2, z = mats
    c0, c1, c2, c3, c4 = TWO_STEPS
    product(w, w, q)
    combine(u, 0.0, [(c3, w), (c4, q)])
    product(q, u, z, c0, [(c1, w), (c2, q)])
    product(z, z, t)
    product(w, t, w2)
    product(w2, w2, q)
    combine(u, 0.0, [(c3, w2), (c4, q)])
    product(q, u, r, c0, [(c1, w2), (c2, q)])
    product(r, r, t)
    product(z, r, u)
    product(w2, t, q)
    combine(q, 1.5, [(-0.5, q)])
    product(u, q, z)
    return z


def make_roots(share, half_ref, other_ref, gram_ref, packed, rolled, mats):
    core = lax.axis_index("tm") % 2
    packed[pl.ds(pl.multiple_of(core * HALF, HALF), HALF), :] = half_ref[...]
    packed[pl.ds(pl.multiple_of((1 - core) * HALF, HALF), HALF), :] = other_ref[...]
    at = lax.axis_index("sx") * lax.axis_size("sy") + lax.axis_index("sy")
    rolled[...] = pltpu.roll(packed[...], (NFREQ - at * share) % NFREQ, 1)
    y, *free = [Hermitian(mats[2 * i], mats[2 * i + 1]) for i in range(MATS)]
    for ref in mats[1::2]:
        ref[...] = jnp.zeros_like(ref)

    def row(ref, part, a, e):
        return ref[pl.ds(ROWS[part, a, e], 1), :]

    trace = 2.0 * sum(row(packed, 0, a, a) for a in range(NBLK))
    norm = 1.0 / jnp.sqrt(trace)
    packed[...] = packed[...] / trace
    zero = jnp.zeros((1, NFREQ), F32)
    for a in range(NBLK):
        y.put(a, a, row(packed, 0, a, a), zero)
        gram_ref[a, a, 0:1, :] = row(rolled, 0, a, a)[:, :share]
        gram_ref[a, a, 1:2, :] = zero[:, :share]
        for e in range(a + 1, NBLK):
            real, imag = row(packed, 0, a, e), row(packed, 1, a, e)
            y.put(a, e, real, imag)
            y.put(e, a, real, -imag)
            real, imag = row(rolled, 0, a, e)[:, :share], row(rolled, 1, a, e)[:, :share]
            gram_ref[a, e, 0:1, :] = real
            gram_ref[e, a, 0:1, :] = real
            gram_ref[a, e, 1:2, :] = imag
            gram_ref[e, a, 1:2, :] = -imag
    z = inverse_root(y, free)
    mean = sum(z.entry(a, a)[0] for a in range(NBLK)) * (1.0 / NBLK)
    sub = lax.broadcasted_iota(jnp.int32, (SUB, NFREQ), 0)
    none = jnp.zeros((SUB - CORNER, NFREQ), F32)
    first = jnp.concatenate([mean * norm, none[1:]], axis=0)
    stacks = []
    for m0 in range(0, NBLK, STACK):
        modes = range(m0, min(m0 + STACK, NBLK))
        stack = []
        for m in modes:
            for c in range(2):
                column = z.main[c, m]
                if c == 0 and m < SUB:
                    column = column - jnp.where(sub == m, mean, 0.0)
                stack.append(column * norm)
                for b in range(SUB, NBLK):
                    real, imag, sign = z.entry(m, b)
                    line = imag * sign if c else real
                    if c == 0 and m == b:
                        line = line - mean
                    stack.append(line * norm)
                stack.append(first if c == 0 and m == 0 else none)
        stack += [jnp.zeros((32, NFREQ), F32)] * (STACK - len(modes))
        stacks.append(jnp.concatenate(stack, axis=0).T)
    return stacks


def mode_kernel(chunks, share, half_ref, other_ref, spread_ref, *refs):
    s_refs = refs[:chunks]
    out_ref, gram_ref, v, mean, packed, rolled, *mats = refs[chunks:]
    step = pl.program_id(0)

    @pl.when(step == 0)
    def _():
        stacks = make_roots(share, half_ref, other_ref, gram_ref, packed, rolled, mats)
        mean[...] = jnp.broadcast_to(stacks[0][:, NBLK : NBLK + 1], (NFREQ, LANE))
        row = lax.broadcasted_iota(jnp.int32, (NFREQ, 2 * HALF_ROWS), 0)
        col = lax.broadcasted_iota(jnp.int32, (NFREQ, 2 * HALF_ROWS), 1)
        same = row % SUB == col % SUB
        place = lax.broadcasted_iota(jnp.int32, (NFREQ, LANE), 1) // 32
        rows = [jnp.where(place == m % STACK, stacks[m // STACK], 0.0) for m in range(NBLK)]
        rows = jnp.concatenate(rows, axis=0).astype(BF16)
        for c in range(2):
            wide = dot(rows, spread_ref[c])[:, : 2 * HALF_ROWS]
            for m in range(NBLK):
                here = wide[m * NFREQ : (m + 1) * NFREQ]
                v[c * NBLK + m] = jnp.where(same, here, 0.0)

    fields = []
    for h in range(STEP_GROUPS):
        at = pl.ds(pl.multiple_of((step * STEP_GROUPS + h) * SUB, SUB), SUB)
        s = jnp.concatenate([r[:, at, :] for r in s_refs], axis=2)
        flat = s.reshape(2 * HALF_ROWS, -1).astype(BF16)
        field = dot(v[:, at, :].reshape(2 * HALF_ROWS, 2 * HALF_ROWS).astype(BF16), flat)
        scale = jnp.concatenate([mean[at, :]] * (s.shape[2] // LANE), axis=1)
        fields.append(field.reshape(s.shape) + s * scale[None])
    both = jnp.concatenate(fields, axis=1).astype(BF16)
    out_ref[...] = both.reshape(out_ref.shape)


def mode_fields(half, other, spread, spectra, share):
    width = sum(s.shape[2] for s in spectra)
    return pl.pallas_call(
        functools.partial(mode_kernel, len(spectra), share),
        grid=(GROUPS // STEP_GROUPS,),
        out_shape=[
            jax.ShapeDtypeStruct((2, NBLK, NFREQ, width), BF16),
            jax.ShapeDtypeStruct((NBLK, NBLK, 2, share), F32),
        ],
        in_specs=[VMEM] * (3 + len(spectra)),
        out_specs=[
            pl.BlockSpec((2, NBLK, STEP_GROUPS * SUB, width), lambda i: (0, 0, i, 0)),
            spec((NBLK, NBLK, 2, share)),
        ],
        scratch_shapes=[
            pltpu.VMEM((2 * NBLK, NFREQ, 2 * HALF_ROWS), F32),
            pltpu.VMEM((NFREQ, LANE), F32),
            pltpu.VMEM((PACKED, NFREQ), F32),
            pltpu.VMEM((PACKED, NFREQ), F32),
        ]
        + [
            pltpu.VMEM((2, NBLK, SUB, NFREQ), F32),
            pltpu.VMEM((2, CORNER, SUB, NFREQ), F32),
        ]
        * MATS,
        compiler_params=pltpu.CompilerParams(vmem_limit_bytes=32 * 2**20),
    )(half, other, spread, *spectra)


def swap(x, axes, mask, size):
    return lax.ppermute(x, axes, [(i, i ^ mask) for i in range(size)])


def powers(size):
    return [1 << i for i in range(size.bit_length() - 1)]


def body(snapshots, weights, block_order, owner, offsets):
    lanes = lax.axis_size("tm")
    groups = lax.axis_size("sx") * lax.axis_size("sy")
    points = snapshots.shape[2]
    chunks = [(0, points // 2), (points // 2, points // 2)]
    scale = 1.0 / (lanes * groups * points)
    tables = (jnp.asarray(fourier_tables()), jnp.asarray(pick_table()))
    weights = weights.reshape(1, -1)

    near = min(2, lanes)
    (base, width), (next_base, next_width) = chunks
    *far, table = pack(owner, snapshots, [(base, width, near, lanes)], True)
    jobs = [(base, width, 0, near), (next_base, next_width, 0, lanes)]
    rest = list(pack(table, snapshots, jobs, False))
    arrived = []
    for packed in (rest[:near] + far, rest[near:]):
        moved = [swap(packed[d], "tm", d, lanes) for d in reversed(range(1, lanes))]
        arrived.append([packed[0]] + moved)

    spectra = []
    before = []
    for at, pieces in enumerate(arrived):
        base, width = chunks[at]
        here = weights[:, base : base + width]
        last = at == len(arrived) - 1
        total = gram_part(block_order, offsets, here, tables, pieces, before, last, scale)
        after = total if last else []
        spectra.append(spectrum(block_order, offsets, tables[0], pieces, after))
        before = [total[0], spectra[-1]]

    axes = ("tm", "sx", "sy")
    size = lanes * groups
    bits = [b * groups for b in powers(lanes)] + powers(groups)
    keep, send = total
    half = keep.astype(F32) + swap(send, axes, bits[0], size).astype(F32)
    for at in range(1, len(bits), 2):
        masks = bits[at : at + 2]
        if len(masks) == 2:
            masks.append(masks[0] ^ masks[1])
        half = half.astype(BF16)
        terms = [half] + [swap(half, axes, mask, size) for mask in masks]
        terms = [t.astype(F32) for t in terms]
        while len(terms) > 1:
            terms = [a + b for a, b in zip(terms[::2], terms[1::2])]
        half = terms[0]
    half, spectra[-1] = lax.optimization_barrier((half, spectra[-1]))
    other = swap(half, axes, bits[0], size)

    spread = jnp.asarray(spread_table())
    modes, gram = mode_fields(half, other, spread, spectra, NFREQ // groups)
    modes = jnp.transpose(modes, (0, 2, 1, 3))[:, :, :, None, :]
    return modes, jnp.transpose(gram, (2, 3, 0, 1))


def solution(mesh):
    placed = (P("tm", None, ("sx", "sy")), P(("sx", "sy")), P(), P(("sx", "sy"), None), P())
    return jax.shard_map(
        body,
        mesh=mesh,
        in_specs=placed,
        out_specs=(P(None, None, None, "tm", ("sx", "sy")), P(None, ("sx", "sy"), None, None)),
        check_vma=False,
    )
```

```python
import functools
import math

import jax
import jax.numpy as jnp
import numpy as np
from jax import lax
from jax.experimental import pallas as pl
from jax.experimental.pallas import tpu as pltpu
from jax.sharding import PartitionSpec as P

NFFT = 256
NFREQ = 128
NBLK = 11
LANE = 128
SUB = 8
HALF_ROWS = NBLK * SUB
GROUPS = NFREQ // SUB
MATS = 7
PACKED = 128
HALF = PACKED // 2
STACK = 4
CORNER = NBLK - SUB
WIDE = 2 * LANE
FIRST_LIMIT = 64 * 2**20
SECOND_LIMIT = FIRST_LIMIT - 1450 * 2**10
BF16 = jnp.bfloat16
F32 = jnp.float32


def fourier_tables():
    n = np.arange(NFFT)
    k = np.arange(NFREQ)
    angles = 2.0 * np.pi * ((k[:, None] * n[None, :]) % NFFT) / NFFT
    scaled = (0.5 - 0.5 * np.cos(2.0 * np.pi * n / NFFT)) / math.sqrt(0.375 * NFFT)
    table = np.concatenate([np.cos(angles) * scaled, -np.sin(angles) * scaled], axis=0)
    high = table.astype(jnp.bfloat16)
    low = (table - high.astype(np.float64)).astype(jnp.bfloat16)
    return np.concatenate([high, low], axis=0)


def packed_rows():
    rows = {}
    for a in range(NBLK):
        for e in range(a, NBLK):
            rows[0, a, e] = len(rows)
        for e in range(a + 1, NBLK):
            rows[1, a, e] = len(rows)
    return rows


ROWS = packed_rows()


def pick_table():
    pick = np.zeros((NBLK, 2, LANE, PACKED), np.float32)
    for (part, a, e), row in ROWS.items():
        pick[a, part, e * SUB : (e + 1) * SUB, row] = 1.0
    return pick.reshape(NBLK * WIDE, PACKED).astype(jnp.bfloat16)


def spread_table():
    spread = np.zeros((2, STACK, 2, 16, WIDE), np.float32)
    for b in range(NBLK):
        first = slice(b * SUB, b * SUB + SUB)
        second = slice(HALF_ROWS + b * SUB, HALF_ROWS + b * SUB + SUB)
        spread[0, :, 0, b, first] = 1.0
        spread[0, :, 1, b, second] = 1.0
        spread[1, :, 1, b, first] = -1.0
        spread[1, :, 0, b, second] = 1.0
    return spread.reshape(2, LANE, WIDE).astype(jnp.bfloat16)


def dot(a, b):
    return jnp.dot(a, b, preferred_element_type=F32)


def dot_nt(a, b):
    return lax.dot_general(a, b, (((1,), (1,)), ((), ())), preferred_element_type=F32)


def spec(shape):
    return pl.BlockSpec(shape, lambda *_: (0,) * len(shape))


SMEM = pl.BlockSpec(memory_space=pltpu.SMEM)
VMEM = pl.BlockSpec(memory_space=pltpu.VMEM)
HBM = pl.BlockSpec(memory_space=pltpu.HBM)


def lane_pick(owner, lanes):
    me = lax.axis_index("tm")
    rows = WIDE // lanes
    out_row = lax.broadcasted_iota(jnp.int32, (WIDE, WIDE), 0)
    in_row = lax.broadcasted_iota(jnp.int32, (WIDE, WIDE), 1)
    row_of = (out_row % rows) * lanes
    for d in range(lanes):
        slot = me ^ d
        source = jnp.int32(0)
        for lane in range(lanes):
            source = source + jnp.where(owner[0, lane] == slot, lane, 0)
        row_of = jnp.where(out_row // rows == d, row_of + source, row_of)
    return jnp.where(in_row == row_of, 1.0, 0.0).astype(BF16)


def pack_kernel(jobs, parts, first, table_hbm, x_hbm, *refs):
    steps, lanes, _ = x_hbm.shape
    base = jobs[0][0]
    table, x_ref, table_sem, x_sem = refs[-4:]
    outs = list(refs[:-4])
    part = steps // parts
    table_copy = pltpu.make_async_copy(table_hbm, table, table_sem)
    table_copy.start()
    copies = []
    for i in range(parts):
        at = slice(i * part, (i + 1) * part)
        source = x_hbm.at[at, :, base : base + x_ref.shape[2]]
        copies.append(pltpu.make_async_copy(source, x_ref.at[at], x_sem.at[i]))
        copies[-1].start()
    table_copy.wait()
    pick = table
    if first:
        pick = outs.pop()
        pick[...] = lane_pick(table, lanes)
    rows = WIDE // lanes
    for i in range(parts):
        copies[i].wait()
        for start in range(i * part, (i + 1) * part, rows):
            at = slice(start, start + rows)
            x = x_ref[at].reshape(WIDE, x_ref.shape[2])
            out = iter(outs)
            for job, width, begin, end in jobs:
                here = x[:, job - base : job - base + width]
                y = dot(pick[begin * rows : end * rows, :], here).astype(BF16)
                for d in range(end - begin):
                    next(out)[at, :] = y[d * rows : (d + 1) * rows]


def pack(table, snapshots, jobs, first):
    steps, lanes, _ = snapshots.shape
    parts = math.gcd(steps * lanes // WIDE, 3)
    outs = [
        jax.ShapeDtypeStruct((steps, width), BF16)
        for _, width, begin, end in jobs
        for _ in range(begin, end)
    ]
    if first:
        outs.append(jax.ShapeDtypeStruct((WIDE, WIDE), BF16))
    columns = jobs[-1][0] + jobs[-1][1] - jobs[0][0]
    return pl.pallas_call(
        functools.partial(pack_kernel, jobs, parts, first),
        out_shape=outs,
        in_specs=[HBM] * 2,
        out_specs=[VMEM] * len(outs),
        scratch_shapes=[
            pltpu.SMEM(table.shape, jnp.int32) if first else pltpu.VMEM(table.shape, BF16),
            pltpu.VMEM((steps, lanes, columns), BF16),
            pltpu.SemaphoreType.DMA,
            pltpu.SemaphoreType.DMA((parts,)),
        ],
        compiler_params=pltpu.CompilerParams(
            vmem_limit_bytes=FIRST_LIMIT if first else SECOND_LIMIT
        ),
        cost_estimate=pl.CostEstimate(
            flops=2 * WIDE * steps * lanes * columns,
            bytes_accessed=4 * steps * lanes * columns,
            transcendentals=0,
        ),
    )(table, snapshots)


def fill_record(order_ref, pieces, record, factor):
    steps, width = pieces[0].shape
    me = lax.axis_index("tm")
    for d, piece in enumerate(pieces):
        partner = me ^ (len(pieces) - d if d else 0)
        start = pl.multiple_of(order_ref[partner] * steps, steps)
        for c in range(width // LANE):
            cols = slice(c * LANE, (c + 1) * LANE)
            part = piece[:, cols].astype(F32)
            record[c, pl.ds(start, steps), :] = part if factor is None else part * factor[:, cols]


def transform(offsets_ref, f, record, s_ref):
    wanted = [(i, c) for i in range(NBLK) for c in range(record.shape[0])]
    for first in range(0, len(wanted), 2):
        pair = wanted[first : first + 2]
        x = [record[c, pl.ds(offsets_ref[i], NFFT), :].astype(BF16) for i, c in pair]
        x = jnp.concatenate(x, axis=1) if len(x) > 1 else x[0]
        y = dot(f, x)
        if f.shape[0] > NFFT:
            y = y[:NFFT] + y[NFFT:]
        for at, (i, c) in enumerate(pair):
            cols = slice(c * LANE, (c + 1) * LANE)
            s_ref[i, :, cols] = y[:NFREQ, at * LANE : (at + 1) * LANE]
            s_ref[NBLK + i, :, cols] = y[NFREQ:, at * LANE : (at + 1) * LANE]


def padded(s):
    width = s.shape[2]
    pad = jnp.zeros((LANE - HALF_ROWS, width), F32)
    real = s[:NBLK].reshape(HALF_ROWS, width)
    imag = s[NBLK:].reshape(HALF_ROWS, width)
    return jnp.concatenate([real, pad, imag, pad], axis=0)


def gram_rows(base, groups, s_ref, pick_ref, masked):
    row = lax.broadcasted_iota(jnp.int32, (HALF_ROWS, LANE), 0)
    col = lax.broadcasted_iota(jnp.int32, (HALF_ROWS, LANE), 1)
    same = row % SUB == col % SUB
    for pair in range(0, groups, 2):
        blocks = []
        for g in (pair, pair + 1):
            s = s_ref[:, pl.ds(pl.multiple_of(base + g * SUB, SUB), SUB), :]
            full = dot_nt(s.reshape(2 * HALF_ROWS, -1).astype(BF16), padded(s).astype(BF16))
            real = full[:HALF_ROWS, :LANE] + full[HALF_ROWS:, LANE:]
            imag = full[:HALF_ROWS, LANE:] - full[HALF_ROWS:, :LANE]
            blocks.append([jnp.where(same, part, 0.0) for part in (real, imag)])
        at = slice(pair * SUB, (pair + 2) * SUB)
        for a in range(NBLK):
            rows = slice(a * SUB, (a + 1) * SUB)
            for part in range(2):
                both = jnp.concatenate([block[part][rows] for block in blocks], axis=0)
                cols = slice(a * WIDE + part * LANE, a * WIDE + (part + 1) * LANE)
                masked[at, cols] = both.astype(BF16)
    return dot(masked[...], pick_ref[...])


def gram_kernel(lanes, scale, last, order_ref, offsets_ref, w_ref, f_ref, pick_ref, *refs):
    pieces = refs[:lanes]
    if not last:
        gram_ref, record, s_ref, masked = refs[lanes:]
    else:
        before_ref, _, gram_ref, s_ref, record, masked = refs[lanes:]
    fill_record(order_ref, pieces, record, jnp.sqrt(w_ref[...]))
    transform(offsets_ref, f_ref[:NFFT] if last else f_ref[...], record, s_ref)
    if not last:
        gram_ref[...] = gram_rows(0, GROUPS, s_ref, pick_ref, masked) * scale
        return
    base = pl.multiple_of((1 - lax.axis_index("tm") % 2) * HALF, HALF)
    total = gram_rows(base, GROUPS // 2, s_ref, pick_ref, masked) * scale
    gram_ref[...] = (total + before_ref[pl.ds(base, HALF), :]).astype(BF16)


def gram_part(order, offsets, weights, tables, pieces, before, scale):
    lanes = len(pieces)
    steps, width = pieces[0].shape
    last = bool(before)
    args = [order, offsets, weights, *tables, *pieces, *before]
    spectrum_shape = (2 * NBLK, NFREQ, width)
    scratch = [pltpu.VMEM((width // LANE, lanes * steps, LANE), F32)]
    if last:
        outs = [jax.ShapeDtypeStruct((HALF, PACKED), BF16)]
        outs.append(jax.ShapeDtypeStruct(spectrum_shape, F32))
    else:
        outs = [jax.ShapeDtypeStruct((NFREQ, PACKED), F32)]
        scratch.append(pltpu.VMEM(spectrum_shape, F32))
    scratch.append(pltpu.VMEM((HALF if last else NFREQ, NBLK * WIDE), BF16))
    return pl.pallas_call(
        functools.partial(gram_kernel, lanes, scale, last),
        out_shape=outs,
        in_specs=[SMEM, SMEM] + [VMEM] * (len(args) - 2),
        out_specs=[VMEM] * len(outs),
        scratch_shapes=scratch,
        compiler_params=pltpu.CompilerParams(vmem_limit_bytes=32 * 2**20),
        cost_estimate=pl.CostEstimate(
            flops=width * 10**7, bytes_accessed=3 * 10**6, transcendentals=0
        ),
    )(*args)


def own_kernel(scale, s_ref, pick_ref, before_ref, gram_ref, masked):
    base = pl.multiple_of(lax.axis_index("tm") % 2 * HALF, HALF)
    total = gram_rows(base, GROUPS // 2, s_ref, pick_ref, masked) * scale
    gram_ref[...] = (total + before_ref[pl.ds(base, HALF), :]).astype(BF16)


def own_part(scaled, pick, before, scale):
    return pl.pallas_call(
        functools.partial(own_kernel, scale),
        out_shape=jax.ShapeDtypeStruct((HALF, PACKED), BF16),
        in_specs=[VMEM] * 3,
        out_specs=VMEM,
        scratch_shapes=[pltpu.VMEM((HALF, NBLK * WIDE), BF16)],
        compiler_params=pltpu.CompilerParams(vmem_limit_bytes=32 * 2**20),
        cost_estimate=pl.CostEstimate(flops=10**9, bytes_accessed=3 * 10**6, transcendentals=0),
    )(scaled, pick, before)


def spectrum_kernel(lanes, order_ref, offsets_ref, f_ref, *refs):
    s_ref, record = refs[-2:]
    fill_record(order_ref, refs[:lanes], record, None)
    transform(offsets_ref, f_ref[...], record, s_ref)


def spectrum(order, offsets, fourier, pieces, after):
    lanes = len(pieces)
    steps, width = pieces[0].shape
    args = [order, offsets, fourier, *pieces, *after]
    return pl.pallas_call(
        functools.partial(spectrum_kernel, lanes),
        out_shape=jax.ShapeDtypeStruct((2 * NBLK, NFREQ, width), F32),
        in_specs=[SMEM, SMEM] + [VMEM] * (len(args) - 2),
        out_specs=VMEM,
        scratch_shapes=[pltpu.VMEM((width // LANE, lanes * steps, LANE), F32)],
        compiler_params=pltpu.CompilerParams(vmem_limit_bytes=32 * 2**20),
        cost_estimate=pl.CostEstimate(
            flops=width * 10**7, bytes_accessed=3 * 10**6, transcendentals=0
        ),
    )(*args)


class Hermitian:
    def __init__(self, main, corner):
        self.main = main
        self.corner = corner

    def entry(self, a, e):
        if e < SUB:
            return self.main[0, a, pl.ds(e, 1), :], self.main[1, a, pl.ds(e, 1), :], 1
        if a < SUB:
            return self.main[0, e, pl.ds(a, 1), :], self.main[1, e, pl.ds(a, 1), :], -1
        at = pl.ds(e - SUB, 1)
        return self.corner[0, a - SUB, at, :], self.corner[1, a - SUB, at, :], 1

    def put(self, a, e, real, imag):
        if e < SUB:
            self.main[0, a, pl.ds(e, 1), :] = real
            self.main[1, a, pl.ds(e, 1), :] = imag
        elif a >= SUB:
            at = pl.ds(e - SUB, 1)
            self.corner[0, a - SUB, at, :] = real
            self.corner[1, a - SUB, at, :] = imag


def product(x, y, out, diagonal=0.0, terms=()):
    sub = lax.broadcasted_iota(jnp.int32, (SUB, NFREQ), 0)
    yr = [y.main[0, b] for b in range(NBLK)]
    yi = [y.main[1, b] for b in range(NBLK)]
    for a in range(NBLK):
        real = imag = None
        for b in range(NBLK):
            pr, pi, sign = x.entry(a, b)
            tr, ti = pi * yi[b], pi * yr[b]
            if sign > 0:
                tr, ti = pr * yr[b] - tr, pr * yi[b] + ti
            else:
                tr, ti = pr * yr[b] + tr, pr * yi[b] - ti
            real = tr if real is None else real + tr
            imag = ti if imag is None else imag + ti
        for factor, term in terms:
            real = real + factor * term.main[0, a]
            imag = imag + factor * term.main[1, a]
        if diagonal and a < SUB:
            real = real + jnp.where(sub == a, diagonal, 0.0)
        out.main[0, a] = real
        out.main[1, a] = imag
    ar = [[x.main[0, SUB + a], x.corner[0, a]] for a in range(CORNER)]
    ai = [[x.main[1, SUB + a], x.corner[1, a]] for a in range(CORNER)]
    er = [[yr[SUB + e], y.corner[0, e]] for e in range(CORNER)]
    ei = [[yi[SUB + e], y.corner[1, e]] for e in range(CORNER)]
    for a in range(CORNER):
        for e in range(a, CORNER):
            real = sum(ar[a][h] * er[e][h] + ai[a][h] * ei[e][h] for h in range(2))
            real = jnp.sum(real, axis=0, keepdims=True)
            imag = jnp.zeros_like(real)
            if a != e:
                imag = sum(ai[a][h] * er[e][h] - ar[a][h] * ei[e][h] for h in range(2))
                imag = jnp.sum(imag, axis=0, keepdims=True)
            for factor, term in terms:
                r, i, _ = term.entry(SUB + a, SUB + e)
                real, imag = real + factor * r, imag + factor * i
            if a == e:
                out.put(SUB + a, SUB + a, real + diagonal, jnp.zeros_like(real))
            else:
                out.put(SUB + a, SUB + e, real, imag)
                out.put(SUB + e, SUB + a, real, -imag)


def combine(out, diagonal, terms):
    sub = lax.broadcasted_iota(jnp.int32, (SUB, NFREQ), 0)
    for name, rows in (("main", NBLK), ("corner", CORNER)):
        target = getattr(out, name)
        for a in range(rows):
            real = sum(factor * getattr(term, name)[0, a] for factor, term in terms)
            imag = sum(factor * getattr(term, name)[1, a] for factor, term in terms)
            if diagonal and (name == "corner" or a < SUB):
                real = real + jnp.where(sub == a, diagonal, 0.0)
            target[0, a] = real
            target[1, a] = imag


TWO_STEPS = (2.25, -2.4375, 1.6875, -0.5625, 0.0625)


def inverse_root(w, mats):
    q, u, r, t, w2, z = mats
    c0, c1, c2, c3, c4 = TWO_STEPS
    product(w, w, q)
    combine(u, 0.0, [(c3, w), (c4, q)])
    product(q, u, z, c0, [(c1, w), (c2, q)])
    product(z, z, t)
    product(w, t, w2)
    product(w2, w2, q)
    combine(u, 0.0, [(c3, w2), (c4, q)])
    product(q, u, r, c0, [(c1, w2), (c2, q)])
    product(r, r, t)
    product(z, r, u)
    product(w2, t, q)
    combine(q, 1.5, [(-0.5, q)])
    product(u, q, z)
    return z


def make_roots(share, half_ref, other_ref, gram_ref, packed, rolled, mats):
    core = lax.axis_index("tm") % 2
    packed[pl.ds(pl.multiple_of(core * HALF, HALF), HALF), :] = half_ref[...]
    packed[pl.ds(pl.multiple_of((1 - core) * HALF, HALF), HALF), :] = other_ref[...]
    packed[...] = packed[...].T
    at = lax.axis_index("sx") * lax.axis_size("sy") + lax.axis_index("sy")
    rolled[...] = pltpu.roll(packed[...], (NFREQ - at * share) % NFREQ, 1)
    y, *free = [Hermitian(mats[2 * i], mats[2 * i + 1]) for i in range(MATS)]
    for ref in mats[1::2]:
        ref[...] = jnp.zeros_like(ref)

    def row(ref, part, a, e):
        return ref[pl.ds(ROWS[part, a, e], 1), :]

    trace = 2.0 * sum(row(packed, 0, a, a) for a in range(NBLK))
    norm = 1.0 / jnp.sqrt(trace)
    packed[...] = packed[...] / trace
    zero = jnp.zeros((1, NFREQ), F32)
    for a in range(NBLK):
        y.put(a, a, row(packed, 0, a, a), zero)
        gram_ref[a, a, 0:1, :] = row(rolled, 0, a, a)[:, :share]
        gram_ref[a, a, 1:2, :] = zero[:, :share]
        for e in range(a + 1, NBLK):
            real, imag = row(packed, 0, a, e), row(packed, 1, a, e)
            y.put(a, e, real, imag)
            y.put(e, a, real, -imag)
            real, imag = row(rolled, 0, a, e)[:, :share], row(rolled, 1, a, e)[:, :share]
            gram_ref[a, e, 0:1, :] = real
            gram_ref[e, a, 0:1, :] = real
            gram_ref[a, e, 1:2, :] = imag
            gram_ref[e, a, 1:2, :] = -imag
    z = inverse_root(y, free)
    mean = sum(z.entry(a, a)[0] for a in range(NBLK)) * (1.0 / NBLK)
    sub = lax.broadcasted_iota(jnp.int32, (SUB, NFREQ), 0)
    none = jnp.zeros((SUB - CORNER, NFREQ), F32)
    first = jnp.concatenate([mean * norm, none[1:]], axis=0)
    stacks = []
    for m0 in range(0, NBLK, STACK):
        modes = range(m0, min(m0 + STACK, NBLK))
        stack = []
        for m in modes:
            for c in range(2):
                column = z.main[c, m]
                if c == 0 and m < SUB:
                    column = column - jnp.where(sub == m, mean, 0.0)
                stack.append(column * norm)
                for b in range(SUB, NBLK):
                    real, imag, sign = z.entry(m, b)
                    line = imag * sign if c else real
                    if c == 0 and m == b:
                        line = line - mean
                    stack.append(line * norm)
                stack.append(first if c == 0 and m == 0 else none)
        stack += [jnp.zeros((32, NFREQ), F32)] * (STACK - len(modes))
        stacks.append(jnp.concatenate(stack, axis=0).T)
    return stacks


def mode_kernel(chunks, share, half_ref, other_ref, spread_ref, *refs):
    s_refs = refs[:chunks]
    out_hbm, gram_ref, out, v, mean, packed, rolled, sem, *mats = refs[chunks:]
    stacks = make_roots(share, half_ref, other_ref, gram_ref, packed, rolled, mats)
    mean[...] = jnp.broadcast_to(stacks[0][:, NBLK : NBLK + 1], (NFREQ, LANE))
    row = lax.broadcasted_iota(jnp.int32, (NFREQ, 2 * HALF_ROWS), 0)
    col = lax.broadcasted_iota(jnp.int32, (NFREQ, 2 * HALF_ROWS), 1)
    same = row % SUB == col % SUB
    place = lax.broadcasted_iota(jnp.int32, (NFREQ, LANE), 1) // 32
    rows = [jnp.where(place == m % STACK, stacks[m // STACK], 0.0) for m in range(NBLK)]
    rows = jnp.concatenate(rows, axis=0).astype(BF16)
    for c in range(2):
        wide = dot(rows, spread_ref[c])[:, : 2 * HALF_ROWS]
        for m in range(NBLK):
            v[c * NBLK + m] = jnp.where(same, wide[m * NFREQ : (m + 1) * NFREQ], 0.0)

    copies = []
    for pair in range(GROUPS // 2):
        fields = []
        for g in (2 * pair, 2 * pair + 1):
            at = slice(g * SUB, (g + 1) * SUB)
            s = jnp.concatenate([r[:, at, :] for r in s_refs], axis=2)
            flat = s.reshape(2 * HALF_ROWS, -1).astype(BF16)
            field = dot(v[:, at, :].reshape(2 * HALF_ROWS, 2 * HALF_ROWS).astype(BF16), flat)
            scale = jnp.concatenate([mean[at, :]] * (s.shape[2] // LANE), axis=1)
            fields.append(field.reshape(s.shape) + s * scale[None])
        both = jnp.concatenate(fields, axis=1).astype(BF16)
        at = slice(pair * 2 * SUB, (pair + 1) * 2 * SUB)
        out[:, :, at, :] = both.reshape(2, NBLK, 2 * SUB, -1)
        copies.append(
            pltpu.make_async_copy(out.at[:, :, at, :], out_hbm.at[:, :, at, :], sem.at[pair])
        )
        copies[-1].start()
    for copy in copies:
        copy.wait()


def mode_fields(half, other, spread, spectra, share):
    shape = (2, NBLK, NFREQ, sum(s.shape[2] for s in spectra))
    return pl.pallas_call(
        functools.partial(mode_kernel, len(spectra), share),
        out_shape=[
            jax.ShapeDtypeStruct(shape, BF16),
            jax.ShapeDtypeStruct((NBLK, NBLK, 2, share), F32),
        ],
        in_specs=[VMEM] * (3 + len(spectra)),
        out_specs=[HBM, VMEM],
        scratch_shapes=[
            pltpu.VMEM(shape, BF16),
            pltpu.VMEM((2 * NBLK, NFREQ, 2 * HALF_ROWS), F32),
            pltpu.VMEM((NFREQ, LANE), F32),
            pltpu.VMEM((PACKED, NFREQ), F32),
            pltpu.VMEM((PACKED, NFREQ), F32),
            pltpu.SemaphoreType.DMA((GROUPS // 2,)),
        ]
        + [
            pltpu.VMEM((2, NBLK, SUB, NFREQ), F32),
            pltpu.VMEM((2, CORNER, SUB, NFREQ), F32),
        ]
        * MATS,
        compiler_params=pltpu.CompilerParams(vmem_limit_bytes=32 * 2**20),
    )(half, other, spread, *spectra)


def swap(x, axes, mask, size):
    return lax.ppermute(x, axes, [(i, i ^ mask) for i in range(size)])


def powers(size):
    return [1 << i for i in range(size.bit_length() - 1)]


def body(snapshots, weights, block_order, owner, offsets):
    lanes = lax.axis_size("tm")
    groups = lax.axis_size("sx") * lax.axis_size("sy")
    points = snapshots.shape[2]
    chunks = [(0, points // 2), (points // 2, points // 2)]
    scale = 1.0 / (lanes * groups * points)
    tables = (jnp.asarray(fourier_tables()), jnp.asarray(pick_table()))
    weights = weights.reshape(1, -1)

    near = min(2, lanes)
    (base, width), (next_base, next_width) = chunks
    *far, table = pack(owner, snapshots, [(base, width, near, lanes)], True)
    jobs = [(base, width, 0, near), (next_base, next_width, 0, lanes)]
    rest = list(pack(table, snapshots, jobs, False))
    arrived = []
    for packed in (rest[:near] + far, rest[near:]):
        moved = [swap(packed[d], "tm", d, lanes) for d in reversed(range(1, lanes))]
        arrived.append([packed[0]] + moved)

    axes = ("tm", "sx", "sy")
    size = lanes * groups
    bits = [b * groups for b in powers(lanes)] + powers(groups)
    parts = [weights[:, base : base + width] for base, width in chunks]
    (before,) = gram_part(block_order, offsets, parts[0], tables, arrived[0], [], scale)
    spectra = [spectrum(block_order, offsets, tables[0], arrived[0], [])]
    send, scaled = gram_part(
        block_order, offsets, parts[1], tables, arrived[1], [before, spectra[0]], scale
    )

    other = swap(send, axes, bits[0], size)
    keep = own_part(scaled, tables[1], before, scale)
    spectra.append(spectrum(block_order, offsets, tables[0], arrived[1], [keep]))
    half = keep.astype(F32) + other.astype(F32)
    for at in range(1, len(bits), 2):
        masks = bits[at : at + 2]
        if len(masks) == 2:
            masks.append(masks[0] ^ masks[1])
        half = half.astype(BF16)
        terms = [half] + [swap(half, axes, mask, size) for mask in masks]
        terms = [t.astype(F32) for t in terms]
        while len(terms) > 1:
            terms = [a + b for a, b in zip(terms[::2], terms[1::2])]
        half = terms[0]
    half, spectra[-1] = lax.optimization_barrier((half, spectra[-1]))
    other = swap(half, axes, bits[0], size)

    spread = jnp.asarray(spread_table())
    modes, gram = mode_fields(half, other, spread, spectra, NFREQ // groups)
    modes = jnp.transpose(modes, (0, 2, 1, 3))[:, :, :, None, :]
    return modes, jnp.transpose(gram, (2, 3, 0, 1))


def solution(mesh):
    placed = (P("tm", None, ("sx", "sy")), P(("sx", "sy")), P(), P(("sx", "sy"), None), P())
    return jax.shard_map(
        body,
        mesh=mesh,
        in_specs=placed,
        out_specs=(P(None, None, None, "tm", ("sx", "sy")), P(None, ("sx", "sy"), None, None)),
        check_vma=False,
    )
```

```python
import functools
import math

import jax
import jax.numpy as jnp
import numpy as np
from jax import lax
from jax.experimental import pallas as pl
from jax.experimental.pallas import tpu as pltpu
from jax.sharding import PartitionSpec as P

NFFT = 256
NFREQ = 128
NBLK = 11
LANE = 128
SUB = 8
TILE = 16
HALF_ROWS = NBLK * SUB
GROUPS = NFREQ // SUB
MATS = 7
PACKED = 128
HALF = PACKED // 2
STACK = 4
CORNER = NBLK - SUB
WIDE = 2 * LANE
FIRST_LIMIT = 64 * 2**20
SECOND_LIMIT = FIRST_LIMIT - 1450 * 2**10
BF16 = jnp.bfloat16
F32 = jnp.float32


def fourier_tables():
    n = np.arange(NFFT)
    k = np.arange(NFREQ)
    angles = 2.0 * np.pi * ((k[:, None] * n[None, :]) % NFFT) / NFFT
    scaled = (0.5 - 0.5 * np.cos(2.0 * np.pi * n / NFFT)) / math.sqrt(0.375 * NFFT)
    table = np.concatenate([np.cos(angles) * scaled, -np.sin(angles) * scaled], axis=0)
    high = table.astype(jnp.bfloat16)
    low = (table - high.astype(np.float64)).astype(jnp.bfloat16)
    both = np.concatenate([high, low], axis=0)
    shifted = np.zeros((TILE, 2 * NFFT, NFFT + TILE), jnp.bfloat16)
    for shift in range(TILE):
        shifted[shift, :, shift : shift + NFFT] = both
    return shifted


def packed_rows():
    rows = {}
    for a in range(NBLK):
        for e in range(a, NBLK):
            rows[0, a, e] = len(rows)
        for e in range(a + 1, NBLK):
            rows[1, a, e] = len(rows)
    return rows


ROWS = packed_rows()


def pick_table():
    pick = np.zeros((NBLK, 2, LANE, PACKED), np.float32)
    for (part, a, e), row in ROWS.items():
        pick[a, part, e * SUB : (e + 1) * SUB, row] = 1.0
    return pick.reshape(NBLK * WIDE, PACKED).astype(jnp.bfloat16)


def spread_table():
    spread = np.zeros((2, STACK, 2, 16, WIDE), np.float32)
    for b in range(NBLK):
        first = slice(b * SUB, b * SUB + SUB)
        second = slice(HALF_ROWS + b * SUB, HALF_ROWS + b * SUB + SUB)
        spread[0, :, 0, b, first] = 1.0
        spread[0, :, 1, b, second] = 1.0
        spread[1, :, 1, b, first] = -1.0
        spread[1, :, 0, b, second] = 1.0
    return spread.reshape(2, LANE, WIDE).astype(jnp.bfloat16)


def dot(a, b):
    return jnp.dot(a, b, preferred_element_type=F32)


def dot_nt(a, b):
    return lax.dot_general(a, b, (((1,), (1,)), ((), ())), preferred_element_type=F32)


def spec(shape):
    return pl.BlockSpec(shape, lambda *_: (0,) * len(shape))


SMEM = pl.BlockSpec(memory_space=pltpu.SMEM)
VMEM = pl.BlockSpec(memory_space=pltpu.VMEM)
HBM = pl.BlockSpec(memory_space=pltpu.HBM)


def lane_pick(owner, lanes):
    me = lax.axis_index("tm")
    rows = WIDE // lanes
    out_row = lax.broadcasted_iota(jnp.int32, (WIDE, WIDE), 0)
    in_row = lax.broadcasted_iota(jnp.int32, (WIDE, WIDE), 1)
    row_of = (out_row % rows) * lanes
    for d in range(lanes):
        slot = me ^ d
        source = jnp.int32(0)
        for lane in range(lanes):
            source = source + jnp.where(owner[0, lane] == slot, lane, 0)
        row_of = jnp.where(out_row // rows == d, row_of + source, row_of)
    return jnp.where(in_row == row_of, 1.0, 0.0).astype(BF16)


def pack_kernel(jobs, parts, first, table_hbm, x_hbm, *refs):
    steps, lanes, _ = x_hbm.shape
    base = jobs[0][0]
    table, x_ref, table_sem, x_sem = refs[-4:]
    outs = list(refs[:-4])
    part = steps // parts
    table_copy = pltpu.make_async_copy(table_hbm, table, table_sem)
    table_copy.start()
    copies = []
    for i in range(parts):
        at = slice(i * part, (i + 1) * part)
        source = x_hbm.at[at, :, base : base + x_ref.shape[2]]
        copies.append(pltpu.make_async_copy(source, x_ref.at[at], x_sem.at[i]))
        copies[-1].start()
    table_copy.wait()
    pick = table
    if first:
        pick = outs.pop()
        pick[...] = lane_pick(table, lanes)
    rows = WIDE // lanes
    for i in range(parts):
        copies[i].wait()
        for start in range(i * part, (i + 1) * part, rows):
            at = slice(start, start + rows)
            x = x_ref[at].reshape(WIDE, x_ref.shape[2])
            out = iter(outs)
            for job, width, begin, end in jobs:
                here = x[:, job - base : job - base + width]
                y = dot(pick[begin * rows : end * rows, :], here).astype(BF16)
                for d in range(end - begin):
                    next(out)[at, :] = y[d * rows : (d + 1) * rows]


def pack(table, snapshots, jobs, first):
    steps, lanes, _ = snapshots.shape
    parts = math.gcd(steps * lanes // WIDE, 3)
    outs = [
        jax.ShapeDtypeStruct((steps, width), BF16)
        for _, width, begin, end in jobs
        for _ in range(begin, end)
    ]
    if first:
        outs.append(jax.ShapeDtypeStruct((WIDE, WIDE), BF16))
    columns = jobs[-1][0] + jobs[-1][1] - jobs[0][0]
    return pl.pallas_call(
        functools.partial(pack_kernel, jobs, parts, first),
        out_shape=outs,
        in_specs=[HBM] * 2,
        out_specs=[VMEM] * len(outs),
        scratch_shapes=[
            pltpu.SMEM(table.shape, jnp.int32) if first else pltpu.VMEM(table.shape, BF16),
            pltpu.VMEM((steps, lanes, columns), BF16),
            pltpu.SemaphoreType.DMA,
            pltpu.SemaphoreType.DMA((parts,)),
        ],
        compiler_params=pltpu.CompilerParams(
            vmem_limit_bytes=FIRST_LIMIT if first else SECOND_LIMIT
        ),
        cost_estimate=pl.CostEstimate(
            flops=2 * WIDE * steps * lanes * columns,
            bytes_accessed=4 * steps * lanes * columns,
            transcendentals=0,
        ),
    )(table, snapshots)


def fill_record(order_ref, pieces, record):
    steps, width = pieces[0].shape
    me = lax.axis_index("tm")
    for d, piece in enumerate(pieces):
        partner = me ^ (len(pieces) - d if d else 0)
        start = pl.multiple_of(order_ref[partner] * steps, steps)
        record[pl.ds(start, steps), :] = piece[...]
    record[len(pieces) * steps :, :] = jnp.zeros((TILE, width), BF16)


def transform(offsets_ref, f_ref, parts, record, s_ref):
    for i in range(NBLK):
        shift = offsets_ref[i] % TILE
        start = pl.multiple_of(offsets_ref[i] - shift, TILE)
        x = record[pl.ds(start, NFFT + TILE), :]
        y = dot(f_ref[shift, : parts * NFFT, :], x)
        if parts == 2:
            y = y[:NFFT] + y[NFFT:]
        s_ref[i] = y[:NFREQ]
        s_ref[NBLK + i] = y[NFREQ:]


def padded(s):
    width = s.shape[2]
    pad = jnp.zeros((LANE - HALF_ROWS, width), F32)
    real = s[:NBLK].reshape(HALF_ROWS, width)
    imag = s[NBLK:].reshape(HALF_ROWS, width)
    return jnp.concatenate([real, pad, imag, pad], axis=0)


def gram_rows(base, groups, w, s_ref, pick_ref, masked):
    row = lax.broadcasted_iota(jnp.int32, (HALF_ROWS, LANE), 0)
    col = lax.broadcasted_iota(jnp.int32, (HALF_ROWS, LANE), 1)
    same = row % SUB == col % SUB
    for pair in range(0, groups, 2):
        blocks = []
        for g in (pair, pair + 1):
            s = s_ref[:, pl.ds(pl.multiple_of(base + g * SUB, SUB), SUB), :]
            weighted = s.reshape(2 * HALF_ROWS, -1) * w
            full = dot_nt(weighted.astype(BF16), padded(s).astype(BF16))
            real = full[:HALF_ROWS, :LANE] + full[HALF_ROWS:, LANE:]
            imag = full[:HALF_ROWS, LANE:] - full[HALF_ROWS:, :LANE]
            blocks.append([jnp.where(same, part, 0.0) for part in (real, imag)])
        at = slice(pair * SUB, (pair + 2) * SUB)
        for a in range(NBLK):
            rows = slice(a * SUB, (a + 1) * SUB)
            for part in range(2):
                both = jnp.concatenate([block[part][rows] for block in blocks], axis=0)
                cols = slice(a * WIDE + part * LANE, a * WIDE + (part + 1) * LANE)
                masked[at, cols] = both.astype(BF16)
    return dot(masked[...], pick_ref[...])


def gram_kernel(lanes, scale, last, order_ref, offsets_ref, w_ref, f_ref, pick_ref, *refs):
    pieces = refs[:lanes]
    if not last:
        gram_ref, record, s_ref, masked = refs[lanes:]
    else:
        before_ref, _, gram_ref, s_ref, record, masked = refs[lanes:]
    fill_record(order_ref, pieces, record)
    transform(offsets_ref, f_ref, 1 if last else 2, record, s_ref)
    w = w_ref[...]
    if not last:
        gram_ref[...] = gram_rows(0, GROUPS, w, s_ref, pick_ref, masked) * scale
        return
    base = pl.multiple_of((1 - lax.axis_index("tm") % 2) * HALF, HALF)
    total = gram_rows(base, GROUPS // 2, w, s_ref, pick_ref, masked) * scale
    gram_ref[...] = (total + before_ref[pl.ds(base, HALF), :]).astype(BF16)


def gram_part(order, offsets, weights, tables, pieces, before, scale):
    lanes = len(pieces)
    steps, width = pieces[0].shape
    last = bool(before)
    args = [order, offsets, weights, *tables, *pieces, *before]
    spectrum_shape = (2 * NBLK, NFREQ, width)
    scratch = [pltpu.VMEM((lanes * steps + TILE, width), BF16)]
    if last:
        outs = [jax.ShapeDtypeStruct((HALF, PACKED), BF16)]
        outs.append(jax.ShapeDtypeStruct(spectrum_shape, F32))
    else:
        outs = [jax.ShapeDtypeStruct((NFREQ, PACKED), F32)]
        scratch.append(pltpu.VMEM(spectrum_shape, F32))
    scratch.append(pltpu.VMEM((HALF if last else NFREQ, NBLK * WIDE), BF16))
    return pl.pallas_call(
        functools.partial(gram_kernel, lanes, scale, last),
        out_shape=outs,
        in_specs=[SMEM, SMEM] + [VMEM] * (len(args) - 2),
        out_specs=[VMEM] * len(outs),
        scratch_shapes=scratch,
        compiler_params=pltpu.CompilerParams(vmem_limit_bytes=32 * 2**20),
        cost_estimate=pl.CostEstimate(
            flops=width * 10**7, bytes_accessed=3 * 10**6, transcendentals=0
        ),
    )(*args)


def own_kernel(scale, w_ref, s_ref, pick_ref, before_ref, gram_ref, masked):
    base = pl.multiple_of(lax.axis_index("tm") % 2 * HALF, HALF)
    w = w_ref[...]
    total = gram_rows(base, GROUPS // 2, w, s_ref, pick_ref, masked) * scale
    gram_ref[...] = (total + before_ref[pl.ds(base, HALF), :]).astype(BF16)


def own_part(weights, rough, pick, before, scale):
    return pl.pallas_call(
        functools.partial(own_kernel, scale),
        out_shape=jax.ShapeDtypeStruct((HALF, PACKED), BF16),
        in_specs=[VMEM] * 4,
        out_specs=VMEM,
        scratch_shapes=[pltpu.VMEM((HALF, NBLK * WIDE), BF16)],
        compiler_params=pltpu.CompilerParams(vmem_limit_bytes=32 * 2**20),
        cost_estimate=pl.CostEstimate(flops=10**9, bytes_accessed=3 * 10**6, transcendentals=0),
    )(weights, rough, pick, before)


def spectrum_kernel(lanes, order_ref, offsets_ref, f_ref, *refs):
    s_ref, record = refs[-2:]
    fill_record(order_ref, refs[:lanes], record)
    transform(offsets_ref, f_ref, 2, record, s_ref)


def spectrum(order, offsets, fourier, pieces, after):
    lanes = len(pieces)
    steps, width = pieces[0].shape
    args = [order, offsets, fourier, *pieces, *after]
    return pl.pallas_call(
        functools.partial(spectrum_kernel, lanes),
        out_shape=jax.ShapeDtypeStruct((2 * NBLK, NFREQ, width), F32),
        in_specs=[SMEM, SMEM] + [VMEM] * (len(args) - 2),
        out_specs=VMEM,
        scratch_shapes=[pltpu.VMEM((lanes * steps + TILE, width), BF16)],
        compiler_params=pltpu.CompilerParams(vmem_limit_bytes=32 * 2**20),
        cost_estimate=pl.CostEstimate(
            flops=width * 10**7, bytes_accessed=3 * 10**6, transcendentals=0
        ),
    )(*args)


class Hermitian:
    def __init__(self, main, corner):
        self.main = main
        self.corner = corner

    def entry(self, a, e):
        if e < SUB:
            return self.main[0, a, pl.ds(e, 1), :], self.main[1, a, pl.ds(e, 1), :], 1
        if a < SUB:
            return self.main[0, e, pl.ds(a, 1), :], self.main[1, e, pl.ds(a, 1), :], -1
        at = pl.ds(e - SUB, 1)
        return self.corner[0, a - SUB, at, :], self.corner[1, a - SUB, at, :], 1

    def put(self, a, e, real, imag):
        if e < SUB:
            self.main[0, a, pl.ds(e, 1), :] = real
            self.main[1, a, pl.ds(e, 1), :] = imag
        elif a >= SUB:
            at = pl.ds(e - SUB, 1)
            self.corner[0, a - SUB, at, :] = real
            self.corner[1, a - SUB, at, :] = imag


def product(x, y, out, diagonal=0.0, terms=()):
    sub = lax.broadcasted_iota(jnp.int32, (SUB, NFREQ), 0)
    yr = [y.main[0, b] for b in range(NBLK)]
    yi = [y.main[1, b] for b in range(NBLK)]
    for a in range(NBLK):
        real = imag = None
        for b in range(NBLK):
            pr, pi, sign = x.entry(a, b)
            tr, ti = pi * yi[b], pi * yr[b]
            if sign > 0:
                tr, ti = pr * yr[b] - tr, pr * yi[b] + ti
            else:
                tr, ti = pr * yr[b] + tr, pr * yi[b] - ti
            real = tr if real is None else real + tr
            imag = ti if imag is None else imag + ti
        for factor, term in terms:
            real = real + factor * term.main[0, a]
            imag = imag + factor * term.main[1, a]
        if diagonal and a < SUB:
            real = real + jnp.where(sub == a, diagonal, 0.0)
        out.main[0, a] = real
        out.main[1, a] = imag
    ar = [[x.main[0, SUB + a], x.corner[0, a]] for a in range(CORNER)]
    ai = [[x.main[1, SUB + a], x.corner[1, a]] for a in range(CORNER)]
    er = [[yr[SUB + e], y.corner[0, e]] for e in range(CORNER)]
    ei = [[yi[SUB + e], y.corner[1, e]] for e in range(CORNER)]
    for a in range(CORNER):
        for e in range(a, CORNER):
            real = sum(ar[a][h] * er[e][h] + ai[a][h] * ei[e][h] for h in range(2))
            real = jnp.sum(real, axis=0, keepdims=True)
            imag = jnp.zeros_like(real)
            if a != e:
                imag = sum(ai[a][h] * er[e][h] - ar[a][h] * ei[e][h] for h in range(2))
                imag = jnp.sum(imag, axis=0, keepdims=True)
            for factor, term in terms:
                r, i, _ = term.entry(SUB + a, SUB + e)
                real, imag = real + factor * r, imag + factor * i
            if a == e:
                out.put(SUB + a, SUB + a, real + diagonal, jnp.zeros_like(real))
            else:
                out.put(SUB + a, SUB + e, real, imag)
                out.put(SUB + e, SUB + a, real, -imag)


def combine(out, diagonal, terms):
    sub = lax.broadcasted_iota(jnp.int32, (SUB, NFREQ), 0)
    for name, rows in (("main", NBLK), ("corner", CORNER)):
        target = getattr(out, name)
        for a in range(rows):
            real = sum(factor * getattr(term, name)[0, a] for factor, term in terms)
            imag = sum(factor * getattr(term, name)[1, a] for factor, term in terms)
            if diagonal and (name == "corner" or a < SUB):
                real = real + jnp.where(sub == a, diagonal, 0.0)
            target[0, a] = real
            target[1, a] = imag


TWO_STEPS = (2.25, -2.4375, 1.6875, -0.5625, 0.0625)


def inverse_root(w, mats):
    q, u, r, t, w2, z = mats
    c0, c1, c2, c3, c4 = TWO_STEPS
    product(w, w, q)
    combine(u, 0.0, [(c3, w), (c4, q)])
    product(q, u, z, c0, [(c1, w), (c2, q)])
    product(z, z, t)
    product(w, t, w2)
    product(w2, w2, q)
    combine(u, 0.0, [(c3, w2), (c4, q)])
    product(q, u, r, c0, [(c1, w2), (c2, q)])
    product(r, r, t)
    product(z, r, u)
    product(w2, t, q)
    combine(q, 1.5, [(-0.5, q)])
    product(u, q, z)
    return z


def make_roots(share, half_ref, other_ref, gram_ref, packed, rolled, mats):
    core = lax.axis_index("tm") % 2
    packed[pl.ds(pl.multiple_of(core * HALF, HALF), HALF), :] = half_ref[...]
    packed[pl.ds(pl.multiple_of((1 - core) * HALF, HALF), HALF), :] = other_ref[...]
    packed[...] = packed[...].T
    at = lax.axis_index("sx") * lax.axis_size("sy") + lax.axis_index("sy")
    rolled[...] = pltpu.roll(packed[...], (NFREQ - at * share) % NFREQ, 1)
    y, *free = [Hermitian(mats[2 * i], mats[2 * i + 1]) for i in range(MATS)]
    for ref in mats[1::2]:
        ref[...] = jnp.zeros_like(ref)

    def row(ref, part, a, e):
        return ref[pl.ds(ROWS[part, a, e], 1), :]

    trace = 2.0 * sum(row(packed, 0, a, a) for a in range(NBLK))
    norm = 1.0 / jnp.sqrt(trace)
    packed[...] = packed[...] / trace
    zero = jnp.zeros((1, NFREQ), F32)
    for a in range(NBLK):
        y.put(a, a, row(packed, 0, a, a), zero)
        gram_ref[a, a, 0:1, :] = row(rolled, 0, a, a)[:, :share]
        gram_ref[a, a, 1:2, :] = zero[:, :share]
        for e in range(a + 1, NBLK):
            real, imag = row(packed, 0, a, e), row(packed, 1, a, e)
            y.put(a, e, real, imag)
            y.put(e, a, real, -imag)
            real, imag = row(rolled, 0, a, e)[:, :share], row(rolled, 1, a, e)[:, :share]
            gram_ref[a, e, 0:1, :] = real
            gram_ref[e, a, 0:1, :] = real
            gram_ref[a, e, 1:2, :] = imag
            gram_ref[e, a, 1:2, :] = -imag
    z = inverse_root(y, free)
    mean = sum(z.entry(a, a)[0] for a in range(NBLK)) * (1.0 / NBLK)
    sub = lax.broadcasted_iota(jnp.int32, (SUB, NFREQ), 0)
    none = jnp.zeros((SUB - CORNER, NFREQ), F32)
    first = jnp.concatenate([mean * norm, none[1:]], axis=0)
    stacks = []
    for m0 in range(0, NBLK, STACK):
        modes = range(m0, min(m0 + STACK, NBLK))
        stack = []
        for m in modes:
            for c in range(2):
                column = z.main[c, m]
                if c == 0 and m < SUB:
                    column = column - jnp.where(sub == m, mean, 0.0)
                stack.append(column * norm)
                for b in range(SUB, NBLK):
                    real, imag, sign = z.entry(m, b)
                    line = imag * sign if c else real
                    if c == 0 and m == b:
                        line = line - mean
                    stack.append(line * norm)
                stack.append(first if c == 0 and m == 0 else none)
        stack += [jnp.zeros((32, NFREQ), F32)] * (STACK - len(modes))
        stacks.append(jnp.concatenate(stack, axis=0).T)
    return stacks


def mode_kernel(chunks, share, half_ref, other_ref, spread_ref, *refs):
    s_refs = refs[:chunks]
    out_hbm, gram_ref, out, v, mean, packed, rolled, sem, *mats = refs[chunks:]
    stacks = make_roots(share, half_ref, other_ref, gram_ref, packed, rolled, mats)
    mean[...] = jnp.broadcast_to(stacks[0][:, NBLK : NBLK + 1], (NFREQ, LANE))
    row = lax.broadcasted_iota(jnp.int32, (NFREQ, 2 * HALF_ROWS), 0)
    col = lax.broadcasted_iota(jnp.int32, (NFREQ, 2 * HALF_ROWS), 1)
    same = row % SUB == col % SUB
    place = lax.broadcasted_iota(jnp.int32, (NFREQ, LANE), 1) // 32
    rows = [jnp.where(place == m % STACK, stacks[m // STACK], 0.0) for m in range(NBLK)]
    rows = jnp.concatenate(rows, axis=0).astype(BF16)
    for c in range(2):
        wide = dot(rows, spread_ref[c])[:, : 2 * HALF_ROWS]
        for m in range(NBLK):
            v[c * NBLK + m] = jnp.where(same, wide[m * NFREQ : (m + 1) * NFREQ], 0.0)

    copies = []
    for pair in range(GROUPS // 2):
        fields = []
        for g in (2 * pair, 2 * pair + 1):
            at = slice(g * SUB, (g + 1) * SUB)
            s = jnp.concatenate([r[:, at, :] for r in s_refs], axis=2)
            flat = s.reshape(2 * HALF_ROWS, -1).astype(BF16)
            field = dot(v[:, at, :].reshape(2 * HALF_ROWS, 2 * HALF_ROWS).astype(BF16), flat)
            scale = jnp.concatenate([mean[at, :]] * (s.shape[2] // LANE), axis=1)
            fields.append(field.reshape(s.shape) + s * scale[None])
        both = jnp.concatenate(fields, axis=1).astype(BF16)
        at = slice(pair * 2 * SUB, (pair + 1) * 2 * SUB)
        out[:, :, at, :] = both.reshape(2, NBLK, 2 * SUB, -1)
        copies.append(
            pltpu.make_async_copy(out.at[:, :, at, :], out_hbm.at[:, :, at, :], sem.at[pair])
        )
        copies[-1].start()
    for copy in copies:
        copy.wait()


def mode_fields(half, other, spread, spectra, share):
    shape = (2, NBLK, NFREQ, sum(s.shape[2] for s in spectra))
    return pl.pallas_call(
        functools.partial(mode_kernel, len(spectra), share),
        out_shape=[
            jax.ShapeDtypeStruct(shape, BF16),
            jax.ShapeDtypeStruct((NBLK, NBLK, 2, share), F32),
        ],
        in_specs=[VMEM] * (3 + len(spectra)),
        out_specs=[HBM, VMEM],
        scratch_shapes=[
            pltpu.VMEM(shape, BF16),
            pltpu.VMEM((2 * NBLK, NFREQ, 2 * HALF_ROWS), F32),
            pltpu.VMEM((NFREQ, LANE), F32),
            pltpu.VMEM((PACKED, NFREQ), F32),
            pltpu.VMEM((PACKED, NFREQ), F32),
            pltpu.SemaphoreType.DMA((GROUPS // 2,)),
        ]
        + [
            pltpu.VMEM((2, NBLK, SUB, NFREQ), F32),
            pltpu.VMEM((2, CORNER, SUB, NFREQ), F32),
        ]
        * MATS,
        compiler_params=pltpu.CompilerParams(vmem_limit_bytes=32 * 2**20),
    )(half, other, spread, *spectra)


def swap(x, axes, mask, size):
    return lax.ppermute(x, axes, [(i, i ^ mask) for i in range(size)])


def powers(size):
    return [1 << i for i in range(size.bit_length() - 1)]


def body(snapshots, weights, block_order, owner, offsets):
    lanes = lax.axis_size("tm")
    groups = lax.axis_size("sx") * lax.axis_size("sy")
    points = snapshots.shape[2]
    chunks = [(0, points // 2), (points // 2, points // 2)]
    scale = 1.0 / (lanes * groups * points)
    tables = (jnp.asarray(fourier_tables()), jnp.asarray(pick_table()))
    weights = weights.reshape(1, -1)

    near = min(2, lanes)
    (base, width), (next_base, next_width) = chunks
    *far, table = pack(owner, snapshots, [(base, width, near, lanes)], True)
    jobs = [(base, width, 0, near), (next_base, next_width, 0, lanes)]
    rest = list(pack(table, snapshots, jobs, False))
    arrived = []
    for packed in (rest[:near] + far, rest[near:]):
        moved = [swap(packed[d], "tm", d, lanes) for d in reversed(range(1, lanes))]
        arrived.append([packed[0]] + moved)

    axes = ("tm", "sx", "sy")
    size = lanes * groups
    bits = [b * groups for b in powers(lanes)] + powers(groups)
    parts = [weights[:, base : base + width] for base, width in chunks]
    (before,) = gram_part(block_order, offsets, parts[0], tables, arrived[0], [], scale)
    spectra = [spectrum(block_order, offsets, tables[0], arrived[0], [])]
    send, rough = gram_part(
        block_order, offsets, parts[1], tables, arrived[1], [before, spectra[0]], scale
    )

    other = swap(send, axes, bits[0], size)
    keep = own_part(parts[1], rough, tables[1], before, scale)
    spectra.append(spectrum(block_order, offsets, tables[0], arrived[1], [keep]))
    half = keep.astype(F32) + other.astype(F32)
    for at in range(1, len(bits), 2):
        masks = bits[at : at + 2]
        if len(masks) == 2:
            masks.append(masks[0] ^ masks[1])
        half = half.astype(BF16)
        terms = [half] + [swap(half, axes, mask, size) for mask in masks]
        terms = [t.astype(F32) for t in terms]
        while len(terms) > 1:
            terms = [a + b for a, b in zip(terms[::2], terms[1::2])]
        half = terms[0]
    half, spectra[-1] = lax.optimization_barrier((half, spectra[-1]))
    other = swap(half, axes, bits[0], size)

    spread = jnp.asarray(spread_table())
    modes, gram = mode_fields(half, other, spread, spectra, NFREQ // groups)
    modes = jnp.transpose(modes, (0, 2, 1, 3))[:, :, :, None, :]
    return modes, jnp.transpose(gram, (2, 3, 0, 1))


def solution(mesh):
    placed = (P("tm", None, ("sx", "sy")), P(("sx", "sy")), P(), P(("sx", "sy"), None), P())
    return jax.shard_map(
        body,
        mesh=mesh,
        in_specs=placed,
        out_specs=(P(None, None, None, "tm", ("sx", "sy")), P(None, ("sx", "sy"), None, None)),
        check_vma=False,
    )
```

```python
import functools
import math

import jax
import jax.numpy as jnp
import numpy as np
from jax import lax
from jax.experimental import pallas as pl
from jax.experimental.pallas import tpu as pltpu
from jax.sharding import PartitionSpec as P

NFFT = 256
NFREQ = 128
NBLK = 11
LANE = 128
SUB = 8
HALF_ROWS = NBLK * SUB
GROUPS = NFREQ // SUB
MATS = 7
PACKED = 128
HALF = PACKED // 2
STACK = 4
CORNER = NBLK - SUB
WIDE = 2 * LANE
FIRST_LIMIT = 64 * 2**20
SECOND_LIMIT = FIRST_LIMIT - 1450 * 2**10
BF16 = jnp.bfloat16
F32 = jnp.float32


def fourier_tables():
    n = np.arange(NFFT)
    k = np.arange(NFREQ)
    angles = 2.0 * np.pi * ((k[:, None] * n[None, :]) % NFFT) / NFFT
    scaled = (0.5 - 0.5 * np.cos(2.0 * np.pi * n / NFFT)) / math.sqrt(0.375 * NFFT)
    table = np.concatenate([np.cos(angles) * scaled, -np.sin(angles) * scaled], axis=0)
    high = table.astype(jnp.bfloat16)
    low = (table - high.astype(np.float64)).astype(jnp.bfloat16)
    return np.concatenate([high, low], axis=0)


def packed_rows():
    rows = {}
    for a in range(NBLK):
        for e in range(a, NBLK):
            rows[0, a, e] = len(rows)
        for e in range(a + 1, NBLK):
            rows[1, a, e] = len(rows)
    return rows


ROWS = packed_rows()


def pick_table():
    pick = np.zeros((NBLK, 2, LANE, PACKED), np.float32)
    for (part, a, e), row in ROWS.items():
        pick[a, part, e * SUB : (e + 1) * SUB, row] = 1.0
    return pick.reshape(NBLK * WIDE, PACKED).astype(jnp.bfloat16)


def spread_table():
    spread = np.zeros((2, STACK, 2, 16, WIDE), np.float32)
    for b in range(NBLK):
        first = slice(b * SUB, b * SUB + SUB)
        second = slice(HALF_ROWS + b * SUB, HALF_ROWS + b * SUB + SUB)
        spread[0, :, 0, b, first] = 1.0
        spread[0, :, 1, b, second] = 1.0
        spread[1, :, 1, b, first] = -1.0
        spread[1, :, 0, b, second] = 1.0
    return spread.reshape(2, LANE, WIDE).astype(jnp.bfloat16)


def dot(a, b):
    return jnp.dot(a, b, preferred_element_type=F32)


def dot_nt(a, b):
    return lax.dot_general(a, b, (((1,), (1,)), ((), ())), preferred_element_type=F32)


def spec(shape):
    return pl.BlockSpec(shape, lambda *_: (0,) * len(shape))


SMEM = pl.BlockSpec(memory_space=pltpu.SMEM)
VMEM = pl.BlockSpec(memory_space=pltpu.VMEM)
HBM = pl.BlockSpec(memory_space=pltpu.HBM)


def lane_pick(owner, lanes):
    me = lax.axis_index("tm")
    rows = WIDE // lanes
    out_row = lax.broadcasted_iota(jnp.int32, (WIDE, WIDE), 0)
    in_row = lax.broadcasted_iota(jnp.int32, (WIDE, WIDE), 1)
    row_of = (out_row % rows) * lanes
    for d in range(lanes):
        slot = me ^ d
        source = jnp.int32(0)
        for lane in range(lanes):
            source = source + jnp.where(owner[0, lane] == slot, lane, 0)
        row_of = jnp.where(out_row // rows == d, row_of + source, row_of)
    return jnp.where(in_row == row_of, 1.0, 0.0).astype(BF16)


def pack_kernel(jobs, parts, first, follows, table_hbm, x_hbm, *refs):
    steps, lanes, _ = x_hbm.shape
    base = jobs[0][0]
    table, x_ref, table_sem, x_sem = refs[-4:]
    outs = list(refs[follows:-4])
    part = steps // parts
    table_copy = pltpu.make_async_copy(table_hbm, table, table_sem)
    table_copy.start()
    copies = []
    for i in range(parts):
        at = slice(i * part, (i + 1) * part)
        source = x_hbm.at[at, :, base : base + x_ref.shape[2]]
        copies.append(pltpu.make_async_copy(source, x_ref.at[at], x_sem.at[i]))
        copies[-1].start()
    table_copy.wait()
    pick = table
    if first:
        pick = outs.pop()
        pick[...] = lane_pick(table, lanes)
    rows = WIDE // lanes
    for i in range(parts):
        copies[i].wait()
        for start in range(i * part, (i + 1) * part, rows):
            at = slice(start, start + rows)
            x = x_ref[at].reshape(WIDE, x_ref.shape[2])
            out = iter(outs)
            for job, width, begin, end in jobs:
                here = x[:, job - base : job - base + width]
                y = dot(pick[begin * rows : end * rows, :], here).astype(BF16)
                for d in range(end - begin):
                    next(out)[at, :] = y[d * rows : (d + 1) * rows]


def pack(table, snapshots, jobs, first, after=()):
    steps, lanes, _ = snapshots.shape
    parts = math.gcd(steps * lanes // WIDE, 3)
    outs = [
        jax.ShapeDtypeStruct((steps, width), BF16)
        for _, width, begin, end in jobs
        for _ in range(begin, end)
    ]
    if first:
        outs.append(jax.ShapeDtypeStruct((WIDE, WIDE), BF16))
    columns = jobs[-1][0] + jobs[-1][1] - jobs[0][0]
    return pl.pallas_call(
        functools.partial(pack_kernel, jobs, parts, first, len(after)),
        out_shape=outs,
        in_specs=[HBM] * (2 + len(after)),
        out_specs=[VMEM] * len(outs),
        scratch_shapes=[
            pltpu.SMEM(table.shape, jnp.int32) if first else pltpu.VMEM(table.shape, BF16),
            pltpu.VMEM((steps, lanes, columns), BF16),
            pltpu.SemaphoreType.DMA,
            pltpu.SemaphoreType.DMA((parts,)),
        ],
        compiler_params=pltpu.CompilerParams(
            vmem_limit_bytes=FIRST_LIMIT if first else 40 * 2**20 if after else SECOND_LIMIT
        ),
        cost_estimate=pl.CostEstimate(flops=1000, bytes_accessed=1000, transcendentals=0),
    )(table, snapshots, *after)


def fill_record(order_ref, pieces, record, factor):
    steps, width = pieces[0].shape
    me = lax.axis_index("tm")
    for d, piece in enumerate(pieces):
        partner = me ^ (len(pieces) - d if d else 0)
        start = pl.multiple_of(order_ref[partner] * steps, steps)
        for c in range(width // LANE):
            cols = slice(c * LANE, (c + 1) * LANE)
            part = piece[:, cols].astype(F32)
            record[c, pl.ds(start, steps), :] = part if factor is None else part * factor[:, cols]


def transform(offsets_ref, f, record, s_ref):
    wanted = [(i, c) for i in range(NBLK) for c in range(record.shape[0])]
    for first in range(0, len(wanted), 2):
        pair = wanted[first : first + 2]
        x = [record[c, pl.ds(offsets_ref[i], NFFT), :].astype(BF16) for i, c in pair]
        x = jnp.concatenate(x, axis=1) if len(x) > 1 else x[0]
        y = dot(f, x)
        if f.shape[0] > NFFT:
            y = y[:NFFT] + y[NFFT:]
        for at, (i, c) in enumerate(pair):
            cols = slice(c * LANE, (c + 1) * LANE)
            s_ref[i, :, cols] = y[:NFREQ, at * LANE : (at + 1) * LANE]
            s_ref[NBLK + i, :, cols] = y[NFREQ:, at * LANE : (at + 1) * LANE]


def padded(s):
    width = s.shape[2]
    pad = jnp.zeros((LANE - HALF_ROWS, width), F32)
    real = s[:NBLK].reshape(HALF_ROWS, width)
    imag = s[NBLK:].reshape(HALF_ROWS, width)
    return jnp.concatenate([real, pad, imag, pad], axis=0)


def gram_rows(base, groups, s_ref, pick_ref, masked):
    row = lax.broadcasted_iota(jnp.int32, (HALF_ROWS, LANE), 0)
    col = lax.broadcasted_iota(jnp.int32, (HALF_ROWS, LANE), 1)
    same = row % SUB == col % SUB
    for pair in range(0, groups, 2):
        blocks = []
        for g in (pair, pair + 1):
            s = s_ref[:, pl.ds(pl.multiple_of(base + g * SUB, SUB), SUB), :]
            full = dot_nt(s.reshape(2 * HALF_ROWS, -1).astype(BF16), padded(s).astype(BF16))
            real = full[:HALF_ROWS, :LANE] + full[HALF_ROWS:, LANE:]
            imag = full[:HALF_ROWS, LANE:] - full[HALF_ROWS:, :LANE]
            blocks.append([jnp.where(same, part, 0.0) for part in (real, imag)])
        at = slice(pair * SUB, (pair + 2) * SUB)
        for a in range(NBLK):
            rows = slice(a * SUB, (a + 1) * SUB)
            for part in range(2):
                both = jnp.concatenate([block[part][rows] for block in blocks], axis=0)
                cols = slice(a * WIDE + part * LANE, a * WIDE + (part + 1) * LANE)
                masked[at, cols] = both.astype(BF16)
    return dot(masked[...], pick_ref[...])


def gram_kernel(lanes, scale, last, order_ref, offsets_ref, w_ref, f_ref, pick_ref, *refs):
    pieces = refs[:lanes]
    refs = refs[lanes:]
    if last:
        before_ref, _, gram_ref, s_ref, record, masked = refs
    else:
        *before_refs, gram_ref, record, s_ref, masked = refs
    fill_record(order_ref, pieces, record, jnp.sqrt(w_ref[...]))
    transform(offsets_ref, f_ref[:NFFT] if last else f_ref[...], record, s_ref)
    if not last:
        total = gram_rows(0, GROUPS, s_ref, pick_ref, masked) * scale
        gram_ref[...] = total + before_refs[0][...] if before_refs else total
        return
    base = pl.multiple_of((1 - lax.axis_index("tm") % 2) * HALF, HALF)
    total = gram_rows(base, GROUPS // 2, s_ref, pick_ref, masked) * scale
    gram_ref[...] = (total + before_ref[pl.ds(base, HALF), :]).astype(BF16)


def gram_part(order, offsets, weights, tables, pieces, before, last, scale):
    lanes = len(pieces)
    steps, width = pieces[0].shape
    args = [order, offsets, weights, *tables, *pieces, *before]
    spectrum_shape = (2 * NBLK, NFREQ, width)
    scratch = [pltpu.VMEM((width // LANE, lanes * steps, LANE), F32)]
    if last:
        outs = [jax.ShapeDtypeStruct((HALF, PACKED), BF16)]
        outs.append(jax.ShapeDtypeStruct(spectrum_shape, F32))
    else:
        outs = [jax.ShapeDtypeStruct((NFREQ, PACKED), F32)]
        scratch.append(pltpu.VMEM(spectrum_shape, F32))
    scratch.append(pltpu.VMEM((HALF if last else NFREQ, NBLK * WIDE), BF16))
    return pl.pallas_call(
        functools.partial(gram_kernel, lanes, scale, last),
        out_shape=outs,
        in_specs=[SMEM, SMEM] + [VMEM] * (len(args) - 2),
        out_specs=[VMEM] * len(outs),
        scratch_shapes=scratch,
        compiler_params=pltpu.CompilerParams(vmem_limit_bytes=32 * 2**20),
        cost_estimate=pl.CostEstimate(flops=1000, bytes_accessed=1000, transcendentals=0),
    )(*args)


def own_kernel(scale, s_ref, pick_ref, before_ref, gram_ref, masked):
    base = pl.multiple_of(lax.axis_index("tm") % 2 * HALF, HALF)
    total = gram_rows(base, GROUPS // 2, s_ref, pick_ref, masked) * scale
    gram_ref[...] = (total + before_ref[pl.ds(base, HALF), :]).astype(BF16)


def own_part(scaled, pick, before, scale):
    return pl.pallas_call(
        functools.partial(own_kernel, scale),
        out_shape=jax.ShapeDtypeStruct((HALF, PACKED), BF16),
        in_specs=[VMEM] * 3,
        out_specs=VMEM,
        scratch_shapes=[pltpu.VMEM((HALF, NBLK * WIDE), BF16)],
        compiler_params=pltpu.CompilerParams(vmem_limit_bytes=32 * 2**20),
        cost_estimate=pl.CostEstimate(flops=10**9, bytes_accessed=3 * 10**6, transcendentals=0),
    )(scaled, pick, before)


def spectrum_kernel(lanes, order_ref, offsets_ref, f_ref, *refs):
    s_ref, record = refs[-2:]
    fill_record(order_ref, refs[:lanes], record, None)
    transform(offsets_ref, f_ref[...], record, s_ref)


def spectrum(order, offsets, fourier, pieces, after):
    lanes = len(pieces)
    steps, width = pieces[0].shape
    args = [order, offsets, fourier, *pieces, *after]
    return pl.pallas_call(
        functools.partial(spectrum_kernel, lanes),
        out_shape=jax.ShapeDtypeStruct((2 * NBLK, NFREQ, width), F32),
        in_specs=[SMEM, SMEM] + [VMEM] * (len(args) - 2),
        out_specs=VMEM,
        scratch_shapes=[pltpu.VMEM((width // LANE, lanes * steps, LANE), F32)],
        compiler_params=pltpu.CompilerParams(vmem_limit_bytes=32 * 2**20),
        cost_estimate=pl.CostEstimate(flops=1000, bytes_accessed=1000, transcendentals=0),
    )(*args)


class Hermitian:
    def __init__(self, main, corner):
        self.main = main
        self.corner = corner

    def entry(self, a, e):
        if e < SUB:
            return self.main[0, a, pl.ds(e, 1), :], self.main[1, a, pl.ds(e, 1), :], 1
        if a < SUB:
            return self.main[0, e, pl.ds(a, 1), :], self.main[1, e, pl.ds(a, 1), :], -1
        at = pl.ds(e - SUB, 1)
        return self.corner[0, a - SUB, at, :], self.corner[1, a - SUB, at, :], 1

    def put(self, a, e, real, imag):
        if e < SUB:
            self.main[0, a, pl.ds(e, 1), :] = real
            self.main[1, a, pl.ds(e, 1), :] = imag
        elif a >= SUB:
            at = pl.ds(e - SUB, 1)
            self.corner[0, a - SUB, at, :] = real
            self.corner[1, a - SUB, at, :] = imag


def product(x, y, out, diagonal=0.0, terms=()):
    sub = lax.broadcasted_iota(jnp.int32, (SUB, NFREQ), 0)
    yr = [y.main[0, b] for b in range(NBLK)]
    yi = [y.main[1, b] for b in range(NBLK)]
    for a in range(NBLK):
        real = imag = None
        for b in range(NBLK):
            pr, pi, sign = x.entry(a, b)
            tr, ti = pi * yi[b], pi * yr[b]
            if sign > 0:
                tr, ti = pr * yr[b] - tr, pr * yi[b] + ti
            else:
                tr, ti = pr * yr[b] + tr, pr * yi[b] - ti
            real = tr if real is None else real + tr
            imag = ti if imag is None else imag + ti
        for factor, term in terms:
            real = real + factor * term.main[0, a]
            imag = imag + factor * term.main[1, a]
        if diagonal and a < SUB:
            real = real + jnp.where(sub == a, diagonal, 0.0)
        out.main[0, a] = real
        out.main[1, a] = imag
    ar = [[x.main[0, SUB + a], x.corner[0, a]] for a in range(CORNER)]
    ai = [[x.main[1, SUB + a], x.corner[1, a]] for a in range(CORNER)]
    er = [[yr[SUB + e], y.corner[0, e]] for e in range(CORNER)]
    ei = [[yi[SUB + e], y.corner[1, e]] for e in range(CORNER)]
    for a in range(CORNER):
        for e in range(a, CORNER):
            real = sum(ar[a][h] * er[e][h] + ai[a][h] * ei[e][h] for h in range(2))
            real = jnp.sum(real, axis=0, keepdims=True)
            imag = jnp.zeros_like(real)
            if a != e:
                imag = sum(ai[a][h] * er[e][h] - ar[a][h] * ei[e][h] for h in range(2))
                imag = jnp.sum(imag, axis=0, keepdims=True)
            for factor, term in terms:
                r, i, _ = term.entry(SUB + a, SUB + e)
                real, imag = real + factor * r, imag + factor * i
            if a == e:
                out.put(SUB + a, SUB + a, real + diagonal, jnp.zeros_like(real))
            else:
                out.put(SUB + a, SUB + e, real, imag)
                out.put(SUB + e, SUB + a, real, -imag)


def combine(out, diagonal, terms):
    sub = lax.broadcasted_iota(jnp.int32, (SUB, NFREQ), 0)
    for name, rows in (("main", NBLK), ("corner", CORNER)):
        target = getattr(out, name)
        for a in range(rows):
            real = sum(factor * getattr(term, name)[0, a] for factor, term in terms)
            imag = sum(factor * getattr(term, name)[1, a] for factor, term in terms)
            if diagonal and (name == "corner" or a < SUB):
                real = real + jnp.where(sub == a, diagonal, 0.0)
            target[0, a] = real
            target[1, a] = imag


TWO_STEPS = (2.25, -2.4375, 1.6875, -0.5625, 0.0625)


def inverse_root(w, mats):
    q, u, r, t, w2, z = mats
    c0, c1, c2, c3, c4 = TWO_STEPS
    product(w, w, q)
    combine(u, 0.0, [(c3, w), (c4, q)])
    product(q, u, z, c0, [(c1, w), (c2, q)])
    product(z, z, t)
    product(w, t, w2)
    product(w2, w2, q)
    combine(u, 0.0, [(c3, w2), (c4, q)])
    product(q, u, r, c0, [(c1, w2), (c2, q)])
    product(r, r, t)
    product(z, r, u)
    product(w2, t, q)
    combine(q, 1.5, [(-0.5, q)])
    product(u, q, z)
    return z


def make_roots(share, half_ref, other_ref, gram_ref, packed, rolled, mats):
    core = lax.axis_index("tm") % 2
    packed[pl.ds(pl.multiple_of(core * HALF, HALF), HALF), :] = half_ref[...]
    packed[pl.ds(pl.multiple_of((1 - core) * HALF, HALF), HALF), :] = other_ref[...]
    packed[...] = packed[...].T
    at = lax.axis_index("sx") * lax.axis_size("sy") + lax.axis_index("sy")
    rolled[...] = pltpu.roll(packed[...], (NFREQ - at * share) % NFREQ, 1)
    y, *free = [Hermitian(mats[2 * i], mats[2 * i + 1]) for i in range(MATS)]
    for ref in mats[1::2]:
        ref[...] = jnp.zeros_like(ref)

    def row(ref, part, a, e):
        return ref[pl.ds(ROWS[part, a, e], 1), :]

    trace = 2.0 * sum(row(packed, 0, a, a) for a in range(NBLK))
    norm = 1.0 / jnp.sqrt(trace)
    packed[...] = packed[...] / trace
    zero = jnp.zeros((1, NFREQ), F32)
    for a in range(NBLK):
        y.put(a, a, row(packed, 0, a, a), zero)
        gram_ref[a, a, 0:1, :] = row(rolled, 0, a, a)[:, :share]
        gram_ref[a, a, 1:2, :] = zero[:, :share]
        for e in range(a + 1, NBLK):
            real, imag = row(packed, 0, a, e), row(packed, 1, a, e)
            y.put(a, e, real, imag)
            y.put(e, a, real, -imag)
            real, imag = row(rolled, 0, a, e)[:, :share], row(rolled, 1, a, e)[:, :share]
            gram_ref[a, e, 0:1, :] = real
            gram_ref[e, a, 0:1, :] = real
            gram_ref[a, e, 1:2, :] = imag
            gram_ref[e, a, 1:2, :] = -imag
    z = inverse_root(y, free)
    mean = sum(z.entry(a, a)[0] for a in range(NBLK)) * (1.0 / NBLK)
    sub = lax.broadcasted_iota(jnp.int32, (SUB, NFREQ), 0)
    none = jnp.zeros((SUB - CORNER, NFREQ), F32)
    first = jnp.concatenate([mean * norm, none[1:]], axis=0)
    stacks = []
    for m0 in range(0, NBLK, STACK):
        modes = range(m0, min(m0 + STACK, NBLK))
        stack = []
        for m in modes:
            for c in range(2):
                column = z.main[c, m]
                if c == 0 and m < SUB:
                    column = column - jnp.where(sub == m, mean, 0.0)
                stack.append(column * norm)
                for b in range(SUB, NBLK):
                    real, imag, sign = z.entry(m, b)
                    line = imag * sign if c else real
                    if c == 0 and m == b:
                        line = line - mean
                    stack.append(line * norm)
                stack.append(first if c == 0 and m == 0 else none)
        stack += [jnp.zeros((32, NFREQ), F32)] * (STACK - len(modes))
        stacks.append(jnp.concatenate(stack, axis=0).T)
    return stacks


def mode_kernel(chunks, share, half_ref, other_ref, spread_ref, *refs):
    s_refs = refs[:chunks]
    out_hbm, gram_ref, out, v, mean, packed, rolled, sem, *mats = refs[chunks:]
    stacks = make_roots(share, half_ref, other_ref, gram_ref, packed, rolled, mats)
    mean[...] = jnp.broadcast_to(stacks[0][:, NBLK : NBLK + 1], (NFREQ, LANE))
    row = lax.broadcasted_iota(jnp.int32, (NFREQ, 2 * HALF_ROWS), 0)
    col = lax.broadcasted_iota(jnp.int32, (NFREQ, 2 * HALF_ROWS), 1)
    same = row % SUB == col % SUB
    place = lax.broadcasted_iota(jnp.int32, (NFREQ, LANE), 1) // 32
    rows = [jnp.where(place == m % STACK, stacks[m // STACK], 0.0) for m in range(NBLK)]
    rows = jnp.concatenate(rows, axis=0).astype(BF16)
    for c in range(2):
        wide = dot(rows, spread_ref[c])[:, : 2 * HALF_ROWS]
        for m in range(NBLK):
            v[c * NBLK + m] = jnp.where(same, wide[m * NFREQ : (m + 1) * NFREQ], 0.0)

    copies = []
    for pair in range(GROUPS // 2):
        fields = []
        for g in (2 * pair, 2 * pair + 1):
            at = slice(g * SUB, (g + 1) * SUB)
            s = jnp.concatenate([r[:, at, :] for r in s_refs], axis=2)
            flat = s.reshape(2 * HALF_ROWS, -1).astype(BF16)
            field = dot(v[:, at, :].reshape(2 * HALF_ROWS, 2 * HALF_ROWS).astype(BF16), flat)
            scale = jnp.concatenate([mean[at, :]] * (s.shape[2] // LANE), axis=1)
            fields.append(field.reshape(s.shape) + s * scale[None])
        both = jnp.concatenate(fields, axis=1).astype(BF16)
        at = slice(pair * 2 * SUB, (pair + 1) * 2 * SUB)
        out[:, :, at, :] = both.reshape(2, NBLK, 2 * SUB, -1)
        copies.append(
            pltpu.make_async_copy(out.at[:, :, at, :], out_hbm.at[:, :, at, :], sem.at[pair])
        )
        copies[-1].start()
    for copy in copies:
        copy.wait()


def mode_fields(half, other, spread, spectra, share):
    shape = (2, NBLK, NFREQ, sum(s.shape[2] for s in spectra))
    return pl.pallas_call(
        functools.partial(mode_kernel, len(spectra), share),
        out_shape=[
            jax.ShapeDtypeStruct(shape, BF16),
            jax.ShapeDtypeStruct((NBLK, NBLK, 2, share), F32),
        ],
        in_specs=[VMEM] * (3 + len(spectra)),
        out_specs=[HBM, VMEM],
        scratch_shapes=[
            pltpu.VMEM(shape, BF16),
            pltpu.VMEM((2 * NBLK, NFREQ, 2 * HALF_ROWS), F32),
            pltpu.VMEM((NFREQ, LANE), F32),
            pltpu.VMEM((PACKED, NFREQ), F32),
            pltpu.VMEM((PACKED, NFREQ), F32),
            pltpu.SemaphoreType.DMA((GROUPS // 2,)),
        ]
        + [
            pltpu.VMEM((2, NBLK, SUB, NFREQ), F32),
            pltpu.VMEM((2, CORNER, SUB, NFREQ), F32),
        ]
        * MATS,
        compiler_params=pltpu.CompilerParams(vmem_limit_bytes=32 * 2**20),
    )(half, other, spread, *spectra)


def swap(x, axes, mask, size):
    return lax.ppermute(x, axes, [(i, i ^ mask) for i in range(size)])


def powers(size):
    return [1 << i for i in range(size.bit_length() - 1)]


def body(snapshots, weights, block_order, owner, offsets):
    lanes = lax.axis_size("tm")
    groups = lax.axis_size("sx") * lax.axis_size("sy")
    points = snapshots.shape[2]
    half, quarter = points // 2, points // 4
    chunks = [(0, half), (half, quarter), (half + quarter, quarter)]
    scale = 1.0 / (lanes * groups * points)
    tables = (jnp.asarray(fourier_tables()), jnp.asarray(pick_table()))
    weights = weights.reshape(1, -1)

    first, table = pack(owner, snapshots, [(*chunks[0], lanes - 1, lanes)], True)
    moved = [swap(first, "tm", lanes - 1, lanes)]
    jobs = [(*chunks[0], 0, lanes - 1), (*chunks[1], 0, lanes)]
    rest = list(pack(table, snapshots, jobs, False))
    moved += [swap(rest[d], "tm", d, lanes) for d in reversed(range(1, lanes - 1))]
    arrived = [[rest[0]] + moved]
    for packed in (rest[lanes - 1 :], None):
        if packed is None:
            packed = pack(table, snapshots, [(*chunks[2], 0, lanes)], False, moved[:1])
        arrived.append([packed[0]])
        arrived[-1] += [swap(packed[d], "tm", d, lanes) for d in reversed(range(1, lanes))]

    axes = ("tm", "sx", "sy")
    size = lanes * groups
    bits = [b * groups for b in powers(lanes)] + powers(groups)
    parts = [weights[:, base : base + width] for base, width in chunks]
    spectra = []
    before = []
    for pieces, part in zip(arrived[:-1], parts):
        (total,) = gram_part(block_order, offsets, part, tables, pieces, before, False, scale)
        spectra.append(spectrum(block_order, offsets, tables[0], pieces, [total]))
        before = [total, spectra[-1]]
    send, scaled = gram_part(
        block_order, offsets, parts[-1], tables, arrived[-1], before, True, scale
    )

    other = swap(send, axes, bits[0], size)
    keep = own_part(scaled, tables[1], before[0], scale)
    spectra.append(spectrum(block_order, offsets, tables[0], arrived[-1], [keep]))
    half = keep.astype(F32) + other.astype(F32)
    for at in range(1, len(bits), 2):
        masks = bits[at : at + 2]
        if len(masks) == 2:
            masks.append(masks[0] ^ masks[1])
        half = half.astype(BF16)
        terms = [half] + [swap(half, axes, mask, size) for mask in masks]
        terms = [t.astype(F32) for t in terms]
        while len(terms) > 1:
            terms = [a + b for a, b in zip(terms[::2], terms[1::2])]
        half = terms[0]
    half, spectra[-1] = lax.optimization_barrier((half, spectra[-1]))
    other = swap(half, axes, bits[0], size)

    spread = jnp.asarray(spread_table())
    modes, gram = mode_fields(half, other, spread, spectra, NFREQ // groups)
    modes = jnp.transpose(modes, (0, 2, 1, 3))[:, :, :, None, :]
    return modes, jnp.transpose(gram, (2, 3, 0, 1))


def solution(mesh):
    placed = (P("tm", None, ("sx", "sy")), P(("sx", "sy")), P(), P(("sx", "sy"), None), P())
    return jax.shard_map(
        body,
        mesh=mesh,
        in_specs=placed,
        out_specs=(P(None, None, None, "tm", ("sx", "sy")), P(None, ("sx", "sy"), None, None)),
        check_vma=False,
    )
```

```python
import functools
import math

import jax
import jax.numpy as jnp
import numpy as np
from jax import lax
from jax.experimental import pallas as pl
from jax.experimental.pallas import tpu as pltpu
from jax.sharding import PartitionSpec as P

NFFT = 256
NFREQ = 128
NBLK = 11
LANE = 128
SUB = 8
HALF_ROWS = NBLK * SUB
GROUPS = NFREQ // SUB
MATS = 7
PACKED = 128
HALF = PACKED // 2
STACK = 4
CORNER = NBLK - SUB
WIDE = 2 * LANE
FIRST_LIMIT = 64 * 2**20
SECOND_LIMIT = FIRST_LIMIT - 1450 * 2**10
BF16 = jnp.bfloat16
F32 = jnp.float32


def fourier_tables():
    n = np.arange(NFFT)
    k = np.arange(NFREQ)
    angles = 2.0 * np.pi * ((k[:, None] * n[None, :]) % NFFT) / NFFT
    scaled = (0.5 - 0.5 * np.cos(2.0 * np.pi * n / NFFT)) / math.sqrt(0.375 * NFFT)
    table = np.concatenate([np.cos(angles) * scaled, -np.sin(angles) * scaled], axis=0)
    high = table.astype(jnp.bfloat16)
    low = (table - high.astype(np.float64)).astype(jnp.bfloat16)
    return np.concatenate([high, low], axis=0)


def packed_rows():
    rows = {}
    for a in range(NBLK):
        for e in range(a, NBLK):
            rows[0, a, e] = len(rows)
        for e in range(a + 1, NBLK):
            rows[1, a, e] = len(rows)
    return rows


ROWS = packed_rows()


def pick_table():
    pick = np.zeros((NBLK, 2, LANE, PACKED), np.float32)
    for (part, a, e), row in ROWS.items():
        pick[a, part, e * SUB : (e + 1) * SUB, row] = 1.0
    return pick.reshape(NBLK * WIDE, PACKED).astype(jnp.bfloat16)


def spread_table():
    spread = np.zeros((2, STACK, 2, 16, WIDE), np.float32)
    for b in range(NBLK):
        first = slice(b * SUB, b * SUB + SUB)
        second = slice(HALF_ROWS + b * SUB, HALF_ROWS + b * SUB + SUB)
        spread[0, :, 0, b, first] = 1.0
        spread[0, :, 1, b, second] = 1.0
        spread[1, :, 1, b, first] = -1.0
        spread[1, :, 0, b, second] = 1.0
    return spread.reshape(2, LANE, WIDE).astype(jnp.bfloat16)


def dot(a, b):
    return jnp.dot(a, b, preferred_element_type=F32)


def dot_nt(a, b):
    return lax.dot_general(a, b, (((1,), (1,)), ((), ())), preferred_element_type=F32)


def spec(shape):
    return pl.BlockSpec(shape, lambda *_: (0,) * len(shape))


SMEM = pl.BlockSpec(memory_space=pltpu.SMEM)
VMEM = pl.BlockSpec(memory_space=pltpu.VMEM)
HBM = pl.BlockSpec(memory_space=pltpu.HBM)


def lane_pick(owner, lanes):
    me = lax.axis_index("tm")
    rows = WIDE // lanes
    out_row = lax.broadcasted_iota(jnp.int32, (WIDE, WIDE), 0)
    in_row = lax.broadcasted_iota(jnp.int32, (WIDE, WIDE), 1)
    row_of = (out_row % rows) * lanes
    for d in range(lanes):
        slot = me ^ d
        source = jnp.int32(0)
        for lane in range(lanes):
            source = source + jnp.where(owner[0, lane] == slot, lane, 0)
        row_of = jnp.where(out_row // rows == d, row_of + source, row_of)
    return jnp.where(in_row == row_of, 1.0, 0.0).astype(BF16)


def pack_kernel(jobs, parts, first, follows, table_hbm, x_hbm, *refs):
    steps, lanes, _ = x_hbm.shape
    base = jobs[0][0]
    table, x_ref, table_sem, x_sem = refs[-4:]
    outs = list(refs[follows:-4])
    part = steps // parts
    table_copy = pltpu.make_async_copy(table_hbm, table, table_sem)
    table_copy.start()
    copies = []
    for i in range(parts):
        at = slice(i * part, (i + 1) * part)
        source = x_hbm.at[at, :, base : base + x_ref.shape[2]]
        copies.append(pltpu.make_async_copy(source, x_ref.at[at], x_sem.at[i]))
        copies[-1].start()
    table_copy.wait()
    pick = table
    if first:
        pick = outs.pop()
        pick[...] = lane_pick(table, lanes)
    rows = WIDE // lanes
    for i in range(parts):
        copies[i].wait()
        for start in range(i * part, (i + 1) * part, rows):
            at = slice(start, start + rows)
            x = x_ref[at].reshape(WIDE, x_ref.shape[2])
            out = iter(outs)
            for job, width, begin, end in jobs:
                here = x[:, job - base : job - base + width]
                y = dot(pick[begin * rows : end * rows, :], here).astype(BF16)
                for d in range(end - begin):
                    next(out)[at, :] = y[d * rows : (d + 1) * rows]


def pack(table, snapshots, jobs, first, after=()):
    steps, lanes, _ = snapshots.shape
    parts = math.gcd(steps * lanes // WIDE, 3)
    outs = [
        jax.ShapeDtypeStruct((steps, width), BF16)
        for _, width, begin, end in jobs
        for _ in range(begin, end)
    ]
    if first:
        outs.append(jax.ShapeDtypeStruct((WIDE, WIDE), BF16))
    columns = jobs[-1][0] + jobs[-1][1] - jobs[0][0]
    return pl.pallas_call(
        functools.partial(pack_kernel, jobs, parts, first, len(after)),
        out_shape=outs,
        in_specs=[HBM] * (2 + len(after)),
        out_specs=[VMEM] * len(outs),
        scratch_shapes=[
            pltpu.SMEM(table.shape, jnp.int32) if first else pltpu.VMEM(table.shape, BF16),
            pltpu.VMEM((steps, lanes, columns), BF16),
            pltpu.SemaphoreType.DMA,
            pltpu.SemaphoreType.DMA((parts,)),
        ],
        compiler_params=pltpu.CompilerParams(
            vmem_limit_bytes=FIRST_LIMIT if first else 40 * 2**20 if after else SECOND_LIMIT
        ),
        cost_estimate=pl.CostEstimate(flops=1000, bytes_accessed=1000, transcendentals=0),
    )(table, snapshots, *after)


def fill_record(order_ref, pieces, record, factor):
    steps, width = pieces[0].shape
    me = lax.axis_index("tm")
    for d, piece in enumerate(pieces):
        partner = me ^ (len(pieces) - d if d else 0)
        start = pl.multiple_of(order_ref[partner] * steps, steps)
        for c in range(width // LANE):
            cols = slice(c * LANE, (c + 1) * LANE)
            part = piece[:, cols].astype(F32)
            record[c, pl.ds(start, steps), :] = part if factor is None else part * factor[:, cols]


def transform(offsets_ref, f, record, s_ref):
    wanted = [(i, c) for i in range(NBLK) for c in range(record.shape[0])]
    for first in range(0, len(wanted), 2):
        pair = wanted[first : first + 2]
        x = [record[c, pl.ds(offsets_ref[i], NFFT), :].astype(BF16) for i, c in pair]
        x = jnp.concatenate(x, axis=1) if len(x) > 1 else x[0]
        y = dot(f, x)
        if f.shape[0] > NFFT:
            y = y[:NFFT] + y[NFFT:]
        for at, (i, c) in enumerate(pair):
            cols = slice(c * LANE, (c + 1) * LANE)
            s_ref[i, :, cols] = y[:NFREQ, at * LANE : (at + 1) * LANE]
            s_ref[NBLK + i, :, cols] = y[NFREQ:, at * LANE : (at + 1) * LANE]


def padded(s):
    width = s.shape[2]
    pad = jnp.zeros((LANE - HALF_ROWS, width), F32)
    real = s[:NBLK].reshape(HALF_ROWS, width)
    imag = s[NBLK:].reshape(HALF_ROWS, width)
    return jnp.concatenate([real, pad, imag, pad], axis=0)


def gram_rows(base, groups, s_ref, pick_ref, masked):
    row = lax.broadcasted_iota(jnp.int32, (HALF_ROWS, LANE), 0)
    col = lax.broadcasted_iota(jnp.int32, (HALF_ROWS, LANE), 1)
    same = row % SUB == col % SUB
    for pair in range(0, groups, 2):
        blocks = []
        for g in (pair, pair + 1):
            s = s_ref[:, pl.ds(pl.multiple_of(base + g * SUB, SUB), SUB), :]
            full = dot_nt(s.reshape(2 * HALF_ROWS, -1).astype(BF16), padded(s).astype(BF16))
            real = full[:HALF_ROWS, :LANE] + full[HALF_ROWS:, LANE:]
            imag = full[:HALF_ROWS, LANE:] - full[HALF_ROWS:, :LANE]
            blocks.append([jnp.where(same, part, 0.0) for part in (real, imag)])
        at = slice(pair * SUB, (pair + 2) * SUB)
        for a in range(NBLK):
            rows = slice(a * SUB, (a + 1) * SUB)
            for part in range(2):
                both = jnp.concatenate([block[part][rows] for block in blocks], axis=0)
                cols = slice(a * WIDE + part * LANE, a * WIDE + (part + 1) * LANE)
                masked[at, cols] = both.astype(BF16)
    return dot(masked[...], pick_ref[...])


def gram_kernel(lanes, scale, last, order_ref, offsets_ref, w_ref, f_ref, pick_ref, *refs):
    pieces = refs[:lanes]
    refs = refs[lanes:]
    if last:
        before_ref, _, gram_ref, s_ref, record, masked = refs
    else:
        *before_refs, gram_ref, record, s_ref, masked = refs
    fill_record(order_ref, pieces, record, jnp.sqrt(w_ref[...]))
    transform(offsets_ref, f_ref[:NFFT] if last else f_ref[...], record, s_ref)
    if not last:
        total = gram_rows(0, GROUPS, s_ref, pick_ref, masked) * scale
        gram_ref[...] = total + before_refs[0][...] if before_refs else total
        return
    base = pl.multiple_of((1 - lax.axis_index("tm") % 2) * HALF, HALF)
    total = gram_rows(base, GROUPS // 2, s_ref, pick_ref, masked) * scale
    gram_ref[...] = (total + before_ref[pl.ds(base, HALF), :]).astype(BF16)


def gram_part(order, offsets, weights, tables, pieces, before, last, scale):
    lanes = len(pieces)
    steps, width = pieces[0].shape
    args = [order, offsets, weights, *tables, *pieces, *before]
    spectrum_shape = (2 * NBLK, NFREQ, width)
    scratch = [pltpu.VMEM((width // LANE, lanes * steps, LANE), F32)]
    if last:
        outs = [jax.ShapeDtypeStruct((HALF, PACKED), BF16)]
        outs.append(jax.ShapeDtypeStruct(spectrum_shape, F32))
    else:
        outs = [jax.ShapeDtypeStruct((NFREQ, PACKED), F32)]
        scratch.append(pltpu.VMEM(spectrum_shape, F32))
    scratch.append(pltpu.VMEM((HALF if last else NFREQ, NBLK * WIDE), BF16))
    return pl.pallas_call(
        functools.partial(gram_kernel, lanes, scale, last),
        out_shape=outs,
        in_specs=[SMEM, SMEM] + [VMEM] * (len(args) - 2),
        out_specs=[VMEM] * len(outs),
        scratch_shapes=scratch,
        compiler_params=pltpu.CompilerParams(vmem_limit_bytes=32 * 2**20),
        cost_estimate=pl.CostEstimate(flops=1000, bytes_accessed=1000, transcendentals=0),
    )(*args)


def own_kernel(scale, s_ref, pick_ref, before_ref, gram_ref, masked):
    base = pl.multiple_of(lax.axis_index("tm") % 2 * HALF, HALF)
    total = gram_rows(base, GROUPS // 2, s_ref, pick_ref, masked) * scale
    gram_ref[...] = (total + before_ref[pl.ds(base, HALF), :]).astype(BF16)


def own_part(scaled, pick, before, scale):
    return pl.pallas_call(
        functools.partial(own_kernel, scale),
        out_shape=jax.ShapeDtypeStruct((HALF, PACKED), BF16),
        in_specs=[VMEM] * 3,
        out_specs=VMEM,
        scratch_shapes=[pltpu.VMEM((HALF, NBLK * WIDE), BF16)],
        compiler_params=pltpu.CompilerParams(vmem_limit_bytes=32 * 2**20),
        cost_estimate=pl.CostEstimate(flops=10**9, bytes_accessed=3 * 10**6, transcendentals=0),
    )(scaled, pick, before)


def spectrum_kernel(lanes, order_ref, offsets_ref, f_ref, *refs):
    s_ref, record = refs[-2:]
    fill_record(order_ref, refs[:lanes], record, None)
    transform(offsets_ref, f_ref[...], record, s_ref)


def spectrum(order, offsets, fourier, pieces, after):
    lanes = len(pieces)
    steps, width = pieces[0].shape
    args = [order, offsets, fourier, *pieces, *after]
    return pl.pallas_call(
        functools.partial(spectrum_kernel, lanes),
        out_shape=jax.ShapeDtypeStruct((2 * NBLK, NFREQ, width), F32),
        in_specs=[SMEM, SMEM] + [VMEM] * (len(args) - 2),
        out_specs=VMEM,
        scratch_shapes=[pltpu.VMEM((width // LANE, lanes * steps, LANE), F32)],
        compiler_params=pltpu.CompilerParams(vmem_limit_bytes=32 * 2**20),
        cost_estimate=pl.CostEstimate(flops=1000, bytes_accessed=1000, transcendentals=0),
    )(*args)


class Hermitian:
    def __init__(self, main, corner):
        self.main = main
        self.corner = corner

    def entry(self, a, e):
        if e < SUB:
            return self.main[0, a, pl.ds(e, 1), :], self.main[1, a, pl.ds(e, 1), :], 1
        if a < SUB:
            return self.main[0, e, pl.ds(a, 1), :], self.main[1, e, pl.ds(a, 1), :], -1
        at = pl.ds(e - SUB, 1)
        return self.corner[0, a - SUB, at, :], self.corner[1, a - SUB, at, :], 1

    def put(self, a, e, real, imag):
        if e < SUB:
            self.main[0, a, pl.ds(e, 1), :] = real
            self.main[1, a, pl.ds(e, 1), :] = imag
        elif a >= SUB:
            at = pl.ds(e - SUB, 1)
            self.corner[0, a - SUB, at, :] = real
            self.corner[1, a - SUB, at, :] = imag


def product(x, y, out, diagonal=0.0, terms=()):
    sub = lax.broadcasted_iota(jnp.int32, (SUB, NFREQ), 0)
    yr = [y.main[0, b] for b in range(NBLK)]
    yi = [y.main[1, b] for b in range(NBLK)]
    for a in range(NBLK):
        real = imag = None
        for b in range(NBLK):
            pr, pi, sign = x.entry(a, b)
            tr, ti = pi * yi[b], pi * yr[b]
            if sign > 0:
                tr, ti = pr * yr[b] - tr, pr * yi[b] + ti
            else:
                tr, ti = pr * yr[b] + tr, pr * yi[b] - ti
            real = tr if real is None else real + tr
            imag = ti if imag is None else imag + ti
        for factor, term in terms:
            real = real + factor * term.main[0, a]
            imag = imag + factor * term.main[1, a]
        if diagonal and a < SUB:
            real = real + jnp.where(sub == a, diagonal, 0.0)
        out.main[0, a] = real
        out.main[1, a] = imag
    ar = [[x.main[0, SUB + a], x.corner[0, a]] for a in range(CORNER)]
    ai = [[x.main[1, SUB + a], x.corner[1, a]] for a in range(CORNER)]
    er = [[yr[SUB + e], y.corner[0, e]] for e in range(CORNER)]
    ei = [[yi[SUB + e], y.corner[1, e]] for e in range(CORNER)]
    for a in range(CORNER):
        for e in range(a, CORNER):
            real = sum(ar[a][h] * er[e][h] + ai[a][h] * ei[e][h] for h in range(2))
            real = jnp.sum(real, axis=0, keepdims=True)
            imag = jnp.zeros_like(real)
            if a != e:
                imag = sum(ai[a][h] * er[e][h] - ar[a][h] * ei[e][h] for h in range(2))
                imag = jnp.sum(imag, axis=0, keepdims=True)
            for factor, term in terms:
                r, i, _ = term.entry(SUB + a, SUB + e)
                real, imag = real + factor * r, imag + factor * i
            if a == e:
                out.put(SUB + a, SUB + a, real + diagonal, jnp.zeros_like(real))
            else:
                out.put(SUB + a, SUB + e, real, imag)
                out.put(SUB + e, SUB + a, real, -imag)


def combine(out, diagonal, terms):
    sub = lax.broadcasted_iota(jnp.int32, (SUB, NFREQ), 0)
    for name, rows in (("main", NBLK), ("corner", CORNER)):
        target = getattr(out, name)
        for a in range(rows):
            real = sum(factor * getattr(term, name)[0, a] for factor, term in terms)
            imag = sum(factor * getattr(term, name)[1, a] for factor, term in terms)
            if diagonal and (name == "corner" or a < SUB):
                real = real + jnp.where(sub == a, diagonal, 0.0)
            target[0, a] = real
            target[1, a] = imag


TWO_STEPS = (2.25, -2.4375, 1.6875, -0.5625, 0.0625)


def inverse_root(w, mats):
    q, u, r, t, w2, z = mats
    c0, c1, c2, c3, c4 = TWO_STEPS
    product(w, w, q)
    combine(u, 0.0, [(c3, w), (c4, q)])
    product(q, u, z, c0, [(c1, w), (c2, q)])
    product(z, z, t)
    product(w, t, w2)
    product(w2, w2, q)
    combine(u, 0.0, [(c3, w2), (c4, q)])
    product(q, u, r, c0, [(c1, w2), (c2, q)])
    product(r, r, t)
    product(z, r, u)
    product(w2, t, q)
    combine(q, 1.5, [(-0.5, q)])
    product(u, q, z)
    return z


def make_roots(share, half_ref, other_ref, gram_ref, packed, rolled, mats):
    core = lax.axis_index("tm") % 2
    packed[pl.ds(pl.multiple_of(core * HALF, HALF), HALF), :] = half_ref[...]
    packed[pl.ds(pl.multiple_of((1 - core) * HALF, HALF), HALF), :] = other_ref[...]
    packed[...] = packed[...].T
    at = lax.axis_index("sx") * lax.axis_size("sy") + lax.axis_index("sy")
    rolled[...] = pltpu.roll(packed[...], (NFREQ - at * share) % NFREQ, 1)
    y, *free = [Hermitian(mats[2 * i], mats[2 * i + 1]) for i in range(MATS)]
    for ref in mats[1::2]:
        ref[...] = jnp.zeros_like(ref)

    def row(ref, part, a, e):
        return ref[pl.ds(ROWS[part, a, e], 1), :]

    trace = 2.0 * sum(row(packed, 0, a, a) for a in range(NBLK))
    norm = 1.0 / jnp.sqrt(trace)
    packed[...] = packed[...] / trace
    zero = jnp.zeros((1, NFREQ), F32)
    for a in range(NBLK):
        y.put(a, a, row(packed, 0, a, a), zero)
        gram_ref[a, a, 0:1, :] = row(rolled, 0, a, a)[:, :share]
        gram_ref[a, a, 1:2, :] = zero[:, :share]
        for e in range(a + 1, NBLK):
            real, imag = row(packed, 0, a, e), row(packed, 1, a, e)
            y.put(a, e, real, imag)
            y.put(e, a, real, -imag)
            real, imag = row(rolled, 0, a, e)[:, :share], row(rolled, 1, a, e)[:, :share]
            gram_ref[a, e, 0:1, :] = real
            gram_ref[e, a, 0:1, :] = real
            gram_ref[a, e, 1:2, :] = imag
            gram_ref[e, a, 1:2, :] = -imag
    z = inverse_root(y, free)
    mean = sum(z.entry(a, a)[0] for a in range(NBLK)) * (1.0 / NBLK)
    sub = lax.broadcasted_iota(jnp.int32, (SUB, NFREQ), 0)
    none = jnp.zeros((SUB - CORNER, NFREQ), F32)
    first = jnp.concatenate([mean * norm, none[1:]], axis=0)
    stacks = []
    for m0 in range(0, NBLK, STACK):
        modes = range(m0, min(m0 + STACK, NBLK))
        stack = []
        for m in modes:
            for c in range(2):
                column = z.main[c, m]
                if c == 0 and m < SUB:
                    column = column - jnp.where(sub == m, mean, 0.0)
                stack.append(column * norm)
                for b in range(SUB, NBLK):
                    real, imag, sign = z.entry(m, b)
                    line = imag * sign if c else real
                    if c == 0 and m == b:
                        line = line - mean
                    stack.append(line * norm)
                stack.append(first if c == 0 and m == 0 else none)
        stack += [jnp.zeros((32, NFREQ), F32)] * (STACK - len(modes))
        stacks.append(jnp.concatenate(stack, axis=0).T)
    return stacks


def mode_kernel(chunks, share, half_ref, other_ref, spread_ref, *refs):
    s_refs = refs[:chunks]
    out_hbm, gram_ref, out, v, mean, packed, rolled, sem, *mats = refs[chunks:]
    stacks = make_roots(share, half_ref, other_ref, gram_ref, packed, rolled, mats)
    mean[...] = jnp.broadcast_to(stacks[0][:, NBLK : NBLK + 1], (NFREQ, LANE))
    row = lax.broadcasted_iota(jnp.int32, (NFREQ, 2 * HALF_ROWS), 0)
    col = lax.broadcasted_iota(jnp.int32, (NFREQ, 2 * HALF_ROWS), 1)
    same = row % SUB == col % SUB
    place = lax.broadcasted_iota(jnp.int32, (NFREQ, LANE), 1) // 32
    rows = [jnp.where(place == m % STACK, stacks[m // STACK], 0.0) for m in range(NBLK)]
    rows = jnp.concatenate(rows, axis=0).astype(BF16)
    for c in range(2):
        wide = dot(rows, spread_ref[c])[:, : 2 * HALF_ROWS]
        for m in range(NBLK):
            v[c * NBLK + m] = jnp.where(same, wide[m * NFREQ : (m + 1) * NFREQ], 0.0)

    copies = []
    for pair in range(GROUPS // 2):
        fields = []
        for g in (2 * pair, 2 * pair + 1):
            at = slice(g * SUB, (g + 1) * SUB)
            s = jnp.concatenate([r[:, at, :] for r in s_refs], axis=2)
            flat = s.reshape(2 * HALF_ROWS, -1).astype(BF16)
            field = dot(v[:, at, :].reshape(2 * HALF_ROWS, 2 * HALF_ROWS).astype(BF16), flat)
            scale = jnp.concatenate([mean[at, :]] * (s.shape[2] // LANE), axis=1)
            fields.append(field.reshape(s.shape) + s * scale[None])
        both = jnp.concatenate(fields, axis=1).astype(BF16)
        at = slice(pair * 2 * SUB, (pair + 1) * 2 * SUB)
        out[:, :, at, :] = both.reshape(2, NBLK, 2 * SUB, -1)
        copies.append(
            pltpu.make_async_copy(out.at[:, :, at, :], out_hbm.at[:, :, at, :], sem.at[pair])
        )
        copies[-1].start()
    for copy in copies:
        copy.wait()


def mode_fields(half, other, spread, spectra, share):
    shape = (2, NBLK, NFREQ, sum(s.shape[2] for s in spectra))
    return pl.pallas_call(
        functools.partial(mode_kernel, len(spectra), share),
        out_shape=[
            jax.ShapeDtypeStruct(shape, BF16),
            jax.ShapeDtypeStruct((NBLK, NBLK, 2, share), F32),
        ],
        in_specs=[VMEM] * (3 + len(spectra)),
        out_specs=[HBM, VMEM],
        scratch_shapes=[
            pltpu.VMEM(shape, BF16),
            pltpu.VMEM((2 * NBLK, NFREQ, 2 * HALF_ROWS), F32),
            pltpu.VMEM((NFREQ, LANE), F32),
            pltpu.VMEM((PACKED, NFREQ), F32),
            pltpu.VMEM((PACKED, NFREQ), F32),
            pltpu.SemaphoreType.DMA((GROUPS // 2,)),
        ]
        + [
            pltpu.VMEM((2, NBLK, SUB, NFREQ), F32),
            pltpu.VMEM((2, CORNER, SUB, NFREQ), F32),
        ]
        * MATS,
        compiler_params=pltpu.CompilerParams(vmem_limit_bytes=32 * 2**20),
    )(half, other, spread, *spectra)


def swap(x, axes, mask, size):
    return lax.ppermute(x, axes, [(i, i ^ mask) for i in range(size)])


def powers(size):
    return [1 << i for i in range(size.bit_length() - 1)]


def body(snapshots, weights, block_order, owner, offsets):
    lanes = lax.axis_size("tm")
    groups = lax.axis_size("sx") * lax.axis_size("sy")
    points = snapshots.shape[2]
    half, quarter = points // 2, points // 4
    chunks = [(0, half), (half, quarter), (half + quarter, quarter)]
    scale = 1.0 / (lanes * groups * points)
    tables = (jnp.asarray(fourier_tables()), jnp.asarray(pick_table()))
    weights = weights.reshape(1, -1)

    first, table = pack(owner, snapshots, [(*chunks[0], lanes - 1, lanes)], True)
    moved = [swap(first, "tm", lanes - 1, lanes)]
    jobs = [(*chunks[0], 0, lanes - 1), (*chunks[1], 0, lanes)]
    rest = list(pack(table, snapshots, jobs, False))
    moved += [swap(rest[d], "tm", d, lanes) for d in reversed(range(1, lanes - 1))]
    arrived = [[rest[0]] + moved]
    for packed in (rest[lanes - 1 :], None):
        if packed is None:
            packed = pack(table, snapshots, [(*chunks[2], 0, lanes)], False, moved[:1])
        arrived.append([packed[0]])
        arrived[-1] += [swap(packed[d], "tm", d, lanes) for d in reversed(range(1, lanes))]

    axes = ("tm", "sx", "sy")
    size = lanes * groups
    bits = [b * groups for b in powers(lanes)] + powers(groups)
    parts = [weights[:, base : base + width] for base, width in chunks]
    (total,) = gram_part(block_order, offsets, parts[0], tables, arrived[0], [], False, scale)
    spectra = [spectrum(block_order, offsets, tables[0], arrived[0], [total])]
    before = [total, spectra[0]]
    before = gram_part(block_order, offsets, parts[1], tables, arrived[1], before, False, scale)
    send, scaled = gram_part(
        block_order, offsets, parts[2], tables, arrived[2], [*before, spectra[0]], True, scale
    )

    other = swap(send, axes, bits[0], size)
    keep = own_part(scaled, tables[1], before[0], scale)
    spectra += [spectrum(block_order, offsets, tables[0], a, [keep]) for a in arrived[1:]]
    half = keep.astype(F32) + other.astype(F32)
    for at in range(1, len(bits), 2):
        masks = bits[at : at + 2]
        if len(masks) == 2:
            masks.append(masks[0] ^ masks[1])
            masks = masks[1:] + masks[:1] if at > 1 else masks
        half = half.astype(BF16)
        terms = [half] + [swap(half, axes, mask, size) for mask in masks]
        terms = [t.astype(F32) for t in terms]
        while len(terms) > 1:
            terms = [a + b for a, b in zip(terms[::2], terms[1::2])]
        half = terms[0]
        if at == 1:
            half, spectra[1] = lax.optimization_barrier((half, spectra[1]))
    half, spectra[2] = lax.optimization_barrier((half, spectra[2]))
    other = swap(half, axes, bits[0], size)

    spread = jnp.asarray(spread_table())
    modes, gram = mode_fields(half, other, spread, spectra, NFREQ // groups)
    modes = jnp.transpose(modes, (0, 2, 1, 3))[:, :, :, None, :]
    return modes, jnp.transpose(gram, (2, 3, 0, 1))


def solution(mesh):
    placed = (P("tm", None, ("sx", "sy")), P(("sx", "sy")), P(), P(("sx", "sy"), None), P())
    return jax.shard_map(
        body,
        mesh=mesh,
        in_specs=placed,
        out_specs=(P(None, None, None, "tm", ("sx", "sy")), P(None, ("sx", "sy"), None, None)),
        check_vma=False,
    )
```

```python
import functools
import math

import jax
import jax.numpy as jnp
import numpy as np
from jax import lax
from jax.experimental import pallas as pl
from jax.experimental.pallas import tpu as pltpu
from jax.sharding import PartitionSpec as P

NFFT = 256
NFREQ = 128
NBLK = 11
LANE = 128
SUB = 8
HALF_ROWS = NBLK * SUB
GROUPS = NFREQ // SUB
MATS = 7
NEAR = 2
PACKED = 128
HALF = PACKED // 2
STACK = 4
CORNER = NBLK - SUB
WIDE = 2 * LANE
FIRST_LIMIT = 64 * 2**20
SECOND_LIMIT = FIRST_LIMIT - 1450 * 2**10
BF16 = jnp.bfloat16
F32 = jnp.float32


def fourier_tables():
    n = np.arange(NFFT)
    k = np.arange(NFREQ)
    angles = 2.0 * np.pi * ((k[:, None] * n[None, :]) % NFFT) / NFFT
    scaled = (0.5 - 0.5 * np.cos(2.0 * np.pi * n / NFFT)) / math.sqrt(0.375 * NFFT)
    table = np.concatenate([np.cos(angles) * scaled, -np.sin(angles) * scaled], axis=0)
    high = table.astype(jnp.bfloat16)
    low = (table - high.astype(np.float64)).astype(jnp.bfloat16)
    return np.concatenate([high, low], axis=0)


def packed_rows():
    rows = {}
    for a in range(NBLK):
        for e in range(a, NBLK):
            rows[0, a, e] = len(rows)
        for e in range(a + 1, NBLK):
            rows[1, a, e] = len(rows)
    return rows


ROWS = packed_rows()


def pick_table():
    pick = np.zeros((NBLK, 2, LANE, PACKED), np.float32)
    for (part, a, e), row in ROWS.items():
        pick[a, part, e * SUB : (e + 1) * SUB, row] = 1.0
    return pick.reshape(NBLK * WIDE, PACKED).astype(jnp.bfloat16)


def spread_table():
    spread = np.zeros((2, STACK, 2, 16, WIDE), np.float32)
    for b in range(NBLK):
        first = slice(b * SUB, b * SUB + SUB)
        second = slice(HALF_ROWS + b * SUB, HALF_ROWS + b * SUB + SUB)
        spread[0, :, 0, b, first] = 1.0
        spread[0, :, 1, b, second] = 1.0
        spread[1, :, 1, b, first] = -1.0
        spread[1, :, 0, b, second] = 1.0
    return spread.reshape(2, LANE, WIDE).astype(jnp.bfloat16)


def dot(a, b):
    return jnp.dot(a, b, preferred_element_type=F32)


def dot_nt(a, b):
    return lax.dot_general(a, b, (((1,), (1,)), ((), ())), preferred_element_type=F32)


def spec(shape):
    return pl.BlockSpec(shape, lambda *_: (0,) * len(shape))


SMEM = pl.BlockSpec(memory_space=pltpu.SMEM)
VMEM = pl.BlockSpec(memory_space=pltpu.VMEM)
HBM = pl.BlockSpec(memory_space=pltpu.HBM)


def lane_pick(owner, lanes):
    me = lax.axis_index("tm")
    rows = WIDE // lanes
    out_row = lax.broadcasted_iota(jnp.int32, (WIDE, WIDE), 0)
    in_row = lax.broadcasted_iota(jnp.int32, (WIDE, WIDE), 1)
    row_of = (out_row % rows) * lanes
    for d in range(lanes):
        slot = me ^ d
        source = jnp.int32(0)
        for lane in range(lanes):
            source = source + jnp.where(owner[0, lane] == slot, lane, 0)
        row_of = jnp.where(out_row // rows == d, row_of + source, row_of)
    return jnp.where(in_row == row_of, 1.0, 0.0).astype(BF16)


def pack_kernel(jobs, parts, first, follows, table_hbm, x_hbm, *refs):
    steps, lanes, _ = x_hbm.shape
    base = jobs[0][0]
    table, x_ref, table_sem, x_sem = refs[-4:]
    outs = list(refs[follows:-4])
    part = steps // parts
    table_copy = pltpu.make_async_copy(table_hbm, table, table_sem)
    table_copy.start()
    copies = []
    for i in range(parts):
        at = slice(i * part, (i + 1) * part)
        source = x_hbm.at[at, :, base : base + x_ref.shape[2]]
        copies.append(pltpu.make_async_copy(source, x_ref.at[at], x_sem.at[i]))
        copies[-1].start()
    table_copy.wait()
    pick = table
    if first:
        pick = outs.pop()
        pick[...] = lane_pick(table, lanes)
    rows = WIDE // lanes
    for i in range(parts):
        copies[i].wait()
        for start in range(i * part, (i + 1) * part, rows):
            at = slice(start, start + rows)
            x = x_ref[at].reshape(WIDE, x_ref.shape[2])
            out = iter(outs)
            for job, width, begin, end in jobs:
                here = x[:, job - base : job - base + width]
                y = dot(pick[begin * rows : end * rows, :], here).astype(BF16)
                for d in range(end - begin):
                    next(out)[at, :] = y[d * rows : (d + 1) * rows]


def pack(table, snapshots, jobs, first, after=()):
    steps, lanes, _ = snapshots.shape
    parts = math.gcd(steps * lanes // WIDE, 3)
    outs = [
        jax.ShapeDtypeStruct((steps, width), BF16)
        for _, width, begin, end in jobs
        for _ in range(begin, end)
    ]
    if first:
        outs.append(jax.ShapeDtypeStruct((WIDE, WIDE), BF16))
    columns = jobs[-1][0] + jobs[-1][1] - jobs[0][0]
    return pl.pallas_call(
        functools.partial(pack_kernel, jobs, parts, first, len(after)),
        out_shape=outs,
        in_specs=[HBM] * (2 + len(after)),
        out_specs=[VMEM] * len(outs),
        scratch_shapes=[
            pltpu.SMEM(table.shape, jnp.int32) if first else pltpu.VMEM(table.shape, BF16),
            pltpu.VMEM((steps, lanes, columns), BF16),
            pltpu.SemaphoreType.DMA,
            pltpu.SemaphoreType.DMA((parts,)),
        ],
        compiler_params=pltpu.CompilerParams(
            vmem_limit_bytes=FIRST_LIMIT if first else 40 * 2**20 if after else SECOND_LIMIT
        ),
        cost_estimate=pl.CostEstimate(flops=1000, bytes_accessed=1000, transcendentals=0),
    )(table, snapshots, *after)


def fill_record(base, order_ref, pieces, record, factor):
    steps = pieces[0].shape[0]
    me = lax.axis_index("tm")
    for d, piece in enumerate(pieces):
        start = pl.multiple_of(order_ref[me ^ d] * steps, steps)
        for c in range(record.shape[0]):
            at = c * LANE + (base if d < NEAR else 0)
            part = piece[:, at : at + LANE].astype(F32)
            if factor is not None:
                part = part * factor[:, c * LANE : (c + 1) * LANE]
            record[c, pl.ds(start, steps), :] = part


def transform(offsets_ref, f, record, s_ref):
    wanted = [(i, c) for i in range(NBLK) for c in range(record.shape[0])]
    for first in range(0, len(wanted), 2):
        pair = wanted[first : first + 2]
        x = [record[c, pl.ds(offsets_ref[i], NFFT), :].astype(BF16) for i, c in pair]
        x = jnp.concatenate(x, axis=1) if len(x) > 1 else x[0]
        y = dot(f, x)
        if f.shape[0] > NFFT:
            y = y[:NFFT] + y[NFFT:]
        for at, (i, c) in enumerate(pair):
            cols = slice(c * LANE, (c + 1) * LANE)
            s_ref[i, :, cols] = y[:NFREQ, at * LANE : (at + 1) * LANE]
            s_ref[NBLK + i, :, cols] = y[NFREQ:, at * LANE : (at + 1) * LANE]


def padded(s):
    width = s.shape[2]
    pad = jnp.zeros((LANE - HALF_ROWS, width), F32)
    real = s[:NBLK].reshape(HALF_ROWS, width)
    imag = s[NBLK:].reshape(HALF_ROWS, width)
    return jnp.concatenate([real, pad, imag, pad], axis=0)


def gram_rows(base, groups, s_ref, pick_ref, masked):
    row = lax.broadcasted_iota(jnp.int32, (HALF_ROWS, LANE), 0)
    col = lax.broadcasted_iota(jnp.int32, (HALF_ROWS, LANE), 1)
    same = row % SUB == col % SUB
    for pair in range(0, groups, 2):
        blocks = []
        for g in (pair, pair + 1):
            s = s_ref[:, pl.ds(pl.multiple_of(base + g * SUB, SUB), SUB), :]
            full = dot_nt(s.reshape(2 * HALF_ROWS, -1).astype(BF16), padded(s).astype(BF16))
            real = full[:HALF_ROWS, :LANE] + full[HALF_ROWS:, LANE:]
            imag = full[:HALF_ROWS, LANE:] - full[HALF_ROWS:, :LANE]
            blocks.append([jnp.where(same, part, 0.0) for part in (real, imag)])
        at = slice(pair * SUB, (pair + 2) * SUB)
        for a in range(NBLK):
            rows = slice(a * SUB, (a + 1) * SUB)
            for part in range(2):
                both = jnp.concatenate([block[part][rows] for block in blocks], axis=0)
                cols = slice(a * WIDE + part * LANE, a * WIDE + (part + 1) * LANE)
                masked[at, cols] = both.astype(BF16)
    return dot(masked[...], pick_ref[...])


def gram_kernel(lanes, base, scale, last, order_ref, offsets_ref, w_ref, f_ref, pick_ref, *refs):
    pieces = refs[:lanes]
    refs = refs[lanes:]
    if last:
        before_ref, gram_ref, s_ref, record, masked = refs
    else:
        *before_refs, gram_ref, record, s_ref, masked = refs
    fill_record(base, order_ref, pieces, record, jnp.sqrt(w_ref[...]))
    transform(offsets_ref, f_ref[:NFFT] if last else f_ref[...], record, s_ref)
    if not last:
        total = gram_rows(0, GROUPS, s_ref, pick_ref, masked) * scale
        gram_ref[...] = total + before_refs[0][...] if before_refs else total
        return
    half = pl.multiple_of((1 - lax.axis_index("tm") % 2) * HALF, HALF)
    total = gram_rows(half, GROUPS // 2, s_ref, pick_ref, masked) * scale
    gram_ref[...] = (total + before_ref[pl.ds(half, HALF), :]).astype(BF16)


def gram_part(order, offsets, weights, tables, pieces, before, base, last, scale):
    lanes = len(pieces)
    steps, width = pieces[-1].shape
    args = [order, offsets, weights, *tables, *pieces, *before]
    spectrum_shape = (2 * NBLK, NFREQ, width)
    scratch = [pltpu.VMEM((width // LANE, lanes * steps, LANE), F32)]
    if last:
        outs = [jax.ShapeDtypeStruct((HALF, PACKED), BF16)]
        outs.append(jax.ShapeDtypeStruct(spectrum_shape, F32))
    else:
        outs = [jax.ShapeDtypeStruct((NFREQ, PACKED), F32)]
        scratch.append(pltpu.VMEM(spectrum_shape, F32))
    scratch.append(pltpu.VMEM((HALF if last else NFREQ, NBLK * WIDE), BF16))
    return pl.pallas_call(
        functools.partial(gram_kernel, lanes, base, scale, last),
        out_shape=outs,
        in_specs=[SMEM, SMEM] + [VMEM] * (len(args) - 2),
        out_specs=[VMEM] * len(outs),
        scratch_shapes=scratch,
        compiler_params=pltpu.CompilerParams(vmem_limit_bytes=32 * 2**20),
        cost_estimate=pl.CostEstimate(flops=1000, bytes_accessed=1000, transcendentals=0),
    )(*args)


def own_kernel(scale, s_ref, pick_ref, before_ref, gram_ref, masked):
    base = pl.multiple_of(lax.axis_index("tm") % 2 * HALF, HALF)
    total = gram_rows(base, GROUPS // 2, s_ref, pick_ref, masked) * scale
    gram_ref[...] = (total + before_ref[pl.ds(base, HALF), :]).astype(BF16)


def own_part(scaled, pick, before, scale):
    return pl.pallas_call(
        functools.partial(own_kernel, scale),
        out_shape=jax.ShapeDtypeStruct((HALF, PACKED), BF16),
        in_specs=[VMEM] * 3,
        out_specs=VMEM,
        scratch_shapes=[pltpu.VMEM((HALF, NBLK * WIDE), BF16)],
        compiler_params=pltpu.CompilerParams(vmem_limit_bytes=32 * 2**20),
        cost_estimate=pl.CostEstimate(flops=10**9, bytes_accessed=3 * 10**6, transcendentals=0),
    )(scaled, pick, before)


def spectrum_kernel(lanes, base, order_ref, offsets_ref, f_ref, *refs):
    s_ref, record = refs[-2:]
    fill_record(base, order_ref, refs[:lanes], record, None)
    transform(offsets_ref, f_ref[...], record, s_ref)


def spectrum(order, offsets, fourier, pieces, base, after):
    lanes = len(pieces)
    steps, width = pieces[-1].shape
    args = [order, offsets, fourier, *pieces, *after]
    return pl.pallas_call(
        functools.partial(spectrum_kernel, lanes, base),
        out_shape=jax.ShapeDtypeStruct((2 * NBLK, NFREQ, width), F32),
        in_specs=[SMEM, SMEM] + [VMEM] * (len(args) - 2),
        out_specs=VMEM,
        scratch_shapes=[pltpu.VMEM((width // LANE, lanes * steps, LANE), F32)],
        compiler_params=pltpu.CompilerParams(vmem_limit_bytes=32 * 2**20),
        cost_estimate=pl.CostEstimate(flops=1000, bytes_accessed=1000, transcendentals=0),
    )(*args)


class Hermitian:
    def __init__(self, main, corner):
        self.main = main
        self.corner = corner

    def entry(self, a, e):
        if e < SUB:
            return self.main[0, a, pl.ds(e, 1), :], self.main[1, a, pl.ds(e, 1), :], 1
        if a < SUB:
            return self.main[0, e, pl.ds(a, 1), :], self.main[1, e, pl.ds(a, 1), :], -1
        at = pl.ds(e - SUB, 1)
        return self.corner[0, a - SUB, at, :], self.corner[1, a - SUB, at, :], 1

    def put(self, a, e, real, imag):
        if e < SUB:
            self.main[0, a, pl.ds(e, 1), :] = real
            self.main[1, a, pl.ds(e, 1), :] = imag
        elif a >= SUB:
            at = pl.ds(e - SUB, 1)
            self.corner[0, a - SUB, at, :] = real
            self.corner[1, a - SUB, at, :] = imag


def product(x, y, out, diagonal=0.0, terms=()):
    sub = lax.broadcasted_iota(jnp.int32, (SUB, NFREQ), 0)
    yr = [y.main[0, b] for b in range(NBLK)]
    yi = [y.main[1, b] for b in range(NBLK)]
    for a in range(NBLK):
        real = imag = None
        for b in range(NBLK):
            pr, pi, sign = x.entry(a, b)
            tr, ti = pi * yi[b], pi * yr[b]
            if sign > 0:
                tr, ti = pr * yr[b] - tr, pr * yi[b] + ti
            else:
                tr, ti = pr * yr[b] + tr, pr * yi[b] - ti
            real = tr if real is None else real + tr
            imag = ti if imag is None else imag + ti
        for factor, term in terms:
            real = real + factor * term.main[0, a]
            imag = imag + factor * term.main[1, a]
        if diagonal and a < SUB:
            real = real + jnp.where(sub == a, diagonal, 0.0)
        out.main[0, a] = real
        out.main[1, a] = imag
    ar = [[x.main[0, SUB + a], x.corner[0, a]] for a in range(CORNER)]
    ai = [[x.main[1, SUB + a], x.corner[1, a]] for a in range(CORNER)]
    er = [[yr[SUB + e], y.corner[0, e]] for e in range(CORNER)]
    ei = [[yi[SUB + e], y.corner[1, e]] for e in range(CORNER)]
    for a in range(CORNER):
        for e in range(a, CORNER):
            real = sum(ar[a][h] * er[e][h] + ai[a][h] * ei[e][h] for h in range(2))
            real = jnp.sum(real, axis=0, keepdims=True)
            imag = jnp.zeros_like(real)
            if a != e:
                imag = sum(ai[a][h] * er[e][h] - ar[a][h] * ei[e][h] for h in range(2))
                imag = jnp.sum(imag, axis=0, keepdims=True)
            for factor, term in terms:
                r, i, _ = term.entry(SUB + a, SUB + e)
                real, imag = real + factor * r, imag + factor * i
            if a == e:
                out.put(SUB + a, SUB + a, real + diagonal, jnp.zeros_like(real))
            else:
                out.put(SUB + a, SUB + e, real, imag)
                out.put(SUB + e, SUB + a, real, -imag)


def combine(out, diagonal, terms):
    sub = lax.broadcasted_iota(jnp.int32, (SUB, NFREQ), 0)
    for name, rows in (("main", NBLK), ("corner", CORNER)):
        target = getattr(out, name)
        for a in range(rows):
            real = sum(factor * getattr(term, name)[0, a] for factor, term in terms)
            imag = sum(factor * getattr(term, name)[1, a] for factor, term in terms)
            if diagonal and (name == "corner" or a < SUB):
                real = real + jnp.where(sub == a, diagonal, 0.0)
            target[0, a] = real
            target[1, a] = imag


TWO_STEPS = (2.25, -2.4375, 1.6875, -0.5625, 0.0625)


def inverse_root(w, mats):
    q, u, r, t, w2, z = mats
    c0, c1, c2, c3, c4 = TWO_STEPS
    product(w, w, q)
    combine(u, 0.0, [(c3, w), (c4, q)])
    product(q, u, z, c0, [(c1, w), (c2, q)])
    product(z, z, t)
    product(w, t, w2)
    product(w2, w2, q)
    combine(u, 0.0, [(c3, w2), (c4, q)])
    product(q, u, r, c0, [(c1, w2), (c2, q)])
    product(r, r, t)
    product(z, r, u)
    product(w2, t, q)
    combine(q, 1.5, [(-0.5, q)])
    product(u, q, z)
    return z


def make_roots(share, half_ref, other_ref, gram_ref, packed, rolled, mats):
    core = lax.axis_index("tm") % 2
    packed[pl.ds(pl.multiple_of(core * HALF, HALF), HALF), :] = half_ref[...]
    packed[pl.ds(pl.multiple_of((1 - core) * HALF, HALF), HALF), :] = other_ref[...]
    packed[...] = packed[...].T
    at = lax.axis_index("sx") * lax.axis_size("sy") + lax.axis_index("sy")
    rolled[...] = pltpu.roll(packed[...], (NFREQ - at * share) % NFREQ, 1)
    y, *free = [Hermitian(mats[2 * i], mats[2 * i + 1]) for i in range(MATS)]
    for ref in mats[1::2]:
        ref[...] = jnp.zeros_like(ref)

    def row(ref, part, a, e):
        return ref[pl.ds(ROWS[part, a, e], 1), :]

    trace = 2.0 * sum(row(packed, 0, a, a) for a in range(NBLK))
    norm = 1.0 / jnp.sqrt(trace)
    packed[...] = packed[...] / trace
    zero = jnp.zeros((1, NFREQ), F32)
    for a in range(NBLK):
        y.put(a, a, row(packed, 0, a, a), zero)
        gram_ref[a, a, 0:1, :] = row(rolled, 0, a, a)[:, :share]
        gram_ref[a, a, 1:2, :] = zero[:, :share]
        for e in range(a + 1, NBLK):
            real, imag = row(packed, 0, a, e), row(packed, 1, a, e)
            y.put(a, e, real, imag)
            y.put(e, a, real, -imag)
            real, imag = row(rolled, 0, a, e)[:, :share], row(rolled, 1, a, e)[:, :share]
            gram_ref[a, e, 0:1, :] = real
            gram_ref[e, a, 0:1, :] = real
            gram_ref[a, e, 1:2, :] = imag
            gram_ref[e, a, 1:2, :] = -imag
    z = inverse_root(y, free)
    mean = sum(z.entry(a, a)[0] for a in range(NBLK)) * (1.0 / NBLK)
    sub = lax.broadcasted_iota(jnp.int32, (SUB, NFREQ), 0)
    none = jnp.zeros((SUB - CORNER, NFREQ), F32)
    first = jnp.concatenate([mean * norm, none[1:]], axis=0)
    stacks = []
    for m0 in range(0, NBLK, STACK):
        modes = range(m0, min(m0 + STACK, NBLK))
        stack = []
        for m in modes:
            for c in range(2):
                column = z.main[c, m]
                if c == 0 and m < SUB:
                    column = column - jnp.where(sub == m, mean, 0.0)
                stack.append(column * norm)
                for b in range(SUB, NBLK):
                    real, imag, sign = z.entry(m, b)
                    line = imag * sign if c else real
                    if c == 0 and m == b:
                        line = line - mean
                    stack.append(line * norm)
                stack.append(first if c == 0 and m == 0 else none)
        stack += [jnp.zeros((32, NFREQ), F32)] * (STACK - len(modes))
        stacks.append(jnp.concatenate(stack, axis=0).T)
    return stacks


def mode_kernel(chunks, share, half_ref, other_ref, spread_ref, *refs):
    s_refs = refs[:chunks]
    out_hbm, gram_ref, out, v, mean, packed, rolled, sem, *mats = refs[chunks:]
    stacks = make_roots(share, half_ref, other_ref, gram_ref, packed, rolled, mats)
    mean[...] = jnp.broadcast_to(stacks[0][:, NBLK : NBLK + 1], (NFREQ, LANE))
    row = lax.broadcasted_iota(jnp.int32, (NFREQ, 2 * HALF_ROWS), 0)
    col = lax.broadcasted_iota(jnp.int32, (NFREQ, 2 * HALF_ROWS), 1)
    same = row % SUB == col % SUB
    place = lax.broadcasted_iota(jnp.int32, (NFREQ, LANE), 1) // 32
    rows = [jnp.where(place == m % STACK, stacks[m // STACK], 0.0) for m in range(NBLK)]
    rows = jnp.concatenate(rows, axis=0).astype(BF16)
    for c in range(2):
        wide = dot(rows, spread_ref[c])[:, : 2 * HALF_ROWS]
        for m in range(NBLK):
            v[c * NBLK + m] = jnp.where(same, wide[m * NFREQ : (m + 1) * NFREQ], 0.0)

    copies = []
    for pair in range(GROUPS // 2):
        fields = []
        for g in (2 * pair, 2 * pair + 1):
            at = slice(g * SUB, (g + 1) * SUB)
            s = jnp.concatenate([r[:, at, :] for r in s_refs], axis=2)
            flat = s.reshape(2 * HALF_ROWS, -1).astype(BF16)
            field = dot(v[:, at, :].reshape(2 * HALF_ROWS, 2 * HALF_ROWS).astype(BF16), flat)
            scale = jnp.concatenate([mean[at, :]] * (s.shape[2] // LANE), axis=1)
            fields.append(field.reshape(s.shape) + s * scale[None])
        both = jnp.concatenate(fields, axis=1).astype(BF16)
        at = slice(pair * 2 * SUB, (pair + 1) * 2 * SUB)
        out[:, :, at, :] = both.reshape(2, NBLK, 2 * SUB, -1)
        copies.append(
            pltpu.make_async_copy(out.at[:, :, at, :], out_hbm.at[:, :, at, :], sem.at[pair])
        )
        copies[-1].start()
    for copy in copies:
        copy.wait()


def mode_fields(half, other, spread, spectra, share):
    shape = (2, NBLK, NFREQ, sum(s.shape[2] for s in spectra))
    return pl.pallas_call(
        functools.partial(mode_kernel, len(spectra), share),
        out_shape=[
            jax.ShapeDtypeStruct(shape, BF16),
            jax.ShapeDtypeStruct((NBLK, NBLK, 2, share), F32),
        ],
        in_specs=[VMEM] * (3 + len(spectra)),
        out_specs=[HBM, VMEM],
        scratch_shapes=[
            pltpu.VMEM(shape, BF16),
            pltpu.VMEM((2 * NBLK, NFREQ, 2 * HALF_ROWS), F32),
            pltpu.VMEM((NFREQ, LANE), F32),
            pltpu.VMEM((PACKED, NFREQ), F32),
            pltpu.VMEM((PACKED, NFREQ), F32),
            pltpu.SemaphoreType.DMA((GROUPS // 2,)),
        ]
        + [
            pltpu.VMEM((2, NBLK, SUB, NFREQ), F32),
            pltpu.VMEM((2, CORNER, SUB, NFREQ), F32),
        ]
        * MATS,
        compiler_params=pltpu.CompilerParams(vmem_limit_bytes=32 * 2**20),
    )(half, other, spread, *spectra)


def swap(x, axes, mask, size):
    return lax.ppermute(x, axes, [(i, i ^ mask) for i in range(size)])


def powers(size):
    return [1 << i for i in range(size.bit_length() - 1)]


def body(snapshots, weights, block_order, owner, offsets):
    lanes = lax.axis_size("tm")
    groups = lax.axis_size("sx") * lax.axis_size("sy")
    points = snapshots.shape[2]
    half, quarter = points // 2, points // 4
    chunks = [(0, half), (half, quarter), (half + quarter, quarter)]
    scale = 1.0 / (lanes * groups * points)
    tables = (jnp.asarray(fourier_tables()), jnp.asarray(pick_table()))
    weights = weights.reshape(1, -1)

    def send(packed, begin, end):
        return [swap(p, "tm", d, lanes) for d, p in zip(range(begin, end), packed)]

    c0, c1, c2 = chunks
    first, table = pack(owner, snapshots, [(*c0, lanes - 1, lanes)], True)
    first = send([first], lanes - 1, lanes)
    middle = pack(table, snapshots, [(*c0, 0, lanes - 1), (*c1, NEAR, lanes)], False)
    jobs = [(c1[0], c1[1] + c2[1], 0, NEAR), (*c2, NEAR, lanes)]
    rest = pack(table, snapshots, jobs, False, first)
    near = [rest[0], *send(rest[1:], 1, NEAR)]
    arrived = [
        [middle[0], *send(middle[1:], 1, lanes - 1), *first],
        [*near, *send(middle[lanes - 1 :], NEAR, lanes)],
        [*near, *send(rest[NEAR:], NEAR, lanes)],
    ]
    starts = (0, 0, c1[1])

    axes = ("tm", "sx", "sy")
    size = lanes * groups
    bits = [b * groups for b in powers(lanes)] + powers(groups)
    parts = [weights[:, base : base + width] for base, width in chunks]
    before = []
    for at, base in enumerate(starts):
        last = at == len(chunks) - 1
        args = (block_order, offsets, parts[at], tables, arrived[at], before, base, last, scale)
        before, before_last = gram_part(*args), before
    before, (given, scaled) = before_last, before

    other = swap(given, axes, bits[0], size)
    keep = own_part(scaled, tables[1], before[0], scale)
    spectra = [
        spectrum(block_order, offsets, tables[0], pieces, base, [keep])
        for base, pieces in zip(starts, arrived)
    ]
    half = keep.astype(F32) + other.astype(F32)
    for at in range(1, len(bits), 2):
        masks = bits[at : at + 2]
        if len(masks) == 2:
            masks.append(masks[0] ^ masks[1])
            masks = masks[1:] + masks[:1] if at > 1 else masks
        half = half.astype(BF16)
        terms = [half] + [swap(half, axes, mask, size) for mask in masks]
        terms = [t.astype(F32) for t in terms]
        while len(terms) > 1:
            terms = [a + b for a, b in zip(terms[::2], terms[1::2])]
        half = terms[0]
        if at == 1:
            half, *spectra[1:] = lax.optimization_barrier((half, *spectra[1:]))
    half, spectra[0] = lax.optimization_barrier((half, spectra[0]))
    other = swap(half, axes, bits[0], size)

    spread = jnp.asarray(spread_table())
    modes, gram = mode_fields(half, other, spread, spectra, NFREQ // groups)
    modes = jnp.transpose(modes, (0, 2, 1, 3))[:, :, :, None, :]
    return modes, jnp.transpose(gram, (2, 3, 0, 1))


def solution(mesh):
    placed = (P("tm", None, ("sx", "sy")), P(("sx", "sy")), P(), P(("sx", "sy"), None), P())
    return jax.shard_map(
        body,
        mesh=mesh,
        in_specs=placed,
        out_specs=(P(None, None, None, "tm", ("sx", "sy")), P(None, ("sx", "sy"), None, None)),
        check_vma=False,
    )
```

```python
import functools
import math

import jax
import jax.numpy as jnp
import numpy as np
from jax import lax
from jax.experimental import pallas as pl
from jax.experimental.pallas import tpu as pltpu
from jax.sharding import PartitionSpec as P

NFFT = 256
NFREQ = 128
NBLK = 11
LANE = 128
SUB = 8
HALF_ROWS = NBLK * SUB
GROUPS = NFREQ // SUB
MATS = 7
NEAR = 2
PACKED = 128
HALF = PACKED // 2
STACK = 4
CORNER = NBLK - SUB
WIDE = 2 * LANE
FIRST_LIMIT = 64 * 2**20
SECOND_LIMIT = FIRST_LIMIT - 1450 * 2**10
LAST_LIMIT = 40 * 2**20
BF16 = jnp.bfloat16
F32 = jnp.float32


def fourier_tables():
    n = np.arange(NFFT)
    k = np.arange(NFREQ)
    angles = 2.0 * np.pi * ((k[:, None] * n[None, :]) % NFFT) / NFFT
    scaled = (0.5 - 0.5 * np.cos(2.0 * np.pi * n / NFFT)) / math.sqrt(0.375 * NFFT)
    table = np.concatenate([np.cos(angles) * scaled, -np.sin(angles) * scaled], axis=0)
    high = table.astype(jnp.bfloat16)
    low = (table - high.astype(np.float64)).astype(jnp.bfloat16)
    return np.concatenate([high, low], axis=0)


def packed_rows():
    rows = {}
    for a in range(NBLK):
        for e in range(a, NBLK):
            rows[0, a, e] = len(rows)
        for e in range(a + 1, NBLK):
            rows[1, a, e] = len(rows)
    return rows


ROWS = packed_rows()


def pick_table():
    pick = np.zeros((NBLK, 2, LANE, PACKED), np.float32)
    for (part, a, e), row in ROWS.items():
        pick[a, part, e * SUB : (e + 1) * SUB, row] = 1.0
    return pick.reshape(NBLK * WIDE, PACKED).astype(jnp.bfloat16)


def spread_table():
    spread = np.zeros((2, STACK, 2, 16, WIDE), np.float32)
    for b in range(NBLK):
        first = slice(b * SUB, b * SUB + SUB)
        second = slice(HALF_ROWS + b * SUB, HALF_ROWS + b * SUB + SUB)
        spread[0, :, 0, b, first] = 1.0
        spread[0, :, 1, b, second] = 1.0
        spread[1, :, 1, b, first] = -1.0
        spread[1, :, 0, b, second] = 1.0
    return spread.reshape(2, LANE, WIDE).astype(jnp.bfloat16)


def dot(a, b):
    return jnp.dot(a, b, preferred_element_type=F32)


def dot_nt(a, b):
    return lax.dot_general(a, b, (((1,), (1,)), ((), ())), preferred_element_type=F32)


def spec(shape):
    return pl.BlockSpec(shape, lambda *_: (0,) * len(shape))


SMEM = pl.BlockSpec(memory_space=pltpu.SMEM)
VMEM = pl.BlockSpec(memory_space=pltpu.VMEM)
HBM = pl.BlockSpec(memory_space=pltpu.HBM)


def lane_pick(owner, lanes, begin, end):
    me = lax.axis_index("tm")
    rows = WIDE // lanes
    shape = ((end - begin) * rows, WIDE)
    out_row = lax.broadcasted_iota(jnp.int32, shape, 0)
    in_row = lax.broadcasted_iota(jnp.int32, shape, 1)
    row_of = (out_row % rows) * lanes
    for d in range(begin, end):
        slot = me ^ d
        source = jnp.int32(0)
        for lane in range(lanes):
            source = source + jnp.where(owner[0, lane] == slot, lane, 0)
        row_of = jnp.where(out_row // rows == d - begin, row_of + source, row_of)
    return jnp.where(in_row == row_of, 1.0, 0.0).astype(BF16)


def pack_kernel(jobs, parts, follows, owner_hbm, x_hbm, *refs):
    steps, lanes, _ = x_hbm.shape
    base = jobs[0][0]
    *outs, owner, pick, x_ref, owner_sem, x_sem = refs[follows:]
    part = steps // parts
    owner_copy = pltpu.make_async_copy(owner_hbm, owner, owner_sem)
    owner_copy.start()
    copies = []
    for i in range(parts):
        at = slice(i * part, (i + 1) * part)
        source = x_hbm.at[at, :, base : base + x_ref.shape[2]]
        copies.append(pltpu.make_async_copy(source, x_ref.at[at], x_sem.at[i]))
        copies[-1].start()
    owner_copy.wait()
    lowest = min(begin for _, _, begin, _ in jobs)
    pick[...] = lane_pick(owner, lanes, lowest, max(end for _, _, _, end in jobs))
    rows = WIDE // lanes
    for i in range(parts):
        copies[i].wait()
        for start in range(i * part, (i + 1) * part, rows):
            at = slice(start, start + rows)
            x = x_ref[at].reshape(WIDE, x_ref.shape[2])
            out = iter(outs)
            for job, width, begin, end in jobs:
                here = x[:, job - base : job - base + width]
                chosen = pick[(begin - lowest) * rows : (end - lowest) * rows, :]
                y = dot(chosen, here).astype(BF16)
                for d in range(end - begin):
                    next(out)[at, :] = y[d * rows : (d + 1) * rows]


def pack(owner, snapshots, jobs, limit, after=()):
    steps, lanes, _ = snapshots.shape
    parts = math.gcd(steps * lanes // WIDE, 3)
    outs = [
        jax.ShapeDtypeStruct((steps, width), BF16)
        for _, width, begin, end in jobs
        for _ in range(begin, end)
    ]
    columns = jobs[-1][0] + jobs[-1][1] - jobs[0][0]
    partners = max(end for _, _, _, end in jobs) - min(begin for _, _, begin, _ in jobs)
    return pl.pallas_call(
        functools.partial(pack_kernel, jobs, parts, len(after)),
        out_shape=outs,
        in_specs=[HBM] * (2 + len(after)),
        out_specs=[VMEM] * len(outs),
        scratch_shapes=[
            pltpu.SMEM(owner.shape, jnp.int32),
            pltpu.VMEM((partners * (WIDE // lanes), WIDE), BF16),
            pltpu.VMEM((steps, lanes, columns), BF16),
            pltpu.SemaphoreType.DMA,
            pltpu.SemaphoreType.DMA((parts,)),
        ],
        compiler_params=pltpu.CompilerParams(vmem_limit_bytes=limit),
        cost_estimate=pl.CostEstimate(flops=1000, bytes_accessed=1000, transcendentals=0),
    )(owner, snapshots, *after)


def fill_record(base, order_ref, pieces, record, factor):
    steps = pieces[0].shape[0]
    me = lax.axis_index("tm")
    for d, piece in enumerate(pieces):
        start = pl.multiple_of(order_ref[me ^ d] * steps, steps)
        for c in range(record.shape[0]):
            at = c * LANE + (base if d < NEAR else 0)
            part = piece[:, at : at + LANE].astype(F32)
            if factor is not None:
                part = part * factor[:, c * LANE : (c + 1) * LANE]
            record[c, pl.ds(start, steps), :] = part


def transform(offsets_ref, f, record, s_ref):
    wanted = [(i, c) for i in range(NBLK) for c in range(record.shape[0])]
    for first in range(0, len(wanted), 2):
        pair = wanted[first : first + 2]
        x = [record[c, pl.ds(offsets_ref[i], NFFT), :].astype(BF16) for i, c in pair]
        x = jnp.concatenate(x, axis=1) if len(x) > 1 else x[0]
        y = dot(f, x)
        if f.shape[0] > NFFT:
            y = y[:NFFT] + y[NFFT:]
        for at, (i, c) in enumerate(pair):
            cols = slice(c * LANE, (c + 1) * LANE)
            s_ref[i, :, cols] = y[:NFREQ, at * LANE : (at + 1) * LANE]
            s_ref[NBLK + i, :, cols] = y[NFREQ:, at * LANE : (at + 1) * LANE]


def padded(s):
    width = s.shape[2]
    pad = jnp.zeros((LANE - HALF_ROWS, width), F32)
    real = s[:NBLK].reshape(HALF_ROWS, width)
    imag = s[NBLK:].reshape(HALF_ROWS, width)
    return jnp.concatenate([real, pad, imag, pad], axis=0)


def gram_rows(base, groups, s_ref, pick_ref, masked):
    row = lax.broadcasted_iota(jnp.int32, (HALF_ROWS, LANE), 0)
    col = lax.broadcasted_iota(jnp.int32, (HALF_ROWS, LANE), 1)
    same = row % SUB == col % SUB
    for pair in range(0, groups, 2):
        blocks = []
        for g in (pair, pair + 1):
            s = s_ref[:, pl.ds(pl.multiple_of(base + g * SUB, SUB), SUB), :]
            full = dot_nt(s.reshape(2 * HALF_ROWS, -1).astype(BF16), padded(s).astype(BF16))
            real = full[:HALF_ROWS, :LANE] + full[HALF_ROWS:, LANE:]
            imag = full[:HALF_ROWS, LANE:] - full[HALF_ROWS:, :LANE]
            blocks.append([jnp.where(same, part, 0.0) for part in (real, imag)])
        at = slice(pair * SUB, (pair + 2) * SUB)
        for a in range(NBLK):
            rows = slice(a * SUB, (a + 1) * SUB)
            for part in range(2):
                both = jnp.concatenate([block[part][rows] for block in blocks], axis=0)
                cols = slice(a * WIDE + part * LANE, a * WIDE + (part + 1) * LANE)
                masked[at, cols] = both.astype(BF16)
    return dot(masked[...], pick_ref[...])


def gram_kernel(lanes, base, scale, last, order_ref, offsets_ref, w_ref, f_ref, pick_ref, *refs):
    pieces = refs[:lanes]
    refs = refs[lanes:]
    if last:
        before_ref, gram_ref, s_ref, record, masked = refs
    else:
        *before_refs, gram_ref, record, s_ref, masked = refs
    fill_record(base, order_ref, pieces, record, jnp.sqrt(w_ref[...]))
    transform(offsets_ref, f_ref[:NFFT] if last else f_ref[...], record, s_ref)
    if not last:
        total = gram_rows(0, GROUPS, s_ref, pick_ref, masked) * scale
        gram_ref[...] = total + before_refs[0][...] if before_refs else total
        return
    half = pl.multiple_of((1 - lax.axis_index("tm") % 2) * HALF, HALF)
    total = gram_rows(half, GROUPS // 2, s_ref, pick_ref, masked) * scale
    gram_ref[...] = (total + before_ref[pl.ds(half, HALF), :]).astype(BF16)


def gram_part(order, offsets, weights, tables, pieces, before, base, last, scale):
    lanes = len(pieces)
    steps, width = pieces[-1].shape
    args = [order, offsets, weights, *tables, *pieces, *before]
    spectrum_shape = (2 * NBLK, NFREQ, width)
    scratch = [pltpu.VMEM((width // LANE, lanes * steps, LANE), F32)]
    if last:
        outs = [jax.ShapeDtypeStruct((HALF, PACKED), BF16)]
        outs.append(jax.ShapeDtypeStruct(spectrum_shape, F32))
    else:
        outs = [jax.ShapeDtypeStruct((NFREQ, PACKED), F32)]
        scratch.append(pltpu.VMEM(spectrum_shape, F32))
    scratch.append(pltpu.VMEM((HALF if last else NFREQ, NBLK * WIDE), BF16))
    return pl.pallas_call(
        functools.partial(gram_kernel, lanes, base, scale, last),
        out_shape=outs,
        in_specs=[SMEM, SMEM] + [VMEM] * (len(args) - 2),
        out_specs=[VMEM] * len(outs),
        scratch_shapes=scratch,
        compiler_params=pltpu.CompilerParams(vmem_limit_bytes=32 * 2**20),
        cost_estimate=pl.CostEstimate(flops=1000, bytes_accessed=1000, transcendentals=0),
    )(*args)


def own_kernel(scale, s_ref, pick_ref, before_ref, gram_ref, masked):
    base = pl.multiple_of(lax.axis_index("tm") % 2 * HALF, HALF)
    total = gram_rows(base, GROUPS // 2, s_ref, pick_ref, masked) * scale
    gram_ref[...] = (total + before_ref[pl.ds(base, HALF), :]).astype(BF16)


def own_part(scaled, pick, before, scale):
    return pl.pallas_call(
        functools.partial(own_kernel, scale),
        out_shape=jax.ShapeDtypeStruct((HALF, PACKED), BF16),
        in_specs=[VMEM] * 3,
        out_specs=VMEM,
        scratch_shapes=[pltpu.VMEM((HALF, NBLK * WIDE), BF16)],
        compiler_params=pltpu.CompilerParams(vmem_limit_bytes=32 * 2**20),
        cost_estimate=pl.CostEstimate(flops=10**9, bytes_accessed=3 * 10**6, transcendentals=0),
    )(scaled, pick, before)


def spectrum_kernel(lanes, base, order_ref, offsets_ref, f_ref, *refs):
    s_ref, record = refs[-2:]
    fill_record(base, order_ref, refs[:lanes], record, None)
    transform(offsets_ref, f_ref[...], record, s_ref)


def spectrum(order, offsets, fourier, pieces, base, after):
    lanes = len(pieces)
    steps, width = pieces[-1].shape
    args = [order, offsets, fourier, *pieces, *after]
    return pl.pallas_call(
        functools.partial(spectrum_kernel, lanes, base),
        out_shape=jax.ShapeDtypeStruct((2 * NBLK, NFREQ, width), F32),
        in_specs=[SMEM, SMEM] + [VMEM] * (len(args) - 2),
        out_specs=VMEM,
        scratch_shapes=[pltpu.VMEM((width // LANE, lanes * steps, LANE), F32)],
        compiler_params=pltpu.CompilerParams(vmem_limit_bytes=32 * 2**20),
        cost_estimate=pl.CostEstimate(flops=1000, bytes_accessed=1000, transcendentals=0),
    )(*args)


class Hermitian:
    def __init__(self, main, corner):
        self.main = main
        self.corner = corner

    def entry(self, a, e):
        if e < SUB:
            return self.main[0, a, pl.ds(e, 1), :], self.main[1, a, pl.ds(e, 1), :], 1
        if a < SUB:
            return self.main[0, e, pl.ds(a, 1), :], self.main[1, e, pl.ds(a, 1), :], -1
        at = pl.ds(e - SUB, 1)
        return self.corner[0, a - SUB, at, :], self.corner[1, a - SUB, at, :], 1

    def put(self, a, e, real, imag):
        if e < SUB:
            self.main[0, a, pl.ds(e, 1), :] = real
            self.main[1, a, pl.ds(e, 1), :] = imag
        elif a >= SUB:
            at = pl.ds(e - SUB, 1)
            self.corner[0, a - SUB, at, :] = real
            self.corner[1, a - SUB, at, :] = imag


def product(x, y, out, sums, diagonal=0.0, terms=()):
    sub = lax.broadcasted_iota(jnp.int32, (SUB, NFREQ), 0)
    yr = [y.main[0, b] for b in range(NBLK)]
    yi = [y.main[1, b] for b in range(NBLK)]
    minus = [yi[b] - yr[b] for b in range(NBLK)]
    plus = [yi[b] + yr[b] for b in range(NBLK)]
    for a in range(NBLK):
        sums[a] = x.main[0, a] + x.main[1, a]
    for a in range(CORNER):
        sums[NBLK + a] = x.corner[0, a] + x.corner[1, a]
        sums[NBLK + CORNER + a] = x.main[0, SUB + a] - x.main[1, SUB + a]
    for a in range(NBLK):
        k1 = k2 = k3 = None
        for b in range(NBLK):
            pr, pi, sign = x.entry(a, b)
            if b < SUB:
                both = sums[a, pl.ds(b, 1), :]
            elif a < SUB:
                both = sums[NBLK + CORNER + b - SUB, pl.ds(a, 1), :]
            else:
                both = sums[NBLK + a - SUB, pl.ds(b - SUB, 1), :]
            t1, t2, t3 = both * yr[b], pr * minus[b], pi * plus[b]
            k1 = t1 if k1 is None else k1 + t1
            k2 = t2 if k2 is None else k2 + t2
            k3 = t3 if k3 is None else k3 + t3 if sign > 0 else k3 - t3
        real, imag = k1 - k3, k1 + k2
        for factor, term in terms:
            real = real + factor * term.main[0, a]
            imag = imag + factor * term.main[1, a]
        if diagonal and a < SUB:
            real = real + jnp.where(sub == a, diagonal, 0.0)
        out.main[0, a] = real
        out.main[1, a] = imag
    ar = [[x.main[0, SUB + a], x.corner[0, a]] for a in range(CORNER)]
    ai = [[x.main[1, SUB + a], x.corner[1, a]] for a in range(CORNER)]
    er = [[yr[SUB + e], y.corner[0, e]] for e in range(CORNER)]
    ei = [[yi[SUB + e], y.corner[1, e]] for e in range(CORNER)]
    for a in range(CORNER):
        for e in range(a, CORNER):
            real = sum(ar[a][h] * er[e][h] + ai[a][h] * ei[e][h] for h in range(2))
            real = jnp.sum(real, axis=0, keepdims=True)
            imag = jnp.zeros_like(real)
            if a != e:
                imag = sum(ai[a][h] * er[e][h] - ar[a][h] * ei[e][h] for h in range(2))
                imag = jnp.sum(imag, axis=0, keepdims=True)
            for factor, term in terms:
                r, i, _ = term.entry(SUB + a, SUB + e)
                real, imag = real + factor * r, imag + factor * i
            if a == e:
                out.put(SUB + a, SUB + a, real + diagonal, jnp.zeros_like(real))
            else:
                out.put(SUB + a, SUB + e, real, imag)
                out.put(SUB + e, SUB + a, real, -imag)


def combine(out, diagonal, terms):
    sub = lax.broadcasted_iota(jnp.int32, (SUB, NFREQ), 0)
    for name, rows in (("main", NBLK), ("corner", CORNER)):
        target = getattr(out, name)
        for a in range(rows):
            real = sum(factor * getattr(term, name)[0, a] for factor, term in terms)
            imag = sum(factor * getattr(term, name)[1, a] for factor, term in terms)
            if diagonal and (name == "corner" or a < SUB):
                real = real + jnp.where(sub == a, diagonal, 0.0)
            target[0, a] = real
            target[1, a] = imag


TWO_STEPS = (2.25, -2.4375, 1.6875, -0.5625, 0.0625)


def inverse_root(w, mats, sums):
    q, u, r, t, w2, z = mats
    c0, c1, c2, c3, c4 = TWO_STEPS
    product(w, w, q, sums)
    combine(u, 0.0, [(c3, w), (c4, q)])
    product(q, u, z, sums, c0, [(c1, w), (c2, q)])
    product(z, z, t, sums)
    product(w, t, w2, sums)
    product(w2, w2, q, sums)
    combine(u, 0.0, [(c3, w2), (c4, q)])
    product(q, u, r, sums, c0, [(c1, w2), (c2, q)])
    product(r, r, t, sums)
    product(z, r, u, sums)
    product(w2, t, q, sums)
    combine(q, 1.5, [(-0.5, q)])
    product(u, q, z, sums)
    return z


def make_roots(share, half_ref, other_ref, gram_ref, packed, rolled, sums, mats):
    core = lax.axis_index("tm") % 2
    packed[pl.ds(pl.multiple_of(core * HALF, HALF), HALF), :] = half_ref[...]
    packed[pl.ds(pl.multiple_of((1 - core) * HALF, HALF), HALF), :] = other_ref[...]
    packed[...] = packed[...].T
    at = lax.axis_index("sx") * lax.axis_size("sy") + lax.axis_index("sy")
    rolled[...] = pltpu.roll(packed[...], (NFREQ - at * share) % NFREQ, 1)
    y, *free = [Hermitian(mats[2 * i], mats[2 * i + 1]) for i in range(MATS)]
    for ref in mats[1::2]:
        ref[...] = jnp.zeros_like(ref)

    def row(ref, part, a, e):
        return ref[pl.ds(ROWS[part, a, e], 1), :]

    trace = 2.0 * sum(row(packed, 0, a, a) for a in range(NBLK))
    norm = 1.0 / jnp.sqrt(trace)
    packed[...] = packed[...] / trace
    zero = jnp.zeros((1, NFREQ), F32)
    for a in range(NBLK):
        y.put(a, a, row(packed, 0, a, a), zero)
        gram_ref[a, a, 0:1, :] = row(rolled, 0, a, a)[:, :share]
        gram_ref[a, a, 1:2, :] = zero[:, :share]
        for e in range(a + 1, NBLK):
            real, imag = row(packed, 0, a, e), row(packed, 1, a, e)
            y.put(a, e, real, imag)
            y.put(e, a, real, -imag)
            real, imag = row(rolled, 0, a, e)[:, :share], row(rolled, 1, a, e)[:, :share]
            gram_ref[a, e, 0:1, :] = real
            gram_ref[e, a, 0:1, :] = real
            gram_ref[a, e, 1:2, :] = imag
            gram_ref[e, a, 1:2, :] = -imag
    z = inverse_root(y, free, sums)
    mean = sum(z.entry(a, a)[0] for a in range(NBLK)) * (1.0 / NBLK)
    sub = lax.broadcasted_iota(jnp.int32, (SUB, NFREQ), 0)
    none = jnp.zeros((SUB - CORNER, NFREQ), F32)
    first = jnp.concatenate([mean * norm, none[1:]], axis=0)
    stacks = []
    for m0 in range(0, NBLK, STACK):
        modes = range(m0, min(m0 + STACK, NBLK))
        stack = []
        for m in modes:
            for c in range(2):
                column = z.main[c, m]
                if c == 0 and m < SUB:
                    column = column - jnp.where(sub == m, mean, 0.0)
                stack.append(column * norm)
                for b in range(SUB, NBLK):
                    real, imag, sign = z.entry(m, b)
                    line = imag * sign if c else real
                    if c == 0 and m == b:
                        line = line - mean
                    stack.append(line * norm)
                stack.append(first if c == 0 and m == 0 else none)
        stack += [jnp.zeros((32, NFREQ), F32)] * (STACK - len(modes))
        stacks.append(jnp.concatenate(stack, axis=0).T)
    return stacks


def mode_kernel(chunks, share, half_ref, other_ref, spread_ref, *refs):
    s_refs = refs[:chunks]
    out_hbm, gram_ref, out, v, mean, packed, rolled, sums, sem, *mats = refs[chunks:]
    stacks = make_roots(share, half_ref, other_ref, gram_ref, packed, rolled, sums, mats)
    mean[...] = jnp.broadcast_to(stacks[0][:, NBLK : NBLK + 1], (NFREQ, LANE))
    row = lax.broadcasted_iota(jnp.int32, (NFREQ, 2 * HALF_ROWS), 0)
    col = lax.broadcasted_iota(jnp.int32, (NFREQ, 2 * HALF_ROWS), 1)
    same = row % SUB == col % SUB
    place = lax.broadcasted_iota(jnp.int32, (NFREQ, LANE), 1) // 32
    rows = [jnp.where(place == m % STACK, stacks[m // STACK], 0.0) for m in range(NBLK)]
    rows = jnp.concatenate(rows, axis=0).astype(BF16)
    for c in range(2):
        wide = dot(rows, spread_ref[c])[:, : 2 * HALF_ROWS]
        for m in range(NBLK):
            v[c * NBLK + m] = jnp.where(same, wide[m * NFREQ : (m + 1) * NFREQ], 0.0)

    copies = []
    for pair in range(GROUPS // 2):
        fields = []
        for g in (2 * pair, 2 * pair + 1):
            at = slice(g * SUB, (g + 1) * SUB)
            s = jnp.concatenate([r[:, at, :] for r in s_refs], axis=2)
            flat = s.reshape(2 * HALF_ROWS, -1).astype(BF16)
            field = dot(v[:, at, :].reshape(2 * HALF_ROWS, 2 * HALF_ROWS).astype(BF16), flat)
            scale = jnp.concatenate([mean[at, :]] * (s.shape[2] // LANE), axis=1)
            fields.append(field.reshape(s.shape) + s * scale[None])
        both = jnp.concatenate(fields, axis=1).astype(BF16)
        at = slice(pair * 2 * SUB, (pair + 1) * 2 * SUB)
        out[:, :, at, :] = both.reshape(2, NBLK, 2 * SUB, -1)
        copies.append(
            pltpu.make_async_copy(out.at[:, :, at, :], out_hbm.at[:, :, at, :], sem.at[pair])
        )
        copies[-1].start()
    for copy in copies:
        copy.wait()


def mode_fields(half, other, spread, spectra, share):
    shape = (2, NBLK, NFREQ, sum(s.shape[2] for s in spectra))
    return pl.pallas_call(
        functools.partial(mode_kernel, len(spectra), share),
        out_shape=[
            jax.ShapeDtypeStruct(shape, BF16),
            jax.ShapeDtypeStruct((NBLK, NBLK, 2, share), F32),
        ],
        in_specs=[VMEM] * (3 + len(spectra)),
        out_specs=[HBM, VMEM],
        scratch_shapes=[
            pltpu.VMEM(shape, BF16),
            pltpu.VMEM((2 * NBLK, NFREQ, 2 * HALF_ROWS), F32),
            pltpu.VMEM((NFREQ, LANE), F32),
            pltpu.VMEM((PACKED, NFREQ), F32),
            pltpu.VMEM((PACKED, NFREQ), F32),
            pltpu.VMEM((NBLK + 2 * CORNER, SUB, NFREQ), F32),
            pltpu.SemaphoreType.DMA((GROUPS // 2,)),
        ]
        + [
            pltpu.VMEM((2, NBLK, SUB, NFREQ), F32),
            pltpu.VMEM((2, CORNER, SUB, NFREQ), F32),
        ]
        * MATS,
        compiler_params=pltpu.CompilerParams(vmem_limit_bytes=32 * 2**20),
    )(half, other, spread, *spectra)


def swap(x, axes, mask, size):
    return lax.ppermute(x, axes, [(i, i ^ mask) for i in range(size)])


def powers(size):
    return [1 << i for i in range(size.bit_length() - 1)]


def body(snapshots, weights, block_order, owner, offsets):
    lanes = lax.axis_size("tm")
    groups = lax.axis_size("sx") * lax.axis_size("sy")
    points = snapshots.shape[2]
    half, quarter = points // 2, points // 4
    chunks = [(0, half), (half, quarter), (half + quarter, quarter)]
    scale = 1.0 / (lanes * groups * points)
    tables = (jnp.asarray(fourier_tables()), jnp.asarray(pick_table()))
    weights = weights.reshape(1, -1)

    def send(packed, begin, end):
        return [swap(p, "tm", d, lanes) for d, p in zip(range(begin, end), packed)]

    c0, c1, c2 = chunks
    packed = pack(owner, snapshots, [(*c0, lanes - 1, lanes)], FIRST_LIMIT)
    first = send(packed, lanes - 1, lanes)
    jobs = [(*c0, 0, lanes - 1), (*c1, NEAR, lanes)]
    middle = pack(owner, snapshots, jobs, SECOND_LIMIT, packed)
    jobs = [(c1[0], c1[1] + c2[1], 0, NEAR), (*c2, NEAR, lanes)]
    rest = pack(owner, snapshots, jobs, LAST_LIMIT, [*first, middle[0]])
    near = [rest[0], *send(rest[1:], 1, NEAR)]
    arrived = [
        [middle[0], *send(middle[1:], 1, lanes - 1), *first],
        [*near, *send(middle[lanes - 1 :], NEAR, lanes)],
        [*near, *send(rest[NEAR:], NEAR, lanes)],
    ]
    starts = (0, 0, c1[1])

    axes = ("tm", "sx", "sy")
    size = lanes * groups
    bits = [b * groups for b in powers(lanes)] + powers(groups)
    parts = [weights[:, base : base + width] for base, width in chunks]
    before = []
    for at, base in enumerate(starts):
        last = at == len(chunks) - 1
        args = (block_order, offsets, parts[at], tables, arrived[at], before, base, last, scale)
        before, before_last = gram_part(*args), before
    before, (given, scaled) = before_last, before

    other = swap(given, axes, bits[0], size)
    keep = own_part(scaled, tables[1], before[0], scale)
    spectra = [
        spectrum(block_order, offsets, tables[0], pieces, base, [keep])
        for base, pieces in zip(starts, arrived)
    ]
    half = keep.astype(F32) + other.astype(F32)
    for at in range(1, len(bits), 2):
        masks = bits[at : at + 2]
        if len(masks) == 2:
            masks.append(masks[0] ^ masks[1])
            masks = masks[1:] + masks[:1] if at > 1 else masks
        half = half.astype(BF16)
        terms = [half] + [swap(half, axes, mask, size) for mask in masks]
        terms = [t.astype(F32) for t in terms]
        while len(terms) > 1:
            terms = [a + b for a, b in zip(terms[::2], terms[1::2])]
        half = terms[0]
        if at == 1:
            half, *spectra[1:] = lax.optimization_barrier((half, *spectra[1:]))
    half, spectra[0] = lax.optimization_barrier((half, spectra[0]))
    other = swap(half, axes, bits[0], size)

    spread = jnp.asarray(spread_table())
    modes, gram = mode_fields(half, other, spread, spectra, NFREQ // groups)
    modes = jnp.transpose(modes, (0, 2, 1, 3))[:, :, :, None, :]
    return modes, jnp.transpose(gram, (2, 3, 0, 1))


def solution(mesh):
    placed = (P("tm", None, ("sx", "sy")), P(("sx", "sy")), P(), P(("sx", "sy"), None), P())
    return jax.shard_map(
        body,
        mesh=mesh,
        in_specs=placed,
        out_specs=(P(None, None, None, "tm", ("sx", "sy")), P(None, ("sx", "sy"), None, None)),
        check_vma=False,
    )
```

```python
import functools
import math

import jax
import jax.numpy as jnp
import numpy as np
from jax import lax
from jax.experimental import pallas as pl
from jax.experimental.pallas import tpu as pltpu
from jax.sharding import PartitionSpec as P

NFFT = 256
NFREQ = 128
NBLK = 11
LANE = 128
SUB = 8
HALF_ROWS = NBLK * SUB
GROUPS = NFREQ // SUB
MATS = 7
NEAR = 2
PACKED = 128
HALF = PACKED // 2
STACK = 4
CORNER = NBLK - SUB
WIDE = 2 * LANE
FIRST_LIMIT = 64 * 2**20
SECOND_LIMIT = FIRST_LIMIT - 1450 * 2**10
LAST_LIMIT = 40 * 2**20
BF16 = jnp.bfloat16
F32 = jnp.float32


def fourier_tables():
    n = np.arange(NFFT)
    k = np.arange(NFREQ)
    angles = 2.0 * np.pi * ((k[:, None] * n[None, :]) % NFFT) / NFFT
    scaled = (0.5 - 0.5 * np.cos(2.0 * np.pi * n / NFFT)) / math.sqrt(0.375 * NFFT)
    table = np.concatenate([np.cos(angles) * scaled, -np.sin(angles) * scaled], axis=0)
    high = table.astype(jnp.bfloat16)
    low = (table - high.astype(np.float64)).astype(jnp.bfloat16)
    return np.concatenate([high, low], axis=0)


def packed_rows():
    rows = {}
    for a in range(NBLK):
        for e in range(a, NBLK):
            rows[0, a, e] = len(rows)
        for e in range(a + 1, NBLK):
            rows[1, a, e] = len(rows)
    return rows


ROWS = packed_rows()


def pick_table():
    pick = np.zeros((NBLK, 2, LANE, PACKED), np.float32)
    for (part, a, e), row in ROWS.items():
        pick[a, part, e * SUB : (e + 1) * SUB, row] = 1.0
    return pick.reshape(NBLK * WIDE, PACKED).astype(jnp.bfloat16)


def spread_table():
    spread = np.zeros((2, STACK, 2, 16, WIDE), np.float32)
    for b in range(NBLK):
        first = slice(b * SUB, b * SUB + SUB)
        second = slice(HALF_ROWS + b * SUB, HALF_ROWS + b * SUB + SUB)
        spread[0, :, 0, b, first] = 1.0
        spread[0, :, 1, b, second] = 1.0
        spread[1, :, 1, b, first] = -1.0
        spread[1, :, 0, b, second] = 1.0
    return spread.reshape(2, LANE, WIDE).astype(jnp.bfloat16)


def dot(a, b):
    return jnp.dot(a, b, preferred_element_type=F32)


def dot_nt(a, b):
    return lax.dot_general(a, b, (((1,), (1,)), ((), ())), preferred_element_type=F32)


def spec(shape):
    return pl.BlockSpec(shape, lambda *_: (0,) * len(shape))


SMEM = pl.BlockSpec(memory_space=pltpu.SMEM)
VMEM = pl.BlockSpec(memory_space=pltpu.VMEM)
HBM = pl.BlockSpec(memory_space=pltpu.HBM)


def lane_pick(owner, lanes, begin, end):
    me = lax.axis_index("tm")
    rows = WIDE // lanes
    shape = ((end - begin) * rows, WIDE)
    out_row = lax.broadcasted_iota(jnp.int32, shape, 0)
    in_row = lax.broadcasted_iota(jnp.int32, shape, 1)
    row_of = (out_row % rows) * lanes
    for d in range(begin, end):
        slot = me ^ d
        source = jnp.int32(0)
        for lane in range(lanes):
            source = source + jnp.where(owner[0, lane] == slot, lane, 0)
        row_of = jnp.where(out_row // rows == d - begin, row_of + source, row_of)
    return jnp.where(in_row == row_of, 1.0, 0.0).astype(BF16)


def pack_kernel(jobs, parts, follows, owner_hbm, x_hbm, *refs):
    steps, lanes, _ = x_hbm.shape
    base = jobs[0][0]
    *outs, owner, pick, x_ref, owner_sem, x_sem = refs[follows:]
    part = steps // parts
    owner_copy = pltpu.make_async_copy(owner_hbm, owner, owner_sem)
    owner_copy.start()
    copies = []
    for i in range(parts):
        at = slice(i * part, (i + 1) * part)
        source = x_hbm.at[at, :, base : base + x_ref.shape[2]]
        copies.append(pltpu.make_async_copy(source, x_ref.at[at], x_sem.at[i]))
        copies[-1].start()
    owner_copy.wait()
    lowest = min(begin for _, _, begin, _ in jobs)
    pick[...] = lane_pick(owner, lanes, lowest, max(end for _, _, _, end in jobs))
    rows = WIDE // lanes
    for i in range(parts):
        copies[i].wait()
        for start in range(i * part, (i + 1) * part, rows):
            at = slice(start, start + rows)
            x = x_ref[at].reshape(WIDE, x_ref.shape[2])
            out = iter(outs)
            for job, width, begin, end in jobs:
                here = x[:, job - base : job - base + width]
                chosen = pick[(begin - lowest) * rows : (end - lowest) * rows, :]
                y = dot(chosen, here).astype(BF16)
                for d in range(end - begin):
                    next(out)[at, :] = y[d * rows : (d + 1) * rows]


def pack(owner, snapshots, jobs, limit, after=()):
    steps, lanes, _ = snapshots.shape
    parts = math.gcd(steps * lanes // WIDE, 3)
    outs = [
        jax.ShapeDtypeStruct((steps, width), BF16)
        for _, width, begin, end in jobs
        for _ in range(begin, end)
    ]
    columns = jobs[-1][0] + jobs[-1][1] - jobs[0][0]
    partners = max(end for _, _, _, end in jobs) - min(begin for _, _, begin, _ in jobs)
    return pl.pallas_call(
        functools.partial(pack_kernel, jobs, parts, len(after)),
        out_shape=outs,
        in_specs=[HBM] * (2 + len(after)),
        out_specs=[VMEM] * len(outs),
        scratch_shapes=[
            pltpu.SMEM(owner.shape, jnp.int32),
            pltpu.VMEM((partners * (WIDE // lanes), WIDE), BF16),
            pltpu.VMEM((steps, lanes, columns), BF16),
            pltpu.SemaphoreType.DMA,
            pltpu.SemaphoreType.DMA((parts,)),
        ],
        compiler_params=pltpu.CompilerParams(vmem_limit_bytes=limit),
        cost_estimate=pl.CostEstimate(flops=1000, bytes_accessed=1000, transcendentals=0),
    )(owner, snapshots, *after)


def fill_record(base, order_ref, pieces, record, factor):
    steps = pieces[0].shape[0]
    me = lax.axis_index("tm")
    for d, piece in enumerate(pieces):
        start = pl.multiple_of(order_ref[me ^ d] * steps, steps)
        for c in range(record.shape[0]):
            at = c * LANE + (base if d < NEAR else 0)
            part = piece[:, at : at + LANE].astype(F32)
            if factor is not None:
                part = part * factor[:, c * LANE : (c + 1) * LANE]
            record[c, pl.ds(start, steps), :] = part


def transform(offsets_ref, f, record, s_ref):
    wanted = [(i, c) for i in range(NBLK) for c in range(record.shape[0])]
    for first in range(0, len(wanted), 2):
        pair = wanted[first : first + 2]
        x = [record[c, pl.ds(offsets_ref[i], NFFT), :].astype(BF16) for i, c in pair]
        x = jnp.concatenate(x, axis=1) if len(x) > 1 else x[0]
        y = dot(f, x)
        if f.shape[0] > NFFT:
            y = y[:NFFT] + y[NFFT:]
        for at, (i, c) in enumerate(pair):
            cols = slice(c * LANE, (c + 1) * LANE)
            s_ref[i, :, cols] = y[:NFREQ, at * LANE : (at + 1) * LANE]
            s_ref[NBLK + i, :, cols] = y[NFREQ:, at * LANE : (at + 1) * LANE]


def padded(s):
    width = s.shape[2]
    pad = jnp.zeros((LANE - HALF_ROWS, width), F32)
    real = s[:NBLK].reshape(HALF_ROWS, width)
    imag = s[NBLK:].reshape(HALF_ROWS, width)
    return jnp.concatenate([real, pad, imag, pad], axis=0)


def gram_rows(base, groups, s_ref, pick_ref, masked):
    row = lax.broadcasted_iota(jnp.int32, (HALF_ROWS, LANE), 0)
    col = lax.broadcasted_iota(jnp.int32, (HALF_ROWS, LANE), 1)
    same = row % SUB == col % SUB
    for pair in range(0, groups, 2):
        blocks = []
        for g in (pair, pair + 1):
            s = s_ref[:, pl.ds(pl.multiple_of(base + g * SUB, SUB), SUB), :]
            full = dot_nt(s.reshape(2 * HALF_ROWS, -1).astype(BF16), padded(s).astype(BF16))
            real = full[:HALF_ROWS, :LANE] + full[HALF_ROWS:, LANE:]
            imag = full[:HALF_ROWS, LANE:] - full[HALF_ROWS:, :LANE]
            blocks.append([jnp.where(same, part, 0.0) for part in (real, imag)])
        at = slice(pair * SUB, (pair + 2) * SUB)
        for a in range(NBLK):
            rows = slice(a * SUB, (a + 1) * SUB)
            for part in range(2):
                both = jnp.concatenate([block[part][rows] for block in blocks], axis=0)
                cols = slice(a * WIDE + part * LANE, a * WIDE + (part + 1) * LANE)
                masked[at, cols] = both.astype(BF16)
    return dot(masked[...], pick_ref[...])


def gram_kernel(lanes, base, scale, last, order_ref, offsets_ref, w_ref, f_ref, pick_ref, *refs):
    pieces = refs[:lanes]
    refs = refs[lanes:]
    if last:
        before_ref, _, gram_ref, s_ref, record, masked = refs
    else:
        *before_refs, gram_ref, record, s_ref, masked = refs
    fill_record(base, order_ref, pieces, record, jnp.sqrt(w_ref[...]))
    transform(offsets_ref, f_ref[:NFFT] if last else f_ref[...], record, s_ref)
    if not last:
        total = gram_rows(0, GROUPS, s_ref, pick_ref, masked) * scale
        gram_ref[...] = total + before_refs[0][...] if before_refs else total
        return
    half = pl.multiple_of((1 - lax.axis_index("tm") % 2) * HALF, HALF)
    total = gram_rows(half, GROUPS // 2, s_ref, pick_ref, masked) * scale
    gram_ref[...] = (total + before_ref[pl.ds(half, HALF), :]).astype(BF16)


def gram_part(order, offsets, weights, tables, pieces, before, base, last, scale):
    lanes = len(pieces)
    steps, width = pieces[-1].shape
    args = [order, offsets, weights, *tables, *pieces, *before]
    spectrum_shape = (2 * NBLK, NFREQ, width)
    scratch = [pltpu.VMEM((width // LANE, lanes * steps, LANE), F32)]
    if last:
        outs = [jax.ShapeDtypeStruct((HALF, PACKED), BF16)]
        outs.append(jax.ShapeDtypeStruct(spectrum_shape, F32))
    else:
        outs = [jax.ShapeDtypeStruct((NFREQ, PACKED), F32)]
        scratch.append(pltpu.VMEM(spectrum_shape, F32))
    scratch.append(pltpu.VMEM((HALF if last else NFREQ, NBLK * WIDE), BF16))
    return pl.pallas_call(
        functools.partial(gram_kernel, lanes, base, scale, last),
        out_shape=outs,
        in_specs=[SMEM, SMEM] + [VMEM] * (len(args) - 2),
        out_specs=[VMEM] * len(outs),
        scratch_shapes=scratch,
        compiler_params=pltpu.CompilerParams(vmem_limit_bytes=32 * 2**20),
        cost_estimate=pl.CostEstimate(flops=1000, bytes_accessed=1000, transcendentals=0),
    )(*args)


def own_kernel(scale, s_ref, pick_ref, before_ref, gram_ref, masked):
    base = pl.multiple_of(lax.axis_index("tm") % 2 * HALF, HALF)
    total = gram_rows(base, GROUPS // 2, s_ref, pick_ref, masked) * scale
    gram_ref[...] = (total + before_ref[pl.ds(base, HALF), :]).astype(BF16)


def own_part(scaled, pick, before, scale):
    return pl.pallas_call(
        functools.partial(own_kernel, scale),
        out_shape=jax.ShapeDtypeStruct((HALF, PACKED), BF16),
        in_specs=[VMEM] * 3,
        out_specs=VMEM,
        scratch_shapes=[pltpu.VMEM((HALF, NBLK * WIDE), BF16)],
        compiler_params=pltpu.CompilerParams(vmem_limit_bytes=32 * 2**20),
        cost_estimate=pl.CostEstimate(flops=10**9, bytes_accessed=3 * 10**6, transcendentals=0),
    )(scaled, pick, before)


def spectrum_kernel(lanes, base, order_ref, offsets_ref, f_ref, *refs):
    s_ref, record = refs[-2:]
    fill_record(base, order_ref, refs[:lanes], record, None)
    transform(offsets_ref, f_ref[...], record, s_ref)


def spectrum(order, offsets, fourier, pieces, base, after):
    lanes = len(pieces)
    steps, width = pieces[-1].shape
    args = [order, offsets, fourier, *pieces, *after]
    return pl.pallas_call(
        functools.partial(spectrum_kernel, lanes, base),
        out_shape=jax.ShapeDtypeStruct((2 * NBLK, NFREQ, width), F32),
        in_specs=[SMEM, SMEM] + [VMEM] * (len(args) - 2),
        out_specs=VMEM,
        scratch_shapes=[pltpu.VMEM((width // LANE, lanes * steps, LANE), F32)],
        compiler_params=pltpu.CompilerParams(vmem_limit_bytes=32 * 2**20),
        cost_estimate=pl.CostEstimate(flops=1000, bytes_accessed=1000, transcendentals=0),
    )(*args)


class Hermitian:
    def __init__(self, main, corner):
        self.main = main
        self.corner = corner

    def entry(self, a, e):
        if e < SUB:
            return self.main[0, a, pl.ds(e, 1), :], self.main[1, a, pl.ds(e, 1), :], 1
        if a < SUB:
            return self.main[0, e, pl.ds(a, 1), :], self.main[1, e, pl.ds(a, 1), :], -1
        at = pl.ds(e - SUB, 1)
        return self.corner[0, a - SUB, at, :], self.corner[1, a - SUB, at, :], 1

    def put(self, a, e, real, imag):
        if e < SUB:
            self.main[0, a, pl.ds(e, 1), :] = real
            self.main[1, a, pl.ds(e, 1), :] = imag
        elif a >= SUB:
            at = pl.ds(e - SUB, 1)
            self.corner[0, a - SUB, at, :] = real
            self.corner[1, a - SUB, at, :] = imag


def product(x, y, out, sums, diagonal=0.0, terms=()):
    sub = lax.broadcasted_iota(jnp.int32, (SUB, NFREQ), 0)
    yr = [y.main[0, b] for b in range(NBLK)]
    yi = [y.main[1, b] for b in range(NBLK)]
    minus = [yi[b] - yr[b] for b in range(NBLK)]
    plus = [yi[b] + yr[b] for b in range(NBLK)]
    for a in range(NBLK):
        sums[a] = x.main[0, a] + x.main[1, a]
    for a in range(CORNER):
        sums[NBLK + a] = x.corner[0, a] + x.corner[1, a]
        sums[NBLK + CORNER + a] = x.main[0, SUB + a] - x.main[1, SUB + a]
    for a in range(NBLK):
        k1 = k2 = k3 = None
        for b in range(NBLK):
            pr, pi, sign = x.entry(a, b)
            if b < SUB:
                both = sums[a, pl.ds(b, 1), :]
            elif a < SUB:
                both = sums[NBLK + CORNER + b - SUB, pl.ds(a, 1), :]
            else:
                both = sums[NBLK + a - SUB, pl.ds(b - SUB, 1), :]
            t1, t2, t3 = both * yr[b], pr * minus[b], pi * plus[b]
            k1 = t1 if k1 is None else k1 + t1
            k2 = t2 if k2 is None else k2 + t2
            k3 = t3 if k3 is None else k3 + t3 if sign > 0 else k3 - t3
        real, imag = k1 - k3, k1 + k2
        for factor, term in terms:
            real = real + factor * term.main[0, a]
            imag = imag + factor * term.main[1, a]
        if diagonal and a < SUB:
            real = real + jnp.where(sub == a, diagonal, 0.0)
        out.main[0, a] = real
        out.main[1, a] = imag
    ar = [[x.main[0, SUB + a], x.corner[0, a]] for a in range(CORNER)]
    ai = [[x.main[1, SUB + a], x.corner[1, a]] for a in range(CORNER)]
    er = [[yr[SUB + e], y.corner[0, e]] for e in range(CORNER)]
    ei = [[yi[SUB + e], y.corner[1, e]] for e in range(CORNER)]
    for a in range(CORNER):
        for e in range(a, CORNER):
            real = sum(ar[a][h] * er[e][h] + ai[a][h] * ei[e][h] for h in range(2))
            real = jnp.sum(real, axis=0, keepdims=True)
            imag = jnp.zeros_like(real)
            if a != e:
                imag = sum(ai[a][h] * er[e][h] - ar[a][h] * ei[e][h] for h in range(2))
                imag = jnp.sum(imag, axis=0, keepdims=True)
            for factor, term in terms:
                r, i, _ = term.entry(SUB + a, SUB + e)
                real, imag = real + factor * r, imag + factor * i
            if a == e:
                out.put(SUB + a, SUB + a, real + diagonal, jnp.zeros_like(real))
            else:
                out.put(SUB + a, SUB + e, real, imag)
                out.put(SUB + e, SUB + a, real, -imag)


def combine(out, diagonal, terms):
    sub = lax.broadcasted_iota(jnp.int32, (SUB, NFREQ), 0)
    for name, rows in (("main", NBLK), ("corner", CORNER)):
        target = getattr(out, name)
        for a in range(rows):
            real = sum(factor * getattr(term, name)[0, a] for factor, term in terms)
            imag = sum(factor * getattr(term, name)[1, a] for factor, term in terms)
            if diagonal and (name == "corner" or a < SUB):
                real = real + jnp.where(sub == a, diagonal, 0.0)
            target[0, a] = real
            target[1, a] = imag


TWO_STEPS = (2.25, -2.4375, 1.6875, -0.5625, 0.0625)


def inverse_root(w, mats, sums):
    q, u, r, t, w2, z = mats
    c0, c1, c2, c3, c4 = TWO_STEPS
    product(w, w, q, sums)
    combine(u, 0.0, [(c3, w), (c4, q)])
    product(q, u, z, sums, c0, [(c1, w), (c2, q)])
    product(z, z, t, sums)
    product(w, t, w2, sums)
    product(w2, w2, q, sums)
    combine(u, 0.0, [(c3, w2), (c4, q)])
    product(q, u, r, sums, c0, [(c1, w2), (c2, q)])
    product(r, r, t, sums)
    product(z, r, u, sums)
    product(w2, t, q, sums)
    combine(q, 1.5, [(-0.5, q)])
    product(u, q, z, sums)
    return z


def make_roots(share, half_ref, other_ref, gram_ref, packed, rolled, sums, mats):
    core = lax.axis_index("tm") % 2
    packed[pl.ds(pl.multiple_of(core * HALF, HALF), HALF), :] = half_ref[...]
    packed[pl.ds(pl.multiple_of((1 - core) * HALF, HALF), HALF), :] = other_ref[...]
    packed[...] = packed[...].T
    at = lax.axis_index("sx") * lax.axis_size("sy") + lax.axis_index("sy")
    rolled[...] = pltpu.roll(packed[...], (NFREQ - at * share) % NFREQ, 1)
    y, *free = [Hermitian(mats[2 * i], mats[2 * i + 1]) for i in range(MATS)]
    for ref in mats[1::2]:
        ref[...] = jnp.zeros_like(ref)

    def row(ref, part, a, e):
        return ref[pl.ds(ROWS[part, a, e], 1), :]

    trace = 2.0 * sum(row(packed, 0, a, a) for a in range(NBLK))
    norm = 1.0 / jnp.sqrt(trace)
    packed[...] = packed[...] / trace
    zero = jnp.zeros((1, NFREQ), F32)
    for a in range(NBLK):
        y.put(a, a, row(packed, 0, a, a), zero)
        gram_ref[a, a, 0:1, :] = row(rolled, 0, a, a)[:, :share]
        gram_ref[a, a, 1:2, :] = zero[:, :share]
        for e in range(a + 1, NBLK):
            real, imag = row(packed, 0, a, e), row(packed, 1, a, e)
            y.put(a, e, real, imag)
            y.put(e, a, real, -imag)
            real, imag = row(rolled, 0, a, e)[:, :share], row(rolled, 1, a, e)[:, :share]
            gram_ref[a, e, 0:1, :] = real
            gram_ref[e, a, 0:1, :] = real
            gram_ref[a, e, 1:2, :] = imag
            gram_ref[e, a, 1:2, :] = -imag
    z = inverse_root(y, free, sums)
    mean = sum(z.entry(a, a)[0] for a in range(NBLK)) * (1.0 / NBLK)
    sub = lax.broadcasted_iota(jnp.int32, (SUB, NFREQ), 0)
    none = jnp.zeros((SUB - CORNER, NFREQ), F32)
    first = jnp.concatenate([mean * norm, none[1:]], axis=0)
    stacks = []
    for m0 in range(0, NBLK, STACK):
        modes = range(m0, min(m0 + STACK, NBLK))
        stack = []
        for m in modes:
            for c in range(2):
                column = z.main[c, m]
                if c == 0 and m < SUB:
                    column = column - jnp.where(sub == m, mean, 0.0)
                stack.append(column * norm)
                for b in range(SUB, NBLK):
                    real, imag, sign = z.entry(m, b)
                    line = imag * sign if c else real
                    if c == 0 and m == b:
                        line = line - mean
                    stack.append(line * norm)
                stack.append(first if c == 0 and m == 0 else none)
        stack += [jnp.zeros((32, NFREQ), F32)] * (STACK - len(modes))
        stacks.append(jnp.concatenate(stack, axis=0).T)
    return stacks


def mode_kernel(chunks, share, half_ref, other_ref, spread_ref, *refs):
    s_refs = refs[:chunks]
    out_hbm, gram_ref, out, v, mean, packed, rolled, sums, sem, *mats = refs[chunks:]
    stacks = make_roots(share, half_ref, other_ref, gram_ref, packed, rolled, sums, mats)
    mean[...] = jnp.broadcast_to(stacks[0][:, NBLK : NBLK + 1], (NFREQ, LANE))
    row = lax.broadcasted_iota(jnp.int32, (NFREQ, 2 * HALF_ROWS), 0)
    col = lax.broadcasted_iota(jnp.int32, (NFREQ, 2 * HALF_ROWS), 1)
    same = row % SUB == col % SUB
    place = lax.broadcasted_iota(jnp.int32, (NFREQ, LANE), 1) // 32
    rows = [jnp.where(place == m % STACK, stacks[m // STACK], 0.0) for m in range(NBLK)]
    rows = jnp.concatenate(rows, axis=0).astype(BF16)
    for c in range(2):
        wide = dot(rows, spread_ref[c])[:, : 2 * HALF_ROWS]
        for m in range(NBLK):
            v[c * NBLK + m] = jnp.where(same, wide[m * NFREQ : (m + 1) * NFREQ], 0.0)

    copies = []
    for pair in range(GROUPS // 2):
        fields = []
        for g in (2 * pair, 2 * pair + 1):
            at = slice(g * SUB, (g + 1) * SUB)
            s = jnp.concatenate([r[:, at, :] for r in s_refs], axis=2)
            flat = s.reshape(2 * HALF_ROWS, -1).astype(BF16)
            field = dot(v[:, at, :].reshape(2 * HALF_ROWS, 2 * HALF_ROWS).astype(BF16), flat)
            scale = jnp.concatenate([mean[at, :]] * (s.shape[2] // LANE), axis=1)
            fields.append(field.reshape(s.shape) + s * scale[None])
        both = jnp.concatenate(fields, axis=1).astype(BF16)
        at = slice(pair * 2 * SUB, (pair + 1) * 2 * SUB)
        out[:, :, at, :] = both.reshape(2, NBLK, 2 * SUB, -1)
        copies.append(
            pltpu.make_async_copy(out.at[:, :, at, :], out_hbm.at[:, :, at, :], sem.at[pair])
        )
        copies[-1].start()
    for copy in copies:
        copy.wait()


def mode_fields(half, other, spread, spectra, share):
    shape = (2, NBLK, NFREQ, sum(s.shape[2] for s in spectra))
    return pl.pallas_call(
        functools.partial(mode_kernel, len(spectra), share),
        out_shape=[
            jax.ShapeDtypeStruct(shape, BF16),
            jax.ShapeDtypeStruct((NBLK, NBLK, 2, share), F32),
        ],
        in_specs=[VMEM] * (3 + len(spectra)),
        out_specs=[HBM, VMEM],
        scratch_shapes=[
            pltpu.VMEM(shape, BF16),
            pltpu.VMEM((2 * NBLK, NFREQ, 2 * HALF_ROWS), F32),
            pltpu.VMEM((NFREQ, LANE), F32),
            pltpu.VMEM((PACKED, NFREQ), F32),
            pltpu.VMEM((PACKED, NFREQ), F32),
            pltpu.VMEM((NBLK + 2 * CORNER, SUB, NFREQ), F32),
            pltpu.SemaphoreType.DMA((GROUPS // 2,)),
        ]
        + [
            pltpu.VMEM((2, NBLK, SUB, NFREQ), F32),
            pltpu.VMEM((2, CORNER, SUB, NFREQ), F32),
        ]
        * MATS,
        compiler_params=pltpu.CompilerParams(vmem_limit_bytes=32 * 2**20),
    )(half, other, spread, *spectra)


def swap(x, axes, mask, size):
    return lax.ppermute(x, axes, [(i, i ^ mask) for i in range(size)])


def powers(size):
    return [1 << i for i in range(size.bit_length() - 1)]


def body(snapshots, weights, block_order, owner, offsets):
    lanes = lax.axis_size("tm")
    groups = lax.axis_size("sx") * lax.axis_size("sy")
    points = snapshots.shape[2]
    half, quarter = points // 2, points // 4
    chunks = [(0, half), (half, quarter), (half + quarter, quarter)]
    scale = 1.0 / (lanes * groups * points)
    tables = (jnp.asarray(fourier_tables()), jnp.asarray(pick_table()))
    weights = weights.reshape(1, -1)

    def send(packed, begin, end):
        return [swap(p, "tm", d, lanes) for d, p in zip(range(begin, end), packed)]

    c0, c1, c2 = chunks
    packed = pack(owner, snapshots, [(*c0, lanes - 1, lanes)], FIRST_LIMIT)
    first = send(packed, lanes - 1, lanes)
    jobs = [(*c0, 0, lanes - 1), (*c1, NEAR, lanes)]
    middle = pack(owner, snapshots, jobs, SECOND_LIMIT, packed)
    jobs = [(c1[0], c1[1] + c2[1], 0, NEAR), (*c2, NEAR, lanes)]
    rest = pack(owner, snapshots, jobs, LAST_LIMIT, [*first, middle[0]])
    near = [rest[0], *send(rest[1:], 1, NEAR)]
    arrived = [
        [middle[0], *send(middle[1:], 1, lanes - 1), *first],
        [*near, *send(middle[lanes - 1 :], NEAR, lanes)],
        [*near, *send(rest[NEAR:], NEAR, lanes)],
    ]
    starts = (0, 0, c1[1])

    axes = ("tm", "sx", "sy")
    size = lanes * groups
    bits = [b * groups for b in powers(lanes)] + powers(groups)
    parts = [weights[:, base : base + width] for base, width in chunks]
    head = (block_order, offsets)
    before = []
    for at in range(2):
        args = (*head, parts[at], tables, arrived[at], before, starts[at], False, scale)
        before = gram_part(*args)
    spectra = [spectrum(*head, tables[0], arrived[0], starts[0], before)]
    args = (*head, parts[2], tables, arrived[2], [*before, spectra[0]], starts[2], True, scale)
    given, scaled = gram_part(*args)

    other = swap(given, axes, bits[0], size)
    keep = own_part(scaled, tables[1], before[0], scale)
    spectra += [
        spectrum(*head, tables[0], pieces, base, [keep])
        for base, pieces in zip(starts[1:], arrived[1:])
    ]
    half = keep.astype(F32) + other.astype(F32)
    for at in range(1, len(bits), 2):
        masks = bits[at : at + 2]
        if len(masks) == 2:
            masks.append(masks[0] ^ masks[1])
            masks = masks[1:] + masks[:1] if at > 1 else masks
        half = half.astype(BF16)
        terms = [half] + [swap(half, axes, mask, size) for mask in masks]
        terms = [t.astype(F32) for t in terms]
        while len(terms) > 1:
            terms = [a + b for a, b in zip(terms[::2], terms[1::2])]
        half = terms[0]
        if at == 1:
            half, spectra[1] = lax.optimization_barrier((half, spectra[1]))
    half, spectra[2] = lax.optimization_barrier((half, spectra[2]))
    other = swap(half, axes, bits[0], size)

    spread = jnp.asarray(spread_table())
    modes, gram = mode_fields(half, other, spread, spectra, NFREQ // groups)
    modes = jnp.transpose(modes, (0, 2, 1, 3))[:, :, :, None, :]
    return modes, jnp.transpose(gram, (2, 3, 0, 1))


def solution(mesh):
    placed = (P("tm", None, ("sx", "sy")), P(("sx", "sy")), P(), P(("sx", "sy"), None), P())
    return jax.shard_map(
        body,
        mesh=mesh,
        in_specs=placed,
        out_specs=(P(None, None, None, "tm", ("sx", "sy")), P(None, ("sx", "sy"), None, None)),
        check_vma=False,
    )
```

```python
import functools
import math

import jax
import jax.numpy as jnp
import numpy as np
from jax import lax
from jax.experimental import pallas as pl
from jax.experimental.pallas import tpu as pltpu
from jax.sharding import PartitionSpec as P

NFFT = 256
NFREQ = 128
NBLK = 11
LANE = 128
SUB = 8
HALF_ROWS = NBLK * SUB
GROUPS = NFREQ // SUB
MATS = 7
NEAR = 2
PACKED = 128
HALF = PACKED // 2
STACK = 4
CORNER = NBLK - SUB
WIDE = 2 * LANE
FIRST_LIMIT = 64 * 2**20
SECOND_LIMIT = FIRST_LIMIT - 1450 * 2**10
LAST_LIMIT = 40 * 2**20
BF16 = jnp.bfloat16
F32 = jnp.float32


def fourier_tables():
    n = np.arange(NFFT)
    k = np.arange(NFREQ)
    angles = 2.0 * np.pi * ((k[:, None] * n[None, :]) % NFFT) / NFFT
    scaled = (0.5 - 0.5 * np.cos(2.0 * np.pi * n / NFFT)) / math.sqrt(0.375 * NFFT)
    table = np.concatenate([np.cos(angles) * scaled, -np.sin(angles) * scaled], axis=0)
    high = table.astype(jnp.bfloat16)
    low = (table - high.astype(np.float64)).astype(jnp.bfloat16)
    return np.concatenate([high, low], axis=0)


def packed_rows():
    rows = {}
    for a in range(NBLK):
        for e in range(a, NBLK):
            rows[0, a, e] = len(rows)
        for e in range(a + 1, NBLK):
            rows[1, a, e] = len(rows)
    return rows


ROWS = packed_rows()


def pick_table():
    pick = np.zeros((NBLK, 2, LANE, PACKED), np.float32)
    for (part, a, e), row in ROWS.items():
        pick[a, part, e * SUB : (e + 1) * SUB, row] = 1.0
    return pick.reshape(NBLK * WIDE, PACKED).astype(jnp.bfloat16)


def spread_table():
    spread = np.zeros((2, STACK, 2, 16, WIDE), np.float32)
    for b in range(NBLK):
        first = slice(b * SUB, b * SUB + SUB)
        second = slice(HALF_ROWS + b * SUB, HALF_ROWS + b * SUB + SUB)
        spread[0, :, 0, b, first] = 1.0
        spread[0, :, 1, b, second] = 1.0
        spread[1, :, 1, b, first] = -1.0
        spread[1, :, 0, b, second] = 1.0
    return spread.reshape(2, LANE, WIDE).astype(jnp.bfloat16)


def dot(a, b):
    return jnp.dot(a, b, preferred_element_type=F32)


def dot_nt(a, b):
    return lax.dot_general(a, b, (((1,), (1,)), ((), ())), preferred_element_type=F32)


def spec(shape):
    return pl.BlockSpec(shape, lambda *_: (0,) * len(shape))


SMEM = pl.BlockSpec(memory_space=pltpu.SMEM)
VMEM = pl.BlockSpec(memory_space=pltpu.VMEM)
HBM = pl.BlockSpec(memory_space=pltpu.HBM)


def lane_pick(owner, lanes, begin, end):
    me = lax.axis_index("tm")
    rows = WIDE // lanes
    shape = ((end - begin) * rows, WIDE)
    out_row = lax.broadcasted_iota(jnp.int32, shape, 0)
    in_row = lax.broadcasted_iota(jnp.int32, shape, 1)
    row_of = (out_row % rows) * lanes
    for d in range(begin, end):
        slot = me ^ d
        source = jnp.int32(0)
        for lane in range(lanes):
            source = source + jnp.where(owner[0, lane] == slot, lane, 0)
        row_of = jnp.where(out_row // rows == d - begin, row_of + source, row_of)
    return jnp.where(in_row == row_of, 1.0, 0.0).astype(BF16)


def pack_kernel(jobs, parts, follows, owner_hbm, x_hbm, *refs):
    steps, lanes, _ = x_hbm.shape
    base = jobs[0][0]
    *outs, owner, pick, x_ref, owner_sem, x_sem = refs[follows:]
    part = steps // parts
    owner_copy = pltpu.make_async_copy(owner_hbm, owner, owner_sem)
    owner_copy.start()
    copies = []
    for i in range(parts):
        at = slice(i * part, (i + 1) * part)
        source = x_hbm.at[at, :, base : base + x_ref.shape[2]]
        copies.append(pltpu.make_async_copy(source, x_ref.at[at], x_sem.at[i]))
        copies[-1].start()
    owner_copy.wait()
    lowest = min(begin for _, _, begin, _ in jobs)
    pick[...] = lane_pick(owner, lanes, lowest, max(end for _, _, _, end in jobs))
    rows = WIDE // lanes
    for i in range(parts):
        copies[i].wait()
        for start in range(i * part, (i + 1) * part, rows):
            at = slice(start, start + rows)
            x = x_ref[at].reshape(WIDE, x_ref.shape[2])
            out = iter(outs)
            for job, width, begin, end in jobs:
                here = x[:, job - base : job - base + width]
                chosen = pick[(begin - lowest) * rows : (end - lowest) * rows, :]
                y = dot(chosen, here).astype(BF16)
                for d in range(end - begin):
                    next(out)[at, :] = y[d * rows : (d + 1) * rows]


def pack(owner, snapshots, jobs, limit, after=()):
    steps, lanes, _ = snapshots.shape
    parts = math.gcd(steps * lanes // WIDE, 3)
    outs = [
        jax.ShapeDtypeStruct((steps, width), BF16)
        for _, width, begin, end in jobs
        for _ in range(begin, end)
    ]
    columns = jobs[-1][0] + jobs[-1][1] - jobs[0][0]
    partners = max(end for _, _, _, end in jobs) - min(begin for _, _, begin, _ in jobs)
    return pl.pallas_call(
        functools.partial(pack_kernel, jobs, parts, len(after)),
        out_shape=outs,
        in_specs=[HBM] * (2 + len(after)),
        out_specs=[VMEM] * len(outs),
        scratch_shapes=[
            pltpu.SMEM(owner.shape, jnp.int32),
            pltpu.VMEM((partners * (WIDE // lanes), WIDE), BF16),
            pltpu.VMEM((steps, lanes, columns), BF16),
            pltpu.SemaphoreType.DMA,
            pltpu.SemaphoreType.DMA((parts,)),
        ],
        compiler_params=pltpu.CompilerParams(vmem_limit_bytes=limit),
        cost_estimate=pl.CostEstimate(flops=1000, bytes_accessed=1000, transcendentals=0),
    )(owner, snapshots, *after)


def fill_record(base, order_ref, pieces, record, factor):
    steps = pieces[0].shape[0]
    me = lax.axis_index("tm")
    for d, piece in enumerate(pieces):
        start = pl.multiple_of(order_ref[me ^ d] * steps, steps)
        for c in range(record.shape[0]):
            at = c * LANE + (base if d < NEAR else 0)
            part = piece[:, at : at + LANE].astype(F32)
            if factor is not None:
                part = part * factor[:, c * LANE : (c + 1) * LANE]
            record[c, pl.ds(start, steps), :] = part


def transform(offsets_ref, f, record, s_ref):
    wanted = [(i, c) for i in range(NBLK) for c in range(record.shape[0])]
    for first in range(0, len(wanted), 2):
        pair = wanted[first : first + 2]
        x = [record[c, pl.ds(offsets_ref[i], NFFT), :].astype(BF16) for i, c in pair]
        x = jnp.concatenate(x, axis=1) if len(x) > 1 else x[0]
        y = dot(f, x)
        if f.shape[0] > NFFT:
            y = y[:NFFT] + y[NFFT:]
        for at, (i, c) in enumerate(pair):
            cols = slice(c * LANE, (c + 1) * LANE)
            s_ref[i, :, cols] = y[:NFREQ, at * LANE : (at + 1) * LANE]
            s_ref[NBLK + i, :, cols] = y[NFREQ:, at * LANE : (at + 1) * LANE]


def padded(s):
    width = s.shape[2]
    pad = jnp.zeros((LANE - HALF_ROWS, width), F32)
    real = s[:NBLK].reshape(HALF_ROWS, width)
    imag = s[NBLK:].reshape(HALF_ROWS, width)
    return jnp.concatenate([real, pad, imag, pad], axis=0)


def gram_rows(base, groups, s_ref, pick_ref, masked):
    row = lax.broadcasted_iota(jnp.int32, (HALF_ROWS, LANE), 0)
    col = lax.broadcasted_iota(jnp.int32, (HALF_ROWS, LANE), 1)
    same = row % SUB == col % SUB
    for pair in range(0, groups, 2):
        blocks = []
        for g in (pair, pair + 1):
            s = s_ref[:, pl.ds(pl.multiple_of(base + g * SUB, SUB), SUB), :]
            full = dot_nt(s.reshape(2 * HALF_ROWS, -1).astype(BF16), padded(s).astype(BF16))
            real = full[:HALF_ROWS, :LANE] + full[HALF_ROWS:, LANE:]
            imag = full[:HALF_ROWS, LANE:] - full[HALF_ROWS:, :LANE]
            blocks.append([jnp.where(same, part, 0.0) for part in (real, imag)])
        at = slice(pair * SUB, (pair + 2) * SUB)
        for a in range(NBLK):
            rows = slice(a * SUB, (a + 1) * SUB)
            for part in range(2):
                both = jnp.concatenate([block[part][rows] for block in blocks], axis=0)
                cols = slice(a * WIDE + part * LANE, a * WIDE + (part + 1) * LANE)
                masked[at, cols] = both.astype(BF16)
    return dot(masked[...], pick_ref[...])


def gram_kernel(lanes, base, scale, last, order_ref, offsets_ref, w_ref, f_ref, pick_ref, *refs):
    pieces = refs[:lanes]
    refs = refs[lanes:]
    if last:
        before_ref, gram_ref, s_ref, record, masked = refs
    else:
        *before_refs, gram_ref, record, s_ref, masked = refs
    fill_record(base, order_ref, pieces, record, jnp.sqrt(w_ref[...]))
    transform(offsets_ref, f_ref[:NFFT] if last else f_ref[...], record, s_ref)
    if not last:
        total = gram_rows(0, GROUPS, s_ref, pick_ref, masked) * scale
        gram_ref[...] = total + before_refs[0][...] if before_refs else total
        return
    half = pl.multiple_of((1 - lax.axis_index("tm") % 2) * HALF, HALF)
    total = gram_rows(half, GROUPS // 2, s_ref, pick_ref, masked) * scale
    gram_ref[...] = (total + before_ref[pl.ds(half, HALF), :]).astype(BF16)


def gram_part(order, offsets, weights, tables, pieces, before, base, last, scale):
    lanes = len(pieces)
    steps, width = pieces[-1].shape
    args = [order, offsets, weights, *tables, *pieces, *before]
    spectrum_shape = (2 * NBLK, NFREQ, width)
    scratch = [pltpu.VMEM((width // LANE, lanes * steps, LANE), F32)]
    if last:
        outs = [jax.ShapeDtypeStruct((HALF, PACKED), BF16)]
        outs.append(jax.ShapeDtypeStruct(spectrum_shape, F32))
    else:
        outs = [jax.ShapeDtypeStruct((NFREQ, PACKED), F32)]
        scratch.append(pltpu.VMEM(spectrum_shape, F32))
    scratch.append(pltpu.VMEM((HALF if last else NFREQ, NBLK * WIDE), BF16))
    return pl.pallas_call(
        functools.partial(gram_kernel, lanes, base, scale, last),
        out_shape=outs,
        in_specs=[SMEM, SMEM] + [VMEM] * (len(args) - 2),
        out_specs=[VMEM] * len(outs),
        scratch_shapes=scratch,
        compiler_params=pltpu.CompilerParams(vmem_limit_bytes=32 * 2**20),
        cost_estimate=pl.CostEstimate(flops=1000, bytes_accessed=1000, transcendentals=0),
    )(*args)


def own_kernel(scale, s_ref, pick_ref, before_ref, gram_ref, masked):
    base = pl.multiple_of(lax.axis_index("tm") % 2 * HALF, HALF)
    total = gram_rows(base, GROUPS // 2, s_ref, pick_ref, masked) * scale
    gram_ref[...] = (total + before_ref[pl.ds(base, HALF), :]).astype(BF16)


def own_part(scaled, pick, before, scale):
    return pl.pallas_call(
        functools.partial(own_kernel, scale),
        out_shape=jax.ShapeDtypeStruct((HALF, PACKED), BF16),
        in_specs=[VMEM] * 3,
        out_specs=VMEM,
        scratch_shapes=[pltpu.VMEM((HALF, NBLK * WIDE), BF16)],
        compiler_params=pltpu.CompilerParams(vmem_limit_bytes=32 * 2**20),
        cost_estimate=pl.CostEstimate(flops=10**9, bytes_accessed=3 * 10**6, transcendentals=0),
    )(scaled, pick, before)


def spectrum_kernel(lanes, base, order_ref, offsets_ref, f_ref, *refs):
    s_ref, record = refs[-2:]
    fill_record(base, order_ref, refs[:lanes], record, None)
    transform(offsets_ref, f_ref[...], record, s_ref)


def spectrum(order, offsets, fourier, pieces, base, after):
    lanes = len(pieces)
    steps, width = pieces[-1].shape
    args = [order, offsets, fourier, *pieces, *after]
    return pl.pallas_call(
        functools.partial(spectrum_kernel, lanes, base),
        out_shape=jax.ShapeDtypeStruct((2 * NBLK, NFREQ, width), F32),
        in_specs=[SMEM, SMEM] + [VMEM] * (len(args) - 2),
        out_specs=VMEM,
        scratch_shapes=[pltpu.VMEM((width // LANE, lanes * steps, LANE), F32)],
        compiler_params=pltpu.CompilerParams(vmem_limit_bytes=32 * 2**20),
        cost_estimate=pl.CostEstimate(flops=1000, bytes_accessed=1000, transcendentals=0),
    )(*args)


class Hermitian:
    def __init__(self, main, corner):
        self.main = main
        self.corner = corner

    def entry(self, a, e):
        if e < SUB:
            return self.main[0, a, pl.ds(e, 1), :], self.main[1, a, pl.ds(e, 1), :], 1
        if a < SUB:
            return self.main[0, e, pl.ds(a, 1), :], self.main[1, e, pl.ds(a, 1), :], -1
        at = pl.ds(e - SUB, 1)
        return self.corner[0, a - SUB, at, :], self.corner[1, a - SUB, at, :], 1

    def put(self, a, e, real, imag):
        if e < SUB:
            self.main[0, a, pl.ds(e, 1), :] = real
            self.main[1, a, pl.ds(e, 1), :] = imag
        elif a >= SUB:
            at = pl.ds(e - SUB, 1)
            self.corner[0, a - SUB, at, :] = real
            self.corner[1, a - SUB, at, :] = imag


def product(x, y, out, sums, diagonal=0.0, terms=()):
    sub = lax.broadcasted_iota(jnp.int32, (SUB, NFREQ), 0)
    yr = [y.main[0, b] for b in range(NBLK)]
    yi = [y.main[1, b] for b in range(NBLK)]
    minus = [yi[b] - yr[b] for b in range(NBLK)]
    plus = [yi[b] + yr[b] for b in range(NBLK)]
    for a in range(NBLK):
        sums[a] = x.main[0, a] + x.main[1, a]
    for a in range(CORNER):
        sums[NBLK + a] = x.corner[0, a] + x.corner[1, a]
        sums[NBLK + CORNER + a] = x.main[0, SUB + a] - x.main[1, SUB + a]
    for a in range(NBLK):
        k1 = k2 = k3 = None
        for b in range(NBLK):
            pr, pi, sign = x.entry(a, b)
            if b < SUB:
                both = sums[a, pl.ds(b, 1), :]
            elif a < SUB:
                both = sums[NBLK + CORNER + b - SUB, pl.ds(a, 1), :]
            else:
                both = sums[NBLK + a - SUB, pl.ds(b - SUB, 1), :]
            t1, t2, t3 = both * yr[b], pr * minus[b], pi * plus[b]
            k1 = t1 if k1 is None else k1 + t1
            k2 = t2 if k2 is None else k2 + t2
            k3 = t3 if k3 is None else k3 + t3 if sign > 0 else k3 - t3
        real, imag = k1 - k3, k1 + k2
        for factor, term in terms:
            real = real + factor * term.main[0, a]
            imag = imag + factor * term.main[1, a]
        if diagonal and a < SUB:
            real = real + jnp.where(sub == a, diagonal, 0.0)
        out.main[0, a] = real
        out.main[1, a] = imag
    ar = [[x.main[0, SUB + a], x.corner[0, a]] for a in range(CORNER)]
    ai = [[x.main[1, SUB + a], x.corner[1, a]] for a in range(CORNER)]
    er = [[yr[SUB + e], y.corner[0, e]] for e in range(CORNER)]
    ei = [[yi[SUB + e], y.corner[1, e]] for e in range(CORNER)]
    for a in range(CORNER):
        for e in range(a, CORNER):
            real = sum(ar[a][h] * er[e][h] + ai[a][h] * ei[e][h] for h in range(2))
            real = jnp.sum(real, axis=0, keepdims=True)
            imag = jnp.zeros_like(real)
            if a != e:
                imag = sum(ai[a][h] * er[e][h] - ar[a][h] * ei[e][h] for h in range(2))
                imag = jnp.sum(imag, axis=0, keepdims=True)
            for factor, term in terms:
                r, i, _ = term.entry(SUB + a, SUB + e)
                real, imag = real + factor * r, imag + factor * i
            if a == e:
                out.put(SUB + a, SUB + a, real + diagonal, jnp.zeros_like(real))
            else:
                out.put(SUB + a, SUB + e, real, imag)
                out.put(SUB + e, SUB + a, real, -imag)


def combine(out, diagonal, terms):
    sub = lax.broadcasted_iota(jnp.int32, (SUB, NFREQ), 0)
    for name, rows in (("main", NBLK), ("corner", CORNER)):
        target = getattr(out, name)
        for a in range(rows):
            real = sum(factor * getattr(term, name)[0, a] for factor, term in terms)
            imag = sum(factor * getattr(term, name)[1, a] for factor, term in terms)
            if diagonal and (name == "corner" or a < SUB):
                real = real + jnp.where(sub == a, diagonal, 0.0)
            target[0, a] = real
            target[1, a] = imag


TWO_STEPS = (2.25, -2.4375, 1.6875, -0.5625, 0.0625)


def inverse_root(w, mats, sums):
    q, u, r, t, w2, z = mats
    c0, c1, c2, c3, c4 = TWO_STEPS
    product(w, w, q, sums)
    combine(u, 0.0, [(c3, w), (c4, q)])
    product(q, u, z, sums, c0, [(c1, w), (c2, q)])
    product(z, z, t, sums)
    product(w, t, w2, sums)
    product(w2, w2, q, sums)
    combine(u, 0.0, [(c3, w2), (c4, q)])
    product(q, u, r, sums, c0, [(c1, w2), (c2, q)])
    product(r, r, t, sums)
    product(z, r, u, sums)
    product(w2, t, q, sums)
    combine(q, 1.5, [(-0.5, q)])
    product(u, q, z, sums)
    return z


def make_roots(share, half_ref, other_ref, gram_ref, packed, rolled, sums, mats):
    core = lax.axis_index("tm") % 2
    packed[pl.ds(pl.multiple_of(core * HALF, HALF), HALF), :] = half_ref[...]
    packed[pl.ds(pl.multiple_of((1 - core) * HALF, HALF), HALF), :] = other_ref[...]
    packed[...] = packed[...].T
    at = lax.axis_index("sx") * lax.axis_size("sy") + lax.axis_index("sy")
    rolled[...] = pltpu.roll(packed[...], (NFREQ - at * share) % NFREQ, 1)
    y, *free = [Hermitian(mats[2 * i], mats[2 * i + 1]) for i in range(MATS)]
    for ref in mats[1::2]:
        ref[...] = jnp.zeros_like(ref)

    def row(ref, part, a, e):
        return ref[pl.ds(ROWS[part, a, e], 1), :]

    trace = 2.0 * sum(row(packed, 0, a, a) for a in range(NBLK))
    norm = 1.0 / jnp.sqrt(trace)
    packed[...] = packed[...] / trace
    zero = jnp.zeros((1, NFREQ), F32)
    for a in range(NBLK):
        y.put(a, a, row(packed, 0, a, a), zero)
        gram_ref[a, a, 0:1, :] = row(rolled, 0, a, a)[:, :share]
        gram_ref[a, a, 1:2, :] = zero[:, :share]
        for e in range(a + 1, NBLK):
            real, imag = row(packed, 0, a, e), row(packed, 1, a, e)
            y.put(a, e, real, imag)
            y.put(e, a, real, -imag)
            real, imag = row(rolled, 0, a, e)[:, :share], row(rolled, 1, a, e)[:, :share]
            gram_ref[a, e, 0:1, :] = real
            gram_ref[e, a, 0:1, :] = real
            gram_ref[a, e, 1:2, :] = imag
            gram_ref[e, a, 1:2, :] = -imag
    z = inverse_root(y, free, sums)
    mean = sum(z.entry(a, a)[0] for a in range(NBLK)) * (1.0 / NBLK)
    sub = lax.broadcasted_iota(jnp.int32, (SUB, NFREQ), 0)
    none = jnp.zeros((SUB - CORNER, NFREQ), F32)
    first = jnp.concatenate([mean * norm, none[1:]], axis=0)
    stacks = []
    for m0 in range(0, NBLK, STACK):
        modes = range(m0, min(m0 + STACK, NBLK))
        stack = []
        for m in modes:
            for c in range(2):
                column = z.main[c, m]
                if c == 0 and m < SUB:
                    column = column - jnp.where(sub == m, mean, 0.0)
                stack.append(column * norm)
                for b in range(SUB, NBLK):
                    real, imag, sign = z.entry(m, b)
                    line = imag * sign if c else real
                    if c == 0 and m == b:
                        line = line - mean
                    stack.append(line * norm)
                stack.append(first if c == 0 and m == 0 else none)
        stack += [jnp.zeros((32, NFREQ), F32)] * (STACK - len(modes))
        stacks.append(jnp.concatenate(stack, axis=0).T)
    return stacks


def mode_kernel(chunks, share, half_ref, other_ref, spread_ref, *refs):
    s_refs = refs[:chunks]
    out_hbm, gram_ref, out, v, mean, packed, rolled, sums, sem, *mats = refs[chunks:]
    stacks = make_roots(share, half_ref, other_ref, gram_ref, packed, rolled, sums, mats)
    mean[...] = jnp.broadcast_to(stacks[0][:, NBLK : NBLK + 1], (NFREQ, LANE))
    row = lax.broadcasted_iota(jnp.int32, (NFREQ, 2 * HALF_ROWS), 0)
    col = lax.broadcasted_iota(jnp.int32, (NFREQ, 2 * HALF_ROWS), 1)
    same = row % SUB == col % SUB
    place = lax.broadcasted_iota(jnp.int32, (NFREQ, LANE), 1) // 32
    rows = [jnp.where(place == m % STACK, stacks[m // STACK], 0.0) for m in range(NBLK)]
    rows = jnp.concatenate(rows, axis=0).astype(BF16)
    for c in range(2):
        wide = dot(rows, spread_ref[c])[:, : 2 * HALF_ROWS]
        for m in range(NBLK):
            v[c * NBLK + m] = jnp.where(same, wide[m * NFREQ : (m + 1) * NFREQ], 0.0)

    copies = []
    for pair in range(GROUPS // 2):
        fields = []
        for g in (2 * pair, 2 * pair + 1):
            at = slice(g * SUB, (g + 1) * SUB)
            s = jnp.concatenate([r[:, at, :] for r in s_refs], axis=2)
            flat = s.reshape(2 * HALF_ROWS, -1).astype(BF16)
            field = dot(v[:, at, :].reshape(2 * HALF_ROWS, 2 * HALF_ROWS).astype(BF16), flat)
            scale = jnp.concatenate([mean[at, :]] * (s.shape[2] // LANE), axis=1)
            fields.append(field.reshape(s.shape) + s * scale[None])
        both = jnp.concatenate(fields, axis=1).astype(BF16)
        at = slice(pair * 2 * SUB, (pair + 1) * 2 * SUB)
        out[:, :, at, :] = both.reshape(2, NBLK, 2 * SUB, -1)
        copies.append(
            pltpu.make_async_copy(out.at[:, :, at, :], out_hbm.at[:, :, at, :], sem.at[pair])
        )
        copies[-1].start()
    for copy in copies:
        copy.wait()


def mode_fields(half, other, spread, spectra, share):
    shape = (2, NBLK, NFREQ, sum(s.shape[2] for s in spectra))
    return pl.pallas_call(
        functools.partial(mode_kernel, len(spectra), share),
        out_shape=[
            jax.ShapeDtypeStruct(shape, BF16),
            jax.ShapeDtypeStruct((NBLK, NBLK, 2, share), F32),
        ],
        in_specs=[VMEM] * (3 + len(spectra)),
        out_specs=[HBM, VMEM],
        scratch_shapes=[
            pltpu.VMEM(shape, BF16),
            pltpu.VMEM((2 * NBLK, NFREQ, 2 * HALF_ROWS), F32),
            pltpu.VMEM((NFREQ, LANE), F32),
            pltpu.VMEM((PACKED, NFREQ), F32),
            pltpu.VMEM((PACKED, NFREQ), F32),
            pltpu.VMEM((NBLK + 2 * CORNER, SUB, NFREQ), F32),
            pltpu.SemaphoreType.DMA((GROUPS // 2,)),
        ]
        + [
            pltpu.VMEM((2, NBLK, SUB, NFREQ), F32),
            pltpu.VMEM((2, CORNER, SUB, NFREQ), F32),
        ]
        * MATS,
        compiler_params=pltpu.CompilerParams(vmem_limit_bytes=32 * 2**20),
    )(half, other, spread, *spectra)


def swap(x, axes, mask, size):
    return lax.ppermute(x, axes, [(i, i ^ mask) for i in range(size)])


def powers(size):
    return [1 << i for i in range(size.bit_length() - 1)]


def body(snapshots, weights, block_order, owner, offsets):
    lanes = lax.axis_size("tm")
    groups = lax.axis_size("sx") * lax.axis_size("sy")
    points = snapshots.shape[2]
    half, quarter = points // 2, points // 4
    chunks = [(0, half), (half, quarter), (half + quarter, quarter)]
    scale = 1.0 / (lanes * groups * points)
    tables = (jnp.asarray(fourier_tables()), jnp.asarray(pick_table()))
    weights = weights.reshape(1, -1)

    def send(packed, begin, end):
        return [swap(p, "tm", d, lanes) for d, p in zip(range(begin, end), packed)]

    c0, c1, c2 = chunks
    packed = pack(owner, snapshots, [(*c0, NEAR, NEAR + 1)], FIRST_LIMIT)
    first = send(packed, NEAR, NEAR + 1)
    jobs = [(*c0, 0, NEAR), (*c0, NEAR + 1, lanes), (*c1, NEAR, lanes)]
    middle = pack(owner, snapshots, jobs, SECOND_LIMIT, packed)
    jobs = [(c1[0], c1[1] + c2[1], 0, NEAR), (*c2, NEAR, lanes)]
    rest = pack(owner, snapshots, jobs, LAST_LIMIT, [*first, middle[0]])
    near = [rest[0], *send(rest[1:], 1, NEAR)]
    arrived = [
        [middle[0], *send(middle[1:], 1, NEAR), *first, *send(middle[NEAR:], NEAR + 1, lanes)],
        [*near, *send(middle[lanes - 1 :], NEAR, lanes)],
        [*near, *send(rest[NEAR:], NEAR, lanes)],
    ]
    starts = (0, 0, c1[1])

    axes = ("tm", "sx", "sy")
    size = lanes * groups
    bits = [b * groups for b in powers(lanes)] + powers(groups)
    parts = [weights[:, base : base + width] for base, width in chunks]
    before = []
    for at, base in enumerate(starts):
        last = at == len(chunks) - 1
        args = (block_order, offsets, parts[at], tables, arrived[at], before, base, last, scale)
        before, before_last = gram_part(*args), before
    before, (given, scaled) = before_last, before

    other = swap(given, axes, bits[0], size)
    keep = own_part(scaled, tables[1], before[0], scale)
    spectra = [
        spectrum(block_order, offsets, tables[0], pieces, base, [keep])
        for base, pieces in zip(starts, arrived)
    ]
    half = keep.astype(F32) + other.astype(F32)
    for at in range(1, len(bits), 2):
        masks = bits[at : at + 2]
        if len(masks) == 2:
            masks.append(masks[0] ^ masks[1])
            masks = masks[1:] + masks[:1] if at > 1 else masks
        half = half.astype(BF16)
        terms = [half] + [swap(half, axes, mask, size) for mask in masks]
        terms = [t.astype(F32) for t in terms]
        while len(terms) > 1:
            terms = [a + b for a, b in zip(terms[::2], terms[1::2])]
        half = terms[0]
        if at == 1:
            half, *spectra[1:] = lax.optimization_barrier((half, *spectra[1:]))
    half, spectra[0] = lax.optimization_barrier((half, spectra[0]))
    other = swap(half, axes, bits[0], size)

    spread = jnp.asarray(spread_table())
    modes, gram = mode_fields(half, other, spread, spectra, NFREQ // groups)
    modes = jnp.transpose(modes, (0, 2, 1, 3))[:, :, :, None, :]
    return modes, jnp.transpose(gram, (2, 3, 0, 1))


def solution(mesh):
    placed = (P("tm", None, ("sx", "sy")), P(("sx", "sy")), P(), P(("sx", "sy"), None), P())
    return jax.shard_map(
        body,
        mesh=mesh,
        in_specs=placed,
        out_specs=(P(None, None, None, "tm", ("sx", "sy")), P(None, ("sx", "sy"), None, None)),
        check_vma=False,
    )
```

```python
import functools
import math

import jax
import jax.numpy as jnp
import numpy as np
from jax import lax
from jax.experimental import pallas as pl
from jax.experimental.pallas import tpu as pltpu
from jax.sharding import PartitionSpec as P

NFFT = 256
NFREQ = 128
NBLK = 11
LANE = 128
SUB = 8
HALF_ROWS = NBLK * SUB
GROUPS = NFREQ // SUB
MATS = 7
NEAR = 2
PACKED = 128
HALF = PACKED // 2
STACK = 4
CORNER = NBLK - SUB
WIDE = 2 * LANE
FIRST_LIMIT = 64 * 2**20
SECOND_LIMIT = FIRST_LIMIT - 1450 * 2**10
LAST_LIMIT = 40 * 2**20
BF16 = jnp.bfloat16
F32 = jnp.float32


def fourier_tables():
    n = np.arange(NFFT)
    k = np.arange(NFREQ)
    angles = 2.0 * np.pi * ((k[:, None] * n[None, :]) % NFFT) / NFFT
    scaled = (0.5 - 0.5 * np.cos(2.0 * np.pi * n / NFFT)) / math.sqrt(0.375 * NFFT)
    table = np.concatenate([np.cos(angles) * scaled, -np.sin(angles) * scaled], axis=0)
    high = table.astype(jnp.bfloat16)
    low = (table - high.astype(np.float64)).astype(jnp.bfloat16)
    return np.concatenate([high, low], axis=0)


def packed_rows():
    rows = {}
    for a in range(NBLK):
        for e in range(a, NBLK):
            rows[0, a, e] = len(rows)
        for e in range(a + 1, NBLK):
            rows[1, a, e] = len(rows)
    return rows


ROWS = packed_rows()


def pick_table():
    pick = np.zeros((NBLK, 2, LANE, PACKED), np.float32)
    for (part, a, e), row in ROWS.items():
        pick[a, part, e * SUB : (e + 1) * SUB, row] = 1.0
    return pick.reshape(NBLK * WIDE, PACKED).astype(jnp.bfloat16)


def spread_table():
    spread = np.zeros((2, STACK, 2, 16, WIDE), np.float32)
    for b in range(NBLK):
        first = slice(b * SUB, b * SUB + SUB)
        second = slice(HALF_ROWS + b * SUB, HALF_ROWS + b * SUB + SUB)
        spread[0, :, 0, b, first] = 1.0
        spread[0, :, 1, b, second] = 1.0
        spread[1, :, 1, b, first] = -1.0
        spread[1, :, 0, b, second] = 1.0
    return spread.reshape(2, LANE, WIDE).astype(jnp.bfloat16)


def dot(a, b):
    return jnp.dot(a, b, preferred_element_type=F32)


def dot_nt(a, b):
    return lax.dot_general(a, b, (((1,), (1,)), ((), ())), preferred_element_type=F32)


def spec(shape):
    return pl.BlockSpec(shape, lambda *_: (0,) * len(shape))


SMEM = pl.BlockSpec(memory_space=pltpu.SMEM)
VMEM = pl.BlockSpec(memory_space=pltpu.VMEM)
HBM = pl.BlockSpec(memory_space=pltpu.HBM)


def lane_pick(owner, lanes, begin, end):
    me = lax.axis_index("tm")
    rows = WIDE // lanes
    shape = ((end - begin) * rows, WIDE)
    out_row = lax.broadcasted_iota(jnp.int32, shape, 0)
    in_row = lax.broadcasted_iota(jnp.int32, shape, 1)
    row_of = (out_row % rows) * lanes
    for d in range(begin, end):
        slot = me ^ d
        source = jnp.int32(0)
        for lane in range(lanes):
            source = source + jnp.where(owner[0, lane] == slot, lane, 0)
        row_of = jnp.where(out_row // rows == d - begin, row_of + source, row_of)
    return jnp.where(in_row == row_of, 1.0, 0.0).astype(BF16)


def pack_kernel(jobs, parts, follows, owner_hbm, x_hbm, *refs):
    steps, lanes, _ = x_hbm.shape
    base = jobs[0][0]
    *outs, owner, pick, x_ref, owner_sem, x_sem = refs[follows:]
    part = steps // parts
    owner_copy = pltpu.make_async_copy(owner_hbm, owner, owner_sem)
    owner_copy.start()
    copies = []
    for i in range(parts):
        at = slice(i * part, (i + 1) * part)
        source = x_hbm.at[at, :, base : base + x_ref.shape[2]]
        copies.append(pltpu.make_async_copy(source, x_ref.at[at], x_sem.at[i]))
        copies[-1].start()
    owner_copy.wait()
    lowest = min(begin for _, _, begin, _ in jobs)
    pick[...] = lane_pick(owner, lanes, lowest, max(end for _, _, _, end in jobs))
    rows = WIDE // lanes
    for i in range(parts):
        copies[i].wait()
        for start in range(i * part, (i + 1) * part, rows):
            at = slice(start, start + rows)
            x = x_ref[at].reshape(WIDE, x_ref.shape[2])
            out = iter(outs)
            for job, width, begin, end in jobs:
                here = x[:, job - base : job - base + width]
                chosen = pick[(begin - lowest) * rows : (end - lowest) * rows, :]
                y = dot(chosen, here).astype(BF16)
                for d in range(end - begin):
                    next(out)[at, :] = y[d * rows : (d + 1) * rows]


def pack(owner, snapshots, jobs, limit, after=()):
    steps, lanes, _ = snapshots.shape
    parts = math.gcd(steps * lanes // WIDE, 3)
    outs = [
        jax.ShapeDtypeStruct((steps, width), BF16)
        for _, width, begin, end in jobs
        for _ in range(begin, end)
    ]
    columns = jobs[-1][0] + jobs[-1][1] - jobs[0][0]
    partners = max(end for _, _, _, end in jobs) - min(begin for _, _, begin, _ in jobs)
    return pl.pallas_call(
        functools.partial(pack_kernel, jobs, parts, len(after)),
        out_shape=outs,
        in_specs=[HBM] * (2 + len(after)),
        out_specs=[VMEM] * len(outs),
        scratch_shapes=[
            pltpu.SMEM(owner.shape, jnp.int32),
            pltpu.VMEM((partners * (WIDE // lanes), WIDE), BF16),
            pltpu.VMEM((steps, lanes, columns), BF16),
            pltpu.SemaphoreType.DMA,
            pltpu.SemaphoreType.DMA((parts,)),
        ],
        compiler_params=pltpu.CompilerParams(vmem_limit_bytes=limit),
        cost_estimate=pl.CostEstimate(flops=1000, bytes_accessed=1000, transcendentals=0),
    )(owner, snapshots, *after)


def fill_record(place, order_ref, pieces, record, factor):
    steps = pieces[0].shape[0]
    me = lax.axis_index("tm")
    base, partners = place
    for d, piece in zip(partners, pieces):
        start = pl.multiple_of(order_ref[me ^ d] * steps, steps)
        for c in range(record.shape[0]):
            at = c * LANE + (base if d < NEAR else 0)
            part = piece[:, at : at + LANE].astype(F32)
            if factor is not None:
                part = part * factor[:, c * LANE : (c + 1) * LANE]
            record[c, pl.ds(start, steps), :] = part


def transform(offsets_ref, f, record, s_ref):
    wanted = [(i, c) for i in range(NBLK) for c in range(record.shape[0])]
    for first in range(0, len(wanted), 2):
        pair = wanted[first : first + 2]
        x = [record[c, pl.ds(offsets_ref[i], NFFT), :].astype(BF16) for i, c in pair]
        x = jnp.concatenate(x, axis=1) if len(x) > 1 else x[0]
        y = dot(f, x)
        if f.shape[0] > NFFT:
            y = y[:NFFT] + y[NFFT:]
        for at, (i, c) in enumerate(pair):
            cols = slice(c * LANE, (c + 1) * LANE)
            s_ref[i, :, cols] = y[:NFREQ, at * LANE : (at + 1) * LANE]
            s_ref[NBLK + i, :, cols] = y[NFREQ:, at * LANE : (at + 1) * LANE]


def padded(s):
    width = s.shape[2]
    pad = jnp.zeros((LANE - HALF_ROWS, width), F32)
    real = s[:NBLK].reshape(HALF_ROWS, width)
    imag = s[NBLK:].reshape(HALF_ROWS, width)
    return jnp.concatenate([real, pad, imag, pad], axis=0)


def gram_rows(base, groups, s_ref, pick_ref, masked):
    row = lax.broadcasted_iota(jnp.int32, (HALF_ROWS, LANE), 0)
    col = lax.broadcasted_iota(jnp.int32, (HALF_ROWS, LANE), 1)
    same = row % SUB == col % SUB
    for pair in range(0, groups, 2):
        blocks = []
        for g in (pair, pair + 1):
            s = s_ref[:, pl.ds(pl.multiple_of(base + g * SUB, SUB), SUB), :]
            full = dot_nt(s.reshape(2 * HALF_ROWS, -1).astype(BF16), padded(s).astype(BF16))
            real = full[:HALF_ROWS, :LANE] + full[HALF_ROWS:, LANE:]
            imag = full[:HALF_ROWS, LANE:] - full[HALF_ROWS:, :LANE]
            blocks.append([jnp.where(same, part, 0.0) for part in (real, imag)])
        at = slice(pair * SUB, (pair + 2) * SUB)
        for a in range(NBLK):
            rows = slice(a * SUB, (a + 1) * SUB)
            for part in range(2):
                both = jnp.concatenate([block[part][rows] for block in blocks], axis=0)
                cols = slice(a * WIDE + part * LANE, a * WIDE + (part + 1) * LANE)
                masked[at, cols] = both.astype(BF16)
    return dot(masked[...], pick_ref[...])


def gram_kernel(lanes, place, scale, last, order_ref, offsets_ref, w_ref, f_ref, pick_ref, *refs):
    pieces = refs[:lanes]
    refs = refs[lanes:]
    if last:
        before_ref, gram_ref, s_ref, record, masked = refs
    else:
        *before_refs, gram_ref, record, s_ref, masked = refs
    fill_record(place, order_ref, pieces, record, jnp.sqrt(w_ref[...]))
    transform(offsets_ref, f_ref[:NFFT] if last else f_ref[...], record, s_ref)
    if not last:
        total = gram_rows(0, GROUPS, s_ref, pick_ref, masked) * scale
        gram_ref[...] = total + before_refs[0][...] if before_refs else total
        return
    half = pl.multiple_of((1 - lax.axis_index("tm") % 2) * HALF, HALF)
    total = gram_rows(half, GROUPS // 2, s_ref, pick_ref, masked) * scale
    gram_ref[...] = (total + before_ref[pl.ds(half, HALF), :]).astype(BF16)


def gram_part(order, offsets, weights, tables, pieces, before, place, last, scale):
    lanes = len(pieces)
    steps, width = pieces[-1].shape
    args = [order, offsets, weights, *tables, *pieces, *before]
    spectrum_shape = (2 * NBLK, NFREQ, width)
    scratch = [pltpu.VMEM((width // LANE, lanes * steps, LANE), F32)]
    if last:
        outs = [jax.ShapeDtypeStruct((HALF, PACKED), BF16)]
        outs.append(jax.ShapeDtypeStruct(spectrum_shape, F32))
    else:
        outs = [jax.ShapeDtypeStruct((NFREQ, PACKED), F32)]
        scratch.append(pltpu.VMEM(spectrum_shape, F32))
    scratch.append(pltpu.VMEM((HALF if last else NFREQ, NBLK * WIDE), BF16))
    return pl.pallas_call(
        functools.partial(gram_kernel, lanes, place, scale, last),
        out_shape=outs,
        in_specs=[SMEM, SMEM] + [VMEM] * (len(args) - 2),
        out_specs=[VMEM] * len(outs),
        scratch_shapes=scratch,
        compiler_params=pltpu.CompilerParams(vmem_limit_bytes=32 * 2**20),
        cost_estimate=pl.CostEstimate(flops=1000, bytes_accessed=1000, transcendentals=0),
    )(*args)


def own_kernel(scale, s_ref, pick_ref, before_ref, gram_ref, masked):
    base = pl.multiple_of(lax.axis_index("tm") % 2 * HALF, HALF)
    total = gram_rows(base, GROUPS // 2, s_ref, pick_ref, masked) * scale
    gram_ref[...] = (total + before_ref[pl.ds(base, HALF), :]).astype(BF16)


def own_part(scaled, pick, before, scale):
    return pl.pallas_call(
        functools.partial(own_kernel, scale),
        out_shape=jax.ShapeDtypeStruct((HALF, PACKED), BF16),
        in_specs=[VMEM] * 3,
        out_specs=VMEM,
        scratch_shapes=[pltpu.VMEM((HALF, NBLK * WIDE), BF16)],
        compiler_params=pltpu.CompilerParams(vmem_limit_bytes=32 * 2**20),
        cost_estimate=pl.CostEstimate(flops=10**9, bytes_accessed=3 * 10**6, transcendentals=0),
    )(scaled, pick, before)


def spectrum_kernel(lanes, place, order_ref, offsets_ref, f_ref, *refs):
    s_ref, record = refs[-2:]
    fill_record(place, order_ref, refs[:lanes], record, None)
    transform(offsets_ref, f_ref[...], record, s_ref)


def spectrum(order, offsets, fourier, pieces, place, after):
    lanes = len(pieces)
    steps, width = pieces[-1].shape
    args = [order, offsets, fourier, *pieces, *after]
    return pl.pallas_call(
        functools.partial(spectrum_kernel, lanes, place),
        out_shape=jax.ShapeDtypeStruct((2 * NBLK, NFREQ, width), F32),
        in_specs=[SMEM, SMEM] + [VMEM] * (len(args) - 2),
        out_specs=VMEM,
        scratch_shapes=[pltpu.VMEM((width // LANE, lanes * steps, LANE), F32)],
        compiler_params=pltpu.CompilerParams(vmem_limit_bytes=32 * 2**20),
        cost_estimate=pl.CostEstimate(flops=1000, bytes_accessed=1000, transcendentals=0),
    )(*args)


class Hermitian:
    def __init__(self, main, corner):
        self.main = main
        self.corner = corner

    def entry(self, a, e):
        if e < SUB:
            return self.main[0, a, pl.ds(e, 1), :], self.main[1, a, pl.ds(e, 1), :], 1
        if a < SUB:
            return self.main[0, e, pl.ds(a, 1), :], self.main[1, e, pl.ds(a, 1), :], -1
        at = pl.ds(e - SUB, 1)
        return self.corner[0, a - SUB, at, :], self.corner[1, a - SUB, at, :], 1

    def put(self, a, e, real, imag):
        if e < SUB:
            self.main[0, a, pl.ds(e, 1), :] = real
            self.main[1, a, pl.ds(e, 1), :] = imag
        elif a >= SUB:
            at = pl.ds(e - SUB, 1)
            self.corner[0, a - SUB, at, :] = real
            self.corner[1, a - SUB, at, :] = imag


def product(x, y, out, sums, diagonal=0.0, terms=()):
    sub = lax.broadcasted_iota(jnp.int32, (SUB, NFREQ), 0)
    yr = [y.main[0, b] for b in range(NBLK)]
    yi = [y.main[1, b] for b in range(NBLK)]
    minus = [yi[b] - yr[b] for b in range(NBLK)]
    plus = [yi[b] + yr[b] for b in range(NBLK)]
    for a in range(NBLK):
        sums[a] = x.main[0, a] + x.main[1, a]
    for a in range(CORNER):
        sums[NBLK + a] = x.corner[0, a] + x.corner[1, a]
        sums[NBLK + CORNER + a] = x.main[0, SUB + a] - x.main[1, SUB + a]
    for a in range(NBLK):
        k1 = k2 = k3 = None
        for b in range(NBLK):
            pr, pi, sign = x.entry(a, b)
            if b < SUB:
                both = sums[a, pl.ds(b, 1), :]
            elif a < SUB:
                both = sums[NBLK + CORNER + b - SUB, pl.ds(a, 1), :]
            else:
                both = sums[NBLK + a - SUB, pl.ds(b - SUB, 1), :]
            t1, t2, t3 = both * yr[b], pr * minus[b], pi * plus[b]
            k1 = t1 if k1 is None else k1 + t1
            k2 = t2 if k2 is None else k2 + t2
            k3 = t3 if k3 is None else k3 + t3 if sign > 0 else k3 - t3
        real, imag = k1 - k3, k1 + k2
        for factor, term in terms:
            real = real + factor * term.main[0, a]
            imag = imag + factor * term.main[1, a]
        if diagonal and a < SUB:
            real = real + jnp.where(sub == a, diagonal, 0.0)
        out.main[0, a] = real
        out.main[1, a] = imag
    ar = [[x.main[0, SUB + a], x.corner[0, a]] for a in range(CORNER)]
    ai = [[x.main[1, SUB + a], x.corner[1, a]] for a in range(CORNER)]
    er = [[yr[SUB + e], y.corner[0, e]] for e in range(CORNER)]
    ei = [[yi[SUB + e], y.corner[1, e]] for e in range(CORNER)]
    for a in range(CORNER):
        for e in range(a, CORNER):
            real = sum(ar[a][h] * er[e][h] + ai[a][h] * ei[e][h] for h in range(2))
            real = jnp.sum(real, axis=0, keepdims=True)
            imag = jnp.zeros_like(real)
            if a != e:
                imag = sum(ai[a][h] * er[e][h] - ar[a][h] * ei[e][h] for h in range(2))
                imag = jnp.sum(imag, axis=0, keepdims=True)
            for factor, term in terms:
                r, i, _ = term.entry(SUB + a, SUB + e)
                real, imag = real + factor * r, imag + factor * i
            if a == e:
                out.put(SUB + a, SUB + a, real + diagonal, jnp.zeros_like(real))
            else:
                out.put(SUB + a, SUB + e, real, imag)
                out.put(SUB + e, SUB + a, real, -imag)


def combine(out, diagonal, terms):
    sub = lax.broadcasted_iota(jnp.int32, (SUB, NFREQ), 0)
    for name, rows in (("main", NBLK), ("corner", CORNER)):
        target = getattr(out, name)
        for a in range(rows):
            real = sum(factor * getattr(term, name)[0, a] for factor, term in terms)
            imag = sum(factor * getattr(term, name)[1, a] for factor, term in terms)
            if diagonal and (name == "corner" or a < SUB):
                real = real + jnp.where(sub == a, diagonal, 0.0)
            target[0, a] = real
            target[1, a] = imag


TWO_STEPS = (2.25, -2.4375, 1.6875, -0.5625, 0.0625)


def inverse_root(w, mats, sums):
    q, u, r, t, w2, z = mats
    c0, c1, c2, c3, c4 = TWO_STEPS
    product(w, w, q, sums)
    combine(u, 0.0, [(c3, w), (c4, q)])
    product(q, u, z, sums, c0, [(c1, w), (c2, q)])
    product(z, z, t, sums)
    product(w, t, w2, sums)
    product(w2, w2, q, sums)
    combine(u, 0.0, [(c3, w2), (c4, q)])
    product(q, u, r, sums, c0, [(c1, w2), (c2, q)])
    product(r, r, t, sums)
    product(z, r, u, sums)
    product(w2, t, q, sums)
    combine(q, 1.5, [(-0.5, q)])
    product(u, q, z, sums)
    return z


def make_roots(share, half_ref, other_ref, gram_ref, packed, rolled, sums, mats):
    core = lax.axis_index("tm") % 2
    packed[pl.ds(pl.multiple_of(core * HALF, HALF), HALF), :] = half_ref[...]
    packed[pl.ds(pl.multiple_of((1 - core) * HALF, HALF), HALF), :] = other_ref[...]
    packed[...] = packed[...].T
    at = lax.axis_index("sx") * lax.axis_size("sy") + lax.axis_index("sy")
    rolled[...] = pltpu.roll(packed[...], (NFREQ - at * share) % NFREQ, 1)
    y, *free = [Hermitian(mats[2 * i], mats[2 * i + 1]) for i in range(MATS)]
    for ref in mats[1::2]:
        ref[...] = jnp.zeros_like(ref)

    def row(ref, part, a, e):
        return ref[pl.ds(ROWS[part, a, e], 1), :]

    trace = 2.0 * sum(row(packed, 0, a, a) for a in range(NBLK))
    norm = 1.0 / jnp.sqrt(trace)
    packed[...] = packed[...] / trace
    zero = jnp.zeros((1, NFREQ), F32)
    for a in range(NBLK):
        y.put(a, a, row(packed, 0, a, a), zero)
        gram_ref[a, a, 0:1, :] = row(rolled, 0, a, a)[:, :share]
        gram_ref[a, a, 1:2, :] = zero[:, :share]
        for e in range(a + 1, NBLK):
            real, imag = row(packed, 0, a, e), row(packed, 1, a, e)
            y.put(a, e, real, imag)
            y.put(e, a, real, -imag)
            real, imag = row(rolled, 0, a, e)[:, :share], row(rolled, 1, a, e)[:, :share]
            gram_ref[a, e, 0:1, :] = real
            gram_ref[e, a, 0:1, :] = real
            gram_ref[a, e, 1:2, :] = imag
            gram_ref[e, a, 1:2, :] = -imag
    z = inverse_root(y, free, sums)
    mean = sum(z.entry(a, a)[0] for a in range(NBLK)) * (1.0 / NBLK)
    sub = lax.broadcasted_iota(jnp.int32, (SUB, NFREQ), 0)
    none = jnp.zeros((SUB - CORNER, NFREQ), F32)
    first = jnp.concatenate([mean * norm, none[1:]], axis=0)
    stacks = []
    for m0 in range(0, NBLK, STACK):
        modes = range(m0, min(m0 + STACK, NBLK))
        stack = []
        for m in modes:
            for c in range(2):
                column = z.main[c, m]
                if c == 0 and m < SUB:
                    column = column - jnp.where(sub == m, mean, 0.0)
                stack.append(column * norm)
                for b in range(SUB, NBLK):
                    real, imag, sign = z.entry(m, b)
                    line = imag * sign if c else real
                    if c == 0 and m == b:
                        line = line - mean
                    stack.append(line * norm)
                stack.append(first if c == 0 and m == 0 else none)
        stack += [jnp.zeros((32, NFREQ), F32)] * (STACK - len(modes))
        stacks.append(jnp.concatenate(stack, axis=0).T)
    return stacks


def mode_kernel(chunks, share, half_ref, other_ref, spread_ref, *refs):
    s_refs = refs[:chunks]
    out_hbm, gram_ref, out, v, mean, packed, rolled, sums, sem, *mats = refs[chunks:]
    stacks = make_roots(share, half_ref, other_ref, gram_ref, packed, rolled, sums, mats)
    mean[...] = jnp.broadcast_to(stacks[0][:, NBLK : NBLK + 1], (NFREQ, LANE))
    row = lax.broadcasted_iota(jnp.int32, (NFREQ, 2 * HALF_ROWS), 0)
    col = lax.broadcasted_iota(jnp.int32, (NFREQ, 2 * HALF_ROWS), 1)
    same = row % SUB == col % SUB
    place = lax.broadcasted_iota(jnp.int32, (NFREQ, LANE), 1) // 32
    rows = [jnp.where(place == m % STACK, stacks[m // STACK], 0.0) for m in range(NBLK)]
    rows = jnp.concatenate(rows, axis=0).astype(BF16)
    for c in range(2):
        wide = dot(rows, spread_ref[c])[:, : 2 * HALF_ROWS]
        for m in range(NBLK):
            v[c * NBLK + m] = jnp.where(same, wide[m * NFREQ : (m + 1) * NFREQ], 0.0)

    copies = []
    for pair in range(GROUPS // 2):
        fields = []
        for g in (2 * pair, 2 * pair + 1):
            at = slice(g * SUB, (g + 1) * SUB)
            s = jnp.concatenate([r[:, at, :] for r in s_refs], axis=2)
            flat = s.reshape(2 * HALF_ROWS, -1).astype(BF16)
            field = dot(v[:, at, :].reshape(2 * HALF_ROWS, 2 * HALF_ROWS).astype(BF16), flat)
            scale = jnp.concatenate([mean[at, :]] * (s.shape[2] // LANE), axis=1)
            fields.append(field.reshape(s.shape) + s * scale[None])
        both = jnp.concatenate(fields, axis=1).astype(BF16)
        at = slice(pair * 2 * SUB, (pair + 1) * 2 * SUB)
        out[:, :, at, :] = both.reshape(2, NBLK, 2 * SUB, -1)
        copies.append(
            pltpu.make_async_copy(out.at[:, :, at, :], out_hbm.at[:, :, at, :], sem.at[pair])
        )
        copies[-1].start()
    for copy in copies:
        copy.wait()


def mode_fields(half, other, spread, spectra, share):
    shape = (2, NBLK, NFREQ, sum(s.shape[2] for s in spectra))
    return pl.pallas_call(
        functools.partial(mode_kernel, len(spectra), share),
        out_shape=[
            jax.ShapeDtypeStruct(shape, BF16),
            jax.ShapeDtypeStruct((NBLK, NBLK, 2, share), F32),
        ],
        in_specs=[VMEM] * (3 + len(spectra)),
        out_specs=[HBM, VMEM],
        scratch_shapes=[
            pltpu.VMEM(shape, BF16),
            pltpu.VMEM((2 * NBLK, NFREQ, 2 * HALF_ROWS), F32),
            pltpu.VMEM((NFREQ, LANE), F32),
            pltpu.VMEM((PACKED, NFREQ), F32),
            pltpu.VMEM((PACKED, NFREQ), F32),
            pltpu.VMEM((NBLK + 2 * CORNER, SUB, NFREQ), F32),
            pltpu.SemaphoreType.DMA((GROUPS // 2,)),
        ]
        + [
            pltpu.VMEM((2, NBLK, SUB, NFREQ), F32),
            pltpu.VMEM((2, CORNER, SUB, NFREQ), F32),
        ]
        * MATS,
        compiler_params=pltpu.CompilerParams(vmem_limit_bytes=32 * 2**20),
    )(half, other, spread, *spectra)


def swap(x, axes, mask, size):
    return lax.ppermute(x, axes, [(i, i ^ mask) for i in range(size)])


def powers(size):
    return [1 << i for i in range(size.bit_length() - 1)]


def body(snapshots, weights, block_order, owner, offsets):
    lanes = lax.axis_size("tm")
    groups = lax.axis_size("sx") * lax.axis_size("sy")
    points = snapshots.shape[2]
    half, quarter = points // 2, points // 4
    chunks = [(0, half), (half, quarter), (half + quarter, quarter)]
    scale = 1.0 / (lanes * groups * points)
    tables = (jnp.asarray(fourier_tables()), jnp.asarray(pick_table()))
    weights = weights.reshape(1, -1)

    def send(packed, begin, end):
        return [swap(p, "tm", d, lanes) for d, p in zip(range(begin, end), packed)]

    c0, c1, c2 = chunks
    packed = pack(owner, snapshots, [(*c0, NEAR, NEAR + 1)], FIRST_LIMIT)
    first = send(packed, NEAR, NEAR + 1)
    jobs = [(*c0, 0, NEAR), (*c0, NEAR + 1, lanes), (*c1, NEAR, lanes)]
    middle = pack(owner, snapshots, jobs, SECOND_LIMIT, packed)
    jobs = [(c1[0], c1[1] + c2[1], 0, NEAR), (*c2, NEAR, lanes)]
    rest = pack(owner, snapshots, jobs, LAST_LIMIT, [*first, middle[0]])
    near = [rest[0], *send(rest[1:], 1, NEAR)]
    arrived = [
        [middle[0], *send(middle[1:], 1, NEAR), *first, *send(middle[NEAR:], NEAR + 1, lanes)],
        [*near, *send(middle[lanes - 1 :], NEAR, lanes)],
        [*near, *send(rest[NEAR:], NEAR, lanes)[::-1]],
    ]
    natural = tuple(range(lanes))
    turned = natural[:NEAR] + natural[NEAR:][::-1]
    places = ((0, natural), (0, natural), (c1[1], turned))

    axes = ("tm", "sx", "sy")
    size = lanes * groups
    bits = [b * groups for b in powers(lanes)] + powers(groups)
    parts = [weights[:, base : base + width] for base, width in chunks]
    before = []
    for at, place in enumerate(places):
        last = at == len(chunks) - 1
        args = (block_order, offsets, parts[at], tables, arrived[at], before, place, last, scale)
        before, before_last = gram_part(*args), before
    before, (given, scaled) = before_last, before

    other = swap(given, axes, bits[0], size)
    keep = own_part(scaled, tables[1], before[0], scale)
    spectra = [
        spectrum(block_order, offsets, tables[0], pieces, place, [keep])
        for place, pieces in zip(places, arrived)
    ]
    half = keep.astype(F32) + other.astype(F32)
    for at in range(1, len(bits), 2):
        masks = bits[at : at + 2]
        if len(masks) == 2:
            masks.append(masks[0] ^ masks[1])
            masks = masks[1:] + masks[:1] if at > 1 else masks
        half = half.astype(BF16)
        terms = [half] + [swap(half, axes, mask, size) for mask in masks]
        terms = [t.astype(F32) for t in terms]
        while len(terms) > 1:
            terms = [a + b for a, b in zip(terms[::2], terms[1::2])]
        half = terms[0]
        if at == 1:
            half, *spectra[1:] = lax.optimization_barrier((half, *spectra[1:]))
    half, spectra[0] = lax.optimization_barrier((half, spectra[0]))
    other = swap(half, axes, bits[0], size)

    spread = jnp.asarray(spread_table())
    modes, gram = mode_fields(half, other, spread, spectra, NFREQ // groups)
    modes = jnp.transpose(modes, (0, 2, 1, 3))[:, :, :, None, :]
    return modes, jnp.transpose(gram, (2, 3, 0, 1))


def solution(mesh):
    placed = (P("tm", None, ("sx", "sy")), P(("sx", "sy")), P(), P(("sx", "sy"), None), P())
    return jax.shard_map(
        body,
        mesh=mesh,
        in_specs=placed,
        out_specs=(P(None, None, None, "tm", ("sx", "sy")), P(None, ("sx", "sy"), None, None)),
        check_vma=False,
    )
```

```python
import functools
import math

import jax
import jax.numpy as jnp
import numpy as np
from jax import lax
from jax.experimental import pallas as pl
from jax.experimental.pallas import tpu as pltpu
from jax.sharding import PartitionSpec as P

NFFT = 256
NFREQ = 128
NBLK = 11
LANE = 128
SUB = 8
HALF_ROWS = NBLK * SUB
GROUPS = NFREQ // SUB
MATS = 7
NEAR = 2
PACKED = 128
HALF = PACKED // 2
STACK = 4
CORNER = NBLK - SUB
WIDE = 2 * LANE
FIRST_LIMIT = 64 * 2**20
SECOND_LIMIT = FIRST_LIMIT - 1450 * 2**10
LAST_LIMIT = 40 * 2**20
BF16 = jnp.bfloat16
F32 = jnp.float32


def fourier_tables():
    n = np.arange(NFFT)
    k = np.arange(NFREQ)
    angles = 2.0 * np.pi * ((k[:, None] * n[None, :]) % NFFT) / NFFT
    scaled = (0.5 - 0.5 * np.cos(2.0 * np.pi * n / NFFT)) / math.sqrt(0.375 * NFFT)
    table = np.concatenate([np.cos(angles) * scaled, -np.sin(angles) * scaled], axis=0)
    high = table.astype(jnp.bfloat16)
    low = (table - high.astype(np.float64)).astype(jnp.bfloat16)
    return np.concatenate([high, low], axis=0)


def packed_rows():
    rows = {}
    for a in range(NBLK):
        for e in range(a, NBLK):
            rows[0, a, e] = len(rows)
        for e in range(a + 1, NBLK):
            rows[1, a, e] = len(rows)
    return rows


ROWS = packed_rows()


def pick_table():
    pick = np.zeros((NBLK, 2, LANE, PACKED), np.float32)
    for (part, a, e), row in ROWS.items():
        pick[a, part, e * SUB : (e + 1) * SUB, row] = 1.0
    return pick.reshape(NBLK * WIDE, PACKED).astype(jnp.bfloat16)


def spread_table():
    spread = np.zeros((2, STACK, 2, 16, WIDE), np.float32)
    for b in range(NBLK):
        first = slice(b * SUB, b * SUB + SUB)
        second = slice(HALF_ROWS + b * SUB, HALF_ROWS + b * SUB + SUB)
        spread[0, :, 0, b, first] = 1.0
        spread[0, :, 1, b, second] = 1.0
        spread[1, :, 1, b, first] = -1.0
        spread[1, :, 0, b, second] = 1.0
    return spread.reshape(2, LANE, WIDE).astype(jnp.bfloat16)


def dot(a, b):
    return jnp.dot(a, b, preferred_element_type=F32)


def dot_nt(a, b):
    return lax.dot_general(a, b, (((1,), (1,)), ((), ())), preferred_element_type=F32)


def spec(shape):
    return pl.BlockSpec(shape, lambda *_: (0,) * len(shape))


SMEM = pl.BlockSpec(memory_space=pltpu.SMEM)
VMEM = pl.BlockSpec(memory_space=pltpu.VMEM)
HBM = pl.BlockSpec(memory_space=pltpu.HBM)


def lane_pick(owner, lanes, begin, end):
    me = lax.axis_index("tm")
    rows = WIDE // lanes
    shape = ((end - begin) * rows, WIDE)
    out_row = lax.broadcasted_iota(jnp.int32, shape, 0)
    in_row = lax.broadcasted_iota(jnp.int32, shape, 1)
    row_of = (out_row % rows) * lanes
    for d in range(begin, end):
        slot = me ^ d
        source = jnp.int32(0)
        for lane in range(lanes):
            source = source + jnp.where(owner[0, lane] == slot, lane, 0)
        row_of = jnp.where(out_row // rows == d - begin, row_of + source, row_of)
    return jnp.where(in_row == row_of, 1.0, 0.0).astype(BF16)


def pack_kernel(jobs, parts, follows, owner_hbm, x_hbm, *refs):
    steps, lanes, _ = x_hbm.shape
    base = jobs[0][0]
    *outs, owner, pick, x_ref, owner_sem, x_sem = refs[follows:]
    part = steps // parts
    owner_copy = pltpu.make_async_copy(owner_hbm, owner, owner_sem)
    owner_copy.start()
    copies = []
    for i in range(parts):
        at = slice(i * part, (i + 1) * part)
        source = x_hbm.at[at, :, base : base + x_ref.shape[2]]
        copies.append(pltpu.make_async_copy(source, x_ref.at[at], x_sem.at[i]))
        copies[-1].start()
    owner_copy.wait()
    lowest = min(begin for _, _, begin, _ in jobs)
    pick[...] = lane_pick(owner, lanes, lowest, max(end for _, _, _, end in jobs))
    rows = WIDE // lanes
    for i in range(parts):
        copies[i].wait()
        for start in range(i * part, (i + 1) * part, rows):
            at = slice(start, start + rows)
            x = x_ref[at].reshape(WIDE, x_ref.shape[2])
            out = iter(outs)
            for job, width, begin, end in jobs:
                here = x[:, job - base : job - base + width]
                chosen = pick[(begin - lowest) * rows : (end - lowest) * rows, :]
                y = dot(chosen, here).astype(BF16)
                for d in range(end - begin):
                    next(out)[at, :] = y[d * rows : (d + 1) * rows]


def pack(owner, snapshots, jobs, limit, after=()):
    steps, lanes, _ = snapshots.shape
    parts = math.gcd(steps * lanes // WIDE, 3)
    outs = [
        jax.ShapeDtypeStruct((steps, width), BF16)
        for _, width, begin, end in jobs
        for _ in range(begin, end)
    ]
    columns = jobs[-1][0] + jobs[-1][1] - jobs[0][0]
    partners = max(end for _, _, _, end in jobs) - min(begin for _, _, begin, _ in jobs)
    return pl.pallas_call(
        functools.partial(pack_kernel, jobs, parts, len(after)),
        out_shape=outs,
        in_specs=[HBM] * (2 + len(after)),
        out_specs=[VMEM] * len(outs),
        scratch_shapes=[
            pltpu.SMEM(owner.shape, jnp.int32),
            pltpu.VMEM((partners * (WIDE // lanes), WIDE), BF16),
            pltpu.VMEM((steps, lanes, columns), BF16),
            pltpu.SemaphoreType.DMA,
            pltpu.SemaphoreType.DMA((parts,)),
        ],
        compiler_params=pltpu.CompilerParams(vmem_limit_bytes=limit),
        cost_estimate=pl.CostEstimate(flops=1000, bytes_accessed=1000, transcendentals=0),
    )(owner, snapshots, *after)


def fill_record(base, order_ref, pieces, record, factor):
    steps = pieces[0].shape[0]
    me = lax.axis_index("tm")
    for d, piece in enumerate(pieces):
        start = pl.multiple_of(order_ref[me ^ d] * steps, steps)
        for c in range(record.shape[0]):
            at = c * LANE + (base if d < NEAR else 0)
            part = piece[:, at : at + LANE].astype(F32)
            if factor is not None:
                part = part * factor[:, c * LANE : (c + 1) * LANE]
            record[c, pl.ds(start, steps), :] = part


def transform(offsets_ref, f, record, s_ref):
    wanted = [(i, c) for i in range(NBLK) for c in range(record.shape[0])]
    for first in range(0, len(wanted), 2):
        pair = wanted[first : first + 2]
        x = [record[c, pl.ds(offsets_ref[i], NFFT), :].astype(BF16) for i, c in pair]
        x = jnp.concatenate(x, axis=1) if len(x) > 1 else x[0]
        y = dot(f, x)
        if f.shape[0] > NFFT:
            y = y[:NFFT] + y[NFFT:]
        for at, (i, c) in enumerate(pair):
            cols = slice(c * LANE, (c + 1) * LANE)
            s_ref[i, :, cols] = y[:NFREQ, at * LANE : (at + 1) * LANE]
            s_ref[NBLK + i, :, cols] = y[NFREQ:, at * LANE : (at + 1) * LANE]


def padded(s):
    width = s.shape[2]
    pad = jnp.zeros((LANE - HALF_ROWS, width), F32)
    real = s[:NBLK].reshape(HALF_ROWS, width)
    imag = s[NBLK:].reshape(HALF_ROWS, width)
    return jnp.concatenate([real, pad, imag, pad], axis=0)


def gram_rows(base, groups, s_ref, pick_ref, masked):
    row = lax.broadcasted_iota(jnp.int32, (HALF_ROWS, LANE), 0)
    col = lax.broadcasted_iota(jnp.int32, (HALF_ROWS, LANE), 1)
    same = row % SUB == col % SUB
    for pair in range(0, groups, 2):
        blocks = []
        for g in (pair, pair + 1):
            s = s_ref[:, pl.ds(pl.multiple_of(base + g * SUB, SUB), SUB), :]
            full = dot_nt(s.reshape(2 * HALF_ROWS, -1).astype(BF16), padded(s).astype(BF16))
            real = full[:HALF_ROWS, :LANE] + full[HALF_ROWS:, LANE:]
            imag = full[:HALF_ROWS, LANE:] - full[HALF_ROWS:, :LANE]
            blocks.append([jnp.where(same, part, 0.0) for part in (real, imag)])
        at = slice(pair * SUB, (pair + 2) * SUB)
        for a in range(NBLK):
            rows = slice(a * SUB, (a + 1) * SUB)
            for part in range(2):
                both = jnp.concatenate([block[part][rows] for block in blocks], axis=0)
                cols = slice(a * WIDE + part * LANE, a * WIDE + (part + 1) * LANE)
                masked[at, cols] = both.astype(BF16)
    return dot(masked[...], pick_ref[...])


def gram_kernel(lanes, base, scale, last, order_ref, offsets_ref, w_ref, f_ref, pick_ref, *refs):
    pieces = refs[:lanes]
    refs = refs[lanes:]
    if last:
        before_ref, gram_ref, s_ref, record, masked = refs
    else:
        *before_refs, gram_ref, record, s_ref, masked = refs
    fill_record(base, order_ref, pieces, record, jnp.sqrt(w_ref[...]))
    transform(offsets_ref, f_ref[:NFFT] if last else f_ref[...], record, s_ref)
    if not last:
        total = gram_rows(0, GROUPS, s_ref, pick_ref, masked) * scale
        gram_ref[...] = total + before_refs[0][...] if before_refs else total
        return
    half = pl.multiple_of((1 - lax.axis_index("tm") % 2) * HALF, HALF)
    total = gram_rows(half, GROUPS // 2, s_ref, pick_ref, masked) * scale
    gram_ref[...] = (total + before_ref[pl.ds(half, HALF), :]).astype(BF16)


def gram_part(order, offsets, weights, tables, pieces, before, base, last, scale):
    lanes = len(pieces)
    steps, width = pieces[-1].shape
    args = [order, offsets, weights, *tables, *pieces, *before]
    spectrum_shape = (2 * NBLK, NFREQ, width)
    scratch = [pltpu.VMEM((width // LANE, lanes * steps, LANE), F32)]
    if last:
        outs = [jax.ShapeDtypeStruct((HALF, PACKED), BF16)]
        outs.append(jax.ShapeDtypeStruct(spectrum_shape, F32))
    else:
        outs = [jax.ShapeDtypeStruct((NFREQ, PACKED), F32)]
        scratch.append(pltpu.VMEM(spectrum_shape, F32))
    scratch.append(pltpu.VMEM((HALF if last else NFREQ, NBLK * WIDE), BF16))
    return pl.pallas_call(
        functools.partial(gram_kernel, lanes, base, scale, last),
        out_shape=outs,
        in_specs=[SMEM, SMEM] + [VMEM] * (len(args) - 2),
        out_specs=[VMEM] * len(outs),
        scratch_shapes=scratch,
        compiler_params=pltpu.CompilerParams(vmem_limit_bytes=32 * 2**20),
        cost_estimate=pl.CostEstimate(flops=1000, bytes_accessed=1000, transcendentals=0),
    )(*args)


def own_kernel(scale, s_ref, pick_ref, before_ref, gram_ref, masked):
    base = pl.multiple_of(lax.axis_index("tm") % 2 * HALF, HALF)
    total = gram_rows(base, GROUPS // 2, s_ref, pick_ref, masked) * scale
    gram_ref[...] = (total + before_ref[pl.ds(base, HALF), :]).astype(BF16)


def own_part(scaled, pick, before, scale):
    return pl.pallas_call(
        functools.partial(own_kernel, scale),
        out_shape=jax.ShapeDtypeStruct((HALF, PACKED), BF16),
        in_specs=[VMEM] * 3,
        out_specs=VMEM,
        scratch_shapes=[pltpu.VMEM((HALF, NBLK * WIDE), BF16)],
        compiler_params=pltpu.CompilerParams(vmem_limit_bytes=32 * 2**20),
        cost_estimate=pl.CostEstimate(flops=10**9, bytes_accessed=3 * 10**6, transcendentals=0),
    )(scaled, pick, before)


def spectrum_kernel(lanes, base, order_ref, offsets_ref, f_ref, *refs):
    s_ref, record = refs[-2:]
    fill_record(base, order_ref, refs[:lanes], record, None)
    transform(offsets_ref, f_ref[...], record, s_ref)


def spectrum(order, offsets, fourier, pieces, base, after):
    lanes = len(pieces)
    steps, width = pieces[-1].shape
    args = [order, offsets, fourier, *pieces, *after]
    return pl.pallas_call(
        functools.partial(spectrum_kernel, lanes, base),
        out_shape=jax.ShapeDtypeStruct((2 * NBLK, NFREQ, width), F32),
        in_specs=[SMEM, SMEM] + [VMEM] * (len(args) - 2),
        out_specs=VMEM,
        scratch_shapes=[pltpu.VMEM((width // LANE, lanes * steps, LANE), F32)],
        compiler_params=pltpu.CompilerParams(vmem_limit_bytes=32 * 2**20),
        cost_estimate=pl.CostEstimate(flops=1000, bytes_accessed=1000, transcendentals=0),
    )(*args)


class Hermitian:
    def __init__(self, main, corner):
        self.main = main
        self.corner = corner

    def entry(self, a, e):
        if e < SUB:
            return self.main[0, a, pl.ds(e, 1), :], self.main[1, a, pl.ds(e, 1), :], 1
        if a < SUB:
            return self.main[0, e, pl.ds(a, 1), :], self.main[1, e, pl.ds(a, 1), :], -1
        at = pl.ds(e - SUB, 1)
        return self.corner[0, a - SUB, at, :], self.corner[1, a - SUB, at, :], 1

    def put(self, a, e, real, imag):
        if e < SUB:
            self.main[0, a, pl.ds(e, 1), :] = real
            self.main[1, a, pl.ds(e, 1), :] = imag
        elif a >= SUB:
            at = pl.ds(e - SUB, 1)
            self.corner[0, a - SUB, at, :] = real
            self.corner[1, a - SUB, at, :] = imag


def product(x, y, out, sums, diagonal=0.0, terms=()):
    sub = lax.broadcasted_iota(jnp.int32, (SUB, NFREQ), 0)
    yr = [y.main[0, b] for b in range(NBLK)]
    yi = [y.main[1, b] for b in range(NBLK)]
    minus = [yi[b] - yr[b] for b in range(NBLK)]
    plus = [yi[b] + yr[b] for b in range(NBLK)]
    for a in range(NBLK):
        sums[a] = x.main[0, a] + x.main[1, a]
    for a in range(CORNER):
        sums[NBLK + a] = x.corner[0, a] + x.corner[1, a]
        sums[NBLK + CORNER + a] = x.main[0, SUB + a] - x.main[1, SUB + a]
    for a in range(NBLK):
        k1 = k2 = k3 = None
        for b in range(NBLK):
            pr, pi, sign = x.entry(a, b)
            if b < SUB:
                both = sums[a, pl.ds(b, 1), :]
            elif a < SUB:
                both = sums[NBLK + CORNER + b - SUB, pl.ds(a, 1), :]
            else:
                both = sums[NBLK + a - SUB, pl.ds(b - SUB, 1), :]
            t1, t2, t3 = both * yr[b], pr * minus[b], pi * plus[b]
            k1 = t1 if k1 is None else k1 + t1
            k2 = t2 if k2 is None else k2 + t2
            k3 = t3 if k3 is None else k3 + t3 if sign > 0 else k3 - t3
        real, imag = k1 - k3, k1 + k2
        for factor, term in terms:
            real = real + factor * term.main[0, a]
            imag = imag + factor * term.main[1, a]
        if diagonal and a < SUB:
            real = real + jnp.where(sub == a, diagonal, 0.0)
        out.main[0, a] = real
        out.main[1, a] = imag
    ar = [[x.main[0, SUB + a], x.corner[0, a]] for a in range(CORNER)]
    ai = [[x.main[1, SUB + a], x.corner[1, a]] for a in range(CORNER)]
    er = [[yr[SUB + e], y.corner[0, e]] for e in range(CORNER)]
    ei = [[yi[SUB + e], y.corner[1, e]] for e in range(CORNER)]
    for a in range(CORNER):
        for e in range(a, CORNER):
            real = sum(ar[a][h] * er[e][h] + ai[a][h] * ei[e][h] for h in range(2))
            real = jnp.sum(real, axis=0, keepdims=True)
            imag = jnp.zeros_like(real)
            if a != e:
                imag = sum(ai[a][h] * er[e][h] - ar[a][h] * ei[e][h] for h in range(2))
                imag = jnp.sum(imag, axis=0, keepdims=True)
            for factor, term in terms:
                r, i, _ = term.entry(SUB + a, SUB + e)
                real, imag = real + factor * r, imag + factor * i
            if a == e:
                out.put(SUB + a, SUB + a, real + diagonal, jnp.zeros_like(real))
            else:
                out.put(SUB + a, SUB + e, real, imag)
                out.put(SUB + e, SUB + a, real, -imag)


def combine(out, diagonal, terms):
    sub = lax.broadcasted_iota(jnp.int32, (SUB, NFREQ), 0)
    for name, rows in (("main", NBLK), ("corner", CORNER)):
        target = getattr(out, name)
        for a in range(rows):
            real = sum(factor * getattr(term, name)[0, a] for factor, term in terms)
            imag = sum(factor * getattr(term, name)[1, a] for factor, term in terms)
            if diagonal and (name == "corner" or a < SUB):
                real = real + jnp.where(sub == a, diagonal, 0.0)
            target[0, a] = real
            target[1, a] = imag


TWO_STEPS = (2.25, -2.4375, 1.6875, -0.5625, 0.0625)


def inverse_root(w, mats, sums):
    q, u, r, t, w2, z = mats
    c0, c1, c2, c3, c4 = TWO_STEPS
    product(w, w, q, sums)
    combine(u, 0.0, [(c3, w), (c4, q)])
    product(q, u, z, sums, c0, [(c1, w), (c2, q)])
    product(z, z, t, sums)
    product(w, t, w2, sums)
    product(w2, w2, q, sums)
    combine(u, 0.0, [(c3, w2), (c4, q)])
    product(q, u, r, sums, c0, [(c1, w2), (c2, q)])
    product(r, r, t, sums)
    product(z, r, u, sums)
    product(w2, t, q, sums)
    combine(q, 1.5, [(-0.5, q)])
    product(u, q, z, sums)
    return z


def make_roots(share, half_ref, other_ref, gram_ref, packed, rolled, sums, mats):
    core = lax.axis_index("tm") % 2
    packed[pl.ds(pl.multiple_of(core * HALF, HALF), HALF), :] = half_ref[...]
    packed[pl.ds(pl.multiple_of((1 - core) * HALF, HALF), HALF), :] = other_ref[...]
    packed[...] = packed[...].T
    at = lax.axis_index("sx") * lax.axis_size("sy") + lax.axis_index("sy")
    rolled[...] = pltpu.roll(packed[...], (NFREQ - at * share) % NFREQ, 1)
    y, *free = [Hermitian(mats[2 * i], mats[2 * i + 1]) for i in range(MATS)]
    for ref in mats[1::2]:
        ref[...] = jnp.zeros_like(ref)

    def row(ref, part, a, e):
        return ref[pl.ds(ROWS[part, a, e], 1), :]

    trace = 2.0 * sum(row(packed, 0, a, a) for a in range(NBLK))
    norm = 1.0 / jnp.sqrt(trace)
    packed[...] = packed[...] / trace
    zero = jnp.zeros((1, NFREQ), F32)
    for a in range(NBLK):
        y.put(a, a, row(packed, 0, a, a), zero)
        gram_ref[a, a, 0:1, :] = row(rolled, 0, a, a)[:, :share]
        gram_ref[a, a, 1:2, :] = zero[:, :share]
        for e in range(a + 1, NBLK):
            real, imag = row(packed, 0, a, e), row(packed, 1, a, e)
            y.put(a, e, real, imag)
            y.put(e, a, real, -imag)
            real, imag = row(rolled, 0, a, e)[:, :share], row(rolled, 1, a, e)[:, :share]
            gram_ref[a, e, 0:1, :] = real
            gram_ref[e, a, 0:1, :] = real
            gram_ref[a, e, 1:2, :] = imag
            gram_ref[e, a, 1:2, :] = -imag
    z = inverse_root(y, free, sums)
    mean = sum(z.entry(a, a)[0] for a in range(NBLK)) * (1.0 / NBLK)
    sub = lax.broadcasted_iota(jnp.int32, (SUB, NFREQ), 0)
    none = jnp.zeros((SUB - CORNER, NFREQ), F32)
    first = jnp.concatenate([mean * norm, none[1:]], axis=0)
    stacks = []
    for m0 in range(0, NBLK, STACK):
        modes = range(m0, min(m0 + STACK, NBLK))
        stack = []
        for m in modes:
            for c in range(2):
                column = z.main[c, m]
                if c == 0 and m < SUB:
                    column = column - jnp.where(sub == m, mean, 0.0)
                stack.append(column * norm)
                for b in range(SUB, NBLK):
                    real, imag, sign = z.entry(m, b)
                    line = imag * sign if c else real
                    if c == 0 and m == b:
                        line = line - mean
                    stack.append(line * norm)
                stack.append(first if c == 0 and m == 0 else none)
        stack += [jnp.zeros((32, NFREQ), F32)] * (STACK - len(modes))
        stacks.append(jnp.concatenate(stack, axis=0).T)
    return stacks


def mode_kernel(chunks, share, half_ref, other_ref, spread_ref, *refs):
    s_refs = refs[:chunks]
    out_hbm, gram_ref, out, v, mean, packed, rolled, sums, sem, *mats = refs[chunks:]
    stacks = make_roots(share, half_ref, other_ref, gram_ref, packed, rolled, sums, mats)
    mean[...] = jnp.broadcast_to(stacks[0][:, NBLK : NBLK + 1], (NFREQ, LANE))
    row = lax.broadcasted_iota(jnp.int32, (NFREQ, 2 * HALF_ROWS), 0)
    col = lax.broadcasted_iota(jnp.int32, (NFREQ, 2 * HALF_ROWS), 1)
    same = row % SUB == col % SUB
    place = lax.broadcasted_iota(jnp.int32, (NFREQ, LANE), 1) // 32
    rows = [jnp.where(place == m % STACK, stacks[m // STACK], 0.0) for m in range(NBLK)]
    rows = jnp.concatenate(rows, axis=0).astype(BF16)
    for c in range(2):
        wide = dot(rows, spread_ref[c])[:, : 2 * HALF_ROWS]
        for m in range(NBLK):
            v[c * NBLK + m] = jnp.where(same, wide[m * NFREQ : (m + 1) * NFREQ], 0.0)

    copies = []
    for pair in range(GROUPS // 2):
        fields = []
        for g in (2 * pair, 2 * pair + 1):
            at = slice(g * SUB, (g + 1) * SUB)
            s = jnp.concatenate([r[:, at, :] for r in s_refs], axis=2)
            flat = s.reshape(2 * HALF_ROWS, -1).astype(BF16)
            field = dot(v[:, at, :].reshape(2 * HALF_ROWS, 2 * HALF_ROWS).astype(BF16), flat)
            scale = jnp.concatenate([mean[at, :]] * (s.shape[2] // LANE), axis=1)
            fields.append(field.reshape(s.shape) + s * scale[None])
        both = jnp.concatenate(fields, axis=1).astype(BF16)
        at = slice(pair * 2 * SUB, (pair + 1) * 2 * SUB)
        out[:, :, at, :] = both.reshape(2, NBLK, 2 * SUB, -1)
        copies.append(
            pltpu.make_async_copy(out.at[:, :, at, :], out_hbm.at[:, :, at, :], sem.at[pair])
        )
        copies[-1].start()
    for copy in copies:
        copy.wait()


def mode_fields(half, other, spread, spectra, share):
    shape = (2, NBLK, NFREQ, sum(s.shape[2] for s in spectra))
    return pl.pallas_call(
        functools.partial(mode_kernel, len(spectra), share),
        out_shape=[
            jax.ShapeDtypeStruct(shape, BF16),
            jax.ShapeDtypeStruct((NBLK, NBLK, 2, share), F32),
        ],
        in_specs=[VMEM] * (3 + len(spectra)),
        out_specs=[HBM, VMEM],
        scratch_shapes=[
            pltpu.VMEM(shape, BF16),
            pltpu.VMEM((2 * NBLK, NFREQ, 2 * HALF_ROWS), F32),
            pltpu.VMEM((NFREQ, LANE), F32),
            pltpu.VMEM((PACKED, NFREQ), F32),
            pltpu.VMEM((PACKED, NFREQ), F32),
            pltpu.VMEM((NBLK + 2 * CORNER, SUB, NFREQ), F32),
            pltpu.SemaphoreType.DMA((GROUPS // 2,)),
        ]
        + [
            pltpu.VMEM((2, NBLK, SUB, NFREQ), F32),
            pltpu.VMEM((2, CORNER, SUB, NFREQ), F32),
        ]
        * MATS,
        compiler_params=pltpu.CompilerParams(vmem_limit_bytes=32 * 2**20),
    )(half, other, spread, *spectra)


def swap(x, axes, mask, size):
    return lax.ppermute(x, axes, [(i, i ^ mask) for i in range(size)])


def powers(size):
    return [1 << i for i in range(size.bit_length() - 1)]


def body(snapshots, weights, block_order, owner, offsets):
    lanes = lax.axis_size("tm")
    groups = lax.axis_size("sx") * lax.axis_size("sy")
    points = snapshots.shape[2]
    half, quarter = points // 2, points // 4
    chunks = [(0, half), (half, quarter), (half + quarter, quarter)]
    scale = 1.0 / (lanes * groups * points)
    tables = (jnp.asarray(fourier_tables()), jnp.asarray(pick_table()))
    weights = weights.reshape(1, -1)

    def send(packed, begin, end):
        return [swap(p, "tm", d, lanes) for d, p in zip(range(begin, end), packed)]

    c0, c1, c2 = chunks
    packed = pack(owner, snapshots, [(*c0, NEAR, NEAR + 1)], FIRST_LIMIT)
    first = send(packed, NEAR, NEAR + 1)
    jobs = [(*c0, 0, NEAR), (*c0, NEAR + 1, lanes), (*c1, NEAR, lanes)]
    middle = pack(owner, snapshots, jobs, SECOND_LIMIT, packed)
    jobs = [(c1[0], c1[1] + c2[1], 0, NEAR), (*c2, NEAR, lanes)]
    rest = pack(owner, snapshots, jobs, LAST_LIMIT, [*first, middle[0]])
    near = [rest[0], *send(rest[1:], 1, NEAR)]
    arrived = [
        [middle[0], *send(middle[1:], 1, NEAR), *first, *send(middle[NEAR:], NEAR + 1, lanes)],
        [*near, *send(middle[lanes - 1 :], NEAR, lanes)],
        [*near, *send(rest[NEAR:], NEAR, lanes)],
    ]
    starts = (0, 0, c1[1])

    axes = ("tm", "sx", "sy")
    size = lanes * groups
    bits = [b * groups for b in powers(lanes)] + powers(groups)
    parts = [weights[:, base : base + width] for base, width in chunks]
    before = []
    for at, base in enumerate(starts):
        last = at == len(chunks) - 1
        args = (block_order, offsets, parts[at], tables, arrived[at], before, base, last, scale)
        before, before_last = gram_part(*args), before
    before, (given, scaled) = before_last, before

    other = swap(given, axes, bits[0], size)
    keep = own_part(scaled, tables[1], before[0], scale)
    spectra = [
        spectrum(block_order, offsets, tables[0], pieces, base, [keep])
        for base, pieces in zip(starts, arrived)
    ]
    half = keep.astype(F32) + other.astype(F32)
    for at in range(1, len(bits), 2):
        masks = bits[at : at + 2]
        if len(masks) == 2:
            masks.append(masks[0] ^ masks[1])
            masks = masks[1:] + masks[:1] if at > 1 else masks[::-1]
        half = half.astype(BF16)
        terms = [half] + [swap(half, axes, mask, size) for mask in masks]
        terms = [t.astype(F32) for t in terms]
        while len(terms) > 1:
            terms = [a + b for a, b in zip(terms[::2], terms[1::2])]
        half = terms[0]
        if at == 1:
            half, *spectra[1:] = lax.optimization_barrier((half, *spectra[1:]))
    half, spectra[0] = lax.optimization_barrier((half, spectra[0]))
    other = swap(half, axes, bits[0], size)

    spread = jnp.asarray(spread_table())
    modes, gram = mode_fields(half, other, spread, spectra, NFREQ // groups)
    modes = jnp.transpose(modes, (0, 2, 1, 3))[:, :, :, None, :]
    return modes, jnp.transpose(gram, (2, 3, 0, 1))


def solution(mesh):
    placed = (P("tm", None, ("sx", "sy")), P(("sx", "sy")), P(), P(("sx", "sy"), None), P())
    return jax.shard_map(
        body,
        mesh=mesh,
        in_specs=placed,
        out_specs=(P(None, None, None, "tm", ("sx", "sy")), P(None, ("sx", "sy"), None, None)),
        check_vma=False,
    )
```
